32 devices in a mesh: dp: 2 (over x), fsdp: 16 (over z, y, core).
Axes of the slice: x: 2, y: 2, z: 4, core: 2. Of those that a mesh axis runs over, the one named last changes fastest.
Arguments:
- hidden: bfloat16 [64, 64, 768], P(('dp', 'fsdp')), may hold values from -6 to 6
- lengths: int32 [64], P(('dp', 'fsdp')), may hold values from 5 to 32, as said below
- features: bfloat16 [64, 257, 1408], P(('dp', 'fsdp')), may hold values from -6 to 6
- cotangent: bfloat16 [64, 64, 768], P(('dp', 'fsdp')), may hold values from -6 to 6
- self_params: bfloat16 [2363392], P('fsdp')
- cross_params: bfloat16 [3346432], P('fsdp')
- ffn_params: bfloat16 [9449472], P('fsdp')
Outputs:
- mixed: bfloat16 [64, 64, 768], P(('dp', 'fsdp'))
- hidden_grad: bfloat16 [64, 64, 768], P(('dp', 'fsdp'))
- self_grad: float32 [2363392], P('fsdp')
- cross_grad: float32 [3346432], P('fsdp')
- ffn_grad: float32 [9449472], P('fsdp')
The draws below stay inside these ranges and needn't reach their ends.
Inputs may be any that keep to these rules, and one draw needn't show every extreme that they name: lengths lie between 5 and 32; some item of every draw has 32.
All inputs are finite; a program needn't handle non-finite values.
Results may differ from the reference program's by a relative error of at most 0.017.
Values may be sent and summed in bfloat16 or wider, within the bound.
A program may use at most 384 MiB of HBM per device.

```python
import math
import jax
import jax.numpy as jnp
from jax import lax

D = 768
HEADS = 12
HDIM = 64
F = 3072
E = 1408
IMG = 257
NQ = 32
TEXT = 32
ITEMS_DEV = 2
S = 64
ITEMS = 64
SELF_FLAT = 2363392
CROSS_FLAT = 3346432
FFN_FLAT = 9449472


def draw_pieces(key, specs, total):
    pieces = []
    keys = jax.random.split(key, len(specs))
    for index in range(len(specs)):
        layout, kind, fan = specs[index]
        noise = jax.random.normal(keys[index], layout, jnp.float32)
        if kind == 'weight':
            value = noise * fan ** (-0.5)
        elif kind == 'gain':
            value = 1.0 + 0.25 * jnp.clip(noise, -2.0, 2.0)
        else:
            value = 0.3 * noise
        pieces.append(value.reshape(-1))
    flat_vec = jnp.concatenate(pieces)
    tail = 0.02 * jax.random.normal(jax.random.fold_in(key, 99), (total - flat_vec.shape[0],), jnp.float32)
    return jnp.concatenate([flat_vec, tail]).astype(jnp.bfloat16)


def draw_self_params(key, part):
    specs = [((D, D), 'weight', D)] * 3 + [((D, D), 'weight', D // 8)]
    specs = specs + [((D,), 'shift', 0)] * 3 + [((D,), 'gain', 0), ((D,), 'shift', 0)]
    return draw_pieces(key, specs, SELF_FLAT)


def draw_cross_params(key, part):
    specs = [((D, D), 'weight', D), ((E, D), 'weight', E), ((E, D), 'weight', E), ((D, D), 'weight', D // 16)]
    specs = specs + [((D,), 'shift', 0)] * 3 + [((D,), 'gain', 0), ((D,), 'shift', 0)]
    return draw_pieces(key, specs, CROSS_FLAT)


def draw_ffn_params(key, part):
    branch = [((D, F), 'weight', D), ((F,), 'shift', 0), ((F, D), 'weight', F), ((D,), 'shift', 0), ((D,), 'gain', 0), ((D,), 'shift', 0)]
    return draw_pieces(key, branch + branch, FFN_FLAT)


def draw_lengths(key, part):
    base = jax.random.randint(key, (ITEMS,), 5, TEXT + 1, dtype=jnp.int32)
    where = jax.random.randint(jax.random.fold_in(key, 7), (), 0, ITEMS, dtype=jnp.int32)
    return base.at[where].set(TEXT)


def block_levels(own_key, shape, shards, smallest, top_value):
    def one(position, parts):
        draws = jax.random.uniform(jax.random.fold_in(jax.random.fold_in(own_key, 6), position), (parts,), jnp.float32, smallest / len(shards), top_value / len(shards))
        return jnp.repeat(jnp.exp(draws), shape[position] // parts).reshape((-1,) + (1,) * (len(shape) - position - 1))

    level = one(*shards[0])
    for cut in shards[1:]:
        level = level * one(*cut)
    return level


def bell_draw(key, dims, spread, bound, cuts=(), kind=jnp.bfloat16):
    drawn = jax.random.normal(key, dims, jnp.float32) * spread
    if len(cuts) > 0:
        drawn = block_levels(key, dims, cuts, -0.22, 0.18) * drawn
    return jnp.clip(drawn, min=-bound, max=bound).astype(kind)


def setup_inputs(seed: int = 0) -> dict:
    key_list = jax.random.split(jax.random.key(seed), 8)
    hidden = bell_draw(key_list[0], (ITEMS, S, D), 1.0, 6.0, ((0, 32),))
    lengths = draw_lengths(jax.random.fold_in(key_list[7], 71), 0)
    features = bell_draw(key_list[2], (ITEMS, IMG, E), 1.0, 6.0, ((0, 32),))
    cotangent = bell_draw(key_list[3], (ITEMS, S, D), 1.0, 6.0, ((0, 32),))
    self_params = draw_self_params(jax.random.fold_in(key_list[7], 71), 0)
    cross_params = draw_cross_params(jax.random.fold_in(key_list[7], 71), 0)
    ffn_params = draw_ffn_params(jax.random.fold_in(key_list[7], 71), 0)
    return {"hidden": hidden, "lengths": lengths, "features": features, "cotangent": cotangent, "self_params": self_params, "cross_params": cross_params, "ffn_params": ffn_params}


EPS = 1e-06
SCALE = 0.125
HIGHEST = lax.Precision.HIGHEST

@jax.custom_vjp
def low(v):
    return lax.optimization_barrier(v.astype(jnp.bfloat16)).astype(jnp.float32)

@jax.custom_vjp
def low_back(v):
    return v

def low_keep(v):
    return (low(v), None)

def low_pass(kept, grad):
    return (grad,)

def back_keep(v):
    return (v, None)

def back_low(kept, grad):
    return (low(grad),)
low.defvjp(low_keep, low_pass)
low_back.defvjp(back_keep, back_low)

def self_layout():
    return [(D, D)] * 4 + [(D,)] * 5

def cross_layout():
    return [(D, D), (E, D), (E, D), (D, D)] + [(D,)] * 5

def ffn_layout():
    return [(D, F), (F,), (F, D), (D,), (D,), (D,)] * 2

def split_flat(flat_vec, layouts):
    pieces = []
    offset = 0
    for layout in layouts:
        amount = math.prod(layout)
        pieces.append(flat_vec[offset:offset + amount].reshape(layout))
        offset = offset + amount
    return pieces

def layer_norm(values, gain, shift):
    average = lax.optimization_barrier(jnp.mean(values, -1, keepdims=True))
    centered = values - average
    variance = lax.optimization_barrier(jnp.mean(centered * centered, -1, keepdims=True))
    return centered * lax.rsqrt(variance + EPS) * gain + shift

def rounded(values):
    return low_back(low(values))

def project(rows, weight):
    return jnp.einsum('isd,de->ise', rows, weight, precision=HIGHEST)

def attend(query, keys, values, mask):
    items, query_len, width = query.shape
    query_heads = query.reshape(items, query_len, HEADS, HDIM)
    key_heads = keys.reshape(items, keys.shape[1], HEADS, HDIM)
    value_heads = values.reshape(items, values.shape[1], HEADS, HDIM)
    scores = low_back(jnp.einsum('iqhd,ikhd->ihqk', query_heads, key_heads, precision=HIGHEST) * SCALE)
    if mask is not None:
        scores = jnp.where(mask, scores, -1e+30)
    probs = jax.nn.softmax(scores, axis=-1)
    context = jnp.einsum('ihqk,ikhd->iqhd', low(probs), value_heads, precision=HIGHEST)
    return context.reshape(items, query_len, width)

def feed_forward(rows, params):
    w_in, b_in, w_out, b_out, gain, shift = params
    hidden_pre = low_back(project(low(rows), w_in) + b_in)
    activated = low(jax.nn.gelu(hidden_pre, approximate=True))
    branch = low_back(project(activated, w_out) + b_out)
    return layer_norm(rows + branch, gain, shift)

def forward(hidden, features, lengths, self_flat, cross_flat, ffn_flat):
    w_q, w_k, w_v, w_o, b_q, b_v, b_o, gain_one, shift_one = split_flat(self_flat, self_layout())
    cross_wq, cross_wk, cross_wv, cross_wo, cross_bq, cross_bv, cross_bo, gain_two, shift_two = split_flat(cross_flat, cross_layout())
    ffn_parts = split_flat(ffn_flat, ffn_layout())
    seq = hidden.shape[1]
    positions = jnp.arange(seq)
    rows_at = positions[:, None]
    cols_at = positions[None, :]
    allowed = (cols_at < NQ)[None] | ((rows_at >= NQ) & (cols_at <= rows_at))[None] & (cols_at[None] < NQ + lengths[:, None, None])
    allowed = allowed[:, None]
    queries = rounded(project(hidden, w_q) + b_q)
    keys = rounded(project(hidden, w_k))
    values = rounded(project(hidden, w_v) + b_v)
    context = rounded(attend(queries, keys, values, allowed))
    attn_out = low_back(project(context, w_o) + b_o)
    first = layer_norm(hidden + attn_out, gain_one, shift_one)
    query_rows = first[:, :NQ]
    text_rows = first[:, NQ:]
    cross_query = rounded(project(low(query_rows), cross_wq) + cross_bq)
    cross_key = rounded(project(features, cross_wk))
    cross_value = rounded(project(features, cross_wv) + cross_bv)
    cross_context = rounded(attend(cross_query, cross_key, cross_value, None))
    cross_out = low_back(project(cross_context, cross_wo) + cross_bo)
    second = layer_norm(query_rows + cross_out, gain_two, shift_two)
    query_final = feed_forward(second, ffn_parts[:6])
    text_final = feed_forward(text_rows, ffn_parts[6:])
    return jnp.concatenate([query_final, text_final], 1)

def reference(hidden, lengths, features, cotangent, self_params, cross_params, ffn_params):
    blocks = hidden.shape[0] // ITEMS_DEV
    flats = (self_params.astype(jnp.float32), cross_params.astype(jnp.float32), ffn_params.astype(jnp.float32))

    def one_block(totals, index):
        start = (index * ITEMS_DEV).astype(jnp.int32)
        block_hidden = lax.dynamic_slice_in_dim(hidden, start, ITEMS_DEV, 0).astype(jnp.float32)
        block_feat = lax.dynamic_slice_in_dim(features, start, ITEMS_DEV, 0).astype(jnp.float32)
        block_lens = lax.dynamic_slice_in_dim(lengths, start, ITEMS_DEV, 0)
        block_cot = lax.dynamic_slice_in_dim(cotangent, start, ITEMS_DEV, 0).astype(jnp.float32)

        def local(states, first_flat, second_flat, third_flat):
            return forward(states, block_feat, block_lens, first_flat, second_flat, third_flat)
        outputs, pullback = jax.vjp(local, block_hidden, flats[0], flats[1], flats[2])
        grads = pullback(block_cot)
        totals = (totals[0] + grads[1], totals[1] + grads[2], totals[2] + grads[3])
        return (totals, (outputs.astype(jnp.bfloat16), grads[0].astype(jnp.bfloat16)))
    zeros = (jnp.zeros(flats[0].shape, jnp.float32), jnp.zeros(flats[1].shape, jnp.float32), jnp.zeros(flats[2].shape, jnp.float32))
    totals, stacked = lax.scan(one_block, zeros, jnp.arange(blocks, dtype=jnp.int32))
    mixed = stacked[0].reshape(hidden.shape)
    hidden_grad = stacked[1].reshape(hidden.shape)
    return (mixed, hidden_grad, totals[0], totals[1], totals[2])
```

```python
from functools import partial
import math

import jax
import jax.numpy as jnp
from jax import lax
from jax.experimental import pallas as pl
from jax.experimental.pallas import tpu as pltpu
from jax.sharding import PartitionSpec as P

D = 768
HEADS = 12
HDIM = 64
F = 3072
E = 1408
NQ = 32


EPS = 1e-06
SCALE = 0.125


def self_layout():
    return [(D, D)] * 4 + [(D,)] * 5


def cross_layout():
    return [(D, D), (E, D), (E, D), (D, D)] + [(D,)] * 5


def ffn_layout():
    return [(D, F), (F,), (F, D), (D,), (D,), (D,)] * 2


def split_flat(flat_vec, layouts):
    pieces = []
    offset = 0
    for layout in layouts:
        amount = math.prod(layout)
        pieces.append(flat_vec[offset : offset + amount].reshape(layout))
        offset = offset + amount
    return pieces


def join_flat(pieces, length):
    flat_vec = jnp.concatenate([piece.reshape(-1) for piece in pieces])
    return jnp.pad(flat_vec, (0, length - flat_vec.shape[0]))


def regroup(flat_vec):
    groups = lax.axis_size("fsdp")
    replicas = lax.axis_size("dp")
    return flat_vec.reshape(groups, replicas, -1).transpose(1, 0, 2).reshape(-1)


def matmul(left, right):
    return jnp.dot(left, right, preferred_element_type=jnp.float32)


def matmul_left(left, right):
    return lax.dot_general(
        left, right, (((0,), (0,)), ((), ())), preferred_element_type=jnp.float32
    )


def matmul_right(left, right):
    return lax.dot_general(
        left, right, (((1,), (1,)), ((), ())), preferred_element_type=jnp.float32
    )


def column_sum(values):
    return jnp.sum(values.astype(jnp.float32), 0)


def layer_norm(values, gain, shift):
    average = jnp.mean(values, -1, keepdims=True)
    centered = values - average
    variance = jnp.mean(centered * centered, -1, keepdims=True)
    return centered * lax.rsqrt(variance + EPS) * gain + shift


def norm_backward(summed, gain, shift, grad_out):
    _, norm_pull = jax.vjp(layer_norm, summed, gain.astype(jnp.float32), shift.astype(jnp.float32))
    return norm_pull(grad_out)


def heads(rows, items):
    return rows.reshape(items, -1, HEADS, HDIM)


def score_block(query, keys, mask):
    scores = jnp.einsum("iqhd,ikhd->ihqk", query, keys, preferred_element_type=jnp.float32) * SCALE
    if mask is not None:
        scores = jnp.where(mask, scores, -1e30)
    return scores


def attend(query, keys, values, mask):
    scores = score_block(query, keys, mask)
    top_sum = jax.nn.logsumexp(scores, axis=-1)
    probs = jnp.exp(scores - top_sum[..., None]).astype(jnp.bfloat16)
    context = jnp.einsum("ihqk,ikhd->iqhd", probs, values, preferred_element_type=jnp.float32)
    return (context, top_sum)


def attend_back(query, keys, values, mask, top_sum, grad_context):
    probs = jnp.exp(score_block(query, keys, mask) - top_sum[..., None])
    grad_probs = jnp.einsum(
        "iqhd,ikhd->ihqk", grad_context, values, preferred_element_type=jnp.float32
    )
    inner = jnp.sum(probs * grad_probs, -1, keepdims=True)
    grad_scores = (probs * (grad_probs - inner)).astype(jnp.bfloat16)
    grad_query = (
        jnp.einsum("ihqk,ikhd->iqhd", grad_scores, keys, preferred_element_type=jnp.float32) * SCALE
    )
    grad_keys = (
        jnp.einsum("ihqk,iqhd->ikhd", grad_scores, query, preferred_element_type=jnp.float32)
        * SCALE
    )
    grad_values = jnp.einsum(
        "ihqk,iqhd->ikhd",
        probs.astype(jnp.bfloat16),
        grad_context,
        preferred_element_type=jnp.float32,
    )
    return (grad_query, grad_keys, grad_values)


def linear_back(inputs, weight, grad_out):
    return (matmul_left(inputs, grad_out), column_sum(grad_out), matmul_right(grad_out, weight))


def ffn_forward(rows, params):
    w_in, b_in, w_out, b_out, gain, shift = params
    rows_low = rows.astype(jnp.bfloat16)
    hidden_pre = matmul(rows_low, w_in) + b_in
    activated = jax.nn.gelu(hidden_pre, approximate=True).astype(jnp.bfloat16)
    summed = rows + (matmul(activated, w_out) + b_out)
    final = layer_norm(summed, gain.astype(jnp.float32), shift.astype(jnp.float32))
    return (final, (rows_low, hidden_pre, activated, summed))


def ffn_backward(grad_out, kept, params):
    w_in, b_in, w_out, b_out, gain, shift = params
    rows_low, hidden_pre, activated, summed = kept
    grad_sum, grad_gain, grad_shift = norm_backward(summed, gain, shift, grad_out)
    grad_branch = grad_sum.astype(jnp.bfloat16)
    grad_w_out, grad_b_out, grad_act = linear_back(activated, w_out, grad_branch)
    _, gelu_pull = jax.vjp(partial(jax.nn.gelu, approximate=True), hidden_pre)
    grad_pre = gelu_pull(grad_act)[0].astype(jnp.bfloat16)
    grad_w_in, grad_b_in, grad_rows = linear_back(rows_low, w_in, grad_pre)
    return (
        grad_sum + grad_rows,
        [grad_w_in, grad_b_in, grad_w_out, grad_b_out, grad_gain, grad_shift],
    )


def per_device(hidden, lengths, features, cotangent, self_params, cross_params, ffn_params):
    items, seq, width = hidden.shape
    self_full = lax.all_gather(self_params, "fsdp", axis=0, tiled=True)
    self_parts = split_flat(self_full, self_layout())
    w_q, w_k, w_v, w_o, b_q, b_v, b_o, gain_one, shift_one = self_parts
    positions = jnp.arange(seq)
    rows_at = positions[:, None]
    cols_at = positions[None, :]
    allowed = (cols_at < NQ)[None] | ((rows_at >= NQ) & (cols_at <= rows_at))[None] & (
        cols_at[None] < NQ + lengths[:, None, None]
    )
    allowed = allowed[:, None]
    inputs = hidden.reshape(-1, width)
    query_low = (matmul(inputs, w_q) + b_q).astype(jnp.bfloat16)
    key_low = matmul(inputs, w_k).astype(jnp.bfloat16)
    value_low = (matmul(inputs, w_v) + b_v).astype(jnp.bfloat16)
    context, self_top = attend(
        heads(query_low, items), heads(key_low, items), heads(value_low, items), allowed
    )
    context_low = context.reshape(-1, width).astype(jnp.bfloat16)
    summed_one = inputs.astype(jnp.float32) + (matmul(context_low, w_o) + b_o)
    first = layer_norm(summed_one, gain_one.astype(jnp.float32), shift_one.astype(jnp.float32))
    first_items = first.reshape(items, seq, width)
    query_rows = first_items[:, :NQ].reshape(-1, width)
    text_rows = first_items[:, NQ:].reshape(-1, width)
    cross_full = lax.all_gather(cross_params, "fsdp", axis=0, tiled=True)
    cross_parts = split_flat(cross_full, cross_layout())
    cross_wq, cross_wk, cross_wv, cross_wo, cross_bq, cross_bv, cross_bo, gain_two, shift_two = (
        cross_parts
    )
    query_in = query_rows.astype(jnp.bfloat16)
    image_rows = features.reshape(-1, features.shape[-1])
    cross_query = (matmul(query_in, cross_wq) + cross_bq).astype(jnp.bfloat16)
    cross_key = matmul(image_rows, cross_wk).astype(jnp.bfloat16)
    cross_value = (matmul(image_rows, cross_wv) + cross_bv).astype(jnp.bfloat16)
    cross_context, cross_top = attend(
        heads(cross_query, items), heads(cross_key, items), heads(cross_value, items), None
    )
    cross_low = cross_context.reshape(-1, width).astype(jnp.bfloat16)
    summed_two = query_rows + (matmul(cross_low, cross_wo) + cross_bo)
    second = layer_norm(summed_two, gain_two.astype(jnp.float32), shift_two.astype(jnp.float32))
    ffn_full = lax.all_gather(ffn_params, "fsdp", axis=0, tiled=True)
    ffn_parts = split_flat(ffn_full, ffn_layout())
    query_final, query_kept = ffn_forward(second, ffn_parts[:6])
    text_final, text_kept = ffn_forward(text_rows, ffn_parts[6:])
    mixed = jnp.concatenate(
        [query_final.reshape(items, NQ, width), text_final.reshape(items, -1, width)], 1
    ).astype(jnp.bfloat16)
    grad_items = cotangent.astype(jnp.float32)
    grad_query_final = grad_items[:, :NQ].reshape(-1, width)
    grad_text_final = grad_items[:, NQ:].reshape(-1, width)
    ffn_back = split_flat(lax.all_gather(ffn_params, "fsdp", axis=0, tiled=True), ffn_layout())
    grad_second, query_grads = ffn_backward(grad_query_final, query_kept, ffn_back[:6])
    grad_text, text_grads = ffn_backward(grad_text_final, text_kept, ffn_back[6:])
    ffn_flat_grad = join_flat(query_grads + text_grads, ffn_full.shape[0])
    ffn_grad = lax.psum_scatter(
        regroup(ffn_flat_grad), ("dp", "fsdp"), scatter_dimension=0, tiled=True
    )
    cross_back = split_flat(
        lax.all_gather(cross_params, "fsdp", axis=0, tiled=True), cross_layout()
    )
    grad_summed_two, grad_gain_two, grad_shift_two = norm_backward(
        summed_two, cross_back[7], cross_back[8], grad_second
    )
    grad_cross_out = grad_summed_two.astype(jnp.bfloat16)
    grad_cross_wo, grad_cross_bo, grad_cross_ctx = linear_back(
        cross_low, cross_back[3], grad_cross_out
    )
    grad_cq, grad_ck, grad_cv = attend_back(
        heads(cross_query, items),
        heads(cross_key, items),
        heads(cross_value, items),
        None,
        cross_top,
        heads(grad_cross_ctx.astype(jnp.bfloat16), items),
    )
    grad_cq = grad_cq.reshape(-1, width).astype(jnp.bfloat16)
    grad_ck = grad_ck.reshape(-1, width).astype(jnp.bfloat16)
    grad_cv = grad_cv.reshape(-1, width).astype(jnp.bfloat16)
    grad_cross_wq, grad_cross_bq, grad_query_in = linear_back(query_in, cross_back[0], grad_cq)
    grad_cross_wk = matmul_left(image_rows, grad_ck)
    grad_cross_wv = matmul_left(image_rows, grad_cv)
    grad_cross_bv = column_sum(grad_cv)
    grad_query_rows = grad_summed_two + grad_query_in
    cross_list = [
        grad_cross_wq,
        grad_cross_wk,
        grad_cross_wv,
        grad_cross_wo,
        grad_cross_bq,
        grad_cross_bv,
        grad_cross_bo,
        grad_gain_two,
        grad_shift_two,
    ]
    cross_flat_grad = join_flat(cross_list, cross_full.shape[0])
    cross_grad = lax.psum_scatter(
        regroup(cross_flat_grad), ("dp", "fsdp"), scatter_dimension=0, tiled=True
    )
    self_back = split_flat(lax.all_gather(self_params, "fsdp", axis=0, tiled=True), self_layout())
    grad_first = jnp.concatenate(
        [grad_query_rows.reshape(items, NQ, width), grad_text.reshape(items, -1, width)], 1
    ).reshape(-1, width)
    grad_summed_one, grad_gain_one, grad_shift_one = norm_backward(
        summed_one, self_back[7], self_back[8], grad_first
    )
    grad_attn = grad_summed_one.astype(jnp.bfloat16)
    grad_w_o, grad_b_o, grad_ctx = linear_back(context_low, self_back[3], grad_attn)
    grad_q, grad_k, grad_v = attend_back(
        heads(query_low, items),
        heads(key_low, items),
        heads(value_low, items),
        allowed,
        self_top,
        heads(grad_ctx.astype(jnp.bfloat16), items),
    )
    grad_q = grad_q.reshape(-1, width).astype(jnp.bfloat16)
    grad_k = grad_k.reshape(-1, width).astype(jnp.bfloat16)
    grad_v = grad_v.reshape(-1, width).astype(jnp.bfloat16)
    grad_w_q, grad_b_q, input_from_q = linear_back(inputs, self_back[0], grad_q)
    grad_w_k = matmul_left(inputs, grad_k)
    input_from_k = matmul_right(grad_k, self_back[1])
    grad_w_v, grad_b_v, input_from_v = linear_back(inputs, self_back[2], grad_v)
    hidden_grad = (
        (grad_summed_one + input_from_q + input_from_k + input_from_v)
        .reshape(items, seq, width)
        .astype(jnp.bfloat16)
    )
    self_list = [
        grad_w_q,
        grad_w_k,
        grad_w_v,
        grad_w_o,
        grad_b_q,
        grad_b_v,
        grad_b_o,
        grad_gain_one,
        grad_shift_one,
    ]
    self_flat_grad = join_flat(self_list, self_full.shape[0])
    self_grad = lax.psum_scatter(
        regroup(self_flat_grad), ("dp", "fsdp"), scatter_dimension=0, tiled=True
    )
    self_grad, cross_grad, ffn_grad = (
        lax.all_gather(self_grad.astype(jnp.bfloat16), "dp", axis=0, tiled=True).astype(
            self_grad.dtype
        ),
        lax.all_gather(cross_grad.astype(jnp.bfloat16), "dp", axis=0, tiled=True).astype(
            cross_grad.dtype
        ),
        lax.all_gather(ffn_grad.astype(jnp.bfloat16), "dp", axis=0, tiled=True).astype(
            ffn_grad.dtype
        ),
    )
    return (mixed, hidden_grad, self_grad, cross_grad, ffn_grad)


MESH = pl.DeviceIdType.MESH
BF = jnp.bfloat16
F32 = jnp.float32
VMEM_BYTES = 62 * 2**20


def place():
    f = lax.axis_index("fsdp")
    return lax.axis_index("dp"), f // 4, (f // 2) % 2, f % 2


def device(x, z, y, c):
    return (x, (z * 2 + y) * 2 + c)


def meet(devices):
    barrier = pltpu.get_barrier_semaphore()
    for d in devices:
        pl.semaphore_signal(barrier, inc=1, device_id=d, device_id_type=MESH)
    pl.semaphore_wait(barrier, len(devices))


def neighbours(x, z, y, c):
    return [
        device(x, z, y, 1 - c),
        device(1 - x, z, y, c),
        device(x, z, 1 - y, c),
        device(x, (z + 1) % 4, y, c),
        device(x, (z + 2) % 4, y, c),
        device(x, (z + 3) % 4, y, c),
    ]


def remote(src, dst, send, recv, target):
    return pltpu.make_async_remote_copy(
        src_ref=src,
        dst_ref=dst,
        send_sem=send,
        recv_sem=recv,
        device_id=target,
        device_id_type=MESH,
    )


def gather_kernel(own_s, own_c, own_f, all_s, all_c, all_f, block_f, loc, *sems):
    x, z, y, c = place()
    core, xn, yn = device(x, z, y, 1 - c), device(1 - x, z, y, c), device(x, z, 1 - y, c)
    meet(neighbours(x, z, y, c))

    def part_s(zz, yy, cc, h):
        rows = pl.ds(pl.multiple_of(192 * (2 * yy + cc), 192), 192)
        if h is None:
            return all_s.at[zz, rows]
        return all_s.at[zz, rows, pl.ds(pl.multiple_of(384 * h, 384), 384)]

    def part_c(zz, yy, cc, h):
        rows = pl.ds(pl.multiple_of(272 * ((zz * 2 + yy) * 2 + cc), 16), 272)
        if h is None:
            return all_c.at[rows]
        return all_c.at[rows, pl.ds(pl.multiple_of(384 * h, 384), 384)]

    def part_f(zz, yy):
        return all_f.at[zz, pl.ds(pl.multiple_of(384 * yy, 384), 384)]

    sent = []
    (zs, zr, ys, yr, xs, xr, cs, cr) = sems

    def go(src, dst, send, recv, target):
        copy = remote(src, dst, send, recv, target)
        copy.start()
        sent.append(copy)

    def arrived(view, recv):
        remote(view, view, recv, recv, core).wait_recv()

    half = pl.ds(pl.multiple_of(384 * x, 384), 384)
    groups = [(0, own_s, part_s), (1, own_c, part_c)]

    fb = pl.ds(pl.multiple_of(192 * c, 192), 192)
    w1 = z % 2 == 0

    def start_own(g, own, part):
        for k in (1, 2, 3):
            go(own.at[:, half], part(z, y, c, x), zs.at[g, k], zr.at[g, k], device(x, (z + k) % 4, y, c))
        go(own.at[:, half], part(z, y, c, x), ys.at[g, 0], yr.at[g, 0], yn)
        go(own, part(z, y, c, None), cs.at[g, 0], cr.at[g, 0], core)

    locals_ = []
    for g, own, part in groups:
        start_own(g, own, part)
        copy = pltpu.make_async_copy(own, part(z, y, c, None), loc.at[g])
        copy.start()
        locals_.append(copy)

    @pl.when(w1)
    def _():
        copy = remote(own_f.at[1], block_f.at[fb], cs.at[2, 0], cr.at[2, 0], core)
        copy.start()
        mine = pltpu.make_async_copy(own_f.at[0], block_f.at[fb], loc.at[2])
        mine.start()
        mine.wait()
        copy.wait()

    @pl.when(jnp.logical_not(w1))
    def _():
        for j in range(2):
            mine = pltpu.make_async_copy(own_f.at[j], block_f.at[pl.ds(192 * j, 192)], loc.at[2])
            mine.start()
            mine.wait()

    for k in (1, 2, 3):
        go(block_f, part_f(z, y), zs.at[2, k], zr.at[2, k], device(x, (z + k) % 4, y, c))
    go(block_f, part_f(z, y), ys.at[2, 0], yr.at[2, 0], yn)
    copy = pltpu.make_async_copy(block_f, part_f(z, y), loc.at[2])
    copy.start()
    locals_.append(copy)

    def z_arrivals(g, part):
        for k in (1, 2, 3):
            view = part((z - k) % 4, y, c, x)
            arrived(view, zr.at[g, k])
            go(view, view, ys.at[g, k], yr.at[g, k], yn)
            go(view, view, xs.at[g, k - 1], xr.at[g, k - 1], xn)
            go(view, view, cs.at[g, k], cr.at[g, k], core)

    def y_arrivals(g, part):
        for j in range(4):
            view = part((z - j) % 4, 1 - y, c, x)
            arrived(view, yr.at[g, j])
            go(view, view, xs.at[g, 3 + j], xr.at[g, 3 + j], xn)
            go(view, view, cs.at[g, 4 + j], cr.at[g, 4 + j], core)

    def x_arrivals(g, part):
        for j in range(7):
            view = part((z - j - 1) % 4, y, c, 1 - x) if j < 3 else part((z - j + 3) % 4, 1 - y, c, 1 - x)
            arrived(view, xr.at[g, j])
            go(view, view, cs.at[g, 8 + j], cr.at[g, 8 + j], core)

    def core_arrivals(g, part):
        for j in range(15):
            if j == 0:
                view = part(z, y, 1 - c, None)
            elif j < 4:
                view = part((z - j) % 4, y, 1 - c, x)
            elif j < 8:
                view = part((z - j + 4) % 4, 1 - y, 1 - c, x)
            elif j < 11:
                view = part((z - j + 7) % 4, y, 1 - c, 1 - x)
            else:
                view = part((z - j + 11) % 4, 1 - y, 1 - c, 1 - x)
            arrived(view, cr.at[g, j])

    z_arrivals(0, part_s)
    z_arrivals(1, part_c)
    y_arrivals(0, part_s)
    for k in (1, 2, 3):
        view = part_f((z - k) % 4, y)
        arrived(view, zr.at[2, k])
        go(view, view, ys.at[2, k], yr.at[2, k], yn)
    y_arrivals(1, part_c)
    x_arrivals(0, part_s)
    x_arrivals(1, part_c)
    for j in range(4):
        arrived(part_f((z - j) % 4, 1 - y), yr.at[2, j])
    core_arrivals(0, part_s)
    core_arrivals(1, part_c)
    for copy in locals_:
        copy.wait()
    for copy in sent:
        copy.wait_send()


def gather_weights(own_s, own_c, own_f):
    dma = pltpu.SemaphoreType.DMA
    anywhere = pl.BlockSpec(memory_space=pl.ANY)
    return pl.pallas_call(
        gather_kernel,
        out_shape=(
            jax.ShapeDtypeStruct((4, D, D), BF),
            jax.ShapeDtypeStruct((4352, D), BF),
            jax.ShapeDtypeStruct((4, D, D), BF),
            jax.ShapeDtypeStruct((384, D), BF),
        ),
        in_specs=[anywhere] * 3,
        out_specs=[anywhere] * 4,
        scratch_shapes=[
            dma((3,)),
            dma((3, 4)),
            dma((3, 4)),
            dma((3, 4)),
            dma((3, 4)),
            dma((2, 7)),
            dma((2, 7)),
            dma((3, 15)),
            dma((3, 15)),
        ],
        compiler_params=pltpu.CompilerParams(collective_id=0, has_side_effects=True),
    )(own_s, own_c, own_f)[:3]


def mm(a, b):
    return jnp.dot(a, b, preferred_element_type=F32)


def mm_nt(a, b):
    return lax.dot_general(a, b, (((1,), (1,)), ((), ())), preferred_element_type=F32)


def mm_tn(a, b):
    return lax.dot_general(a, b, (((0,), (0,)), ((), ())), preferred_element_type=F32)


def normed(v):
    centered = v - jnp.mean(v, -1, keepdims=True)
    r = lax.rsqrt(jnp.mean(centered * centered, -1, keepdims=True) + EPS)
    return centered * r, r


def norm_back(v, gain, g_out):
    xh, r = normed(v)
    gg = g_out * gain
    dv = r * (gg - jnp.mean(gg, -1, keepdims=True) - xh * jnp.mean(gg * xh, -1, keepdims=True))
    return dv, jnp.sum(g_out * xh, 0, keepdims=True), jnp.sum(g_out, 0, keepdims=True)


GELU_A = math.sqrt(2.0 / math.pi)
GELU_B = 0.044715


def gelu(v):
    return 0.5 * v * (1.0 + jnp.tanh(GELU_A * (v + GELU_B * (v * v * v))))


def gelu_slope(v):
    t = jnp.tanh(GELU_A * (v + GELU_B * (v * v * v)))
    return 0.5 * (1.0 + t) + 0.5 * v * (1.0 - t * t) * (GELU_A * (1.0 + 3.0 * GELU_B * (v * v)))


def head_mask(h):
    lane = lax.broadcasted_iota(jnp.int32, (1, 256), 1)
    return jnp.where(lane // HDIM == h, 1.0, 0.0)


def spread(rows):
    wide = rows.astype(F32)
    return jnp.concatenate([(wide * head_mask(h)).astype(BF) for h in range(4)], 0)


def fold(stacked):
    n = stacked.shape[0] // 4
    total = stacked[:n] * head_mask(0)
    for h in range(1, 4):
        total = total + stacked[h * n : (h + 1) * n] * head_mask(h)
    return total


def attend_block(q, k, v, allowed):
    s = mm_nt(spread(q), k) * SCALE
    s = jnp.where(allowed > 0.5, s, -1e30)
    e = jnp.exp(s - jnp.max(s, -1, keepdims=True))
    p = e / jnp.sum(e, -1, keepdims=True)
    return p, fold(mm(p.astype(BF), v)).astype(BF)


def attend_block_back(q, k, v, p, da):
    dax = spread(da)
    dp = mm_nt(dax, v)
    ds = (p * (dp - jnp.sum(p * dp, -1, keepdims=True))).astype(BF)
    dq = (fold(mm(ds, k)) * SCALE).astype(BF)
    dk = (mm_tn(ds, spread(q)) * SCALE).astype(BF)
    dv = mm_tn(p.astype(BF), dax).astype(BF)
    return dq, dk, dv


def rows_of(ref, first):
    return jnp.concatenate([ref[first : first + 32], ref[64 + first : 96 + first]], 0)


def compute_kernel(
    hid, allowed, feat, cot, vec, ws, wc, wf,
    mixed, hgrad, gs, gc, gf, vg,
    q_s, k_s, v_s, a_s, p_s, sum1, first,
    cq_s, ck_s, cv_s, ca_s, p_c, sum2, second,
    xg, pre, act, part, send_p, recv_p, send_x, recv_x, sum3, gb, dsum3, dfirst,
    dq_s, dk_s, dv_s, dck, dcv, ex_s, ex_r, rs_s, rs_r,
):
    x, z, y, c = place()
    core, xn = device(x, z, y, 1 - c), device(1 - x, z, y, c)
    meet([core, xn])

    def slot(xx, cc):
        return 2 * cc + xx

    def exchange(phase, buf):
        me, xs_, ps_, ds_ = slot(x, c), slot(1 - x, c), slot(x, 1 - c), slot(1 - x, 1 - c)
        to_x = remote(buf.at[me], buf.at[me], ex_s.at[phase, 0], ex_r.at[phase, 0], xn)
        to_x.start()
        to_p = remote(buf.at[me], buf.at[me], ex_s.at[phase, 1], ex_r.at[phase, 1], core)
        to_p.start()
        to_x.wait_recv()
        fwd = remote(buf.at[xs_], buf.at[xs_], ex_s.at[phase, 2], ex_r.at[phase, 2], core)
        fwd.start()
        to_p.wait_recv()
        fwd.wait_recv()
        to_x.wait_send()
        to_p.wait_send()
        fwd.wait_send()

    def scatter_sum(phase, part):
        send_p[phase, 0] = part[slot(1 - x, 1 - c)].astype(BF)
        send_p[phase, 1] = part[slot(x, 1 - c)].astype(BF)
        far = remote(send_p.at[phase, 0], recv_p.at[phase, 0], rs_s.at[phase, 0], rs_r.at[phase, 0], core)
        far.start()
        near = remote(send_p.at[phase, 1], recv_p.at[phase, 1], rs_s.at[phase, 1], rs_r.at[phase, 1], core)
        near.start()
        far.wait_recv()
        send_x[phase] = (part[slot(1 - x, c)] + recv_p[phase, 0].astype(F32)).astype(BF)
        over = remote(send_x.at[phase], recv_x.at[phase], rs_s.at[phase, 2], rs_r.at[phase, 2], xn)
        over.start()
        near.wait_recv()
        over.wait_recv()
        far.wait_send()
        near.wait_send()
        over.wait_send()
        return part[slot(x, c)] + recv_p[phase, 1].astype(F32) + recv_x[phase].astype(F32)

    def v_(i):
        return vec[i : i + 1]

    h = hid[...]
    q_s[...] = (mm(h, ws[0]) + v_(0)).astype(BF)
    k_s[...] = mm(h, ws[1]).astype(BF)
    v_s[...] = (mm(h, ws[2]) + v_(1)).astype(BF)
    for i in range(2):
        rows = slice(64 * i, 64 * i + 64)
        ok = jnp.concatenate([allowed[i]] * 4, 0)
        for g in range(3):
            lanes = slice(256 * g, 256 * g + 256)
            p, a = attend_block(q_s[rows, lanes], k_s[rows, lanes], v_s[rows, lanes], ok)
            p_s[i, g] = p
            a_s[rows, lanes] = a
    sum1[...] = h.astype(F32) + (mm(a_s[...], ws[3]) + v_(2))
    xh, _ = normed(sum1[...])
    first[...] = xh * v_(3) + v_(4)
    me = slot(x, c)
    xg[0, me, 64:128] = rows_of(first, 32).astype(BF)

    u = rows_of(first, 0)
    cq_s[...] = (mm(u.astype(BF), wc[0:768]) + v_(5)).astype(BF)
    for i in range(2):
        rows = slice(272 * i, 272 * i + 272)
        ck_s[rows] = mm(feat[rows], wc[768:2176]).astype(BF)
        cv_s[rows] = (mm(feat[rows], wc[2176:3584]) + v_(6)).astype(BF)
    ok = jnp.where(lax.broadcasted_iota(jnp.int32, (128, 272), 1) < 257, 1.0, 0.0)
    for i in range(2):
        rows = slice(272 * i, 272 * i + 272)
        mine = slice(32 * i, 32 * i + 32)
        for g in range(3):
            lanes = slice(256 * g, 256 * g + 256)
            p, a = attend_block(cq_s[mine, lanes], ck_s[rows, lanes], cv_s[rows, lanes], ok)
            p_c[i, g] = p
            ca_s[mine, lanes] = a
    sum2[...] = u + (mm(ca_s[...], wc[3584:4352]) + v_(7))
    xh, _ = normed(sum2[...])
    second[...] = xh * v_(8) + v_(9)
    xg[0, me, 0:64] = second[...].astype(BF)

    exchange(0, xg.at[0])
    for b in range(2):
        r = slice(64 * b, 64 * b + 64)
        rows = xg[0, :, r].reshape(256, D)
        pre[b] = mm(rows, wf[2 * b]) + v_(10 + 4 * b)
        act[b] = gelu(pre[b]).astype(BF)
        part[:, r] = mm(act[b], wf[2 * b + 1]).reshape(4, 64, D)
    out = scatter_sum(0, part)
    for b in range(2):
        rows = second[...] if b == 0 else rows_of(first, 32)
        s3 = rows + (out[64 * b : 64 * b + 64] + v_(11 + 4 * b))
        sum3[b] = s3
        xh, _ = normed(s3)
        done = (xh * v_(12 + 4 * b) + v_(13 + 4 * b)).astype(BF)
        for i in range(2):
            mixed[64 * i + 32 * b : 64 * i + 32 * b + 32] = done[32 * i : 32 * i + 32]
        g_out = rows_of(cot, 32 * b).astype(F32)
        dsum, dgain, dshift = norm_back(s3, v_(12 + 4 * b), g_out)
        dsum3[b] = dsum
        low = dsum.astype(BF)
        xg[1, me, 64 * b : 64 * b + 64] = low
        o = 10 + 7 * b
        vg[o + 4 : o + 5] = jnp.sum(low.astype(F32), 0, keepdims=True)
        vg[o + 5 : o + 6] = dgain
        vg[o + 6 : o + 7] = dshift
    exchange(1, xg.at[1])
    for b in range(2):
        r = slice(64 * b, 64 * b + 64)
        up = xg[1, :, r].reshape(256, D)
        dpre = (mm_nt(up, wf[2 * b + 1]) * gelu_slope(pre[b])).astype(BF)
        gb[b] = dpre
        part[:, r] = mm_nt(dpre, wf[2 * b]).reshape(4, 64, D)
        db1 = jnp.sum(dpre.astype(F32), 0, keepdims=True)
        for j in range(4):
            vg[10 + 7 * b + j : 11 + 7 * b + j] = jnp.where(j == me, db1, 0.0)
    dx = scatter_sum(1, part)
    for b in range(2):
        r = slice(64 * b, 64 * b + 64)
        rows = xg[0, :, r].reshape(256, D)
        up = xg[1, :, r].reshape(256, D)
        gf[2 * b] = mm_tn(rows, gb[b]).astype(BF)
        gf[2 * b + 1] = mm_tn(act[b], up).astype(BF)
    d_second = dsum3[0] + dx[0:64]
    d_text = dsum3[1] + dx[64:128]
    for i in range(2):
        dfirst[64 * i + 32 : 64 * i + 64] = d_text[32 * i : 32 * i + 32]

    du2, dgain, dshift = norm_back(sum2[...], v_(8), d_second)
    vg[8:9] = dgain
    vg[9:10] = dshift
    go = du2.astype(BF)
    vg[7:8] = jnp.sum(go.astype(F32), 0, keepdims=True)
    gc[3584:4352] = mm_tn(ca_s[...], go).astype(BF)
    dca = mm_nt(go, wc[3584:4352]).astype(BF)
    dcq = []
    for i in range(2):
        rows = slice(272 * i, 272 * i + 272)
        mine = slice(32 * i, 32 * i + 32)
        blocks = []
        for g in range(3):
            lanes = slice(256 * g, 256 * g + 256)
            dq, dk, dv = attend_block_back(
                cq_s[mine, lanes], ck_s[rows, lanes], cv_s[rows, lanes], p_c[i, g], dca[mine, lanes]
            )
            blocks.append(dq)
            dck[rows, lanes] = dk
            dcv[rows, lanes] = dv
        dcq.append(jnp.concatenate(blocks, 1))
    dcq = jnp.concatenate(dcq, 0)
    vg[5:6] = jnp.sum(dcq.astype(F32), 0, keepdims=True)
    vg[6:7] = jnp.sum(dcv[...].astype(F32), 0, keepdims=True)
    u_low = rows_of(first, 0).astype(BF)
    gc[0:768] = mm_tn(u_low, dcq).astype(BF)
    for j in range(11):
        block = feat[:, 128 * j : 128 * j + 128]
        gc[768 + 128 * j : 896 + 128 * j] = mm_tn(block, dck[...]).astype(BF)
        gc[2176 + 128 * j : 2304 + 128 * j] = mm_tn(block, dcv[...]).astype(BF)
    du = du2 + mm_nt(dcq, wc[0:768])
    for i in range(2):
        dfirst[64 * i : 64 * i + 32] = du[32 * i : 32 * i + 32]

    dsum1, dgain, dshift = norm_back(sum1[...], v_(3), dfirst[...])
    vg[3:4] = dgain
    vg[4:5] = dshift
    go = dsum1.astype(BF)
    vg[2:3] = jnp.sum(go.astype(F32), 0, keepdims=True)
    gs[3] = mm_tn(a_s[...], go).astype(BF)
    da = mm_nt(go, ws[3]).astype(BF)
    for i in range(2):
        rows = slice(64 * i, 64 * i + 64)
        for g in range(3):
            lanes = slice(256 * g, 256 * g + 256)
            dq, dk, dv = attend_block_back(
                q_s[rows, lanes], k_s[rows, lanes], v_s[rows, lanes], p_s[i, g], da[rows, lanes]
            )
            dq_s[rows, lanes] = dq
            dk_s[rows, lanes] = dk
            dv_s[rows, lanes] = dv
    vg[0:1] = jnp.sum(dq_s[...].astype(F32), 0, keepdims=True)
    vg[1:2] = jnp.sum(dv_s[...].astype(F32), 0, keepdims=True)
    gs[0] = mm_tn(hid[...], dq_s[...]).astype(BF)
    gs[1] = mm_tn(hid[...], dk_s[...]).astype(BF)
    gs[2] = mm_tn(hid[...], dv_s[...]).astype(BF)
    total = dsum1 + mm_nt(dq_s[...], ws[0]) + mm_nt(dk_s[...], ws[1]) + mm_nt(dv_s[...], ws[2])
    hgrad[...] = total.astype(BF)


def layer(hid, allowed, feat, cot, vec, ws, wc, wf):
    dma = pltpu.SemaphoreType.DMA
    vm = pl.BlockSpec(memory_space=pltpu.VMEM)
    b = lambda *s: pltpu.VMEM(s, BF)
    f = lambda *s: pltpu.VMEM(s, F32)
    return pl.pallas_call(
        compute_kernel,
        out_shape=(
            jax.ShapeDtypeStruct((128, D), BF),
            jax.ShapeDtypeStruct((128, D), BF),
            jax.ShapeDtypeStruct((4, D, D), BF),
            jax.ShapeDtypeStruct((4352, D), BF),
            jax.ShapeDtypeStruct((4, D, D), BF),
            jax.ShapeDtypeStruct((24, D), F32),
        ),
        in_specs=[vm] * 8,
        out_specs=[vm] * 6,
        scratch_shapes=[
            b(128, D), b(128, D), b(128, D), b(128, D), f(2, 3, 256, 64), f(128, D), f(128, D),
            b(64, D), b(544, D), b(544, D), b(64, D), f(2, 3, 128, 272), f(64, D), f(64, D),
            b(2, 4, 128, D), f(2, 256, D), b(2, 256, D), f(4, 128, D),
            b(2, 2, 128, D), b(2, 2, 128, D), b(2, 128, D), b(2, 128, D),
            f(2, 64, D), b(2, 256, D), f(2, 64, D), f(128, D),
            b(128, D), b(128, D), b(128, D), b(544, D), b(544, D),
            dma((2, 3)), dma((2, 3)), dma((2, 3)), dma((2, 3)),
        ],
        compiler_params=pltpu.CompilerParams(
            collective_id=1, has_side_effects=True, vmem_limit_bytes=VMEM_BYTES
        ),
    )(hid, allowed, feat, cot, vec, ws, wc, wf)


def reduce_kernel(
    gs, gc, gf, out_s, out_c, out_f,
    cs_buf, cc_buf, xs_buf, xc_buf, ys_buf, yc_buf, zs_buf, zc_buf, yf_buf, zf_buf, fin_s, fin_c, fin_f,
    co_s, co_r, xx_s, xx_r, yy_s, yy_r, zz_s, zz_r, fi_s, fi_r,
):
    x, z, y, c = place()
    core, xn, yn = device(x, z, y, 1 - c), device(1 - x, z, y, c), device(x, z, 1 - y, c)
    diag = device(1 - x, z, y, 1 - c)
    meet(neighbours(x, z, y, c) + [diag])
    sent = []

    def go(src, dst, send, recv, target):
        copy = remote(src, dst, send, recv, target)
        copy.start()
        sent.append(copy)

    def arrived(view, recv):
        remote(view, view, recv, recv, core).wait_recv()

    def add(a, b):
        return (a.astype(F32) + b.astype(F32)).astype(BF)

    mine_cols = pl.ds(pl.multiple_of(384 * x, 384), 384)
    their_cols = pl.ds(pl.multiple_of(384 * (1 - x), 384), 384)

    def view_s(zz, yy, cc):
        return gs.at[zz, pl.ds(pl.multiple_of(192 * (2 * yy + cc), 192), 192)]

    def view_c(zz, yy, cc):
        return gc.at[pl.ds(pl.multiple_of(272 * ((zz * 2 + yy) * 2 + cc), 16), 272)]

    def view_f(zz, yy):
        return gf.at[zz, pl.ds(pl.multiple_of(384 * yy, 384), 384)]

    groups = [
        (0, view_c, cc_buf, xc_buf, yc_buf, zc_buf, fin_c, out_c),
        (1, view_s, cs_buf, xs_buf, ys_buf, zs_buf, fin_s, out_s),
    ]
    order = (1, 2, 3, 0)
    for d in order:
        zz = (z + d) % 4
        go(view_f(zz, 1 - y), yf_buf.at[zz], yy_s.at[2, d], yy_r.at[2, d], yn)
    for g, view, cb, xb, yb, zb, fin, out in groups:
        for far in range(2):
            for d in order:
                zz = (z + d) % 4
                go(view(zz, y if far else 1 - y, 1 - c), cb.at[far, zz], co_s.at[g, far, d], co_r.at[g, far, d], core)
    for g, view, cb, xb, yb, zb, fin, out in groups:
        for far in range(2):
            for d in order:
                zz = (z + d) % 4
                arrived(cb.at[far, zz], co_r.at[g, far, d])
                cb[far, zz] = add(cb[far, zz], view(zz, y if far else 1 - y, c)[...])
                go(cb.at[far, zz, :, their_cols], xb.at[far, zz], xx_s.at[g, far, d], xx_r.at[g, far, d], xn)
    for d in order:
        zz = (z + d) % 4
        arrived(yf_buf.at[zz], yy_r.at[2, d])
        yf_buf[zz] = add(yf_buf[zz], view_f(zz, y)[...])
        if d:
            go(yf_buf.at[zz], zf_buf.at[d - 1], zz_s.at[2, d - 1], zz_r.at[2, d - 1], device(x, zz, y, c))
    for g, view, cb, xb, yb, zb, fin, out in groups:
        for far in range(2):
            for d in order:
                zz = (z + d) % 4
                arrived(xb.at[far, zz], xx_r.at[g, far, d])
                xb[far, zz] = add(xb[far, zz], cb[far, zz, :, mine_cols])
                if far == 0:
                    go(xb.at[0, zz], yb.at[zz], yy_s.at[g, d], yy_r.at[g, d], yn)
        for d in order:
            zz = (z + d) % 4
            arrived(yb.at[zz], yy_r.at[g, d])
            yb[zz] = add(yb[zz], xb[1, zz])
            if d:
                go(yb.at[zz], zb.at[d - 1], zz_s.at[g, d - 1], zz_r.at[g, d - 1], device(x, zz, y, c))
    for k in range(3):
        arrived(zf_buf.at[k], zz_r.at[2, k])
    total = yf_buf[z].astype(F32)
    for k in range(3):
        total = total + zf_buf[k].astype(F32)
    fin_f[...] = total.astype(BF).reshape(2, 192, D)
    quarter = 2 * c + x
    w1 = z % 2 == 0

    @pl.when(w1)
    def _():
        out_f[quarter] = fin_f[c]
        copies = [
            remote(fin_f.at[c], out_f.at[quarter], fi_s.at[2], fi_r.at[2], xn),
            remote(fin_f.at[1 - c], out_f.at[quarter], fi_s.at[3], fi_r.at[3], core),
            remote(fin_f.at[1 - c], out_f.at[quarter], fi_s.at[4], fi_r.at[4], diag),
        ]
        for copy in copies:
            copy.start()
        for copy in copies:
            copy.wait()

    @pl.when(jnp.logical_not(w1))
    def _():
        copies = []
        for j in range(2):
            out_f[2 * x + j] = fin_f[j]
            copies.append(remote(fin_f.at[j], out_f.at[2 * x + j], fi_s.at[2 + j], fi_r.at[2 + j], xn))
        for copy in copies:
            copy.start()
        for copy in copies:
            copy.wait()

    for g, view, cb, xb, yb, zb, fin, out in groups:
        for k in range(3):
            arrived(zb.at[k], zz_r.at[g, k])
        total = yb[z].astype(F32)
        for k in range(3):
            total = total + zb[k].astype(F32)
        fin[...] = total.astype(BF)
        out[:, mine_cols] = fin[...]
        go(fin, out.at[:, mine_cols], fi_s.at[g], fi_r.at[g], xn)
    for g, view, cb, xb, yb, zb, fin, out in groups:
        arrived(out.at[:, their_cols], fi_r.at[g])
    for copy in sent:
        copy.wait_send()


def reduce_grads(gs, gc, gf):
    dma = pltpu.SemaphoreType.DMA
    vm = pl.BlockSpec(memory_space=pltpu.VMEM)
    b = lambda *s: pltpu.VMEM(s, BF)
    return pl.pallas_call(
        reduce_kernel,
        out_shape=(
            jax.ShapeDtypeStruct((192, D), BF),
            jax.ShapeDtypeStruct((272, D), BF),
            jax.ShapeDtypeStruct((4, 192, D), BF),
        ),
        in_specs=[vm] * 3,
        out_specs=[vm] * 3,
        scratch_shapes=[
            b(2, 4, 192, D), b(2, 4, 272, D), b(2, 4, 192, 384), b(2, 4, 272, 384),
            b(4, 192, 384), b(4, 272, 384), b(3, 192, 384), b(3, 272, 384),
            b(4, 384, D), b(3, 384, D), b(192, 384), b(272, 384), b(2, 192, D),
            dma((2, 2, 4)), dma((2, 2, 4)), dma((2, 2, 4)), dma((2, 2, 4)),
            dma((3, 4)), dma((3, 4)), dma((3, 3)), dma((3, 3)), dma((5,)), dma((5,)),
        ],
        compiler_params=pltpu.CompilerParams(
            collective_id=2, has_side_effects=True, vmem_limit_bytes=VMEM_BYTES
        ),
    )(gs, gc, gf)


def own_rows(self_params, cross_params, ffn_params):
    x, z, y, c = place()
    f = lax.axis_index("fsdp")
    k = f % 4
    flats = [v.reshape(-1, 128) for v in (self_params, cross_params, ffn_params)]
    tails = lax.all_gather(jnp.concatenate([v[-32:] for v in flats]), "fsdp")
    before = lax.dynamic_index_in_dim(tails, (f + 15) % 16, keepdims=False)
    back = [2 * f, 2 * f, 6 * k + jnp.where(z >= 2, 6, 0)]
    nice = []
    for i, (v, rows) in enumerate(zip(flats, (1152, 1632, 4608))):
        both = jnp.concatenate([before[32 * i : 32 * i + 32], v])
        nice.append(lax.dynamic_slice_in_dim(both, 32 - back[i], rows))
    own_s = nice[0].reshape(192, D)
    own_c = nice[1].reshape(272, D)
    cols = nice[2].reshape(192, 2, 4, 3, 128)
    pick = lambda cc: lax.dynamic_index_in_dim(cols, 2 * cc + x, 2, keepdims=False).reshape(192, D)
    as_w1 = jnp.stack([pick(c), pick(1 - c)])
    as_w2 = lax.dynamic_index_in_dim(nice[2].reshape(2, 2, 192, D), x, keepdims=False)
    own_f = jnp.where(z % 2 == 0, as_w1, as_w2)

    q = 2 * c + x
    part = lambda b1: lax.dynamic_index_in_dim(b1.reshape(2, 4, 384), q, 1, keepdims=False).reshape(1, D)
    vecs = [
        tails[15, 0:30].reshape(5, D),
        tails[15, 32:62].reshape(5, D),
        part(tails[3, 72:96]),
        tails[7, 72:90].reshape(3, D),
        part(tails[11, 66:90]),
        tails[15, 66:84].reshape(3, D),
        jnp.zeros((6, D), BF),
    ]
    return own_s, own_c, own_f, jnp.concatenate(vecs).astype(F32)


def flat_grads(out_s, out_c, out_f, vg):
    x, z, y, c = place()
    f = lax.axis_index("fsdp")
    k = f % 4
    w1 = out_f.reshape(4, 192, 2, 3, 128).transpose(1, 2, 0, 3, 4).reshape(4608, 128)
    w2 = out_f.reshape(4608, 128)
    nice = [out_s.reshape(1152, 128), out_c.reshape(1632, 128), jnp.where(z % 2 == 0, w1, w2)]
    heads = jnp.concatenate([v[:32] for v in nice])
    after = lax.ppermute(heads, "fsdp", [(i, (i + 15) % 16) for i in range(16)]).astype(F32)
    vg = lax.psum(vg, ("dp", "fsdp"))
    zeros = lambda n: jnp.zeros((n, 128), F32)
    b1 = lambda v: v.reshape(4, 2, 384).transpose(1, 0, 2).reshape(24, 128)
    flat = lambda v: v.reshape(-1, 128)
    tail_s = jnp.where(f == 15, jnp.concatenate([flat(vg[0:5]), zeros(2)]), after[0:32])
    tail_c = jnp.where(f == 15, jnp.concatenate([flat(vg[5:10]), zeros(2)]), after[32:64])
    nxt = after[64:96]
    ends = jnp.stack([
        jnp.concatenate([b1(vg[10:14]), zeros(8)]),
        jnp.concatenate([flat(vg[14:17]), nxt[:14]]),
        jnp.concatenate([b1(vg[17:21]), nxt[:8]]),
        jnp.concatenate([flat(vg[21:24]), zeros(14)]),
    ])
    tail_f = jnp.where(k == 3, lax.dynamic_index_in_dim(ends, z, keepdims=False), nxt)
    skip = [2 * f, 2 * f, 6 * k + jnp.where(z >= 2, 6, 0)]
    outs = []
    for v, tail, start, rows in zip(nice, (tail_s, tail_c, tail_f), skip, (1154, 1634, 4614)):
        both = jnp.concatenate([v.astype(F32), tail])
        outs.append(lax.dynamic_slice_in_dim(both, start, rows).reshape(-1))
    return outs


def per_device_fast(hidden, lengths, features, cotangent, self_params, cross_params, ffn_params):
    own_s, own_c, own_f, vec = own_rows(self_params, cross_params, ffn_params)
    ws, wc, wf = gather_weights(own_s, own_c, own_f)
    at = jnp.arange(64)
    r, k = at[:, None], at[None, :]
    allowed = (k < NQ)[None] | ((r >= NQ) & (k <= r))[None] & (k[None] < NQ + lengths[:, None, None])
    feat = jnp.pad(features, ((0, 0), (0, 15), (0, 0))).reshape(544, E)
    mixed, hgrad, gs, gc, gf, vg = layer(
        hidden.reshape(128, D), allowed.astype(F32), feat, cotangent.reshape(128, D), vec, ws, wc, wf
    )
    grads = flat_grads(*reduce_grads(gs, gc, gf), vg)
    return (mixed.reshape(2, 64, D), hgrad.reshape(2, 64, D), *grads)


def solution(mesh):
    fast = mesh.shape["dp"] == 2 and mesh.shape["fsdp"] == 16
    return jax.shard_map(
        per_device_fast if fast else per_device,
        mesh=mesh,
        in_specs=(
            P(("dp", "fsdp"), None, None),
            P(("dp", "fsdp")),
            P(("dp", "fsdp"), None, None),
            P(("dp", "fsdp"), None, None),
            P("fsdp"),
            P("fsdp"),
            P("fsdp"),
        ),
        out_specs=(
            P(("dp", "fsdp"), None, None),
            P(("dp", "fsdp"), None, None),
            P("fsdp"),
            P("fsdp"),
            P("fsdp"),
        ),
        check_vma=False,
    )
```

```python
from functools import partial
import math
from types import SimpleNamespace

import jax
import jax.numpy as jnp
from jax import lax
from jax.experimental import pallas as pl
from jax.experimental.pallas import tpu as pltpu
from jax.sharding import PartitionSpec as P

D = 768
HEADS = 12
HDIM = 64
F = 3072
E = 1408
NQ = 32


EPS = 1e-06
SCALE = 0.125


def self_layout():
    return [(D, D)] * 4 + [(D,)] * 5


def cross_layout():
    return [(D, D), (E, D), (E, D), (D, D)] + [(D,)] * 5


def ffn_layout():
    return [(D, F), (F,), (F, D), (D,), (D,), (D,)] * 2


def split_flat(flat_vec, layouts):
    pieces = []
    offset = 0
    for layout in layouts:
        amount = math.prod(layout)
        pieces.append(flat_vec[offset : offset + amount].reshape(layout))
        offset = offset + amount
    return pieces


def join_flat(pieces, length):
    flat_vec = jnp.concatenate([piece.reshape(-1) for piece in pieces])
    return jnp.pad(flat_vec, (0, length - flat_vec.shape[0]))


def regroup(flat_vec):
    groups = lax.axis_size("fsdp")
    replicas = lax.axis_size("dp")
    return flat_vec.reshape(groups, replicas, -1).transpose(1, 0, 2).reshape(-1)


def matmul(left, right):
    return jnp.dot(left, right, preferred_element_type=jnp.float32)


def matmul_left(left, right):
    return lax.dot_general(
        left, right, (((0,), (0,)), ((), ())), preferred_element_type=jnp.float32
    )


def matmul_right(left, right):
    return lax.dot_general(
        left, right, (((1,), (1,)), ((), ())), preferred_element_type=jnp.float32
    )


def column_sum(values):
    return jnp.sum(values.astype(jnp.float32), 0)


def layer_norm(values, gain, shift):
    average = jnp.mean(values, -1, keepdims=True)
    centered = values - average
    variance = jnp.mean(centered * centered, -1, keepdims=True)
    return centered * lax.rsqrt(variance + EPS) * gain + shift


def norm_backward(summed, gain, shift, grad_out):
    _, norm_pull = jax.vjp(layer_norm, summed, gain.astype(jnp.float32), shift.astype(jnp.float32))
    return norm_pull(grad_out)


def heads(rows, items):
    return rows.reshape(items, -1, HEADS, HDIM)


def score_block(query, keys, mask):
    scores = jnp.einsum("iqhd,ikhd->ihqk", query, keys, preferred_element_type=jnp.float32) * SCALE
    if mask is not None:
        scores = jnp.where(mask, scores, -1e30)
    return scores


def attend(query, keys, values, mask):
    scores = score_block(query, keys, mask)
    top_sum = jax.nn.logsumexp(scores, axis=-1)
    probs = jnp.exp(scores - top_sum[..., None]).astype(jnp.bfloat16)
    context = jnp.einsum("ihqk,ikhd->iqhd", probs, values, preferred_element_type=jnp.float32)
    return (context, top_sum)


def attend_back(query, keys, values, mask, top_sum, grad_context):
    probs = jnp.exp(score_block(query, keys, mask) - top_sum[..., None])
    grad_probs = jnp.einsum(
        "iqhd,ikhd->ihqk", grad_context, values, preferred_element_type=jnp.float32
    )
    inner = jnp.sum(probs * grad_probs, -1, keepdims=True)
    grad_scores = (probs * (grad_probs - inner)).astype(jnp.bfloat16)
    grad_query = (
        jnp.einsum("ihqk,ikhd->iqhd", grad_scores, keys, preferred_element_type=jnp.float32) * SCALE
    )
    grad_keys = (
        jnp.einsum("ihqk,iqhd->ikhd", grad_scores, query, preferred_element_type=jnp.float32)
        * SCALE
    )
    grad_values = jnp.einsum(
        "ihqk,iqhd->ikhd",
        probs.astype(jnp.bfloat16),
        grad_context,
        preferred_element_type=jnp.float32,
    )
    return (grad_query, grad_keys, grad_values)


def linear_back(inputs, weight, grad_out):
    return (matmul_left(inputs, grad_out), column_sum(grad_out), matmul_right(grad_out, weight))


def ffn_forward(rows, params):
    w_in, b_in, w_out, b_out, gain, shift = params
    rows_low = rows.astype(jnp.bfloat16)
    hidden_pre = matmul(rows_low, w_in) + b_in
    activated = jax.nn.gelu(hidden_pre, approximate=True).astype(jnp.bfloat16)
    summed = rows + (matmul(activated, w_out) + b_out)
    final = layer_norm(summed, gain.astype(jnp.float32), shift.astype(jnp.float32))
    return (final, (rows_low, hidden_pre, activated, summed))


def ffn_backward(grad_out, kept, params):
    w_in, b_in, w_out, b_out, gain, shift = params
    rows_low, hidden_pre, activated, summed = kept
    grad_sum, grad_gain, grad_shift = norm_backward(summed, gain, shift, grad_out)
    grad_branch = grad_sum.astype(jnp.bfloat16)
    grad_w_out, grad_b_out, grad_act = linear_back(activated, w_out, grad_branch)
    _, gelu_pull = jax.vjp(partial(jax.nn.gelu, approximate=True), hidden_pre)
    grad_pre = gelu_pull(grad_act)[0].astype(jnp.bfloat16)
    grad_w_in, grad_b_in, grad_rows = linear_back(rows_low, w_in, grad_pre)
    return (
        grad_sum + grad_rows,
        [grad_w_in, grad_b_in, grad_w_out, grad_b_out, grad_gain, grad_shift],
    )


def per_device(hidden, lengths, features, cotangent, self_params, cross_params, ffn_params):
    items, seq, width = hidden.shape
    self_full = lax.all_gather(self_params, "fsdp", axis=0, tiled=True)
    self_parts = split_flat(self_full, self_layout())
    w_q, w_k, w_v, w_o, b_q, b_v, b_o, gain_one, shift_one = self_parts
    positions = jnp.arange(seq)
    rows_at = positions[:, None]
    cols_at = positions[None, :]
    allowed = (cols_at < NQ)[None] | ((rows_at >= NQ) & (cols_at <= rows_at))[None] & (
        cols_at[None] < NQ + lengths[:, None, None]
    )
    allowed = allowed[:, None]
    inputs = hidden.reshape(-1, width)
    query_low = (matmul(inputs, w_q) + b_q).astype(jnp.bfloat16)
    key_low = matmul(inputs, w_k).astype(jnp.bfloat16)
    value_low = (matmul(inputs, w_v) + b_v).astype(jnp.bfloat16)
    context, self_top = attend(
        heads(query_low, items), heads(key_low, items), heads(value_low, items), allowed
    )
    context_low = context.reshape(-1, width).astype(jnp.bfloat16)
    summed_one = inputs.astype(jnp.float32) + (matmul(context_low, w_o) + b_o)
    first = layer_norm(summed_one, gain_one.astype(jnp.float32), shift_one.astype(jnp.float32))
    first_items = first.reshape(items, seq, width)
    query_rows = first_items[:, :NQ].reshape(-1, width)
    text_rows = first_items[:, NQ:].reshape(-1, width)
    cross_full = lax.all_gather(cross_params, "fsdp", axis=0, tiled=True)
    cross_parts = split_flat(cross_full, cross_layout())
    cross_wq, cross_wk, cross_wv, cross_wo, cross_bq, cross_bv, cross_bo, gain_two, shift_two = (
        cross_parts
    )
    query_in = query_rows.astype(jnp.bfloat16)
    image_rows = features.reshape(-1, features.shape[-1])
    cross_query = (matmul(query_in, cross_wq) + cross_bq).astype(jnp.bfloat16)
    cross_key = matmul(image_rows, cross_wk).astype(jnp.bfloat16)
    cross_value = (matmul(image_rows, cross_wv) + cross_bv).astype(jnp.bfloat16)
    cross_context, cross_top = attend(
        heads(cross_query, items), heads(cross_key, items), heads(cross_value, items), None
    )
    cross_low = cross_context.reshape(-1, width).astype(jnp.bfloat16)
    summed_two = query_rows + (matmul(cross_low, cross_wo) + cross_bo)
    second = layer_norm(summed_two, gain_two.astype(jnp.float32), shift_two.astype(jnp.float32))
    ffn_full = lax.all_gather(ffn_params, "fsdp", axis=0, tiled=True)
    ffn_parts = split_flat(ffn_full, ffn_layout())
    query_final, query_kept = ffn_forward(second, ffn_parts[:6])
    text_final, text_kept = ffn_forward(text_rows, ffn_parts[6:])
    mixed = jnp.concatenate(
        [query_final.reshape(items, NQ, width), text_final.reshape(items, -1, width)], 1
    ).astype(jnp.bfloat16)
    grad_items = cotangent.astype(jnp.float32)
    grad_query_final = grad_items[:, :NQ].reshape(-1, width)
    grad_text_final = grad_items[:, NQ:].reshape(-1, width)
    ffn_back = split_flat(lax.all_gather(ffn_params, "fsdp", axis=0, tiled=True), ffn_layout())
    grad_second, query_grads = ffn_backward(grad_query_final, query_kept, ffn_back[:6])
    grad_text, text_grads = ffn_backward(grad_text_final, text_kept, ffn_back[6:])
    ffn_flat_grad = join_flat(query_grads + text_grads, ffn_full.shape[0])
    ffn_grad = lax.psum_scatter(
        regroup(ffn_flat_grad), ("dp", "fsdp"), scatter_dimension=0, tiled=True
    )
    cross_back = split_flat(
        lax.all_gather(cross_params, "fsdp", axis=0, tiled=True), cross_layout()
    )
    grad_summed_two, grad_gain_two, grad_shift_two = norm_backward(
        summed_two, cross_back[7], cross_back[8], grad_second
    )
    grad_cross_out = grad_summed_two.astype(jnp.bfloat16)
    grad_cross_wo, grad_cross_bo, grad_cross_ctx = linear_back(
        cross_low, cross_back[3], grad_cross_out
    )
    grad_cq, grad_ck, grad_cv = attend_back(
        heads(cross_query, items),
        heads(cross_key, items),
        heads(cross_value, items),
        None,
        cross_top,
        heads(grad_cross_ctx.astype(jnp.bfloat16), items),
    )
    grad_cq = grad_cq.reshape(-1, width).astype(jnp.bfloat16)
    grad_ck = grad_ck.reshape(-1, width).astype(jnp.bfloat16)
    grad_cv = grad_cv.reshape(-1, width).astype(jnp.bfloat16)
    grad_cross_wq, grad_cross_bq, grad_query_in = linear_back(query_in, cross_back[0], grad_cq)
    grad_cross_wk = matmul_left(image_rows, grad_ck)
    grad_cross_wv = matmul_left(image_rows, grad_cv)
    grad_cross_bv = column_sum(grad_cv)
    grad_query_rows = grad_summed_two + grad_query_in
    cross_list = [
        grad_cross_wq,
        grad_cross_wk,
        grad_cross_wv,
        grad_cross_wo,
        grad_cross_bq,
        grad_cross_bv,
        grad_cross_bo,
        grad_gain_two,
        grad_shift_two,
    ]
    cross_flat_grad = join_flat(cross_list, cross_full.shape[0])
    cross_grad = lax.psum_scatter(
        regroup(cross_flat_grad), ("dp", "fsdp"), scatter_dimension=0, tiled=True
    )
    self_back = split_flat(lax.all_gather(self_params, "fsdp", axis=0, tiled=True), self_layout())
    grad_first = jnp.concatenate(
        [grad_query_rows.reshape(items, NQ, width), grad_text.reshape(items, -1, width)], 1
    ).reshape(-1, width)
    grad_summed_one, grad_gain_one, grad_shift_one = norm_backward(
        summed_one, self_back[7], self_back[8], grad_first
    )
    grad_attn = grad_summed_one.astype(jnp.bfloat16)
    grad_w_o, grad_b_o, grad_ctx = linear_back(context_low, self_back[3], grad_attn)
    grad_q, grad_k, grad_v = attend_back(
        heads(query_low, items),
        heads(key_low, items),
        heads(value_low, items),
        allowed,
        self_top,
        heads(grad_ctx.astype(jnp.bfloat16), items),
    )
    grad_q = grad_q.reshape(-1, width).astype(jnp.bfloat16)
    grad_k = grad_k.reshape(-1, width).astype(jnp.bfloat16)
    grad_v = grad_v.reshape(-1, width).astype(jnp.bfloat16)
    grad_w_q, grad_b_q, input_from_q = linear_back(inputs, self_back[0], grad_q)
    grad_w_k = matmul_left(inputs, grad_k)
    input_from_k = matmul_right(grad_k, self_back[1])
    grad_w_v, grad_b_v, input_from_v = linear_back(inputs, self_back[2], grad_v)
    hidden_grad = (
        (grad_summed_one + input_from_q + input_from_k + input_from_v)
        .reshape(items, seq, width)
        .astype(jnp.bfloat16)
    )
    self_list = [
        grad_w_q,
        grad_w_k,
        grad_w_v,
        grad_w_o,
        grad_b_q,
        grad_b_v,
        grad_b_o,
        grad_gain_one,
        grad_shift_one,
    ]
    self_flat_grad = join_flat(self_list, self_full.shape[0])
    self_grad = lax.psum_scatter(
        regroup(self_flat_grad), ("dp", "fsdp"), scatter_dimension=0, tiled=True
    )
    self_grad, cross_grad, ffn_grad = (
        lax.all_gather(self_grad.astype(jnp.bfloat16), "dp", axis=0, tiled=True).astype(
            self_grad.dtype
        ),
        lax.all_gather(cross_grad.astype(jnp.bfloat16), "dp", axis=0, tiled=True).astype(
            cross_grad.dtype
        ),
        lax.all_gather(ffn_grad.astype(jnp.bfloat16), "dp", axis=0, tiled=True).astype(
            ffn_grad.dtype
        ),
    )
    return (mixed, hidden_grad, self_grad, cross_grad, ffn_grad)


MESH = pl.DeviceIdType.MESH
BF = jnp.bfloat16
F32 = jnp.float32
VMEM_BYTES = 62 * 2**20


def place():
    f = lax.axis_index("fsdp")
    return lax.axis_index("dp"), f // 4, (f // 2) % 2, f % 2


def device(x, z, y, c):
    return (x, (z * 2 + y) * 2 + c)


def meet(devices):
    barrier = pltpu.get_barrier_semaphore()
    for d in devices:
        pl.semaphore_signal(barrier, inc=1, device_id=d, device_id_type=MESH)
    pl.semaphore_wait(barrier, len(devices))


def remote(src, dst, send, recv, target):
    return pltpu.make_async_remote_copy(
        src_ref=src,
        dst_ref=dst,
        send_sem=send,
        recv_sem=recv,
        device_id=target,
        device_id_type=MESH,
    )


def mm(a, b):
    return jnp.dot(a, b, preferred_element_type=F32)


def mm_nt(a, b):
    return lax.dot_general(a, b, (((1,), (1,)), ((), ())), preferred_element_type=F32)


def mm_tn(a, b):
    return lax.dot_general(a, b, (((0,), (0,)), ((), ())), preferred_element_type=F32)


def rows_sum(v):
    return jnp.sum(v.astype(F32), 0, keepdims=True)


def add(a, b):
    return (a.astype(F32) + b.astype(F32)).astype(BF)


def normed(v):
    centered = v - jnp.mean(v, -1, keepdims=True)
    r = lax.rsqrt(jnp.mean(centered * centered, -1, keepdims=True) + EPS)
    return centered * r, r


def norm_back(v, gain, g_out):
    xh, r = normed(v)
    gg = g_out * gain
    dv = r * (gg - jnp.mean(gg, -1, keepdims=True) - xh * jnp.mean(gg * xh, -1, keepdims=True))
    return dv, rows_sum(g_out * xh), rows_sum(g_out)


GELU_A = math.sqrt(2.0 / math.pi)
GELU_B = 0.044715


def gelu(v):
    return 0.5 * v * (1.0 + jnp.tanh(GELU_A * (v + GELU_B * (v * v * v))))


def gelu_slope(v):
    t = jnp.tanh(GELU_A * (v + GELU_B * (v * v * v)))
    return 0.5 * (1.0 + t) + 0.5 * v * (1.0 - t * t) * (GELU_A * (1.0 + 3.0 * GELU_B * (v * v)))


def head_mask(h):
    lane = lax.broadcasted_iota(jnp.int32, (1, 256), 1)
    return jnp.where(lane // HDIM == h, 1.0, 0.0)


def spread(rows):
    wide = rows.astype(F32)
    return jnp.concatenate([(wide * head_mask(h)).astype(BF) for h in range(4)], 0)


def fold(stacked):
    n = stacked.shape[0] // 4
    total = stacked[:n] * head_mask(0)
    for h in range(1, 4):
        total = total + stacked[h * n : (h + 1) * n] * head_mask(h)
    return total


def attend_block(q, k, v, allowed):
    s = mm_nt(spread(q), k) * SCALE
    s = jnp.where(allowed > 0.5, s, -1e30)
    e = jnp.exp(s - jnp.max(s, -1, keepdims=True))
    p = e / jnp.sum(e, -1, keepdims=True)
    return p, fold(mm(p.astype(BF), v)).astype(BF)


def attend_block_back(q, k, v, p, da):
    dax = spread(da)
    dp = mm_nt(dax, v)
    ds = (p * (dp - jnp.sum(p * dp, -1, keepdims=True))).astype(BF)
    dq = (fold(mm(ds, k)) * SCALE).astype(BF)
    dk = (mm_tn(ds, spread(q)) * SCALE).astype(BF)
    dv = mm_tn(p.astype(BF), dax).astype(BF)
    return dq, dk, dv


def rows_of(ref, first):
    return jnp.concatenate([ref[first : first + 32], ref[64 + first : 96 + first]], 0)


def scratch():
    dma = lambda *s: pltpu.SemaphoreType.DMA(s)
    b = lambda *s: pltpu.VMEM(s, BF)
    f = lambda *s: pltpu.VMEM(s, F32)
    return dict(
        ws=b(4, D, D), wc=b(4352, D), wf=b(4, D, D), block_f=b(384, D), tb=b(4, 16, D),
        tv=f(4, 16, D), vg=f(4, 16, D),
        q=b(128, D), k=b(128, D), v=b(128, D), a=b(128, D), p=f(2, 3, 256, 64),
        sum1=f(128, D), first=f(128, D), cq=b(64, D), ck=b(544, D), cv=b(544, D), ca=b(64, D),
        pc=f(2, 3, 128, 272), sum2=f(64, D), second=f(64, D),
        xg=b(2, 2, 4, 64, D), pre=f(2, 256, D), act=b(2, 256, D), part=f(2, 4, 64, D),
        send_p=b(2, 2, 2, 64, D), recv_p=b(2, 2, 2, 64, D), send_x=b(2, 2, 64, D), recv_x=b(2, 2, 64, D),
        sum3=f(2, 64, D), dpre=b(2, 256, D), dsum3=f(2, 64, D), dfirst=f(128, D),
        dq=b(128, D), dk=b(128, D), dv=b(128, D), dck=b(544, D), dcv=b(544, D),
        core_s=b(2, 4, 192, D), core_c=b(2, 4, 272, D), xs=b(2, 4, 192, 384), xc=b(2, 4, 272, 384),
        ys=b(4, 192, 384), yc=b(4, 272, 384), zs=b(3, 192, 384), zc=b(3, 272, 384),
        yf=b(4, 384, D), zf=b(4, 384, D), fin_s=b(192, 384), fin_c=b(272, 384), fin_f=b(2, 192, D),
        v_send=b(4, 16, D), v_in=b(3, 4, 16, D), v_z=b(4, 16, D), v_zin=b(3, 16, D), v_x=b(16, D), v_xin=b(16, D),
        loc=dma(4), gz_s=dma(3, 4), gz_r=dma(3, 4), gy_s=dma(3, 4), gy_r=dma(3, 4), gx_s=dma(2, 7), gx_r=dma(2, 7),
        gc_s=dma(3, 15), gc_r=dma(3, 15), t_s=dma(6), t_r=dma(4),
        ex_s=dma(2, 2, 3), ex_r=dma(2, 2, 3), rs_s=dma(2, 2, 3), rs_r=dma(2, 2, 3),
        co_s=dma(2, 2, 4), co_r=dma(2, 2, 4), xx_s=dma(2, 2, 4), xx_r=dma(2, 2, 4), yy_s=dma(3, 4), yy_r=dma(3, 4),
        zz_s=dma(3, 4), zz_r=dma(3, 4), fi_s=dma(5), fi_r=dma(5), vv_s=dma(5), vv_r=dma(7),
    )


def layer_kernel(*refs):
    names = [
        "own_s", "own_c", "own_f", "own_t", "hid", "allowed", "feat", "cot",
        "mixed", "hgrad", "out_s", "out_c", "out_f", "out_v",
    ] + list(scratch())
    r = SimpleNamespace(**dict(zip(names, refs)))
    x, z, y, c = place()
    core, xn, yn = device(x, z, y, 1 - c), device(1 - x, z, y, c), device(x, z, 1 - y, c)
    diag = device(1 - x, z, y, 1 - c)
    zdev = lambda d: device(x, (z + d) % 4, y, c)
    meet([core, xn, yn, diag, device(x, z, 1 - y, 1 - c), zdev(1), zdev(2), zdev(3)])
    me = 2 * c + x
    cols = lambda h: pl.ds(pl.multiple_of(384 * h, 384), 384)
    root = jnp.logical_and(y == 1, c == 1)
    w1 = z % 2 == 0

    def go(sent, src, dst, send, recv, target):
        copy = remote(src, dst, send, recv, target)
        copy.start()
        sent.append(copy)

    def arrived(view, recv):
        remote(view, view, recv, recv, core).wait_recv()

    def drain(sent):
        for copy in sent:
            copy.wait_send()

    def shard_s(zz, yy, cc):
        return r.ws.at[zz, pl.ds(pl.multiple_of(192 * (2 * yy + cc), 192), 192)]

    def shard_c(zz, yy, cc):
        return r.wc.at[pl.ds(pl.multiple_of(272 * ((zz * 2 + yy) * 2 + cc), 16), 272)]

    def part_f(zz, yy):
        return r.wf.at[zz, pl.ds(pl.multiple_of(384 * yy, 384), 384)]

    shards = (shard_s, shard_c)
    sent_w = ([], [], [])

    def part(g, zz, yy, cc, h):
        view = shards[g](zz, yy, cc)
        return view if h is None else view.at[:, cols(h)]

    def gather_own(g, own):
        s = sent_w[g]
        for k in (1, 2, 3):
            go(s, own.at[:, cols(x)], part(g, z, y, c, x), r.gz_s.at[g, k], r.gz_r.at[g, k], zdev(k))
        go(s, own.at[:, cols(x)], part(g, z, y, c, x), r.gy_s.at[g, 0], r.gy_r.at[g, 0], yn)
        go(s, own, part(g, z, y, c, None), r.gc_s.at[g, 0], r.gc_r.at[g, 0], core)
        copy = pltpu.make_async_copy(own, part(g, z, y, c, None), r.loc.at[g])
        copy.start()
        return copy

    def gather_z(g):
        for k in (1, 2, 3):
            view = part(g, (z - k) % 4, y, c, x)
            arrived(view, r.gz_r.at[g, k])
            go(sent_w[g], view, view, r.gy_s.at[g, k], r.gy_r.at[g, k], yn)
            go(sent_w[g], view, view, r.gx_s.at[g, k - 1], r.gx_r.at[g, k - 1], xn)
            go(sent_w[g], view, view, r.gc_s.at[g, k], r.gc_r.at[g, k], core)

    def gather_y(g):
        for j in range(4):
            view = part(g, (z - j) % 4, 1 - y, c, x)
            arrived(view, r.gy_r.at[g, j])
            go(sent_w[g], view, view, r.gx_s.at[g, 3 + j], r.gx_r.at[g, 3 + j], xn)
            go(sent_w[g], view, view, r.gc_s.at[g, 4 + j], r.gc_r.at[g, 4 + j], core)

    def gather_x(g):
        for j in range(7):
            view = part(g, (z - j - 1) % 4, y, c, 1 - x) if j < 3 else part(g, (z - j + 3) % 4, 1 - y, c, 1 - x)
            arrived(view, r.gx_r.at[g, j])
            go(sent_w[g], view, view, r.gc_s.at[g, 8 + j], r.gc_r.at[g, 8 + j], core)

    def gather_core(g, which):
        for j in which:
            if j == 0:
                view = part(g, z, y, 1 - c, None)
            elif j < 4:
                view = part(g, (z - j) % 4, y, 1 - c, x)
            elif j < 8:
                view = part(g, (z - j + 4) % 4, 1 - y, 1 - c, x)
            elif j < 11:
                view = part(g, (z - j + 7) % 4, y, 1 - c, 1 - x)
            else:
                view = part(g, (z - j + 11) % 4, 1 - y, 1 - c, 1 - x)
            arrived(view, r.gc_r.at[g, j])

    loc_s = gather_own(0, r.own_s)

    @pl.when(root)
    def _():
        mine = pltpu.make_async_copy(r.own_t, r.tb.at[z], r.loc.at[3])
        mine.start()
        out = []
        for k in (1, 2, 3):
            go(out, r.own_t, r.tb.at[z], r.t_s.at[k - 1], r.t_r.at[k], zdev(k))
        mine.wait()
        for k in (1, 2, 3):
            arrived(r.tb.at[(z - k) % 4], r.t_r.at[k])
        for i, (yy, cc) in enumerate(((0, 0), (0, 1), (1, 0))):
            go(out, r.tb, r.tb, r.t_s.at[3 + i], r.t_r.at[0], device(x, z, yy, cc))
        drain(out)

    loc_c = gather_own(1, r.own_c)
    fb = pl.ds(pl.multiple_of(192 * c, 192), 192)

    @pl.when(w1)
    def _():
        copy = remote(r.own_f.at[1], r.block_f.at[fb], r.gc_s.at[2, 0], r.gc_r.at[2, 0], core)
        copy.start()
        mine = pltpu.make_async_copy(r.own_f.at[0], r.block_f.at[fb], r.loc.at[2])
        mine.start()
        mine.wait()
        copy.wait()

    @pl.when(jnp.logical_not(w1))
    def _():
        for j in range(2):
            mine = pltpu.make_async_copy(r.own_f.at[j], r.block_f.at[pl.ds(192 * j, 192)], r.loc.at[2])
            mine.start()
            mine.wait()

    for k in (1, 2, 3):
        go(sent_w[2], r.block_f, part_f(z, y), r.gz_s.at[2, k], r.gz_r.at[2, k], zdev(k))
    go(sent_w[2], r.block_f, part_f(z, y), r.gy_s.at[2, 0], r.gy_r.at[2, 0], yn)
    loc_f = pltpu.make_async_copy(r.block_f, part_f(z, y), r.loc.at[2])
    loc_f.start()
    r.vg[...] = jnp.zeros_like(r.vg)

    gather_z(0)
    gather_y(0)
    gather_z(1)
    gather_x(0)
    gather_y(1)
    loc_s.wait()

    @pl.when(jnp.logical_not(root))
    def _():
        arrived(r.tb, r.t_r.at[0])

    r.tv[...] = r.tb[...].astype(F32)
    gather_core(0, range(15))

    self_v = lambda j: r.tv[3, j : j + 1]
    cross_v = lambda j: r.tv[3, 5 + j : 6 + j]
    ffn_b1 = lambda b: r.tv[2 * b, pl.ds(10 + me, 1)]
    ffn_v = lambda b, j: r.tv[2 * b + 1, 10 + j : 11 + j]

    def slot(xx, cc):
        return 2 * cc + xx

    def ag_copies(ph, b):
        buf = r.xg.at[ph, b]
        pair = [(me, xn), (me, core), (slot(1 - x, c), core)]
        return [
            remote(buf.at[s], buf.at[s], r.ex_s.at[ph, b, i], r.ex_r.at[ph, b, i], t)
            for i, (s, t) in enumerate(pair)
        ]

    def ag_start(ph, b):
        to_x, to_p, fwd = ag_copies(ph, b)
        to_x.start()
        to_p.start()

    def ag_mid(ph, b):
        to_x, to_p, fwd = ag_copies(ph, b)
        to_x.wait_recv()
        fwd.start()

    def ag_end(ph, b):
        to_x, to_p, fwd = ag_copies(ph, b)
        to_p.wait_recv()
        fwd.wait_recv()
        to_x.wait_send()
        to_p.wait_send()
        fwd.wait_send()

    def rs_copies(ph, b):
        far = remote(r.send_p.at[ph, b, 0], r.recv_p.at[ph, b, 0], r.rs_s.at[ph, b, 0], r.rs_r.at[ph, b, 0], core)
        near = remote(r.send_p.at[ph, b, 1], r.recv_p.at[ph, b, 1], r.rs_s.at[ph, b, 1], r.rs_r.at[ph, b, 1], core)
        over = remote(r.send_x.at[ph, b], r.recv_x.at[ph, b], r.rs_s.at[ph, b, 2], r.rs_r.at[ph, b, 2], xn)
        return far, near, over

    def rs_start(ph, b):
        far, near, over = rs_copies(ph, b)
        r.send_p[ph, b, 0] = r.part[b, slot(1 - x, 1 - c)].astype(BF)
        far.start()
        r.send_p[ph, b, 1] = r.part[b, slot(x, 1 - c)].astype(BF)
        near.start()

    def rs_mid(ph, b):
        far, near, over = rs_copies(ph, b)
        far.wait_recv()
        r.send_x[ph, b] = (r.part[b, slot(1 - x, c)] + r.recv_p[ph, b, 0].astype(F32)).astype(BF)
        over.start()

    def rs_end(ph, b):
        far, near, over = rs_copies(ph, b)
        near.wait_recv()
        over.wait_recv()
        far.wait_send()
        near.wait_send()
        over.wait_send()
        return r.part[b, me] + r.recv_p[ph, b, 1].astype(F32) + r.recv_x[ph, b].astype(F32)

    h = r.hid[...]
    r.q[...] = (mm(h, r.ws[0]) + self_v(0)).astype(BF)
    r.k[...] = mm(h, r.ws[1]).astype(BF)
    r.v[...] = (mm(h, r.ws[2]) + self_v(1)).astype(BF)
    for i in range(2):
        rows = slice(64 * i, 64 * i + 64)
        ok = jnp.concatenate([r.allowed[i]] * 4, 0)
        for g in range(3):
            lanes = slice(256 * g, 256 * g + 256)
            p, a = attend_block(r.q[rows, lanes], r.k[rows, lanes], r.v[rows, lanes], ok)
            r.p[i, g] = p
            r.a[rows, lanes] = a
    r.sum1[...] = h.astype(F32) + (mm(r.a[...], r.ws[3]) + self_v(2))
    xh, _ = normed(r.sum1[...])
    r.first[...] = xh * self_v(3) + self_v(4)
    r.xg[0, 1, me] = rows_of(r.first, 32).astype(BF)
    ag_start(0, 1)

    loc_c.wait()
    gather_core(1, range(8))
    for i in range(2):
        rows = slice(272 * i, 272 * i + 272)
        r.ck[rows, cols(x)] = mm(r.feat[rows], r.wc[768:2176, cols(x)]).astype(BF)
        bias = r.tv[3, 6:7, cols(x)]
        r.cv[rows, cols(x)] = (mm(r.feat[rows], r.wc[2176:3584, cols(x)]) + bias).astype(BF)
    ag_mid(0, 1)
    for k in (1, 2, 3):
        view = part_f((z - k) % 4, y)
        arrived(view, r.gz_r.at[2, k])
        go(sent_w[2], view, view, r.gy_s.at[2, k], r.gy_r.at[2, k], yn)
    gather_x(1)
    gather_core(1, range(8, 15))
    far_cols = cols(1 - x)
    for i in range(2):
        rows = slice(272 * i, 272 * i + 272)
        r.ck[rows, far_cols] = mm(r.feat[rows], r.wc[768:2176, far_cols]).astype(BF)
        bias = r.tv[3, 6:7, far_cols]
        r.cv[rows, far_cols] = (mm(r.feat[rows], r.wc[2176:3584, far_cols]) + bias).astype(BF)
    u = rows_of(r.first, 0)
    r.cq[...] = (mm(u.astype(BF), r.wc[0:768]) + cross_v(0)).astype(BF)
    ok = jnp.where(lax.broadcasted_iota(jnp.int32, (128, 272), 1) < 257, 1.0, 0.0)
    for i in range(2):
        rows = slice(272 * i, 272 * i + 272)
        mine = slice(32 * i, 32 * i + 32)
        for g in range(3):
            lanes = slice(256 * g, 256 * g + 256)
            p, a = attend_block(r.cq[mine, lanes], r.ck[rows, lanes], r.cv[rows, lanes], ok)
            r.pc[i, g] = p
            r.ca[mine, lanes] = a
    r.sum2[...] = u + (mm(r.ca[...], r.wc[3584:4352]) + cross_v(2))
    xh, _ = normed(r.sum2[...])
    r.second[...] = xh * cross_v(3) + cross_v(4)
    r.xg[0, 0, me] = r.second[...].astype(BF)
    ag_start(0, 0)

    loc_f.wait()
    for j in range(4):
        arrived(part_f((z - j) % 4, 1 - y), r.gy_r.at[2, j])

    def ffn_forward_part(b):
        rows = r.xg[0, b].reshape(256, D)
        r.pre[b] = mm(rows, r.wf[2 * b]) + ffn_b1(b)
        r.act[b] = gelu(r.pre[b]).astype(BF)
        r.part[b] = mm(r.act[b], r.wf[2 * b + 1]).reshape(4, 64, D)

    def ffn_turn(b):
        rows = r.second[...] if b == 0 else rows_of(r.first, 32)
        s3 = rows + (rs_end(0, b) + ffn_v(b, 0))
        xh, _ = normed(s3)
        done = (xh * ffn_v(b, 1) + ffn_v(b, 2)).astype(BF)
        for i in range(2):
            r.mixed[64 * i + 32 * b : 64 * i + 32 * b + 32] = done[32 * i : 32 * i + 32]
        g_out = rows_of(r.cot, 32 * b).astype(F32)
        dsum, dgain, dshift = norm_back(s3, ffn_v(b, 1), g_out)
        r.dsum3[b] = dsum
        low = dsum.astype(BF)
        r.xg[1, b, me] = low
        r.vg[2 * b + 1, 10:11] = rows_sum(low)
        r.vg[2 * b + 1, 11:12] = dgain
        r.vg[2 * b + 1, 12:13] = dshift

    def ffn_backward_part(b):
        up = r.xg[1, b].reshape(256, D)
        r.dpre[b] = (mm_nt(up, r.wf[2 * b + 1]) * gelu_slope(r.pre[b])).astype(BF)
        r.part[b] = mm_nt(r.dpre[b], r.wf[2 * b]).reshape(4, 64, D)
        db1 = rows_sum(r.dpre[b])
        for j in range(4):
            r.vg[2 * b, 10 + j : 11 + j] = jnp.where(j == me, db1, 0.0)

    sent = []

    def ffn_weight_grads(b):
        rows = r.xg[0, b].reshape(256, D)
        up = r.xg[1, b].reshape(256, D)
        r.wf[2 * b] = mm_tn(rows, r.dpre[b]).astype(BF)
        r.wf[2 * b + 1] = mm_tn(r.act[b], up).astype(BF)
        for p in (2 * b, 2 * b + 1):
            go(sent, part_f(p, 1 - y), r.yf.at[p], r.yy_s.at[2, p], r.yy_r.at[2, p], yn)

    def ffn_sum_y(p):
        arrived(r.yf.at[p], r.yy_r.at[2, p])
        r.yf[p] = add(r.yf[p], part_f(p, y)[...])

        @pl.when(z != p)
        def _():
            remote(r.yf.at[p], r.zf.at[z], r.zz_s.at[2, p], r.zz_r.at[2, z], device(x, p, y, c)).start()

    ag_end(0, 1)
    ffn_forward_part(1)
    rs_start(0, 1)
    ag_mid(0, 0)
    ag_end(0, 0)
    rs_mid(0, 1)
    ffn_forward_part(0)
    rs_start(0, 0)
    ffn_turn(1)
    ag_start(1, 1)
    rs_mid(0, 0)
    ag_mid(1, 1)
    ag_end(1, 1)
    ffn_backward_part(1)
    rs_start(1, 1)
    ffn_turn(0)
    ag_start(1, 0)
    rs_mid(1, 1)
    drain(sent_w[2])
    ffn_weight_grads(1)
    ag_mid(1, 0)
    ag_end(1, 0)
    ffn_backward_part(0)
    rs_start(1, 0)
    d_text = r.dsum3[1] + rs_end(1, 1)
    for i in range(2):
        r.dfirst[64 * i + 32 : 64 * i + 64] = d_text[32 * i : 32 * i + 32]
    rs_mid(1, 0)
    ffn_weight_grads(0)
    d_second = r.dsum3[0] + rs_end(1, 0)

    groups = (
        (shard_s, r.core_s, r.xs, r.ys, r.zs, r.fin_s, r.out_s),
        (shard_c, r.core_c, r.xc, r.yc, r.zc, r.fin_c, r.out_c),
    )
    order = (1, 2, 3, 0)

    def sum_start(g):
        view, cb = groups[g][:2]
        for far in range(2):
            for d in order:
                zz = (z + d) % 4
                go(sent, view(zz, y if far else 1 - y, 1 - c), cb.at[far, zz], r.co_s.at[g, far, d], r.co_r.at[g, far, d], core)

    def sum_core(g):
        view, cb, xb = groups[g][:3]
        for far in range(2):
            for d in order:
                zz = (z + d) % 4
                arrived(cb.at[far, zz], r.co_r.at[g, far, d])
                cb[far, zz] = add(cb[far, zz], view(zz, y if far else 1 - y, c)[...])
                go(sent, cb.at[far, zz, :, cols(1 - x)], xb.at[far, zz], r.xx_s.at[g, far, d], r.xx_r.at[g, far, d], xn)

    def sum_x(g, far):
        view, cb, xb, yb = groups[g][:4]
        for d in order:
            zz = (z + d) % 4
            arrived(xb.at[far, zz], r.xx_r.at[g, far, d])
            xb[far, zz] = add(xb[far, zz], cb[far, zz, :, cols(x)])
            if far == 0:
                go(sent, xb.at[0, zz], yb.at[zz], r.yy_s.at[g, d], r.yy_r.at[g, d], yn)

    def sum_y(g):
        view, cb, xb, yb, zb = groups[g][:5]
        for d in order:
            zz = (z + d) % 4
            arrived(yb.at[zz], r.yy_r.at[g, d])
            yb[zz] = add(yb[zz], xb[1, zz])
            if d:
                go(sent, yb.at[zz], zb.at[d - 1], r.zz_s.at[g, d - 1], r.zz_r.at[g, d - 1], device(x, zz, y, c))

    def sum_z(g):
        view, cb, xb, yb, zb, fin, out = groups[g]
        for k in range(3):
            arrived(zb.at[k], r.zz_r.at[g, k])
        total = yb[z].astype(F32)
        for k in range(3):
            total = total + zb[k].astype(F32)
        fin[...] = total.astype(BF)
        out[:, cols(x)] = fin[...]
        go(sent, fin, out.at[:, cols(x)], r.fi_s.at[g], r.fi_r.at[g], xn)

    def ffn_sum_z():
        total = r.yf[z].astype(F32)
        for k in (1, 2, 3):
            zz = (z + k) % 4
            arrived(r.zf.at[zz], r.zz_r.at[2, zz])
            total = total + r.zf[zz].astype(F32)
        r.fin_f[...] = total.astype(BF).reshape(2, 192, D)

        def both(copies):
            for copy in copies:
                copy.start()
            for copy in copies:
                copy.wait()

        @pl.when(w1)
        def _():
            r.out_f[me] = r.fin_f[c]
            both([
                remote(r.fin_f.at[c], r.out_f.at[me], r.fi_s.at[2], r.fi_r.at[2], xn),
                remote(r.fin_f.at[1 - c], r.out_f.at[me], r.fi_s.at[3], r.fi_r.at[3], core),
                remote(r.fin_f.at[1 - c], r.out_f.at[me], r.fi_s.at[4], r.fi_r.at[4], diag),
            ])

        @pl.when(jnp.logical_not(w1))
        def _():
            copies = []
            for j in range(2):
                r.out_f[2 * x + j] = r.fin_f[j]
                copies.append(remote(r.fin_f.at[j], r.out_f.at[2 * x + j], r.fi_s.at[2 + j], r.fi_r.at[2 + j], xn))
            both(copies)

    du2, dgain, dshift = norm_back(r.sum2[...], cross_v(3), d_second)
    r.vg[3, 8:9] = dgain
    r.vg[3, 9:10] = dshift
    low = du2.astype(BF)
    r.vg[3, 7:8] = rows_sum(low)
    dca = mm_nt(low, r.wc[3584:4352]).astype(BF)
    drain(sent_w[1])
    r.wc[3584:4352] = mm_tn(r.ca[...], low).astype(BF)
    dcq = []
    for i in range(2):
        rows = slice(272 * i, 272 * i + 272)
        mine = slice(32 * i, 32 * i + 32)
        blocks = []
        for g in range(3):
            lanes = slice(256 * g, 256 * g + 256)
            dq, dk, dv = attend_block_back(
                r.cq[mine, lanes], r.ck[rows, lanes], r.cv[rows, lanes], r.pc[i, g], dca[mine, lanes]
            )
            blocks.append(dq)
            r.dck[rows, lanes] = dk
            r.dcv[rows, lanes] = dv
        dcq.append(jnp.concatenate(blocks, 1))
    dcq = jnp.concatenate(dcq, 0)
    r.vg[3, 5:6] = rows_sum(dcq)
    r.vg[3, 6:7] = rows_sum(r.dcv[...])
    du = du2 + mm_nt(dcq, r.wc[0:768])
    for i in range(2):
        r.dfirst[64 * i : 64 * i + 32] = du[32 * i : 32 * i + 32]
    r.wc[0:768] = mm_tn(rows_of(r.first, 0).astype(BF), dcq).astype(BF)
    for j in range(11):
        block = r.feat[:, 128 * j : 128 * j + 128]
        r.wc[768 + 128 * j : 896 + 128 * j] = mm_tn(block, r.dck[...]).astype(BF)
        r.wc[2176 + 128 * j : 2304 + 128 * j] = mm_tn(block, r.dcv[...]).astype(BF)
    sum_start(1)
    ffn_sum_y(2)
    ffn_sum_y(3)

    dsum1, dgain, dshift = norm_back(r.sum1[...], self_v(3), r.dfirst[...])
    r.vg[3, 3:4] = dgain
    r.vg[3, 4:5] = dshift
    low = dsum1.astype(BF)
    r.vg[3, 2:3] = rows_sum(low)
    da = mm_nt(low, r.ws[3]).astype(BF)
    drain(sent_w[0])
    r.ws[3] = mm_tn(r.a[...], low).astype(BF)
    for i in range(2):
        rows = slice(64 * i, 64 * i + 64)
        for g in range(3):
            lanes = slice(256 * g, 256 * g + 256)
            dq, dk, dv = attend_block_back(
                r.q[rows, lanes], r.k[rows, lanes], r.v[rows, lanes], r.p[i, g], da[rows, lanes]
            )
            r.dq[rows, lanes] = dq
            r.dk[rows, lanes] = dk
            r.dv[rows, lanes] = dv
    sum_core(1)
    r.vg[3, 0:1] = rows_sum(r.dq[...])
    r.vg[3, 1:2] = rows_sum(r.dv[...])
    total = dsum1 + mm_nt(r.dq[...], r.ws[0]) + mm_nt(r.dk[...], r.ws[1]) + mm_nt(r.dv[...], r.ws[2])
    r.hgrad[...] = total.astype(BF)
    r.ws[0] = mm_tn(r.hid[...], r.dq[...]).astype(BF)
    r.ws[1] = mm_tn(r.hid[...], r.dk[...]).astype(BF)
    r.ws[2] = mm_tn(r.hid[...], r.dv[...]).astype(BF)
    sum_start(0)

    r.v_send[...] = r.vg[...].astype(BF)
    index = 2 * y + c
    home = device(x, z, 1, 1)

    @pl.when(jnp.logical_not(root))
    def _():
        remote(r.v_send, r.v_in.at[index], r.vv_s.at[0], r.vv_r.at[index], home).start()

    ffn_sum_y(0)
    ffn_sum_y(1)
    sum_x(1, 0)
    sum_core(0)

    @pl.when(root)
    def _():
        total = r.vg[...]
        for i in range(3):
            arrived(r.v_in.at[i], r.vv_r.at[i])
            total = total + r.v_in[i].astype(F32)
        r.v_z[...] = total.astype(BF)
        for k in (1, 2, 3):
            zz = (z + k) % 4
            remote(r.v_z.at[zz], r.v_zin.at[k - 1], r.vv_s.at[k], r.vv_r.at[2 + k], device(x, zz, y, c)).start()

    sum_x(1, 1)
    sum_y(1)
    ffn_sum_z()
    sum_x(0, 0)
    sum_x(0, 1)

    @pl.when(root)
    def _():
        total = r.v_z[z].astype(F32)
        for k in (1, 2, 3):
            arrived(r.v_zin.at[k - 1], r.vv_r.at[2 + k])
            total = total + r.v_zin[k - 1].astype(F32)
        r.v_x[...] = total.astype(BF)
        remote(r.v_x, r.v_xin, r.vv_s.at[4], r.vv_r.at[6], xn).start()

    sum_y(0)
    sum_z(1)
    sum_z(0)

    @pl.when(root)
    def _():
        arrived(r.v_xin, r.vv_r.at[6])
        r.out_v[...] = r.v_x[...].astype(F32) + r.v_xin[...].astype(F32)
        for k in (1, 2, 3):
            zz = (z + k) % 4
            remote(r.v_z.at[zz], r.v_zin.at[k - 1], r.vv_s.at[k], r.vv_r.at[2 + k], device(x, zz, y, c)).wait_send()
        remote(r.v_x, r.v_xin, r.vv_s.at[4], r.vv_r.at[6], xn).wait_send()

    @pl.when(jnp.logical_not(root))
    def _():
        r.out_v[...] = jnp.zeros_like(r.out_v)
        remote(r.v_send, r.v_in.at[index], r.vv_s.at[0], r.vv_r.at[index], home).wait_send()

    for g in range(2):
        arrived(groups[g][6].at[:, cols(1 - x)], r.fi_r.at[g])
    for p in range(4):

        @pl.when(z != p)
        def _():
            remote(r.yf.at[p], r.zf.at[z], r.zz_s.at[2, p], r.zz_r.at[2, z], device(x, p, y, c)).wait_send()

    drain(sent)


def layer(own_s, own_c, own_f, own_t, hid, allowed, feat, cot):
    vm = pl.BlockSpec(memory_space=pltpu.VMEM)
    anywhere = pl.BlockSpec(memory_space=pl.ANY)
    return pl.pallas_call(
        layer_kernel,
        out_shape=(
            jax.ShapeDtypeStruct((128, D), BF),
            jax.ShapeDtypeStruct((128, D), BF),
            jax.ShapeDtypeStruct((192, D), BF),
            jax.ShapeDtypeStruct((272, D), BF),
            jax.ShapeDtypeStruct((4, 192, D), BF),
            jax.ShapeDtypeStruct((16, D), F32),
        ),
        in_specs=[anywhere] * 4 + [vm] * 4,
        out_specs=[vm] * 6,
        scratch_shapes=list(scratch().values()),
        compiler_params=pltpu.CompilerParams(
            collective_id=0, has_side_effects=True, vmem_limit_bytes=VMEM_BYTES
        ),
    )(own_s, own_c, own_f, own_t, hid, allowed, feat, cot)


def shift_back():
    x, z, y, c = place()
    f = lax.axis_index("fsdp")
    return 2 * f, 2 * f, 6 * (f % 4) + jnp.where(z >= 2, 6, 0)


def own_rows(self_params, cross_params, ffn_params):
    x, z, y, c = place()
    flats = [v.reshape(-1, 128) for v in (self_params, cross_params, ffn_params)]
    tails = jnp.concatenate([v[-32:] for v in flats])
    before = lax.ppermute(tails, "fsdp", [(i, (i + 1) % 16) for i in range(16)])
    nice = []
    for i, (v, rows, back) in enumerate(zip(flats, (1152, 1632, 4608), shift_back())):
        both = jnp.concatenate([before[32 * i : 32 * i + 32], v])
        nice.append(lax.dynamic_slice_in_dim(both, 32 - back, rows))
    own_s = nice[0].reshape(192, D)
    own_c = nice[1].reshape(272, D)
    cols = nice[2].reshape(192, 2, 4, 3, 128)
    pick = lambda cc: lax.dynamic_index_in_dim(cols, 2 * cc + x, 2, keepdims=False).reshape(192, D)
    as_w1 = jnp.stack([pick(c), pick(1 - c)])
    as_w2 = lax.dynamic_index_in_dim(nice[2].reshape(2, 2, 192, D), x, keepdims=False)
    own_f = jnp.where(z % 2 == 0, as_w1, as_w2)

    b1 = lambda v: v.reshape(2, 4, 384).transpose(1, 0, 2).reshape(4, D)
    rest = lambda v: jnp.concatenate([v.reshape(3, D), jnp.zeros((1, D), BF)])
    ffn = jnp.stack([b1(tails[72:96]), rest(tails[72:90]), b1(tails[66:90]), rest(tails[66:84])])
    own_t = jnp.concatenate([
        tails[0:30].reshape(5, D),
        tails[32:62].reshape(5, D),
        lax.dynamic_index_in_dim(ffn, z, keepdims=False),
        jnp.zeros((2, D), BF),
    ])
    return own_s, own_c, own_f, own_t


def flat_grads(out_s, out_c, out_f, out_v):
    x, z, y, c = place()
    f = lax.axis_index("fsdp")
    k = f % 4
    w1 = out_f.reshape(4, 192, 2, 3, 128).transpose(1, 2, 0, 3, 4).reshape(4608, 128)
    w2 = out_f.reshape(4608, 128)
    nice = [out_s.reshape(1152, 128), out_c.reshape(1632, 128), jnp.where(z % 2 == 0, w1, w2)]
    heads = jnp.concatenate([v[:32] for v in nice])
    after = lax.ppermute(heads, "fsdp", [(i, (i + 15) % 16) for i in range(16)]).astype(F32)
    zeros = lambda n: jnp.zeros((n, 128), F32)
    flat = lambda v: v.reshape(-1, 128)
    tail_s = jnp.where(f == 15, jnp.concatenate([flat(out_v[0:5]), zeros(2)]), after[0:32])
    tail_c = jnp.where(f == 15, jnp.concatenate([flat(out_v[5:10]), zeros(2)]), after[32:64])
    nxt = after[64:96]
    b1 = out_v[10:14].reshape(4, 2, 384).transpose(1, 0, 2).reshape(24, 128)
    rest = flat(out_v[10:13])
    ends = jnp.stack([
        jnp.concatenate([b1, zeros(8)]),
        jnp.concatenate([rest, nxt[:14]]),
        jnp.concatenate([b1, nxt[:8]]),
        jnp.concatenate([rest, zeros(14)]),
    ])
    tail_f = jnp.where(k == 3, lax.dynamic_index_in_dim(ends, z, keepdims=False), nxt)
    outs = []
    for v, tail, start, rows in zip(nice, (tail_s, tail_c, tail_f), shift_back(), (1154, 1634, 4614)):
        both = jnp.concatenate([v.astype(F32), tail])
        outs.append(lax.dynamic_slice_in_dim(both, start, rows).reshape(-1))
    return outs


def per_device_fast(hidden, lengths, features, cotangent, self_params, cross_params, ffn_params):
    own = own_rows(self_params, cross_params, ffn_params)
    at = jnp.arange(64)
    r, k = at[:, None], at[None, :]
    allowed = (k < NQ)[None] | ((r >= NQ) & (k <= r))[None] & (k[None] < NQ + lengths[:, None, None])
    feat = jnp.pad(features, ((0, 0), (0, 15), (0, 0))).reshape(544, E)
    mixed, hgrad, *sums = layer(
        *own, hidden.reshape(128, D), allowed.astype(F32), feat, cotangent.reshape(128, D)
    )
    return (mixed.reshape(2, 64, D), hgrad.reshape(2, 64, D), *flat_grads(*sums))


def solution(mesh):
    fast = mesh.shape["dp"] == 2 and mesh.shape["fsdp"] == 16
    return jax.shard_map(
        per_device_fast if fast else per_device,
        mesh=mesh,
        in_specs=(
            P(("dp", "fsdp"), None, None),
            P(("dp", "fsdp")),
            P(("dp", "fsdp"), None, None),
            P(("dp", "fsdp"), None, None),
            P("fsdp"),
            P("fsdp"),
            P("fsdp"),
        ),
        out_specs=(
            P(("dp", "fsdp"), None, None),
            P(("dp", "fsdp"), None, None),
            P("fsdp"),
            P("fsdp"),
            P("fsdp"),
        ),
        check_vma=False,
    )
```

```python
from functools import partial
import math
from types import SimpleNamespace

import jax
import jax.numpy as jnp
from jax import lax
from jax.experimental import pallas as pl
from jax.experimental.pallas import tpu as pltpu
from jax.sharding import PartitionSpec as P

D = 768
HEADS = 12
HDIM = 64
F = 3072
E = 1408
NQ = 32


EPS = 1e-06
SCALE = 0.125


def self_layout():
    return [(D, D)] * 4 + [(D,)] * 5


def cross_layout():
    return [(D, D), (E, D), (E, D), (D, D)] + [(D,)] * 5


def ffn_layout():
    return [(D, F), (F,), (F, D), (D,), (D,), (D,)] * 2


def split_flat(flat_vec, layouts):
    pieces = []
    offset = 0
    for layout in layouts:
        amount = math.prod(layout)
        pieces.append(flat_vec[offset : offset + amount].reshape(layout))
        offset = offset + amount
    return pieces


def join_flat(pieces, length):
    flat_vec = jnp.concatenate([piece.reshape(-1) for piece in pieces])
    return jnp.pad(flat_vec, (0, length - flat_vec.shape[0]))


def regroup(flat_vec):
    groups = lax.axis_size("fsdp")
    replicas = lax.axis_size("dp")
    return flat_vec.reshape(groups, replicas, -1).transpose(1, 0, 2).reshape(-1)


def matmul(left, right):
    return jnp.dot(left, right, preferred_element_type=jnp.float32)


def matmul_left(left, right):
    return lax.dot_general(
        left, right, (((0,), (0,)), ((), ())), preferred_element_type=jnp.float32
    )


def matmul_right(left, right):
    return lax.dot_general(
        left, right, (((1,), (1,)), ((), ())), preferred_element_type=jnp.float32
    )


def column_sum(values):
    return jnp.sum(values.astype(jnp.float32), 0)


def layer_norm(values, gain, shift):
    average = jnp.mean(values, -1, keepdims=True)
    centered = values - average
    variance = jnp.mean(centered * centered, -1, keepdims=True)
    return centered * lax.rsqrt(variance + EPS) * gain + shift


def norm_backward(summed, gain, shift, grad_out):
    _, norm_pull = jax.vjp(layer_norm, summed, gain.astype(jnp.float32), shift.astype(jnp.float32))
    return norm_pull(grad_out)


def heads(rows, items):
    return rows.reshape(items, -1, HEADS, HDIM)


def score_block(query, keys, mask):
    scores = jnp.einsum("iqhd,ikhd->ihqk", query, keys, preferred_element_type=jnp.float32) * SCALE
    if mask is not None:
        scores = jnp.where(mask, scores, -1e30)
    return scores


def attend(query, keys, values, mask):
    scores = score_block(query, keys, mask)
    top_sum = jax.nn.logsumexp(scores, axis=-1)
    probs = jnp.exp(scores - top_sum[..., None]).astype(jnp.bfloat16)
    context = jnp.einsum("ihqk,ikhd->iqhd", probs, values, preferred_element_type=jnp.float32)
    return (context, top_sum)


def attend_back(query, keys, values, mask, top_sum, grad_context):
    probs = jnp.exp(score_block(query, keys, mask) - top_sum[..., None])
    grad_probs = jnp.einsum(
        "iqhd,ikhd->ihqk", grad_context, values, preferred_element_type=jnp.float32
    )
    inner = jnp.sum(probs * grad_probs, -1, keepdims=True)
    grad_scores = (probs * (grad_probs - inner)).astype(jnp.bfloat16)
    grad_query = (
        jnp.einsum("ihqk,ikhd->iqhd", grad_scores, keys, preferred_element_type=jnp.float32) * SCALE
    )
    grad_keys = (
        jnp.einsum("ihqk,iqhd->ikhd", grad_scores, query, preferred_element_type=jnp.float32)
        * SCALE
    )
    grad_values = jnp.einsum(
        "ihqk,iqhd->ikhd",
        probs.astype(jnp.bfloat16),
        grad_context,
        preferred_element_type=jnp.float32,
    )
    return (grad_query, grad_keys, grad_values)


def linear_back(inputs, weight, grad_out):
    return (matmul_left(inputs, grad_out), column_sum(grad_out), matmul_right(grad_out, weight))


def ffn_forward(rows, params):
    w_in, b_in, w_out, b_out, gain, shift = params
    rows_low = rows.astype(jnp.bfloat16)
    hidden_pre = matmul(rows_low, w_in) + b_in
    activated = jax.nn.gelu(hidden_pre, approximate=True).astype(jnp.bfloat16)
    summed = rows + (matmul(activated, w_out) + b_out)
    final = layer_norm(summed, gain.astype(jnp.float32), shift.astype(jnp.float32))
    return (final, (rows_low, hidden_pre, activated, summed))


def ffn_backward(grad_out, kept, params):
    w_in, b_in, w_out, b_out, gain, shift = params
    rows_low, hidden_pre, activated, summed = kept
    grad_sum, grad_gain, grad_shift = norm_backward(summed, gain, shift, grad_out)
    grad_branch = grad_sum.astype(jnp.bfloat16)
    grad_w_out, grad_b_out, grad_act = linear_back(activated, w_out, grad_branch)
    _, gelu_pull = jax.vjp(partial(jax.nn.gelu, approximate=True), hidden_pre)
    grad_pre = gelu_pull(grad_act)[0].astype(jnp.bfloat16)
    grad_w_in, grad_b_in, grad_rows = linear_back(rows_low, w_in, grad_pre)
    return (
        grad_sum + grad_rows,
        [grad_w_in, grad_b_in, grad_w_out, grad_b_out, grad_gain, grad_shift],
    )


def per_device(hidden, lengths, features, cotangent, self_params, cross_params, ffn_params):
    items, seq, width = hidden.shape
    self_full = lax.all_gather(self_params, "fsdp", axis=0, tiled=True)
    self_parts = split_flat(self_full, self_layout())
    w_q, w_k, w_v, w_o, b_q, b_v, b_o, gain_one, shift_one = self_parts
    positions = jnp.arange(seq)
    rows_at = positions[:, None]
    cols_at = positions[None, :]
    allowed = (cols_at < NQ)[None] | ((rows_at >= NQ) & (cols_at <= rows_at))[None] & (
        cols_at[None] < NQ + lengths[:, None, None]
    )
    allowed = allowed[:, None]
    inputs = hidden.reshape(-1, width)
    query_low = (matmul(inputs, w_q) + b_q).astype(jnp.bfloat16)
    key_low = matmul(inputs, w_k).astype(jnp.bfloat16)
    value_low = (matmul(inputs, w_v) + b_v).astype(jnp.bfloat16)
    context, self_top = attend(
        heads(query_low, items), heads(key_low, items), heads(value_low, items), allowed
    )
    context_low = context.reshape(-1, width).astype(jnp.bfloat16)
    summed_one = inputs.astype(jnp.float32) + (matmul(context_low, w_o) + b_o)
    first = layer_norm(summed_one, gain_one.astype(jnp.float32), shift_one.astype(jnp.float32))
    first_items = first.reshape(items, seq, width)
    query_rows = first_items[:, :NQ].reshape(-1, width)
    text_rows = first_items[:, NQ:].reshape(-1, width)
    cross_full = lax.all_gather(cross_params, "fsdp", axis=0, tiled=True)
    cross_parts = split_flat(cross_full, cross_layout())
    cross_wq, cross_wk, cross_wv, cross_wo, cross_bq, cross_bv, cross_bo, gain_two, shift_two = (
        cross_parts
    )
    query_in = query_rows.astype(jnp.bfloat16)
    image_rows = features.reshape(-1, features.shape[-1])
    cross_query = (matmul(query_in, cross_wq) + cross_bq).astype(jnp.bfloat16)
    cross_key = matmul(image_rows, cross_wk).astype(jnp.bfloat16)
    cross_value = (matmul(image_rows, cross_wv) + cross_bv).astype(jnp.bfloat16)
    cross_context, cross_top = attend(
        heads(cross_query, items), heads(cross_key, items), heads(cross_value, items), None
    )
    cross_low = cross_context.reshape(-1, width).astype(jnp.bfloat16)
    summed_two = query_rows + (matmul(cross_low, cross_wo) + cross_bo)
    second = layer_norm(summed_two, gain_two.astype(jnp.float32), shift_two.astype(jnp.float32))
    ffn_full = lax.all_gather(ffn_params, "fsdp", axis=0, tiled=True)
    ffn_parts = split_flat(ffn_full, ffn_layout())
    query_final, query_kept = ffn_forward(second, ffn_parts[:6])
    text_final, text_kept = ffn_forward(text_rows, ffn_parts[6:])
    mixed = jnp.concatenate(
        [query_final.reshape(items, NQ, width), text_final.reshape(items, -1, width)], 1
    ).astype(jnp.bfloat16)
    grad_items = cotangent.astype(jnp.float32)
    grad_query_final = grad_items[:, :NQ].reshape(-1, width)
    grad_text_final = grad_items[:, NQ:].reshape(-1, width)
    ffn_back = split_flat(lax.all_gather(ffn_params, "fsdp", axis=0, tiled=True), ffn_layout())
    grad_second, query_grads = ffn_backward(grad_query_final, query_kept, ffn_back[:6])
    grad_text, text_grads = ffn_backward(grad_text_final, text_kept, ffn_back[6:])
    ffn_flat_grad = join_flat(query_grads + text_grads, ffn_full.shape[0])
    ffn_grad = lax.psum_scatter(
        regroup(ffn_flat_grad), ("dp", "fsdp"), scatter_dimension=0, tiled=True
    )
    cross_back = split_flat(
        lax.all_gather(cross_params, "fsdp", axis=0, tiled=True), cross_layout()
    )
    grad_summed_two, grad_gain_two, grad_shift_two = norm_backward(
        summed_two, cross_back[7], cross_back[8], grad_second
    )
    grad_cross_out = grad_summed_two.astype(jnp.bfloat16)
    grad_cross_wo, grad_cross_bo, grad_cross_ctx = linear_back(
        cross_low, cross_back[3], grad_cross_out
    )
    grad_cq, grad_ck, grad_cv = attend_back(
        heads(cross_query, items),
        heads(cross_key, items),
        heads(cross_value, items),
        None,
        cross_top,
        heads(grad_cross_ctx.astype(jnp.bfloat16), items),
    )
    grad_cq = grad_cq.reshape(-1, width).astype(jnp.bfloat16)
    grad_ck = grad_ck.reshape(-1, width).astype(jnp.bfloat16)
    grad_cv = grad_cv.reshape(-1, width).astype(jnp.bfloat16)
    grad_cross_wq, grad_cross_bq, grad_query_in = linear_back(query_in, cross_back[0], grad_cq)
    grad_cross_wk = matmul_left(image_rows, grad_ck)
    grad_cross_wv = matmul_left(image_rows, grad_cv)
    grad_cross_bv = column_sum(grad_cv)
    grad_query_rows = grad_summed_two + grad_query_in
    cross_list = [
        grad_cross_wq,
        grad_cross_wk,
        grad_cross_wv,
        grad_cross_wo,
        grad_cross_bq,
        grad_cross_bv,
        grad_cross_bo,
        grad_gain_two,
        grad_shift_two,
    ]
    cross_flat_grad = join_flat(cross_list, cross_full.shape[0])
    cross_grad = lax.psum_scatter(
        regroup(cross_flat_grad), ("dp", "fsdp"), scatter_dimension=0, tiled=True
    )
    self_back = split_flat(lax.all_gather(self_params, "fsdp", axis=0, tiled=True), self_layout())
    grad_first = jnp.concatenate(
        [grad_query_rows.reshape(items, NQ, width), grad_text.reshape(items, -1, width)], 1
    ).reshape(-1, width)
    grad_summed_one, grad_gain_one, grad_shift_one = norm_backward(
        summed_one, self_back[7], self_back[8], grad_first
    )
    grad_attn = grad_summed_one.astype(jnp.bfloat16)
    grad_w_o, grad_b_o, grad_ctx = linear_back(context_low, self_back[3], grad_attn)
    grad_q, grad_k, grad_v = attend_back(
        heads(query_low, items),
        heads(key_low, items),
        heads(value_low, items),
        allowed,
        self_top,
        heads(grad_ctx.astype(jnp.bfloat16), items),
    )
    grad_q = grad_q.reshape(-1, width).astype(jnp.bfloat16)
    grad_k = grad_k.reshape(-1, width).astype(jnp.bfloat16)
    grad_v = grad_v.reshape(-1, width).astype(jnp.bfloat16)
    grad_w_q, grad_b_q, input_from_q = linear_back(inputs, self_back[0], grad_q)
    grad_w_k = matmul_left(inputs, grad_k)
    input_from_k = matmul_right(grad_k, self_back[1])
    grad_w_v, grad_b_v, input_from_v = linear_back(inputs, self_back[2], grad_v)
    hidden_grad = (
        (grad_summed_one + input_from_q + input_from_k + input_from_v)
        .reshape(items, seq, width)
        .astype(jnp.bfloat16)
    )
    self_list = [
        grad_w_q,
        grad_w_k,
        grad_w_v,
        grad_w_o,
        grad_b_q,
        grad_b_v,
        grad_b_o,
        grad_gain_one,
        grad_shift_one,
    ]
    self_flat_grad = join_flat(self_list, self_full.shape[0])
    self_grad = lax.psum_scatter(
        regroup(self_flat_grad), ("dp", "fsdp"), scatter_dimension=0, tiled=True
    )
    self_grad, cross_grad, ffn_grad = (
        lax.all_gather(self_grad.astype(jnp.bfloat16), "dp", axis=0, tiled=True).astype(
            self_grad.dtype
        ),
        lax.all_gather(cross_grad.astype(jnp.bfloat16), "dp", axis=0, tiled=True).astype(
            cross_grad.dtype
        ),
        lax.all_gather(ffn_grad.astype(jnp.bfloat16), "dp", axis=0, tiled=True).astype(
            ffn_grad.dtype
        ),
    )
    return (mixed, hidden_grad, self_grad, cross_grad, ffn_grad)


MESH = pl.DeviceIdType.MESH
BF = jnp.bfloat16
F32 = jnp.float32
VMEM_BYTES = 62 * 2**20


def place():
    f = lax.axis_index("fsdp")
    return lax.axis_index("dp"), f // 4, (f // 2) % 2, f % 2


def device(x, z, y, c):
    return (x, (z * 2 + y) * 2 + c)


def meet(devices):
    barrier = pltpu.get_barrier_semaphore()
    for d in devices:
        pl.semaphore_signal(barrier, inc=1, device_id=d, device_id_type=MESH)
    pl.semaphore_wait(barrier, len(devices))


def remote(src, dst, send, recv, target):
    return pltpu.make_async_remote_copy(
        src_ref=src,
        dst_ref=dst,
        send_sem=send,
        recv_sem=recv,
        device_id=target,
        device_id_type=MESH,
    )


def mm(a, b):
    return jnp.dot(a, b, preferred_element_type=F32)


def mm_nt(a, b):
    return lax.dot_general(a, b, (((1,), (1,)), ((), ())), preferred_element_type=F32)


def mm_tn(a, b):
    return lax.dot_general(a, b, (((0,), (0,)), ((), ())), preferred_element_type=F32)


def rows_sum(v):
    return jnp.sum(v.astype(F32), 0, keepdims=True)


def add(a, b):
    return (a.astype(F32) + b.astype(F32)).astype(BF)


def normed(v):
    centered = v - jnp.mean(v, -1, keepdims=True)
    r = lax.rsqrt(jnp.mean(centered * centered, -1, keepdims=True) + EPS)
    return centered * r, r


def norm_back(v, gain, g_out):
    xh, r = normed(v)
    gg = g_out * gain
    dv = r * (gg - jnp.mean(gg, -1, keepdims=True) - xh * jnp.mean(gg * xh, -1, keepdims=True))
    return dv, rows_sum(g_out * xh), rows_sum(g_out)


GELU_A = math.sqrt(2.0 / math.pi)
GELU_B = 0.044715


def gelu(v):
    return 0.5 * v * (1.0 + jnp.tanh(GELU_A * (v + GELU_B * (v * v * v))))


def gelu_slope(v):
    t = jnp.tanh(GELU_A * (v + GELU_B * (v * v * v)))
    return 0.5 * (1.0 + t) + 0.5 * v * (1.0 - t * t) * (GELU_A * (1.0 + 3.0 * GELU_B * (v * v)))


def head_mask(h):
    lane = lax.broadcasted_iota(jnp.int32, (1, 256), 1)
    return jnp.where(lane // HDIM == h, 1.0, 0.0)


def spread(rows):
    wide = rows.astype(F32)
    return jnp.concatenate([(wide * head_mask(h)).astype(BF) for h in range(4)], 0)


def fold(stacked):
    n = stacked.shape[0] // 4
    total = stacked[:n] * head_mask(0)
    for h in range(1, 4):
        total = total + stacked[h * n : (h + 1) * n] * head_mask(h)
    return total


def attend_block(q, k, v, allowed):
    s = mm_nt(spread(q), k) * SCALE
    s = jnp.where(allowed > 0.5, s, -1e30)
    e = jnp.exp(s - jnp.max(s, -1, keepdims=True))
    p = e / jnp.sum(e, -1, keepdims=True)
    return p, fold(mm(p.astype(BF), v)).astype(BF)


def attend_block_back(q, k, v, p, da):
    dax = spread(da)
    dp = mm_nt(dax, v)
    ds = (p * (dp - jnp.sum(p * dp, -1, keepdims=True))).astype(BF)
    dq = (fold(mm(ds, k)) * SCALE).astype(BF)
    dk = (mm_tn(ds, spread(q)) * SCALE).astype(BF)
    dv = mm_tn(p.astype(BF), dax).astype(BF)
    return dq, dk, dv


def rows_of(ref, first):
    return jnp.concatenate([ref[first : first + 32], ref[64 + first : 96 + first]], 0)


SPLIT = 288
REST = 384 - SPLIT
STREAMS = ((192, 384), (272, 384), (SPLIT, D), (REST, D), (REST, D))


def scratch():
    dma = lambda *s: pltpu.SemaphoreType.DMA(s)
    b = lambda *s: pltpu.VMEM(s, BF)
    f = lambda *s: pltpu.VMEM(s, F32)
    return dict(
        ws=b(4, D, D), wc=b(4352, D), wf=b(4, D, D), block_f=b(384, D), tb=b(4, 16, D),
        tv=f(4, 16, D), vg=f(4, 16, D),
        q=b(128, D), k=b(128, D), v=b(128, D), a=b(128, D), p=f(2, 3, 256, 64),
        sum1=f(128, D), first=f(128, D), cq=b(64, D), ck=b(544, D), cv=b(544, D), ca=b(64, D),
        pc=f(2, 3, 128, 272), sum2=f(64, D), second=f(64, D),
        xg=b(2, 2, 4, 64, D), pre=f(2, 256, D), act=b(2, 256, D), part=f(2, 4, 64, D),
        send_p=b(2, 2, 2, 64, D), recv_p=b(2, 2, 2, 64, D), send_x=b(2, 2, 64, D), recv_x=b(2, 2, 64, D),
        sum3=f(2, 64, D), dpre=b(2, 256, D), dsum3=f(2, 64, D), dfirst=f(128, D),
        dq=b(128, D), dk=b(128, D), dv=b(128, D), dck=b(544, D), dcv=b(544, D),
        core_s=b(2, 4, 192, D), core_c=b(2, 4, 272, D), xs=b(2, 4, 192, 384), xc=b(2, 4, 272, 384),
        ys=b(4, 192, 384), yc=b(4, 272, 384), yf=b(4, SPLIT, D), yf2=b(REST, D), of=b(REST, D),
        fin_s=b(192, 384), fin_c=b(272, 384), fin_f=b(384, D),
        **{f"{n}{i}": b(*lead, *shape) for i, shape in enumerate(STREAMS) for n, lead in (("zb", (3,)), ("zr", ()), ("zq", ()))},
        v_send=b(4, 16, D), v_in=b(3, 4, 16, D), v_z=b(4, 16, D), v_zin=b(3, 16, D), v_x=b(16, D), v_xin=b(16, D),
        loc=dma(4), gz_s=dma(7, 4), gz_r=dma(7, 4), gy_s=dma(7, 4), gy_r=dma(7, 4), gx_s=dma(2, 7), gx_r=dma(2, 7),
        gc_s=dma(3, 15), gc_r=dma(3, 15), t_s=dma(6), t_r=dma(4),
        ex_s=dma(2, 2, 3), ex_r=dma(2, 2, 3), rs_s=dma(2, 2, 3), rs_r=dma(2, 2, 3),
        co_s=dma(2, 2, 4), co_r=dma(2, 2, 4), xx_s=dma(2, 2, 4), xx_r=dma(2, 2, 4), yy_s=dma(4, 4), yy_r=dma(4, 4),
        zz_s=dma(5, 4), zz_r=dma(5, 4), zq_s=dma(5), zq_r=dma(5), fi_s=dma(5), fi_r=dma(5), vv_s=dma(5), vv_r=dma(7),
    )


def layer_kernel(*refs):
    names = [
        "own_s", "own_c", "own_f", "own_t", "hid", "allowed", "feat", "cot",
        "mixed", "hgrad", "out_s", "out_c", "out_f", "out_v",
    ] + list(scratch())
    r = SimpleNamespace(**dict(zip(names, refs)))
    x, z, y, c = place()
    core, xn, yn = device(x, z, y, 1 - c), device(1 - x, z, y, c), device(x, z, 1 - y, c)
    diag = device(1 - x, z, y, 1 - c)
    zdev = lambda d: device(x, (z + d) % 4, y, c)
    meet([core, xn, yn, diag, device(x, z, 1 - y, 1 - c), zdev(1), zdev(2), zdev(3)])
    me = 2 * c + x
    cols = lambda h: pl.ds(pl.multiple_of(384 * h, 384), 384)
    root = jnp.logical_and(y == 1, c == 1)
    w1 = z % 2 == 0

    inner = jnp.logical_and(z > 0, z < 3)
    outer = jnp.logical_not(inner)

    def when(cond, what):
        if cond is None:
            what()
        else:
            pl.when(cond)(what)

    def go(sent, src, dst, send, recv, target, cond=None):
        make = lambda: remote(src, dst, send, recv, target)
        when(cond, lambda: make().start())
        sent.append((make, cond))

    def arrived(view, recv):
        remote(view, view, recv, recv, core).wait_recv()

    def drain(sent):
        for make, cond in sent:
            when(cond, lambda: make().wait_send())

    def shard_s(zz, yy, cc):
        return r.ws.at[zz, pl.ds(pl.multiple_of(192 * (2 * yy + cc), 192), 192)]

    def shard_c(zz, yy, cc):
        return r.wc.at[pl.ds(pl.multiple_of(272 * ((zz * 2 + yy) * 2 + cc), 16), 272)]

    def part_f(zz, yy, lo=0, n=384):
        return r.wf.at[zz, pl.ds(pl.multiple_of(384 * yy + lo, 16), n)]

    shards = (shard_s, shard_c)
    sent_w = ([], [], [])
    steps = [jnp.where(z == 0, 3 - i, jnp.where(z == 3, 1 + i, (2, 1, 3)[i])) for i in range(3)]

    def part(g, zz, yy, cc, h):
        if g >= 2:
            return part_f(zz, yy, 96 * (g - 2), 96)
        view = shards[g](zz, yy, cc)
        return view if h is None else view.at[:, cols(h)]

    def own_part(g):
        if g >= 2:
            return r.block_f.at[pl.ds(96 * (g - 2), 96)]
        return (r.own_s, r.own_c)[g].at[:, cols(x)]

    def z_out(src, dst, g, i):
        for k in (2, 1, 3):
            cond = {1: z != 3, 2: None, 3: z != 0}[k]
            go(sent_w[min(g, 2)], src, dst, r.gz_s.at[i, k], r.gz_r.at[i, k], zdev(k), cond)

    def z_on(view, g, i, k):
        cond = jnp.logical_and(inner, k == 2)
        go(sent_w[min(g, 2)], view, view, r.gz_s.at[i, 0], r.gz_r.at[i, 2 * z - 1], device(x, 3 * (z - 1), y, c), cond)

    def own_z(g):
        z_out(own_part(g), part(g, z, y, c, x), g, g)

    def own_y(g):
        go(sent_w[min(g, 2)], own_part(g), part(g, z, y, c, x), r.gy_s.at[g, 0], r.gy_r.at[g, 0], yn)

    def own_core(g):
        own = (r.own_s, r.own_c)[g]
        go(sent_w[g], own, part(g, z, y, c, None), r.gc_s.at[g, 0], r.gc_r.at[g, 0], core)
        copy = pltpu.make_async_copy(own, part(g, z, y, c, None), r.loc.at[g])
        copy.start()
        return copy

    def gather_z(g, last=False):
        for k in steps:
            view = part(g, (z - k) % 4, y, c, x)
            arrived(view, r.gz_r.at[g, k])
            z_on(view, g, g, k)
            if not last:
                go(sent_w[min(g, 2)], view, view, r.gy_s.at[g, k], r.gy_r.at[g, k], yn)
            if g < 2:
                go(sent_w[g], view, view, r.gx_s.at[g, k - 1], r.gx_r.at[g, k - 1], xn)
                go(sent_w[g], view, view, r.gc_s.at[g, k], r.gc_r.at[g, k], core)

    def gather_y(g, which=(0, 1, 2, 3)):
        for j in which:
            view = part(g, (z - j) % 4, 1 - y, c, x)
            arrived(view, r.gy_r.at[g, j])
            if g < 2:
                go(sent_w[g], view, view, r.gx_s.at[g, 3 + j], r.gx_r.at[g, 3 + j], xn)
                go(sent_w[g], view, view, r.gc_s.at[g, 4 + j], r.gc_r.at[g, 4 + j], core)

    def other_z():
        view = part(5, z, 1 - y, c, x)
        arrived(view, r.gy_r.at[5, 0])
        z_out(view, view, 5, 6)

    def other_arrivals():
        for k in steps:
            view = part(5, (z - k) % 4, 1 - y, c, x)
            arrived(view, r.gz_r.at[6, k])
            z_on(view, 5, 6, k)

    def gather_x(g):
        for j in range(7):
            view = part(g, (z - j - 1) % 4, y, c, 1 - x) if j < 3 else part(g, (z - j + 3) % 4, 1 - y, c, 1 - x)
            arrived(view, r.gx_r.at[g, j])
            go(sent_w[g], view, view, r.gc_s.at[g, 8 + j], r.gc_r.at[g, 8 + j], core)

    def gather_core(g, which):
        for j in which:
            if j == 0:
                view = part(g, z, y, 1 - c, None)
            elif j < 4:
                view = part(g, (z - j) % 4, y, 1 - c, x)
            elif j < 8:
                view = part(g, (z - j + 4) % 4, 1 - y, 1 - c, x)
            elif j < 11:
                view = part(g, (z - j + 7) % 4, y, 1 - c, 1 - x)
            else:
                view = part(g, (z - j + 11) % 4, 1 - y, 1 - c, 1 - x)
            arrived(view, r.gc_r.at[g, j])

    own_z(0)
    own_y(0)
    loc_s = own_core(0)

    @pl.when(root)
    def _():
        mine = pltpu.make_async_copy(r.own_t, r.tb.at[z], r.loc.at[3])
        mine.start()
        out = []
        for k in (1, 2, 3):
            go(out, r.own_t, r.tb.at[z], r.t_s.at[k - 1], r.t_r.at[k], zdev(k))
        mine.wait()
        for k in (1, 2, 3):
            arrived(r.tb.at[(z - k) % 4], r.t_r.at[k])
        for i, (yy, cc) in enumerate(((0, 0), (0, 1), (1, 0))):
            go(out, r.tb, r.tb, r.t_s.at[3 + i], r.t_r.at[0], device(x, z, yy, cc))
        drain(out)

    own_z(1)
    own_y(1)
    loc_c = own_core(1)
    fb = pl.ds(pl.multiple_of(192 * c, 192), 192)

    @pl.when(w1)
    def _():
        copy = remote(r.own_f.at[1], r.block_f.at[fb], r.gc_s.at[2, 0], r.gc_r.at[2, 0], core)
        copy.start()
        mine = pltpu.make_async_copy(r.own_f.at[0], r.block_f.at[fb], r.loc.at[2])
        mine.start()
        mine.wait()
        copy.wait()

    @pl.when(jnp.logical_not(w1))
    def _():
        for j in range(2):
            mine = pltpu.make_async_copy(r.own_f.at[j], r.block_f.at[pl.ds(192 * j, 192)], r.loc.at[2])
            mine.start()
            mine.wait()

    loc_f = pltpu.make_async_copy(r.block_f, part_f(z, y), r.loc.at[2])
    loc_f.start()
    r.vg[...] = jnp.zeros_like(r.vg)

    own_y(5)
    gather_z(0)
    own_z(2)
    for g in (2, 3, 4):
        own_y(g)
    gather_y(0)
    own_z(3)
    gather_z(1)
    own_z(4)
    own_z(5)
    other_z()
    gather_y(1, (0,))
    gather_z(2)
    gather_x(0)
    gather_y(1, (1, 2, 3))
    loc_s.wait()

    @pl.when(jnp.logical_not(root))
    def _():
        arrived(r.tb, r.t_r.at[0])

    r.tv[...] = r.tb[...].astype(F32)
    gather_core(0, range(15))

    self_v = lambda j: r.tv[3, j : j + 1]
    cross_v = lambda j: r.tv[3, 5 + j : 6 + j]
    ffn_b1 = lambda b: r.tv[2 * b, pl.ds(10 + me, 1)]
    ffn_v = lambda b, j: r.tv[2 * b + 1, 10 + j : 11 + j]

    def slot(xx, cc):
        return 2 * cc + xx

    def ag_copy(ph, b, i):
        buf = r.xg.at[ph, b]
        pair = [(me, xn), (me, core), (slot(1 - x, c), core)]
        s, t = pair[i]
        return remote(buf.at[s], buf.at[s], r.ex_s.at[ph, b, i], r.ex_r.at[ph, b, i], t)

    def ag_start(ph, b):
        ag_copy(ph, b, 0).start()
        ag_copy(ph, b, 1).start()

    def ag_mid(ph, b):
        ag_copy(ph, b, 0).wait_recv()
        ag_copy(ph, b, 2).start()

    def ag_end(ph, b):
        ag_copy(ph, b, 1).wait_recv()
        ag_copy(ph, b, 2).wait_recv()
        for i in range(3):
            ag_copy(ph, b, i).wait_send()

    def rs_copy(ph, b, i):
        src = r.send_x.at[ph, b] if i == 2 else r.send_p.at[ph, b, i]
        dst = r.recv_x.at[ph, b] if i == 2 else r.recv_p.at[ph, b, i]
        return remote(src, dst, r.rs_s.at[ph, b, i], r.rs_r.at[ph, b, i], xn if i == 2 else core)

    def rs_start(ph, b):
        r.send_p[ph, b, 0] = r.part[b, slot(1 - x, 1 - c)].astype(BF)
        rs_copy(ph, b, 0).start()
        r.send_p[ph, b, 1] = r.part[b, slot(x, 1 - c)].astype(BF)
        rs_copy(ph, b, 1).start()

    def rs_mid(ph, b):
        rs_copy(ph, b, 0).wait_recv()
        r.send_x[ph, b] = (r.part[b, slot(1 - x, c)] + r.recv_p[ph, b, 0].astype(F32)).astype(BF)
        rs_copy(ph, b, 2).start()

    def rs_end(ph, b):
        rs_copy(ph, b, 1).wait_recv()
        rs_copy(ph, b, 2).wait_recv()
        for i in range(3):
            rs_copy(ph, b, i).wait_send()
        return r.part[b, me] + r.recv_p[ph, b, 1].astype(F32) + r.recv_x[ph, b].astype(F32)

    h = r.hid[...]
    r.q[...] = (mm(h, r.ws[0]) + self_v(0)).astype(BF)
    r.k[...] = mm(h, r.ws[1]).astype(BF)
    r.v[...] = (mm(h, r.ws[2]) + self_v(1)).astype(BF)
    for i in range(2):
        rows = slice(64 * i, 64 * i + 64)
        ok = jnp.concatenate([r.allowed[i]] * 4, 0)
        for g in range(3):
            lanes = slice(256 * g, 256 * g + 256)
            p, a = attend_block(r.q[rows, lanes], r.k[rows, lanes], r.v[rows, lanes], ok)
            r.p[i, g] = p
            r.a[rows, lanes] = a
    r.sum1[...] = h.astype(F32) + (mm(r.a[...], r.ws[3]) + self_v(2))
    xh, _ = normed(r.sum1[...])
    r.first[...] = xh * self_v(3) + self_v(4)
    r.xg[0, 1, me] = rows_of(r.first, 32).astype(BF)
    ag_start(0, 1)

    loc_c.wait()
    gather_core(1, range(8))
    for i in range(2):
        rows = slice(272 * i, 272 * i + 272)
        r.ck[rows, cols(x)] = mm(r.feat[rows], r.wc[768:2176, cols(x)]).astype(BF)
        bias = r.tv[3, 6:7, cols(x)]
        r.cv[rows, cols(x)] = (mm(r.feat[rows], r.wc[2176:3584, cols(x)]) + bias).astype(BF)
    ag_mid(0, 1)
    gather_z(3)
    gather_z(4)
    gather_x(1)
    gather_core(1, range(8, 15))
    far_cols = cols(1 - x)
    for i in range(2):
        rows = slice(272 * i, 272 * i + 272)
        r.ck[rows, far_cols] = mm(r.feat[rows], r.wc[768:2176, far_cols]).astype(BF)
        bias = r.tv[3, 6:7, far_cols]
        r.cv[rows, far_cols] = (mm(r.feat[rows], r.wc[2176:3584, far_cols]) + bias).astype(BF)
    u = rows_of(r.first, 0)
    r.cq[...] = (mm(u.astype(BF), r.wc[0:768]) + cross_v(0)).astype(BF)
    ok = jnp.where(lax.broadcasted_iota(jnp.int32, (128, 272), 1) < 257, 1.0, 0.0)
    for i in range(2):
        rows = slice(272 * i, 272 * i + 272)
        mine = slice(32 * i, 32 * i + 32)
        for g in range(3):
            lanes = slice(256 * g, 256 * g + 256)
            p, a = attend_block(r.cq[mine, lanes], r.ck[rows, lanes], r.cv[rows, lanes], ok)
            r.pc[i, g] = p
            r.ca[mine, lanes] = a
    r.sum2[...] = u + (mm(r.ca[...], r.wc[3584:4352]) + cross_v(2))
    xh, _ = normed(r.sum2[...])
    r.second[...] = xh * cross_v(3) + cross_v(4)
    r.xg[0, 0, me] = r.second[...].astype(BF)
    ag_start(0, 0)

    loc_f.wait()
    gather_z(5, last=True)
    other_arrivals()
    for g in (2, 3, 4):
        gather_y(g)

    def ffn_forward_part(b):
        rows = r.xg[0, b].reshape(256, D)
        r.pre[b] = mm(rows, r.wf[2 * b]) + ffn_b1(b)
        r.act[b] = gelu(r.pre[b]).astype(BF)
        r.part[b] = mm(r.act[b], r.wf[2 * b + 1]).reshape(4, 64, D)

    def ffn_turn(b):
        rows = r.second[...] if b == 0 else rows_of(r.first, 32)
        s3 = rows + (rs_end(0, b) + ffn_v(b, 0))
        xh, _ = normed(s3)
        done = (xh * ffn_v(b, 1) + ffn_v(b, 2)).astype(BF)
        for i in range(2):
            r.mixed[64 * i + 32 * b : 64 * i + 32 * b + 32] = done[32 * i : 32 * i + 32]
        g_out = rows_of(r.cot, 32 * b).astype(F32)
        dsum, dgain, dshift = norm_back(s3, ffn_v(b, 1), g_out)
        r.dsum3[b] = dsum
        low = dsum.astype(BF)
        r.xg[1, b, me] = low
        r.vg[2 * b + 1, 10:11] = rows_sum(low)
        r.vg[2 * b + 1, 11:12] = dgain
        r.vg[2 * b + 1, 12:13] = dshift

    def ffn_backward_part(b):
        up = r.xg[1, b].reshape(256, D)
        r.dpre[b] = (mm_nt(up, r.wf[2 * b + 1]) * gelu_slope(r.pre[b])).astype(BF)
        r.part[b] = mm_nt(r.dpre[b], r.wf[2 * b]).reshape(4, 64, D)
        db1 = rows_sum(r.dpre[b])
        for j in range(4):
            r.vg[2 * b, 10 + j : 11 + j] = jnp.where(j == me, db1, 0.0)

    sent = []

    def ffn_weight_grads(b):
        rows = r.xg[0, b].reshape(256, D)
        up = r.xg[1, b].reshape(256, D)
        r.wf[2 * b] = mm_tn(rows, r.dpre[b]).astype(BF)
        r.wf[2 * b + 1] = mm_tn(r.act[b], up).astype(BF)
        for p in (2 * b, 2 * b + 1):
            go(sent, part_f(p, 1 - y, 0, SPLIT), r.yf.at[p], r.yy_s.at[2, p], r.yy_r.at[2, p], yn)
        for p in (2 * b, 2 * b + 1):
            for i, yy in ((4, 1 - y), (3, y)):
                z_out_sum(i, part_f(p, yy, SPLIT, REST), p)

    hop = jnp.where(z < 2, 1, 2)

    def z_out_sum(i, src, p):
        zb, zr = getattr(r, f"zb{i}"), getattr(r, f"zr{i}")
        d = (p - z) % 4
        far = {0: z == 3, 3: z == 0}.get(p)
        later = {0: z == 2, 3: z == 1}.get(p)
        direct = z != p
        if far is not None:
            go(sent, src, zr, r.zq_s.at[i], r.zq_r.at[i], device(x, hop, y, c), far)
            direct = jnp.logical_and(direct, jnp.logical_not(jnp.logical_or(far, later)))
        go(sent, src, zb.at[d - 1], r.zz_s.at[i, p], r.zz_r.at[i, d], device(x, p, y, c), direct)

    def z_add_sum(i, src, p):
        later = {0: z == 2, 3: z == 1}.get(p)
        if later is None:
            return
        zb, zr, zq = (getattr(r, f"{n}{i}") for n in ("zb", "zr", "zq"))

        @pl.when(later)
        def _():
            arrived(zr, r.zq_r.at[i])
            zq[...] = add(zr[...], src[...])

        go(sent, zq, zb.at[1], r.zz_s.at[i, p], r.zz_r.at[i, 2], device(x, p, y, c), later)

    def z_total(i, own, out):
        zb = getattr(r, f"zb{i}")
        arrived(zb.at[1], r.zz_r.at[i, 2])
        out[...] = add(own, zb[1])
        for d, without in ((1, 0), (3, 3)):

            @pl.when(z != without)
            def _():
                arrived(zb.at[d - 1], r.zz_r.at[i, d])
                out[...] = add(out[...], zb[d - 1])

    def ffn_sum_y(p):
        arrived(r.yf.at[p], r.yy_r.at[2, p])
        r.yf[p] = add(r.yf[p], part_f(p, y, 0, SPLIT)[...])
        z_out_sum(2, r.yf.at[p], p)

    def ffn_add(p):
        for i, yy in ((4, 1 - y), (3, y)):
            z_add_sum(i, part_f(p, yy, SPLIT, REST), p)

    def ffn_sum_other():
        z_total(4, part_f(z, 1 - y, SPLIT, REST)[...], r.of)
        go(sent, r.of, r.yf2, r.yy_s.at[3, 0], r.yy_r.at[3, 0], yn)

    ag_end(0, 1)
    ffn_forward_part(1)
    rs_start(0, 1)
    ag_mid(0, 0)
    ag_end(0, 0)
    rs_mid(0, 1)
    ffn_forward_part(0)
    rs_start(0, 0)
    ffn_turn(1)
    ag_start(1, 1)
    rs_mid(0, 0)
    ag_mid(1, 1)
    ag_end(1, 1)
    ffn_backward_part(1)
    rs_start(1, 1)
    ffn_turn(0)
    ag_start(1, 0)
    rs_mid(1, 1)
    drain(sent_w[2])
    ffn_weight_grads(1)
    ag_mid(1, 0)
    ag_end(1, 0)
    ffn_backward_part(0)
    rs_start(1, 0)
    d_text = r.dsum3[1] + rs_end(1, 1)
    for i in range(2):
        r.dfirst[64 * i + 32 : 64 * i + 64] = d_text[32 * i : 32 * i + 32]
    rs_mid(1, 0)
    ffn_weight_grads(0)
    d_second = r.dsum3[0] + rs_end(1, 0)

    groups = (
        (shard_s, r.core_s, r.xs, r.ys, r.fin_s, r.out_s),
        (shard_c, r.core_c, r.xc, r.yc, r.fin_c, r.out_c),
    )
    order = (3, 1, 2, 0)

    def sum_start(g):
        view, cb = groups[g][:2]
        for far in range(2):
            for d in order:
                zz = (z + d) % 4
                go(sent, view(zz, y if far else 1 - y, 1 - c), cb.at[far, zz], r.co_s.at[g, far, d], r.co_r.at[g, far, d], core)

    def sum_core(g):
        view, cb, xb = groups[g][:3]
        for far in range(2):
            for d in order:
                zz = (z + d) % 4
                arrived(cb.at[far, zz], r.co_r.at[g, far, d])
                cb[far, zz] = add(cb[far, zz], view(zz, y if far else 1 - y, c)[...])
                go(sent, cb.at[far, zz, :, cols(1 - x)], xb.at[far, zz], r.xx_s.at[g, far, d], r.xx_r.at[g, far, d], xn)

    def sum_x(g, far):
        view, cb, xb, yb = groups[g][:4]
        for d in order:
            zz = (z + d) % 4
            arrived(xb.at[far, zz], r.xx_r.at[g, far, d])
            xb[far, zz] = add(xb[far, zz], cb[far, zz, :, cols(x)])
            if far == 0:
                go(sent, xb.at[0, zz], yb.at[zz], r.yy_s.at[g, d], r.yy_r.at[g, d], yn)

    def sum_y(g):
        view, cb, xb, yb = groups[g][:4]
        zb, zr, zq = (getattr(r, f"{n}{g}") for n in ("zb", "zr", "zq"))
        for d in order:
            zz = (z + d) % 4
            arrived(yb.at[zz], r.yy_r.at[g, d])
            yb[zz] = add(yb[zz], xb[1, zz])
            if d == 2:

                @pl.when(inner)
                def _():
                    arrived(zr, r.zq_r.at[g])
                    zq[...] = add(zr[...], yb[zz])

                go(sent, zq, zb.at[1], r.zz_s.at[g, 2], r.zz_r.at[g, 2], zdev(2), inner)
                go(sent, yb.at[zz], zb.at[1], r.zz_s.at[g, 2], r.zz_r.at[g, 2], zdev(2), outer)
            elif d:
                far = z == (0 if d == 3 else 3)
                go(sent, yb.at[zz], zr, r.zq_s.at[g], r.zq_r.at[g], device(x, hop, y, c), far)
                go(sent, yb.at[zz], zb.at[d - 1], r.zz_s.at[g, d], r.zz_r.at[g, d], zdev(d), jnp.logical_not(far))

    def sum_z(g):
        view, cb, xb, yb, fin, out = groups[g]
        z_total(g, yb[z], fin)
        out[:, cols(x)] = fin[...]
        go(sent, fin, out.at[:, cols(x)], r.fi_s.at[g], r.fi_r.at[g], xn)

    def ffn_sum_z():
        z_total(2, r.yf[z], r.fin_f.at[0:SPLIT])
        last = r.fin_f.at[SPLIT:384]
        z_total(3, part_f(z, y, SPLIT, REST)[...], last)
        arrived(r.yf2, r.yy_r.at[3, 0])
        last[...] = add(last[...], r.yf2[...])
        half = lambda j: r.fin_f.at[pl.ds(pl.multiple_of(192 * j, 192), 192)]

        @pl.when(w1)
        def _():
            r.out_f[me] = half(c)[...]
            remote(half(c), r.out_f.at[me], r.fi_s.at[2], r.fi_r.at[2], xn).start()
            remote(half(1 - c), r.out_f.at[me], r.fi_s.at[3], r.fi_r.at[3], core).start()
            remote(half(1 - c), r.out_f.at[me], r.fi_s.at[4], r.fi_r.at[4], diag).start()

        @pl.when(jnp.logical_not(w1))
        def _():
            for j in range(2):
                r.out_f[2 * x + j] = half(j)[...]
                remote(half(j), r.out_f.at[2 * x + j], r.fi_s.at[2 + j], r.fi_r.at[2 + j], xn).start()

    def ffn_end():
        def ends(n):
            for j in range(n):
                remote(r.fin_f.at[0:192], r.out_f.at[0], r.fi_s.at[2 + j], r.fi_r.at[2 + j], xn).wait()

        pl.when(w1)(lambda: ends(3))
        pl.when(jnp.logical_not(w1))(lambda: ends(2))

    du2, dgain, dshift = norm_back(r.sum2[...], cross_v(3), d_second)
    r.vg[3, 8:9] = dgain
    r.vg[3, 9:10] = dshift
    low = du2.astype(BF)
    r.vg[3, 7:8] = rows_sum(low)
    dca = mm_nt(low, r.wc[3584:4352]).astype(BF)
    drain(sent_w[1])
    r.wc[3584:4352] = mm_tn(r.ca[...], low).astype(BF)
    dcq = []
    for i in range(2):
        rows = slice(272 * i, 272 * i + 272)
        mine = slice(32 * i, 32 * i + 32)
        blocks = []
        for g in range(3):
            lanes = slice(256 * g, 256 * g + 256)
            dq, dk, dv = attend_block_back(
                r.cq[mine, lanes], r.ck[rows, lanes], r.cv[rows, lanes], r.pc[i, g], dca[mine, lanes]
            )
            blocks.append(dq)
            r.dck[rows, lanes] = dk
            r.dcv[rows, lanes] = dv
        dcq.append(jnp.concatenate(blocks, 1))
    dcq = jnp.concatenate(dcq, 0)
    r.vg[3, 5:6] = rows_sum(dcq)
    r.vg[3, 6:7] = rows_sum(r.dcv[...])
    du = du2 + mm_nt(dcq, r.wc[0:768])
    for i in range(2):
        r.dfirst[64 * i : 64 * i + 32] = du[32 * i : 32 * i + 32]
    r.wc[0:768] = mm_tn(rows_of(r.first, 0).astype(BF), dcq).astype(BF)
    for j in range(11):
        block = r.feat[:, 128 * j : 128 * j + 128]
        r.wc[768 + 128 * j : 896 + 128 * j] = mm_tn(block, r.dck[...]).astype(BF)
        r.wc[2176 + 128 * j : 2304 + 128 * j] = mm_tn(block, r.dcv[...]).astype(BF)
    sum_start(1)
    ffn_add(3)
    ffn_sum_y(2)
    ffn_sum_y(3)

    dsum1, dgain, dshift = norm_back(r.sum1[...], self_v(3), r.dfirst[...])
    r.vg[3, 3:4] = dgain
    r.vg[3, 4:5] = dshift
    low = dsum1.astype(BF)
    r.vg[3, 2:3] = rows_sum(low)
    da = mm_nt(low, r.ws[3]).astype(BF)
    drain(sent_w[0])
    r.ws[3] = mm_tn(r.a[...], low).astype(BF)
    for i in range(2):
        rows = slice(64 * i, 64 * i + 64)
        for g in range(3):
            lanes = slice(256 * g, 256 * g + 256)
            dq, dk, dv = attend_block_back(
                r.q[rows, lanes], r.k[rows, lanes], r.v[rows, lanes], r.p[i, g], da[rows, lanes]
            )
            r.dq[rows, lanes] = dq
            r.dk[rows, lanes] = dk
            r.dv[rows, lanes] = dv
    sum_core(1)
    r.vg[3, 0:1] = rows_sum(r.dq[...])
    r.vg[3, 1:2] = rows_sum(r.dv[...])
    total = dsum1 + mm_nt(r.dq[...], r.ws[0]) + mm_nt(r.dk[...], r.ws[1]) + mm_nt(r.dv[...], r.ws[2])
    r.hgrad[...] = total.astype(BF)
    r.ws[0] = mm_tn(r.hid[...], r.dq[...]).astype(BF)
    r.ws[1] = mm_tn(r.hid[...], r.dk[...]).astype(BF)
    r.ws[2] = mm_tn(r.hid[...], r.dv[...]).astype(BF)
    sum_start(0)

    r.v_send[...] = r.vg[...].astype(BF)
    index = 2 * y + c
    home = device(x, z, 1, 1)

    @pl.when(jnp.logical_not(root))
    def _():
        remote(r.v_send, r.v_in.at[index], r.vv_s.at[0], r.vv_r.at[index], home).start()

    ffn_add(0)
    ffn_sum_y(0)
    ffn_sum_y(1)
    z_add_sum(2, r.yf.at[0], 0)
    z_add_sum(2, r.yf.at[3], 3)
    sum_x(1, 0)
    sum_core(0)

    @pl.when(root)
    def _():
        total = r.vg[...]
        for i in range(3):
            arrived(r.v_in.at[i], r.vv_r.at[i])
            total = total + r.v_in[i].astype(F32)
        r.v_z[...] = total.astype(BF)
        for k in (1, 2, 3):
            zz = (z + k) % 4
            remote(r.v_z.at[zz], r.v_zin.at[k - 1], r.vv_s.at[k], r.vv_r.at[2 + k], device(x, zz, y, c)).start()

    sum_x(1, 1)
    ffn_sum_other()
    sum_y(1)
    ffn_sum_z()
    sum_x(0, 0)
    sum_x(0, 1)

    @pl.when(root)
    def _():
        total = r.v_z[z].astype(F32)
        for k in (1, 2, 3):
            arrived(r.v_zin.at[k - 1], r.vv_r.at[2 + k])
            total = total + r.v_zin[k - 1].astype(F32)
        r.v_x[...] = total.astype(BF)
        remote(r.v_x, r.v_xin, r.vv_s.at[4], r.vv_r.at[6], xn).start()

    sum_y(0)
    sum_z(1)
    sum_z(0)

    @pl.when(root)
    def _():
        arrived(r.v_xin, r.vv_r.at[6])
        r.out_v[...] = r.v_x[...].astype(F32) + r.v_xin[...].astype(F32)
        for k in (1, 2, 3):
            zz = (z + k) % 4
            remote(r.v_z.at[zz], r.v_zin.at[k - 1], r.vv_s.at[k], r.vv_r.at[2 + k], device(x, zz, y, c)).wait_send()
        remote(r.v_x, r.v_xin, r.vv_s.at[4], r.vv_r.at[6], xn).wait_send()

    @pl.when(jnp.logical_not(root))
    def _():
        r.out_v[...] = jnp.zeros_like(r.out_v)
        remote(r.v_send, r.v_in.at[index], r.vv_s.at[0], r.vv_r.at[index], home).wait_send()

    for g in range(2):
        arrived(groups[g][5].at[:, cols(1 - x)], r.fi_r.at[g])
    ffn_end()
    drain(sent)


def layer(own_s, own_c, own_f, own_t, hid, allowed, feat, cot):
    vm = pl.BlockSpec(memory_space=pltpu.VMEM)
    anywhere = pl.BlockSpec(memory_space=pl.ANY)
    return pl.pallas_call(
        layer_kernel,
        out_shape=(
            jax.ShapeDtypeStruct((128, D), BF),
            jax.ShapeDtypeStruct((128, D), BF),
            jax.ShapeDtypeStruct((192, D), BF),
            jax.ShapeDtypeStruct((272, D), BF),
            jax.ShapeDtypeStruct((4, 192, D), BF),
            jax.ShapeDtypeStruct((16, D), F32),
        ),
        in_specs=[anywhere] * 4 + [vm] * 4,
        out_specs=[vm] * 6,
        scratch_shapes=list(scratch().values()),
        compiler_params=pltpu.CompilerParams(
            collective_id=0, has_side_effects=True, vmem_limit_bytes=VMEM_BYTES
        ),
    )(own_s, own_c, own_f, own_t, hid, allowed, feat, cot)


def shift_back():
    x, z, y, c = place()
    f = lax.axis_index("fsdp")
    return 2 * f, 2 * f, 6 * (f % 4) + jnp.where(z >= 2, 6, 0)


def own_rows(self_params, cross_params, ffn_params):
    x, z, y, c = place()
    flats = [v.reshape(-1, 128) for v in (self_params, cross_params, ffn_params)]
    tails = jnp.concatenate([v[-32:] for v in flats])
    before = lax.ppermute(tails, "fsdp", [(i, (i + 1) % 16) for i in range(16)])
    nice = []
    for i, (v, rows, back) in enumerate(zip(flats, (1152, 1632, 4608), shift_back())):
        both = jnp.concatenate([before[32 * i : 32 * i + 32], v])
        nice.append(lax.dynamic_slice_in_dim(both, 32 - back, rows))
    own_s = nice[0].reshape(192, D)
    own_c = nice[1].reshape(272, D)
    cols = nice[2].reshape(192, 2, 4, 3, 128)
    pick = lambda cc: lax.dynamic_index_in_dim(cols, 2 * cc + x, 2, keepdims=False).reshape(192, D)
    as_w1 = jnp.stack([pick(c), pick(1 - c)])
    as_w2 = lax.dynamic_index_in_dim(nice[2].reshape(2, 2, 192, D), x, keepdims=False)
    own_f = jnp.where(z % 2 == 0, as_w1, as_w2)

    b1 = lambda v: v.reshape(2, 4, 384).transpose(1, 0, 2).reshape(4, D)
    rest = lambda v: jnp.concatenate([v.reshape(3, D), jnp.zeros((1, D), BF)])
    ffn = jnp.stack([b1(tails[72:96]), rest(tails[72:90]), b1(tails[66:90]), rest(tails[66:84])])
    own_t = jnp.concatenate([
        tails[0:30].reshape(5, D),
        tails[32:62].reshape(5, D),
        lax.dynamic_index_in_dim(ffn, z, keepdims=False),
        jnp.zeros((2, D), BF),
    ])
    return own_s, own_c, own_f, own_t


def flat_grads(out_s, out_c, out_f, out_v):
    x, z, y, c = place()
    f = lax.axis_index("fsdp")
    k = f % 4
    w1 = out_f.reshape(4, 192, 2, 3, 128).transpose(1, 2, 0, 3, 4).reshape(4608, 128)
    w2 = out_f.reshape(4608, 128)
    nice = [out_s.reshape(1152, 128), out_c.reshape(1632, 128), jnp.where(z % 2 == 0, w1, w2)]
    heads = jnp.concatenate([v[:32] for v in nice])
    after = lax.ppermute(heads, "fsdp", [(i, (i + 15) % 16) for i in range(16)]).astype(F32)
    zeros = lambda n: jnp.zeros((n, 128), F32)
    flat = lambda v: v.reshape(-1, 128)
    tail_s = jnp.where(f == 15, jnp.concatenate([flat(out_v[0:5]), zeros(2)]), after[0:32])
    tail_c = jnp.where(f == 15, jnp.concatenate([flat(out_v[5:10]), zeros(2)]), after[32:64])
    nxt = after[64:96]
    b1 = out_v[10:14].reshape(4, 2, 384).transpose(1, 0, 2).reshape(24, 128)
    rest = flat(out_v[10:13])
    ends = jnp.stack([
        jnp.concatenate([b1, zeros(8)]),
        jnp.concatenate([rest, nxt[:14]]),
        jnp.concatenate([b1, nxt[:8]]),
        jnp.concatenate([rest, zeros(14)]),
    ])
    tail_f = jnp.where(k == 3, lax.dynamic_index_in_dim(ends, z, keepdims=False), nxt)
    outs = []
    for v, tail, start, rows in zip(nice, (tail_s, tail_c, tail_f), shift_back(), (1154, 1634, 4614)):
        both = jnp.concatenate([v.astype(F32), tail])
        outs.append(lax.dynamic_slice_in_dim(both, start, rows).reshape(-1))
    return outs


def per_device_fast(hidden, lengths, features, cotangent, self_params, cross_params, ffn_params):
    own = own_rows(self_params, cross_params, ffn_params)
    at = jnp.arange(64)
    r, k = at[:, None], at[None, :]
    allowed = (k < NQ)[None] | ((r >= NQ) & (k <= r))[None] & (k[None] < NQ + lengths[:, None, None])
    feat = jnp.pad(features, ((0, 0), (0, 15), (0, 0))).reshape(544, E)
    mixed, hgrad, *sums = layer(
        *own, hidden.reshape(128, D), allowed.astype(F32), feat, cotangent.reshape(128, D)
    )
    return (mixed.reshape(2, 64, D), hgrad.reshape(2, 64, D), *flat_grads(*sums))


def solution(mesh):
    fast = mesh.shape["dp"] == 2 and mesh.shape["fsdp"] == 16
    return jax.shard_map(
        per_device_fast if fast else per_device,
        mesh=mesh,
        in_specs=(
            P(("dp", "fsdp"), None, None),
            P(("dp", "fsdp")),
            P(("dp", "fsdp"), None, None),
            P(("dp", "fsdp"), None, None),
            P("fsdp"),
            P("fsdp"),
            P("fsdp"),
        ),
        out_specs=(
            P(("dp", "fsdp"), None, None),
            P(("dp", "fsdp"), None, None),
            P("fsdp"),
            P("fsdp"),
            P("fsdp"),
        ),
        check_vma=False,
    )
```

```python
from functools import partial
import math
from types import SimpleNamespace

import jax
import jax.numpy as jnp
from jax import lax
from jax.experimental import pallas as pl
from jax.experimental.pallas import tpu as pltpu
from jax.sharding import PartitionSpec as P

D = 768
HEADS = 12
HDIM = 64
F = 3072
E = 1408
NQ = 32


EPS = 1e-06
SCALE = 0.125


def self_layout():
    return [(D, D)] * 4 + [(D,)] * 5


def cross_layout():
    return [(D, D), (E, D), (E, D), (D, D)] + [(D,)] * 5


def ffn_layout():
    return [(D, F), (F,), (F, D), (D,), (D,), (D,)] * 2


def split_flat(flat_vec, layouts):
    pieces = []
    offset = 0
    for layout in layouts:
        amount = math.prod(layout)
        pieces.append(flat_vec[offset : offset + amount].reshape(layout))
        offset = offset + amount
    return pieces


def join_flat(pieces, length):
    flat_vec = jnp.concatenate([piece.reshape(-1) for piece in pieces])
    return jnp.pad(flat_vec, (0, length - flat_vec.shape[0]))


def regroup(flat_vec):
    groups = lax.axis_size("fsdp")
    replicas = lax.axis_size("dp")
    return flat_vec.reshape(groups, replicas, -1).transpose(1, 0, 2).reshape(-1)


def matmul(left, right):
    return jnp.dot(left, right, preferred_element_type=jnp.float32)


def matmul_left(left, right):
    return lax.dot_general(
        left, right, (((0,), (0,)), ((), ())), preferred_element_type=jnp.float32
    )


def matmul_right(left, right):
    return lax.dot_general(
        left, right, (((1,), (1,)), ((), ())), preferred_element_type=jnp.float32
    )


def column_sum(values):
    return jnp.sum(values.astype(jnp.float32), 0)


def layer_norm(values, gain, shift):
    average = jnp.mean(values, -1, keepdims=True)
    centered = values - average
    variance = jnp.mean(centered * centered, -1, keepdims=True)
    return centered * lax.rsqrt(variance + EPS) * gain + shift


def norm_backward(summed, gain, shift, grad_out):
    _, norm_pull = jax.vjp(layer_norm, summed, gain.astype(jnp.float32), shift.astype(jnp.float32))
    return norm_pull(grad_out)


def heads(rows, items):
    return rows.reshape(items, -1, HEADS, HDIM)


def score_block(query, keys, mask):
    scores = jnp.einsum("iqhd,ikhd->ihqk", query, keys, preferred_element_type=jnp.float32) * SCALE
    if mask is not None:
        scores = jnp.where(mask, scores, -1e30)
    return scores


def attend(query, keys, values, mask):
    scores = score_block(query, keys, mask)
    top_sum = jax.nn.logsumexp(scores, axis=-1)
    probs = jnp.exp(scores - top_sum[..., None]).astype(jnp.bfloat16)
    context = jnp.einsum("ihqk,ikhd->iqhd", probs, values, preferred_element_type=jnp.float32)
    return (context, top_sum)


def attend_back(query, keys, values, mask, top_sum, grad_context):
    probs = jnp.exp(score_block(query, keys, mask) - top_sum[..., None])
    grad_probs = jnp.einsum(
        "iqhd,ikhd->ihqk", grad_context, values, preferred_element_type=jnp.float32
    )
    inner = jnp.sum(probs * grad_probs, -1, keepdims=True)
    grad_scores = (probs * (grad_probs - inner)).astype(jnp.bfloat16)
    grad_query = (
        jnp.einsum("ihqk,ikhd->iqhd", grad_scores, keys, preferred_element_type=jnp.float32) * SCALE
    )
    grad_keys = (
        jnp.einsum("ihqk,iqhd->ikhd", grad_scores, query, preferred_element_type=jnp.float32)
        * SCALE
    )
    grad_values = jnp.einsum(
        "ihqk,iqhd->ikhd",
        probs.astype(jnp.bfloat16),
        grad_context,
        preferred_element_type=jnp.float32,
    )
    return (grad_query, grad_keys, grad_values)


def linear_back(inputs, weight, grad_out):
    return (matmul_left(inputs, grad_out), column_sum(grad_out), matmul_right(grad_out, weight))


def ffn_forward(rows, params):
    w_in, b_in, w_out, b_out, gain, shift = params
    rows_low = rows.astype(jnp.bfloat16)
    hidden_pre = matmul(rows_low, w_in) + b_in
    activated = jax.nn.gelu(hidden_pre, approximate=True).astype(jnp.bfloat16)
    summed = rows + (matmul(activated, w_out) + b_out)
    final = layer_norm(summed, gain.astype(jnp.float32), shift.astype(jnp.float32))
    return (final, (rows_low, hidden_pre, activated, summed))


def ffn_backward(grad_out, kept, params):
    w_in, b_in, w_out, b_out, gain, shift = params
    rows_low, hidden_pre, activated, summed = kept
    grad_sum, grad_gain, grad_shift = norm_backward(summed, gain, shift, grad_out)
    grad_branch = grad_sum.astype(jnp.bfloat16)
    grad_w_out, grad_b_out, grad_act = linear_back(activated, w_out, grad_branch)
    _, gelu_pull = jax.vjp(partial(jax.nn.gelu, approximate=True), hidden_pre)
    grad_pre = gelu_pull(grad_act)[0].astype(jnp.bfloat16)
    grad_w_in, grad_b_in, grad_rows = linear_back(rows_low, w_in, grad_pre)
    return (
        grad_sum + grad_rows,
        [grad_w_in, grad_b_in, grad_w_out, grad_b_out, grad_gain, grad_shift],
    )


def per_device(hidden, lengths, features, cotangent, self_params, cross_params, ffn_params):
    items, seq, width = hidden.shape
    self_full = lax.all_gather(self_params, "fsdp", axis=0, tiled=True)
    self_parts = split_flat(self_full, self_layout())
    w_q, w_k, w_v, w_o, b_q, b_v, b_o, gain_one, shift_one = self_parts
    positions = jnp.arange(seq)
    rows_at = positions[:, None]
    cols_at = positions[None, :]
    allowed = (cols_at < NQ)[None] | ((rows_at >= NQ) & (cols_at <= rows_at))[None] & (
        cols_at[None] < NQ + lengths[:, None, None]
    )
    allowed = allowed[:, None]
    inputs = hidden.reshape(-1, width)
    query_low = (matmul(inputs, w_q) + b_q).astype(jnp.bfloat16)
    key_low = matmul(inputs, w_k).astype(jnp.bfloat16)
    value_low = (matmul(inputs, w_v) + b_v).astype(jnp.bfloat16)
    context, self_top = attend(
        heads(query_low, items), heads(key_low, items), heads(value_low, items), allowed
    )
    context_low = context.reshape(-1, width).astype(jnp.bfloat16)
    summed_one = inputs.astype(jnp.float32) + (matmul(context_low, w_o) + b_o)
    first = layer_norm(summed_one, gain_one.astype(jnp.float32), shift_one.astype(jnp.float32))
    first_items = first.reshape(items, seq, width)
    query_rows = first_items[:, :NQ].reshape(-1, width)
    text_rows = first_items[:, NQ:].reshape(-1, width)
    cross_full = lax.all_gather(cross_params, "fsdp", axis=0, tiled=True)
    cross_parts = split_flat(cross_full, cross_layout())
    cross_wq, cross_wk, cross_wv, cross_wo, cross_bq, cross_bv, cross_bo, gain_two, shift_two = (
        cross_parts
    )
    query_in = query_rows.astype(jnp.bfloat16)
    image_rows = features.reshape(-1, features.shape[-1])
    cross_query = (matmul(query_in, cross_wq) + cross_bq).astype(jnp.bfloat16)
    cross_key = matmul(image_rows, cross_wk).astype(jnp.bfloat16)
    cross_value = (matmul(image_rows, cross_wv) + cross_bv).astype(jnp.bfloat16)
    cross_context, cross_top = attend(
        heads(cross_query, items), heads(cross_key, items), heads(cross_value, items), None
    )
    cross_low = cross_context.reshape(-1, width).astype(jnp.bfloat16)
    summed_two = query_rows + (matmul(cross_low, cross_wo) + cross_bo)
    second = layer_norm(summed_two, gain_two.astype(jnp.float32), shift_two.astype(jnp.float32))
    ffn_full = lax.all_gather(ffn_params, "fsdp", axis=0, tiled=True)
    ffn_parts = split_flat(ffn_full, ffn_layout())
    query_final, query_kept = ffn_forward(second, ffn_parts[:6])
    text_final, text_kept = ffn_forward(text_rows, ffn_parts[6:])
    mixed = jnp.concatenate(
        [query_final.reshape(items, NQ, width), text_final.reshape(items, -1, width)], 1
    ).astype(jnp.bfloat16)
    grad_items = cotangent.astype(jnp.float32)
    grad_query_final = grad_items[:, :NQ].reshape(-1, width)
    grad_text_final = grad_items[:, NQ:].reshape(-1, width)
    ffn_back = split_flat(lax.all_gather(ffn_params, "fsdp", axis=0, tiled=True), ffn_layout())
    grad_second, query_grads = ffn_backward(grad_query_final, query_kept, ffn_back[:6])
    grad_text, text_grads = ffn_backward(grad_text_final, text_kept, ffn_back[6:])
    ffn_flat_grad = join_flat(query_grads + text_grads, ffn_full.shape[0])
    ffn_grad = lax.psum_scatter(
        regroup(ffn_flat_grad), ("dp", "fsdp"), scatter_dimension=0, tiled=True
    )
    cross_back = split_flat(
        lax.all_gather(cross_params, "fsdp", axis=0, tiled=True), cross_layout()
    )
    grad_summed_two, grad_gain_two, grad_shift_two = norm_backward(
        summed_two, cross_back[7], cross_back[8], grad_second
    )
    grad_cross_out = grad_summed_two.astype(jnp.bfloat16)
    grad_cross_wo, grad_cross_bo, grad_cross_ctx = linear_back(
        cross_low, cross_back[3], grad_cross_out
    )
    grad_cq, grad_ck, grad_cv = attend_back(
        heads(cross_query, items),
        heads(cross_key, items),
        heads(cross_value, items),
        None,
        cross_top,
        heads(grad_cross_ctx.astype(jnp.bfloat16), items),
    )
    grad_cq = grad_cq.reshape(-1, width).astype(jnp.bfloat16)
    grad_ck = grad_ck.reshape(-1, width).astype(jnp.bfloat16)
    grad_cv = grad_cv.reshape(-1, width).astype(jnp.bfloat16)
    grad_cross_wq, grad_cross_bq, grad_query_in = linear_back(query_in, cross_back[0], grad_cq)
    grad_cross_wk = matmul_left(image_rows, grad_ck)
    grad_cross_wv = matmul_left(image_rows, grad_cv)
    grad_cross_bv = column_sum(grad_cv)
    grad_query_rows = grad_summed_two + grad_query_in
    cross_list = [
        grad_cross_wq,
        grad_cross_wk,
        grad_cross_wv,
        grad_cross_wo,
        grad_cross_bq,
        grad_cross_bv,
        grad_cross_bo,
        grad_gain_two,
        grad_shift_two,
    ]
    cross_flat_grad = join_flat(cross_list, cross_full.shape[0])
    cross_grad = lax.psum_scatter(
        regroup(cross_flat_grad), ("dp", "fsdp"), scatter_dimension=0, tiled=True
    )
    self_back = split_flat(lax.all_gather(self_params, "fsdp", axis=0, tiled=True), self_layout())
    grad_first = jnp.concatenate(
        [grad_query_rows.reshape(items, NQ, width), grad_text.reshape(items, -1, width)], 1
    ).reshape(-1, width)
    grad_summed_one, grad_gain_one, grad_shift_one = norm_backward(
        summed_one, self_back[7], self_back[8], grad_first
    )
    grad_attn = grad_summed_one.astype(jnp.bfloat16)
    grad_w_o, grad_b_o, grad_ctx = linear_back(context_low, self_back[3], grad_attn)
    grad_q, grad_k, grad_v = attend_back(
        heads(query_low, items),
        heads(key_low, items),
        heads(value_low, items),
        allowed,
        self_top,
        heads(grad_ctx.astype(jnp.bfloat16), items),
    )
    grad_q = grad_q.reshape(-1, width).astype(jnp.bfloat16)
    grad_k = grad_k.reshape(-1, width).astype(jnp.bfloat16)
    grad_v = grad_v.reshape(-1, width).astype(jnp.bfloat16)
    grad_w_q, grad_b_q, input_from_q = linear_back(inputs, self_back[0], grad_q)
    grad_w_k = matmul_left(inputs, grad_k)
    input_from_k = matmul_right(grad_k, self_back[1])
    grad_w_v, grad_b_v, input_from_v = linear_back(inputs, self_back[2], grad_v)
    hidden_grad = (
        (grad_summed_one + input_from_q + input_from_k + input_from_v)
        .reshape(items, seq, width)
        .astype(jnp.bfloat16)
    )
    self_list = [
        grad_w_q,
        grad_w_k,
        grad_w_v,
        grad_w_o,
        grad_b_q,
        grad_b_v,
        grad_b_o,
        grad_gain_one,
        grad_shift_one,
    ]
    self_flat_grad = join_flat(self_list, self_full.shape[0])
    self_grad = lax.psum_scatter(
        regroup(self_flat_grad), ("dp", "fsdp"), scatter_dimension=0, tiled=True
    )
    self_grad, cross_grad, ffn_grad = (
        lax.all_gather(self_grad.astype(jnp.bfloat16), "dp", axis=0, tiled=True).astype(
            self_grad.dtype
        ),
        lax.all_gather(cross_grad.astype(jnp.bfloat16), "dp", axis=0, tiled=True).astype(
            cross_grad.dtype
        ),
        lax.all_gather(ffn_grad.astype(jnp.bfloat16), "dp", axis=0, tiled=True).astype(
            ffn_grad.dtype
        ),
    )
    return (mixed, hidden_grad, self_grad, cross_grad, ffn_grad)


MESH = pl.DeviceIdType.MESH
BF = jnp.bfloat16
F32 = jnp.float32
VMEM_BYTES = 62 * 2**20


def place():
    f = lax.axis_index("fsdp")
    return lax.axis_index("dp"), f // 4, (f // 2) % 2, f % 2


def device(x, z, y, c):
    return (x, (z * 2 + y) * 2 + c)


def meet(devices):
    barrier = pltpu.get_barrier_semaphore()
    for d in devices:
        pl.semaphore_signal(barrier, inc=1, device_id=d, device_id_type=MESH)
    pl.semaphore_wait(barrier, len(devices))


def remote(src, dst, send, recv, target):
    return pltpu.make_async_remote_copy(
        src_ref=src,
        dst_ref=dst,
        send_sem=send,
        recv_sem=recv,
        device_id=target,
        device_id_type=MESH,
    )


def mm(a, b):
    return jnp.dot(a, b, preferred_element_type=F32)


def mm_nt(a, b):
    return lax.dot_general(a, b, (((1,), (1,)), ((), ())), preferred_element_type=F32)


def mm_tn(a, b):
    return lax.dot_general(a, b, (((0,), (0,)), ((), ())), preferred_element_type=F32)


def rows_sum(v):
    return jnp.sum(v.astype(F32), 0, keepdims=True)


def add(a, b):
    return (a.astype(F32) + b.astype(F32)).astype(BF)


def normed(v):
    centered = v - jnp.mean(v, -1, keepdims=True)
    r = lax.rsqrt(jnp.mean(centered * centered, -1, keepdims=True) + EPS)
    return centered * r, r


def norm_back(v, gain, g_out):
    xh, r = normed(v)
    gg = g_out * gain
    dv = r * (gg - jnp.mean(gg, -1, keepdims=True) - xh * jnp.mean(gg * xh, -1, keepdims=True))
    return dv, rows_sum(g_out * xh), rows_sum(g_out)


GELU_A = math.sqrt(2.0 / math.pi)
GELU_B = 0.044715


def gelu(v):
    return 0.5 * v * (1.0 + jnp.tanh(GELU_A * (v + GELU_B * (v * v * v))))


def gelu_slope(v):
    t = jnp.tanh(GELU_A * (v + GELU_B * (v * v * v)))
    return 0.5 * (1.0 + t) + 0.5 * v * (1.0 - t * t) * (GELU_A * (1.0 + 3.0 * GELU_B * (v * v)))


def head_mask(h):
    lane = lax.broadcasted_iota(jnp.int32, (1, 256), 1)
    return jnp.where(lane // HDIM == h, 1.0, 0.0)


def spread(rows):
    wide = rows.astype(F32)
    return jnp.concatenate([(wide * head_mask(h)).astype(BF) for h in range(4)], 0)


def fold(stacked):
    n = stacked.shape[0] // 4
    total = stacked[:n] * head_mask(0)
    for h in range(1, 4):
        total = total + stacked[h * n : (h + 1) * n] * head_mask(h)
    return total


def attend_block(q, k, v, allowed):
    s = mm_nt(spread(q), k) * SCALE
    s = jnp.where(allowed > 0.5, s, -1e30)
    e = jnp.exp(s - jnp.max(s, -1, keepdims=True))
    p = e / jnp.sum(e, -1, keepdims=True)
    return p, fold(mm(p.astype(BF), v)).astype(BF)


def attend_block_back(q, k, v, p, da):
    dax = spread(da)
    dp = mm_nt(dax, v)
    ds = (p * (dp - jnp.sum(p * dp, -1, keepdims=True))).astype(BF)
    dq = (fold(mm(ds, k)) * SCALE).astype(BF)
    dk = (mm_tn(ds, spread(q)) * SCALE).astype(BF)
    dv = mm_tn(p.astype(BF), dax).astype(BF)
    return dq, dk, dv


def rows_of(ref, first):
    return jnp.concatenate([ref[first : first + 32], ref[64 + first : 96 + first]], 0)


SPLIT = 288
REST = 384 - SPLIT
STREAMS = ((192, 384), (272, 384), (SPLIT, D), (REST, D), (REST, D))


def scratch():
    dma = lambda *s: pltpu.SemaphoreType.DMA(s)
    b = lambda *s: pltpu.VMEM(s, BF)
    f = lambda *s: pltpu.VMEM(s, F32)
    return dict(
        ws=b(4, D, D), wc=b(4352, D), wf=b(4, D, D), theirs=b(192, D), own_t=b(16, D), tb=b(4, 16, D), before=b(96, 128),
        tv=f(4, 16, D), vg=f(4, 16, D),
        q=b(128, D), k=b(128, D), v=b(128, D), a=b(128, D), p=f(2, 3, 256, 64),
        sum1=f(128, D), first=f(128, D), cq=b(64, D), ck=b(544, D), cv=b(544, D), ca=b(64, D),
        pc=f(2, 3, 128, 272), sum2=f(64, D), second=f(64, D),
        xg=b(2, 2, 4, 64, D), pre=f(2, 256, D), act=b(2, 256, D), part=f(2, 4, 64, D),
        send_p=b(2, 2, 2, 64, D), recv_p=b(2, 2, 2, 64, D), send_x=b(2, 2, 64, D), recv_x=b(2, 2, 64, D),
        sum3=f(2, 64, D), dpre=b(2, 256, D), dsum3=f(2, 64, D), dfirst=f(128, D),
        core_s=b(2, 4, 192, D), core_c=b(2, 4, 272, D), xs=b(2, 4, 192, 384), xc=b(2, 4, 272, 384),
        ys=b(4, 192, 384), yc=b(4, 272, 384), yf=b(4, SPLIT, D), yf2=b(REST, D), of=b(REST, D),
        fin_s=b(192, 384), fin_c=b(272, 384), fin_f=b(384, D),
        **{f"{n}{i}": b(*lead, *shape) for i, shape in enumerate(STREAMS) for n, lead in (("zb", (3,)), ("zr", ()))},
        v_send=b(4, 16, D), v_in=b(3, 4, 16, D), v_z=b(4, 16, D), v_zin=b(3, 16, D), v_x=b(16, D), v_xin=b(16, D),
        nice_s=b(192, D), nice_c=b(272, D), nice_f=b(4, 192, D), total_v=b(16, D), heads=b(3, 32, 128), after=b(3, 32, 128),
        fl_s=f(1184, 128), fl_c=f(1664, 128), fl_f=f(4640, 128),
        loc=dma(1), out_sem=dma(3), tail_s=dma(1), tail_r=dma(1), head_s=dma(3), head_r=dma(3), gz_s=dma(7, 4), gz_r=dma(7, 4), gy_s=dma(7, 4), gy_r=dma(7, 4), gx_s=dma(2, 7), gx_r=dma(2, 7),
        gc_s=dma(3, 15), gc_r=dma(3, 15), t_s=dma(6), t_r=dma(4),
        ex_s=dma(2, 2, 3), ex_r=dma(2, 2, 3), rs_s=dma(2, 2, 3), rs_r=dma(2, 2, 3),
        co_s=dma(2, 2, 4), co_r=dma(2, 2, 4), xx_s=dma(2, 2, 4), xx_r=dma(2, 2, 4), yy_s=dma(4, 4), yy_r=dma(4, 4),
        zz_s=dma(5, 4), zz_r=dma(5, 4), zq_s=dma(5), zq_r=dma(5), fi_s=dma(5), fi_r=dma(5), vv_s=dma(5), vv_r=dma(7),
    )


def layer_kernel(*refs):
    names = [
        "flat_s", "flat_c", "flat_f", "tails", "lens", "hid", "feat", "cot",
        "mixed", "hgrad", "out_s", "out_c", "out_f",
    ] + list(scratch())
    r = SimpleNamespace(**dict(zip(names, refs)))
    x, z, y, c = place()
    core, xn, yn = device(x, z, y, 1 - c), device(1 - x, z, y, c), device(x, z, 1 - y, c)
    diag = device(1 - x, z, y, 1 - c)
    zdev = lambda d: device(x, (z + d) % 4, y, c)
    f = lax.axis_index("fsdp")
    following, preceding = (x, (f + 1) % 16), (x, (f + 15) % 16)
    meet([core, xn, yn, diag, device(x, z, 1 - y, 1 - c), zdev(1), zdev(2), zdev(3), following, preceding])
    me = 2 * c + x
    cols = lambda h: pl.ds(pl.multiple_of(384 * h, 384), 384)
    root = jnp.logical_and(y == 1, c == 1)
    w1 = z % 2 == 0

    inner = jnp.logical_and(z > 0, z < 3)
    outer = jnp.logical_not(inner)

    def when(cond, what):
        if cond is None:
            what()
        else:
            pl.when(cond)(what)

    def go(sent, src, dst, send, recv, target, cond=None):
        make = lambda: remote(src, dst, send, recv, target)
        when(cond, lambda: make().start())
        sent.append((make, cond))

    def arrived(view, recv):
        remote(view, view, recv, recv, core).wait_recv()

    def drain(sent):
        for make, cond in sent:
            when(cond, lambda: make().wait_send())

    def shard_s(zz, yy, cc):
        return r.ws.at[zz, pl.ds(pl.multiple_of(192 * (2 * yy + cc), 192), 192)]

    def shard_c(zz, yy, cc):
        return r.wc.at[pl.ds(pl.multiple_of(272 * ((zz * 2 + yy) * 2 + cc), 16), 272)]

    def part_f(zz, yy, lo=0, n=384):
        return r.wf.at[zz, pl.ds(pl.multiple_of(384 * yy + lo, 16), n)]

    shards = (shard_s, shard_c)
    sent_w = ([], [], [])
    steps = [jnp.where(z == 0, 3 - i, jnp.where(z == 3, 1 + i, (2, 1, 3)[i])) for i in range(3)]

    def part(g, zz, yy, cc, h):
        if g >= 2:
            return part_f(zz, yy, 96 * (g - 2), 96)
        view = shards[g](zz, yy, cc)
        return view if h is None else view.at[:, cols(h)]

    def own_part(g):
        return part(g, z, y, c, x)

    def z_out(src, dst, g, i):
        for k in (2, 1, 3):
            cond = {1: z != 3, 2: None, 3: z != 0}[k]
            go(sent_w[min(g, 2)], src, dst, r.gz_s.at[i, k], r.gz_r.at[i, k], zdev(k), cond)

    def z_on(view, g, i, k):
        cond = jnp.logical_and(inner, k == 2)
        go(sent_w[min(g, 2)], view, view, r.gz_s.at[i, 0], r.gz_r.at[i, 2 * z - 1], device(x, 3 * (z - 1), y, c), cond)

    def own_z(g):
        z_out(own_part(g), part(g, z, y, c, x), g, g)

    def own_y(g):
        go(sent_w[min(g, 2)], own_part(g), part(g, z, y, c, x), r.gy_s.at[g, 0], r.gy_r.at[g, 0], yn)

    def own_core(g):
        own = part(g, z, y, c, None)
        go(sent_w[g], own, own, r.gc_s.at[g, 0], r.gc_r.at[g, 0], core)

    def gather_z(g, last=False):
        for k in steps:
            view = part(g, (z - k) % 4, y, c, x)
            arrived(view, r.gz_r.at[g, k])
            z_on(view, g, g, k)
            if not last:
                go(sent_w[min(g, 2)], view, view, r.gy_s.at[g, k], r.gy_r.at[g, k], yn)
            if g < 2:
                go(sent_w[g], view, view, r.gx_s.at[g, k - 1], r.gx_r.at[g, k - 1], xn)
                go(sent_w[g], view, view, r.gc_s.at[g, k], r.gc_r.at[g, k], core)

    def gather_y(g, which=(0, 1, 2, 3)):
        for j in which:
            view = part(g, (z - j) % 4, 1 - y, c, x)
            arrived(view, r.gy_r.at[g, j])
            if g < 2:
                go(sent_w[g], view, view, r.gx_s.at[g, 3 + j], r.gx_r.at[g, 3 + j], xn)
                go(sent_w[g], view, view, r.gc_s.at[g, 4 + j], r.gc_r.at[g, 4 + j], core)

    def other_z():
        view = part(5, z, 1 - y, c, x)
        arrived(view, r.gy_r.at[5, 0])
        z_out(view, view, 5, 6)

    def other_arrivals():
        for k in steps:
            view = part(5, (z - k) % 4, 1 - y, c, x)
            arrived(view, r.gz_r.at[6, k])
            z_on(view, 5, 6, k)

    def gather_x(g):
        for j in range(7):
            view = part(g, (z - j - 1) % 4, y, c, 1 - x) if j < 3 else part(g, (z - j + 3) % 4, 1 - y, c, 1 - x)
            arrived(view, r.gx_r.at[g, j])
            go(sent_w[g], view, view, r.gc_s.at[g, 8 + j], r.gc_r.at[g, 8 + j], core)

    def gather_core(g, which):
        for j in which:
            if j == 0:
                view = part(g, z, y, 1 - c, None)
            elif j < 4:
                view = part(g, (z - j) % 4, y, 1 - c, x)
            elif j < 8:
                view = part(g, (z - j + 4) % 4, 1 - y, 1 - c, x)
            elif j < 11:
                view = part(g, (z - j + 7) % 4, y, 1 - c, 1 - x)
            else:
                view = part(g, (z - j + 11) % 4, 1 - y, 1 - c, 1 - x)
            arrived(view, r.gc_r.at[g, j])

    tail = remote(r.tails, r.before, r.tail_s.at[0], r.tail_r.at[0], following)
    tail.start()
    back = (2 * f, 2 * f, 6 * (f % 4) + jnp.where(z >= 2, 6, 0))

    def one_hot(shape, pick):
        row = lax.broadcasted_iota(jnp.int32, shape, 0)
        col = lax.broadcasted_iota(jnp.int32, shape, 1)
        return jnp.where(col == pick(row), 1.0, 0.0).astype(BF)

    def to_rows(g):
        return one_hot((96, 128), lambda i: 32 - back[g] + 6 * (i % 16) + i // 16)

    def store_rows(dst, row, tiles, n=6):
        for j in range(n):
            dst[pl.ds(pl.multiple_of(row, 16), 16), 128 * j : 128 * j + 128] = tiles[16 * j : 16 * j + 16]

    def first_window(g, flat, n):
        return jnp.concatenate([r.before[32 * g : 32 * g + 32], flat[0:n]], 0)

    def lay_rows(g, flat, dst, n):
        perm = to_rows(g)

        def body(i, carry):
            window = flat[pl.ds(pl.multiple_of(96 * i - 32, 32), 128)]
            store_rows(dst, 16 * i, mm(perm, window).astype(BF))
            return carry

        lax.fori_loop(1, n, body, 0)
        return perm

    tail_v = one_hot(
        (96, 96),
        lambda i: jnp.where(
            i % 16 < 5,
            6 * (i % 16) + i // 16,
            jnp.where(
                i % 16 < 10,
                32 + 6 * (i % 16 - 5) + i // 16,
                jnp.where(z < 2, 72, 66)
                + jnp.where(
                    z % 2 == 0,
                    12 * (i // 48) + 3 * (i % 16 - 10) + (i // 16) % 3,
                    6 * (i % 16 - 10) + i // 16,
                ),
            ),
        ),
    )
    store_rows(r.own_t, 0, mm(tail_v, r.tails[...]).astype(BF))
    mine_s, mine_c = part(0, z, y, c, None), part(1, z, y, c, None)
    perm = lay_rows(0, r.flat_s, mine_s, 12)
    tail.wait_recv()
    store_rows(mine_s, 0, mm(perm, first_window(0, r.flat_s, 96)).astype(BF))
    own_z(0)
    own_y(0)
    own_core(0)

    @pl.when(root)
    def _():
        mine = pltpu.make_async_copy(r.own_t, r.tb.at[z], r.loc.at[0])
        mine.start()
        out = []
        for k in (1, 2, 3):
            go(out, r.own_t, r.tb.at[z], r.t_s.at[k - 1], r.t_r.at[k], zdev(k))
        mine.wait()
        for k in (1, 2, 3):
            arrived(r.tb.at[(z - k) % 4], r.t_r.at[k])
        for i, (yy, cc) in enumerate(((0, 0), (0, 1), (1, 0))):
            go(out, r.tb, r.tb, r.t_s.at[3 + i], r.t_r.at[0], device(x, z, yy, cc))
        drain(out)

    perm = lay_rows(1, r.flat_c, mine_c, 17)
    store_rows(mine_c, 0, mm(perm, first_window(1, r.flat_c, 96)).astype(BF))
    own_z(1)
    own_y(1)
    own_core(1)

    @pl.when(w1)
    def _():
        def pick(i):
            m, j = i % 16, i // 16
            q = 2 * jnp.where(j < 6, c, 1 - c) + x
            j = j % 6
            return 32 - back[2] + 24 * m + 12 * (j // 3) + 3 * q + j % 3

        perm = one_hot((192, 416), pick)
        mine = part_f(z, y, 192 * c, 192)

        def put(i, window):
            tiles = mm(perm, window).astype(BF)
            store_rows(r.theirs, 16 * i, tiles[96:192])
            store_rows(mine, 16 * i, tiles[0:96])

        def body(i, carry):
            put(i, r.flat_f[pl.ds(pl.multiple_of(384 * i - 32, 32), 416)])
            return carry

        put(0, first_window(2, r.flat_f, 384))
        lax.fori_loop(1, 12, body, 0)
        swap = remote(r.theirs, mine, r.gc_s.at[2, 0], r.gc_r.at[2, 0], core)
        swap.start()
        swap.wait()

    @pl.when(jnp.logical_not(w1))
    def _():
        perm = to_rows(2)
        mine = part_f(z, y)

        def body(i, carry):
            window = r.flat_f[pl.ds(pl.multiple_of(2304 * x + 96 * i - 32, 32), 128)]
            store_rows(mine, 16 * i, mm(perm, window).astype(BF))
            return carry

        lax.fori_loop(1, 24, body, 0)
        lead = jnp.where(x == 0, r.before[64:96], r.flat_f[2304 - 32 : 2304])
        rest = r.flat_f[pl.ds(pl.multiple_of(2304 * x, 32), 96)]
        store_rows(mine, 0, mm(perm, jnp.concatenate([lead, rest], 0)).astype(BF))

    tail.wait_send()
    r.vg[...] = jnp.zeros_like(r.vg)

    own_y(5)
    gather_z(0)
    own_z(2)
    for g in (2, 3, 4):
        own_y(g)
    gather_y(0)
    own_z(3)
    gather_z(1)
    own_z(4)
    own_z(5)
    other_z()
    gather_y(1, (0,))
    gather_z(2)
    gather_x(0)
    gather_y(1, (1, 2, 3))

    @pl.when(jnp.logical_not(root))
    def _():
        arrived(r.tb, r.t_r.at[0])

    r.tv[...] = r.tb[...].astype(F32)
    gather_core(0, range(15))

    self_v = lambda j: r.tv[3, j : j + 1]
    cross_v = lambda j: r.tv[3, 5 + j : 6 + j]
    ffn_b1 = lambda b: r.tv[2 * b, pl.ds(10 + me, 1)]
    ffn_v = lambda b, j: r.tv[2 * b + 1, 10 + j : 11 + j]

    def slot(xx, cc):
        return 2 * cc + xx

    def ag_copy(ph, b, i):
        buf = r.xg.at[ph, b]
        pair = [(me, xn), (me, core), (slot(1 - x, c), core)]
        s, t = pair[i]
        return remote(buf.at[s], buf.at[s], r.ex_s.at[ph, b, i], r.ex_r.at[ph, b, i], t)

    def ag_start(ph, b):
        ag_copy(ph, b, 0).start()
        ag_copy(ph, b, 1).start()

    def ag_mid(ph, b):
        ag_copy(ph, b, 0).wait_recv()
        ag_copy(ph, b, 2).start()

    def ag_end(ph, b):
        ag_copy(ph, b, 1).wait_recv()
        ag_copy(ph, b, 2).wait_recv()
        for i in range(3):
            ag_copy(ph, b, i).wait_send()

    def rs_copy(ph, b, i):
        src = r.send_x.at[ph, b] if i == 2 else r.send_p.at[ph, b, i]
        dst = r.recv_x.at[ph, b] if i == 2 else r.recv_p.at[ph, b, i]
        return remote(src, dst, r.rs_s.at[ph, b, i], r.rs_r.at[ph, b, i], xn if i == 2 else core)

    def rs_start(ph, b):
        r.send_p[ph, b, 0] = r.part[b, slot(1 - x, 1 - c)].astype(BF)
        rs_copy(ph, b, 0).start()
        r.send_p[ph, b, 1] = r.part[b, slot(x, 1 - c)].astype(BF)
        rs_copy(ph, b, 1).start()

    def rs_mid(ph, b):
        rs_copy(ph, b, 0).wait_recv()
        r.send_x[ph, b] = (r.part[b, slot(1 - x, c)] + r.recv_p[ph, b, 0].astype(F32)).astype(BF)
        rs_copy(ph, b, 2).start()

    def rs_end(ph, b):
        rs_copy(ph, b, 1).wait_recv()
        rs_copy(ph, b, 2).wait_recv()
        for i in range(3):
            rs_copy(ph, b, i).wait_send()
        return r.part[b, me] + r.recv_p[ph, b, 1].astype(F32) + r.recv_x[ph, b].astype(F32)

    h = r.hid[...]
    r.q[...] = (mm(h, r.ws[0]) + self_v(0)).astype(BF)
    r.k[...] = mm(h, r.ws[1]).astype(BF)
    r.v[...] = (mm(h, r.ws[2]) + self_v(1)).astype(BF)
    for i in range(2):
        rows = slice(64 * i, 64 * i + 64)
        at = lax.broadcasted_iota(jnp.int32, (256, 64), 0) % 64
        key = lax.broadcasted_iota(jnp.int32, (256, 64), 1)
        caption = jnp.where(at >= NQ, 1.0, 0.0) * jnp.where(key <= at, 1.0, 0.0)
        ok = jnp.where(key < NQ, 1.0, caption * jnp.where(key < NQ + r.lens[i], 1.0, 0.0))
        for g in range(3):
            lanes = slice(256 * g, 256 * g + 256)
            p, a = attend_block(r.q[rows, lanes], r.k[rows, lanes], r.v[rows, lanes], ok)
            r.p[i, g] = p
            r.a[rows, lanes] = a
    r.sum1[...] = h.astype(F32) + (mm(r.a[...], r.ws[3]) + self_v(2))
    xh, _ = normed(r.sum1[...])
    r.first[...] = xh * self_v(3) + self_v(4)
    r.xg[0, 1, me] = rows_of(r.first, 32).astype(BF)
    ag_start(0, 1)

    for i in range(2):
        r.ck[272 * i + 256 : 272 * i + 272] = jnp.zeros((16, D), BF)
        r.cv[272 * i + 256 : 272 * i + 272] = jnp.zeros((16, D), BF)
    gather_core(1, range(8))
    for i in range(2):
        rows = slice(272 * i, 272 * i + 257)
        r.ck[rows, cols(x)] = mm(r.feat[i], r.wc[768:2176, cols(x)]).astype(BF)
        bias = r.tv[3, 6:7, cols(x)]
        r.cv[rows, cols(x)] = (mm(r.feat[i], r.wc[2176:3584, cols(x)]) + bias).astype(BF)
    ag_mid(0, 1)
    gather_z(3)
    gather_z(4)
    gather_x(1)
    gather_core(1, range(8, 15))
    far_cols = cols(1 - x)
    for i in range(2):
        rows = slice(272 * i, 272 * i + 257)
        r.ck[rows, far_cols] = mm(r.feat[i], r.wc[768:2176, far_cols]).astype(BF)
        bias = r.tv[3, 6:7, far_cols]
        r.cv[rows, far_cols] = (mm(r.feat[i], r.wc[2176:3584, far_cols]) + bias).astype(BF)
    u = rows_of(r.first, 0)
    r.cq[...] = (mm(u.astype(BF), r.wc[0:768]) + cross_v(0)).astype(BF)
    ok = jnp.where(lax.broadcasted_iota(jnp.int32, (128, 272), 1) < 257, 1.0, 0.0)
    for i in range(2):
        rows = slice(272 * i, 272 * i + 272)
        mine = slice(32 * i, 32 * i + 32)
        for g in range(3):
            lanes = slice(256 * g, 256 * g + 256)
            p, a = attend_block(r.cq[mine, lanes], r.ck[rows, lanes], r.cv[rows, lanes], ok)
            r.pc[i, g] = p
            r.ca[mine, lanes] = a
    r.sum2[...] = u + (mm(r.ca[...], r.wc[3584:4352]) + cross_v(2))
    xh, _ = normed(r.sum2[...])
    r.second[...] = xh * cross_v(3) + cross_v(4)
    r.xg[0, 0, me] = r.second[...].astype(BF)
    ag_start(0, 0)

    gather_z(5, last=True)
    other_arrivals()
    for g in (2, 3, 4):
        gather_y(g)

    def ffn_forward_part(b):
        rows = r.xg[0, b].reshape(256, D)
        r.pre[b] = mm(rows, r.wf[2 * b]) + ffn_b1(b)
        r.act[b] = gelu(r.pre[b]).astype(BF)
        r.part[b] = mm(r.act[b], r.wf[2 * b + 1]).reshape(4, 64, D)

    def ffn_turn(b):
        rows = r.second[...] if b == 0 else rows_of(r.first, 32)
        s3 = rows + (rs_end(0, b) + ffn_v(b, 0))
        xh, _ = normed(s3)
        done = (xh * ffn_v(b, 1) + ffn_v(b, 2)).astype(BF)
        for i in range(2):
            r.mixed[64 * i + 32 * b : 64 * i + 32 * b + 32] = done[32 * i : 32 * i + 32]
        g_out = rows_of(r.cot, 32 * b).astype(F32)
        dsum, dgain, dshift = norm_back(s3, ffn_v(b, 1), g_out)
        r.dsum3[b] = dsum
        low = dsum.astype(BF)
        r.xg[1, b, me] = low
        r.vg[2 * b + 1, 10:11] = rows_sum(low)
        r.vg[2 * b + 1, 11:12] = dgain
        r.vg[2 * b + 1, 12:13] = dshift

    def ffn_backward_part(b):
        up = r.xg[1, b].reshape(256, D)
        r.dpre[b] = (mm_nt(up, r.wf[2 * b + 1]) * gelu_slope(r.pre[b])).astype(BF)
        r.part[b] = mm_nt(r.dpre[b], r.wf[2 * b]).reshape(4, 64, D)
        db1 = rows_sum(r.dpre[b])
        for j in range(4):
            r.vg[2 * b, 10 + j : 11 + j] = jnp.where(j == me, db1, 0.0)

    sent = []

    def ffn_weight_grads(b):
        rows = r.xg[0, b].reshape(256, D)
        up = r.xg[1, b].reshape(256, D)
        r.wf[2 * b] = mm_tn(rows, r.dpre[b]).astype(BF)
        r.wf[2 * b + 1] = mm_tn(r.act[b], up).astype(BF)
        for p in (2 * b, 2 * b + 1):
            go(sent, part_f(p, 1 - y, 0, SPLIT), r.yf.at[p], r.yy_s.at[2, p], r.yy_r.at[2, p], yn)
        for p in (2 * b, 2 * b + 1):
            for i, yy in ((4, 1 - y), (3, y)):
                z_out_sum(i, part_f(p, yy, SPLIT, REST), p)

    hop = jnp.where(z < 2, 1, 2)

    def z_out_sum(i, src, p):
        zb, zr = getattr(r, f"zb{i}"), getattr(r, f"zr{i}")
        d = (p - z) % 4
        far = {0: z == 3, 3: z == 0}.get(p)
        later = {0: z == 2, 3: z == 1}.get(p)
        direct = z != p
        if far is not None:
            go(sent, src, zr, r.zq_s.at[i], r.zq_r.at[i], device(x, hop, y, c), far)
            direct = jnp.logical_and(direct, jnp.logical_not(jnp.logical_or(far, later)))
        go(sent, src, zb.at[d - 1], r.zz_s.at[i, p], r.zz_r.at[i, d], device(x, p, y, c), direct)

    def z_add_sum(i, src, p):
        later = {0: z == 2, 3: z == 1}.get(p)
        if later is None:
            return
        zb, zr = getattr(r, f"zb{i}"), getattr(r, f"zr{i}")

        @pl.when(later)
        def _():
            arrived(zr, r.zq_r.at[i])
            zr[...] = add(zr[...], src[...])

        go(sent, zr, zb.at[1], r.zz_s.at[i, p], r.zz_r.at[i, 2], device(x, p, y, c), later)

    def z_total(i, own, out):
        zb = getattr(r, f"zb{i}")
        arrived(zb.at[1], r.zz_r.at[i, 2])
        out[...] = add(own, zb[1])
        for d, without in ((1, 0), (3, 3)):

            @pl.when(z != without)
            def _():
                arrived(zb.at[d - 1], r.zz_r.at[i, d])
                out[...] = add(out[...], zb[d - 1])

    def ffn_sum_y(p):
        arrived(r.yf.at[p], r.yy_r.at[2, p])
        r.yf[p] = add(r.yf[p], part_f(p, y, 0, SPLIT)[...])
        z_out_sum(2, r.yf.at[p], p)

    def ffn_add(p):
        for i, yy in ((4, 1 - y), (3, y)):
            z_add_sum(i, part_f(p, yy, SPLIT, REST), p)

    def ffn_sum_other():
        z_total(4, part_f(z, 1 - y, SPLIT, REST)[...], r.of)
        go(sent, r.of, r.yf2, r.yy_s.at[3, 0], r.yy_r.at[3, 0], yn)

    ag_end(0, 1)
    ffn_forward_part(1)
    rs_start(0, 1)
    ag_mid(0, 0)
    ag_end(0, 0)
    rs_mid(0, 1)
    ffn_forward_part(0)
    rs_start(0, 0)
    ffn_turn(1)
    ag_start(1, 1)
    rs_mid(0, 0)
    ag_mid(1, 1)
    ag_end(1, 1)
    ffn_backward_part(1)
    rs_start(1, 1)
    ffn_turn(0)
    ag_start(1, 0)
    rs_mid(1, 1)
    drain(sent_w[2])
    ffn_weight_grads(1)
    ag_mid(1, 0)
    ag_end(1, 0)
    ffn_backward_part(0)
    rs_start(1, 0)
    d_text = r.dsum3[1] + rs_end(1, 1)
    for i in range(2):
        r.dfirst[64 * i + 32 : 64 * i + 64] = d_text[32 * i : 32 * i + 32]
    rs_mid(1, 0)
    ffn_weight_grads(0)
    d_second = r.dsum3[0] + rs_end(1, 0)

    groups = (
        (shard_s, r.core_s, r.xs, r.ys, r.fin_s, r.nice_s),
        (shard_c, r.core_c, r.xc, r.yc, r.fin_c, r.nice_c),
    )
    order = (3, 1, 2, 0)

    def sum_start(g):
        view, cb = groups[g][:2]
        for far in range(2):
            for d in order:
                zz = (z + d) % 4
                go(sent, view(zz, y if far else 1 - y, 1 - c), cb.at[far, zz], r.co_s.at[g, far, d], r.co_r.at[g, far, d], core)

    def sum_core(g):
        view, cb, xb = groups[g][:3]
        for far in range(2):
            for d in order:
                zz = (z + d) % 4
                arrived(cb.at[far, zz], r.co_r.at[g, far, d])
                cb[far, zz] = add(cb[far, zz], view(zz, y if far else 1 - y, c)[...])
                go(sent, cb.at[far, zz, :, cols(1 - x)], xb.at[far, zz], r.xx_s.at[g, far, d], r.xx_r.at[g, far, d], xn)

    def sum_x(g, far):
        view, cb, xb, yb = groups[g][:4]
        for d in order:
            zz = (z + d) % 4
            arrived(xb.at[far, zz], r.xx_r.at[g, far, d])
            xb[far, zz] = add(xb[far, zz], cb[far, zz, :, cols(x)])
            if far == 0:
                go(sent, xb.at[0, zz], yb.at[zz], r.yy_s.at[g, d], r.yy_r.at[g, d], yn)

    def sum_y(g):
        view, cb, xb, yb = groups[g][:4]
        zb, zr = getattr(r, f"zb{g}"), getattr(r, f"zr{g}")
        for d in order:
            zz = (z + d) % 4
            arrived(yb.at[zz], r.yy_r.at[g, d])
            yb[zz] = add(yb[zz], xb[1, zz])
            if d == 2:

                @pl.when(inner)
                def _():
                    arrived(zr, r.zq_r.at[g])
                    zr[...] = add(zr[...], yb[zz])

                go(sent, zr, zb.at[1], r.zz_s.at[g, 2], r.zz_r.at[g, 2], zdev(2), inner)
                go(sent, yb.at[zz], zb.at[1], r.zz_s.at[g, 2], r.zz_r.at[g, 2], zdev(2), outer)
            elif d:
                far = z == (0 if d == 3 else 3)
                go(sent, yb.at[zz], zr, r.zq_s.at[g], r.zq_r.at[g], device(x, hop, y, c), far)
                go(sent, yb.at[zz], zb.at[d - 1], r.zz_s.at[g, d], r.zz_r.at[g, d], zdev(d), jnp.logical_not(far))

    def sum_z(g):
        view, cb, xb, yb, fin, out = groups[g]
        z_total(g, yb[z], fin)
        out[:, cols(x)] = fin[...]
        go(sent, fin, out.at[:, cols(x)], r.fi_s.at[g], r.fi_r.at[g], xn)

    def ffn_sum_z():
        z_total(2, r.yf[z], r.fin_f.at[0:SPLIT])
        last = r.fin_f.at[SPLIT:384]
        z_total(3, part_f(z, y, SPLIT, REST)[...], last)
        arrived(r.yf2, r.yy_r.at[3, 0])
        last[...] = add(last[...], r.yf2[...])
        half = lambda j: r.fin_f.at[pl.ds(pl.multiple_of(192 * j, 192), 192)]

        @pl.when(w1)
        def _():
            r.nice_f[me] = half(c)[...]
            remote(half(c), r.nice_f.at[me], r.fi_s.at[2], r.fi_r.at[2], xn).start()
            remote(half(1 - c), r.nice_f.at[me], r.fi_s.at[3], r.fi_r.at[3], core).start()
            remote(half(1 - c), r.nice_f.at[me], r.fi_s.at[4], r.fi_r.at[4], diag).start()

        @pl.when(jnp.logical_not(w1))
        def _():
            for j in range(2):
                r.nice_f[2 * x + j] = half(j)[...]
                remote(half(j), r.nice_f.at[2 * x + j], r.fi_s.at[2 + j], r.fi_r.at[2 + j], xn).start()

    def ffn_end():
        def ends(n):
            for j in range(n):
                remote(r.fin_f.at[0:192], r.nice_f.at[0], r.fi_s.at[2 + j], r.fi_r.at[2 + j], xn).wait()

        pl.when(w1)(lambda: ends(3))
        pl.when(jnp.logical_not(w1))(lambda: ends(2))

    du2, dgain, dshift = norm_back(r.sum2[...], cross_v(3), d_second)
    r.vg[3, 8:9] = dgain
    r.vg[3, 9:10] = dshift
    low = du2.astype(BF)
    r.vg[3, 7:8] = rows_sum(low)
    dca = mm_nt(low, r.wc[3584:4352]).astype(BF)
    drain(sent_w[1])
    r.wc[3584:4352] = mm_tn(r.ca[...], low).astype(BF)
    dcq = []
    for i in range(2):
        rows = slice(272 * i, 272 * i + 272)
        mine = slice(32 * i, 32 * i + 32)
        blocks = []
        for g in range(3):
            lanes = slice(256 * g, 256 * g + 256)
            dq, dk, dv = attend_block_back(
                r.cq[mine, lanes], r.ck[rows, lanes], r.cv[rows, lanes], r.pc[i, g], dca[mine, lanes]
            )
            blocks.append(dq)
            r.ck[rows, lanes] = dk
            r.cv[rows, lanes] = dv
        dcq.append(jnp.concatenate(blocks, 1))
    dcq = jnp.concatenate(dcq, 0)
    r.vg[3, 5:6] = rows_sum(dcq)
    r.vg[3, 6:7] = rows_sum(r.cv[...])
    du = du2 + mm_nt(dcq, r.wc[0:768])
    for i in range(2):
        r.dfirst[64 * i : 64 * i + 32] = du[32 * i : 32 * i + 32]
    r.wc[0:768] = mm_tn(rows_of(r.first, 0).astype(BF), dcq).astype(BF)
    for j in range(11):
        block = [r.feat[i, :, 128 * j : 128 * j + 128] for i in range(2)]
        both = lambda d: mm_tn(block[0], d[0:257]) + mm_tn(block[1], d[272:529])
        r.wc[768 + 128 * j : 896 + 128 * j] = both(r.ck).astype(BF)
        r.wc[2176 + 128 * j : 2304 + 128 * j] = both(r.cv).astype(BF)
    sum_start(1)
    ffn_add(3)
    ffn_sum_y(2)
    ffn_sum_y(3)

    dsum1, dgain, dshift = norm_back(r.sum1[...], self_v(3), r.dfirst[...])
    r.vg[3, 3:4] = dgain
    r.vg[3, 4:5] = dshift
    low = dsum1.astype(BF)
    r.vg[3, 2:3] = rows_sum(low)
    da = mm_nt(low, r.ws[3]).astype(BF)
    drain(sent_w[0])
    r.ws[3] = mm_tn(r.a[...], low).astype(BF)
    for i in range(2):
        rows = slice(64 * i, 64 * i + 64)
        for g in range(3):
            lanes = slice(256 * g, 256 * g + 256)
            dq, dk, dv = attend_block_back(
                r.q[rows, lanes], r.k[rows, lanes], r.v[rows, lanes], r.p[i, g], da[rows, lanes]
            )
            r.q[rows, lanes] = dq
            r.k[rows, lanes] = dk
            r.v[rows, lanes] = dv
    sum_core(1)
    r.vg[3, 0:1] = rows_sum(r.q[...])
    r.vg[3, 1:2] = rows_sum(r.v[...])
    total = dsum1 + mm_nt(r.q[...], r.ws[0]) + mm_nt(r.k[...], r.ws[1]) + mm_nt(r.v[...], r.ws[2])
    r.hgrad[...] = total.astype(BF)
    r.ws[0] = mm_tn(r.hid[...], r.q[...]).astype(BF)
    r.ws[1] = mm_tn(r.hid[...], r.k[...]).astype(BF)
    r.ws[2] = mm_tn(r.hid[...], r.v[...]).astype(BF)
    sum_start(0)

    r.v_send[...] = r.vg[...].astype(BF)
    index = 2 * y + c
    home = device(x, z, 1, 1)

    @pl.when(jnp.logical_not(root))
    def _():
        remote(r.v_send, r.v_in.at[index], r.vv_s.at[0], r.vv_r.at[index], home).start()

    ffn_add(0)
    ffn_sum_y(0)
    ffn_sum_y(1)
    z_add_sum(2, r.yf.at[0], 0)
    z_add_sum(2, r.yf.at[3], 3)
    sum_x(1, 0)
    sum_core(0)

    @pl.when(root)
    def _():
        total = r.vg[...]
        for i in range(3):
            arrived(r.v_in.at[i], r.vv_r.at[i])
            total = total + r.v_in[i].astype(F32)
        r.v_z[...] = total.astype(BF)
        for k in (1, 2, 3):
            zz = (z + k) % 4
            remote(r.v_z.at[zz], r.v_zin.at[k - 1], r.vv_s.at[k], r.vv_r.at[2 + k], device(x, zz, y, c)).start()

    sum_x(1, 1)
    ffn_sum_other()
    sum_y(1)
    ffn_sum_z()
    sum_x(0, 0)
    sum_x(0, 1)

    @pl.when(root)
    def _():
        total = r.v_z[z].astype(F32)
        for k in (1, 2, 3):
            arrived(r.v_zin.at[k - 1], r.vv_r.at[2 + k])
            total = total + r.v_zin[k - 1].astype(F32)
        r.v_x[...] = total.astype(BF)
        remote(r.v_x, r.v_xin, r.vv_s.at[4], r.vv_r.at[6], xn).start()

    sum_y(0)
    sum_z(1)
    sum_z(0)

    @pl.when(root)
    def _():
        arrived(r.v_xin, r.vv_r.at[6])
        r.total_v[...] = add(r.v_x[...], r.v_xin[...])
        for k in (1, 2, 3):
            zz = (z + k) % 4
            remote(r.v_z.at[zz], r.v_zin.at[k - 1], r.vv_s.at[k], r.vv_r.at[2 + k], device(x, zz, y, c)).wait_send()
        remote(r.v_x, r.v_xin, r.vv_s.at[4], r.vv_r.at[6], xn).wait_send()

    @pl.when(jnp.logical_not(root))
    def _():
        r.total_v[...] = jnp.zeros_like(r.total_v)
        remote(r.v_send, r.v_in.at[index], r.vv_s.at[0], r.vv_r.at[index], home).wait_send()

    ffn_end()

    def stack(src, row, n=6):
        return jnp.concatenate(
            [src[pl.ds(pl.multiple_of(row, 16), 16), 128 * j : 128 * j + 128] for j in range(n)], 0
        )

    to_flat = one_hot((96, 96), lambda i: 16 * (i % 6) + i // 6)

    def lay_flat(src, dst, n, base=0):
        def body(i, carry):
            dst[pl.ds(pl.multiple_of(base + 96 * i, 32), 96)] = mm(to_flat, stack(src, 16 * i))
            return carry

        lax.fori_loop(0, n, body, 0)

    def head_out(g, fl):
        r.heads[g] = fl[0:32].astype(BF)
        go(sent, r.heads.at[g], r.after.at[g], r.head_s.at[g], r.head_r.at[g], preceding)

    @pl.when(w1)
    def _():
        def pick(i):
            m, t = i // 24, i % 24
            return 96 * ((t % 12) // 3) + 16 * (3 * (t // 12) + t % 3) + m

        perm = one_hot((384, 384), pick)

        def body(i, carry):
            tiles = jnp.concatenate([stack(r.nice_f.at[q], 16 * i) for q in range(4)], 0)
            r.fl_f[pl.ds(pl.multiple_of(384 * i, 128), 384)] = mm(perm, tiles)
            return carry

        lax.fori_loop(0, 12, body, 0)

    @pl.when(jnp.logical_not(w1))
    def _():
        for q in range(4):
            lay_flat(r.nice_f.at[q], r.fl_f, 12, 1152 * q)

    head_out(2, r.fl_f)
    arrived(groups[1][5].at[:, cols(1 - x)], r.fi_r.at[1])
    lay_flat(r.nice_c, r.fl_c, 17)
    head_out(1, r.fl_c)
    arrived(groups[0][5].at[:, cols(1 - x)], r.fi_r.at[0])
    lay_flat(r.nice_s, r.fl_s, 12)
    head_out(0, r.fl_s)

    vectors = stack(r.total_v, 0)
    end = (f == 15, f == 15, f % 4 == 3)
    plain = lambda first: lambda i: 16 * (i % 6) + first + i // 6
    hidden = lambda i: 16 * (3 * (i // 12) + i % 3) + 10 + (i % 12) // 3
    none = -1
    count = jnp.where(w1, 24, 18)

    def from_vectors(g):
        if g < 2:
            return lambda i: jnp.where(jnp.logical_and(end[g], i < 30), plain(5 * g)(i), none)
        pick = lambda i: jnp.where(w1, hidden(i), plain(10)(i))
        return lambda i: jnp.where(jnp.logical_and(end[2], i < count), pick(i), none)

    def from_next(g):
        if g < 2:
            return lambda i: jnp.where(end[g], none, i)
        inside = jnp.logical_or(z == 1, z == 2)
        return lambda i: jnp.where(
            end[2], jnp.where(jnp.logical_and(inside, i >= count), i - count, none), i
        )

    ends = ((r.fl_s, r.out_s, 1152, 1154), (r.fl_c, r.out_c, 1632, 1634), (r.fl_f, r.out_f, 4608, 4614))
    copies = []
    for g in (2, 1, 0):
        fl, out, rows, size = ends[g]
        arrived(r.after.at[g], r.head_r.at[g])
        fl[rows : rows + 32] = mm(one_hot((32, 96), from_vectors(g)), vectors) + mm(
            one_hot((32, 32), from_next(g)), r.after[g]
        )

        def body(i, carry):
            fl[pl.ds(pl.multiple_of(128 * i, 128), 128)] = fl[pl.ds(back[g] + 128 * i, 128)]
            return carry

        lax.fori_loop(0, size // 128, body, 0)
        done = size // 128 * 128
        fl[done:size] = fl[pl.ds(back[g] + done, size - done)]
        copy = pltpu.make_async_copy(fl.at[0:size], out, r.out_sem.at[g])
        copy.start()
        copies.append(copy)
    for copy in copies:
        copy.wait()

    drain(sent)


def layer(flat_s, flat_c, flat_f, tails, lens, hid, feat, cot):
    vm = pl.BlockSpec(memory_space=pltpu.VMEM)
    return pl.pallas_call(
        layer_kernel,
        out_shape=(
            jax.ShapeDtypeStruct((128, D), BF),
            jax.ShapeDtypeStruct((128, D), BF),
            *[jax.ShapeDtypeStruct((v.shape[0], 128), F32) for v in (flat_s, flat_c, flat_f)],
        ),
        in_specs=[vm] * 4 + [pl.BlockSpec(memory_space=pltpu.SMEM)] + [vm] * 3,
        out_specs=[vm] * 2 + [pl.BlockSpec(memory_space=pl.ANY)] * 3,
        scratch_shapes=list(scratch().values()),
        compiler_params=pltpu.CompilerParams(
            collective_id=0, has_side_effects=True, vmem_limit_bytes=VMEM_BYTES
        ),
    )(flat_s, flat_c, flat_f, tails, lens, hid, feat, cot)


def per_device_fast(hidden, lengths, features, cotangent, self_params, cross_params, ffn_params):
    flats = [v.reshape(-1, 128) for v in (self_params, cross_params, ffn_params)]
    tails = jnp.concatenate([v[-32:] for v in flats])
    mixed, hgrad, *grads = layer(
        *flats, tails, lengths, hidden.reshape(128, D), features, cotangent.reshape(128, D)
    )
    return (mixed.reshape(2, 64, D), hgrad.reshape(2, 64, D), *[v.reshape(-1) for v in grads])


def solution(mesh):
    fast = mesh.shape["dp"] == 2 and mesh.shape["fsdp"] == 16
    return jax.shard_map(
        per_device_fast if fast else per_device,
        mesh=mesh,
        in_specs=(
            P(("dp", "fsdp"), None, None),
            P(("dp", "fsdp")),
            P(("dp", "fsdp"), None, None),
            P(("dp", "fsdp"), None, None),
            P("fsdp"),
            P("fsdp"),
            P("fsdp"),
        ),
        out_specs=(
            P(("dp", "fsdp"), None, None),
            P(("dp", "fsdp"), None, None),
            P("fsdp"),
            P("fsdp"),
            P("fsdp"),
        ),
        check_vma=False,
    )
```

```python
from functools import partial
import math
from types import SimpleNamespace

import jax
import jax.numpy as jnp
from jax import lax
from jax.experimental import pallas as pl
from jax.experimental.pallas import tpu as pltpu
from jax.sharding import PartitionSpec as P

D = 768
HEADS = 12
HDIM = 64
F = 3072
E = 1408
NQ = 32


EPS = 1e-06
SCALE = 0.125


def self_layout():
    return [(D, D)] * 4 + [(D,)] * 5


def cross_layout():
    return [(D, D), (E, D), (E, D), (D, D)] + [(D,)] * 5


def ffn_layout():
    return [(D, F), (F,), (F, D), (D,), (D,), (D,)] * 2


def split_flat(flat_vec, layouts):
    pieces = []
    offset = 0
    for layout in layouts:
        amount = math.prod(layout)
        pieces.append(flat_vec[offset : offset + amount].reshape(layout))
        offset = offset + amount
    return pieces


def join_flat(pieces, length):
    flat_vec = jnp.concatenate([piece.reshape(-1) for piece in pieces])
    return jnp.pad(flat_vec, (0, length - flat_vec.shape[0]))


def regroup(flat_vec):
    groups = lax.axis_size("fsdp")
    replicas = lax.axis_size("dp")
    return flat_vec.reshape(groups, replicas, -1).transpose(1, 0, 2).reshape(-1)


def matmul(left, right):
    return jnp.dot(left, right, preferred_element_type=jnp.float32)


def matmul_left(left, right):
    return lax.dot_general(
        left, right, (((0,), (0,)), ((), ())), preferred_element_type=jnp.float32
    )


def matmul_right(left, right):
    return lax.dot_general(
        left, right, (((1,), (1,)), ((), ())), preferred_element_type=jnp.float32
    )


def column_sum(values):
    return jnp.sum(values.astype(jnp.float32), 0)


def layer_norm(values, gain, shift):
    average = jnp.mean(values, -1, keepdims=True)
    centered = values - average
    variance = jnp.mean(centered * centered, -1, keepdims=True)
    return centered * lax.rsqrt(variance + EPS) * gain + shift


def norm_backward(summed, gain, shift, grad_out):
    _, norm_pull = jax.vjp(layer_norm, summed, gain.astype(jnp.float32), shift.astype(jnp.float32))
    return norm_pull(grad_out)


def heads(rows, items):
    return rows.reshape(items, -1, HEADS, HDIM)


def score_block(query, keys, mask):
    scores = jnp.einsum("iqhd,ikhd->ihqk", query, keys, preferred_element_type=jnp.float32) * SCALE
    if mask is not None:
        scores = jnp.where(mask, scores, -1e30)
    return scores


def attend(query, keys, values, mask):
    scores = score_block(query, keys, mask)
    top_sum = jax.nn.logsumexp(scores, axis=-1)
    probs = jnp.exp(scores - top_sum[..., None]).astype(jnp.bfloat16)
    context = jnp.einsum("ihqk,ikhd->iqhd", probs, values, preferred_element_type=jnp.float32)
    return (context, top_sum)


def attend_back(query, keys, values, mask, top_sum, grad_context):
    probs = jnp.exp(score_block(query, keys, mask) - top_sum[..., None])
    grad_probs = jnp.einsum(
        "iqhd,ikhd->ihqk", grad_context, values, preferred_element_type=jnp.float32
    )
    inner = jnp.sum(probs * grad_probs, -1, keepdims=True)
    grad_scores = (probs * (grad_probs - inner)).astype(jnp.bfloat16)
    grad_query = (
        jnp.einsum("ihqk,ikhd->iqhd", grad_scores, keys, preferred_element_type=jnp.float32) * SCALE
    )
    grad_keys = (
        jnp.einsum("ihqk,iqhd->ikhd", grad_scores, query, preferred_element_type=jnp.float32)
        * SCALE
    )
    grad_values = jnp.einsum(
        "ihqk,iqhd->ikhd",
        probs.astype(jnp.bfloat16),
        grad_context,
        preferred_element_type=jnp.float32,
    )
    return (grad_query, grad_keys, grad_values)


def linear_back(inputs, weight, grad_out):
    return (matmul_left(inputs, grad_out), column_sum(grad_out), matmul_right(grad_out, weight))


def ffn_forward(rows, params):
    w_in, b_in, w_out, b_out, gain, shift = params
    rows_low = rows.astype(jnp.bfloat16)
    hidden_pre = matmul(rows_low, w_in) + b_in
    activated = jax.nn.gelu(hidden_pre, approximate=True).astype(jnp.bfloat16)
    summed = rows + (matmul(activated, w_out) + b_out)
    final = layer_norm(summed, gain.astype(jnp.float32), shift.astype(jnp.float32))
    return (final, (rows_low, hidden_pre, activated, summed))


def ffn_backward(grad_out, kept, params):
    w_in, b_in, w_out, b_out, gain, shift = params
    rows_low, hidden_pre, activated, summed = kept
    grad_sum, grad_gain, grad_shift = norm_backward(summed, gain, shift, grad_out)
    grad_branch = grad_sum.astype(jnp.bfloat16)
    grad_w_out, grad_b_out, grad_act = linear_back(activated, w_out, grad_branch)
    _, gelu_pull = jax.vjp(partial(jax.nn.gelu, approximate=True), hidden_pre)
    grad_pre = gelu_pull(grad_act)[0].astype(jnp.bfloat16)
    grad_w_in, grad_b_in, grad_rows = linear_back(rows_low, w_in, grad_pre)
    return (
        grad_sum + grad_rows,
        [grad_w_in, grad_b_in, grad_w_out, grad_b_out, grad_gain, grad_shift],
    )


def per_device(hidden, lengths, features, cotangent, self_params, cross_params, ffn_params):
    items, seq, width = hidden.shape
    self_full = lax.all_gather(self_params, "fsdp", axis=0, tiled=True)
    self_parts = split_flat(self_full, self_layout())
    w_q, w_k, w_v, w_o, b_q, b_v, b_o, gain_one, shift_one = self_parts
    positions = jnp.arange(seq)
    rows_at = positions[:, None]
    cols_at = positions[None, :]
    allowed = (cols_at < NQ)[None] | ((rows_at >= NQ) & (cols_at <= rows_at))[None] & (
        cols_at[None] < NQ + lengths[:, None, None]
    )
    allowed = allowed[:, None]
    inputs = hidden.reshape(-1, width)
    query_low = (matmul(inputs, w_q) + b_q).astype(jnp.bfloat16)
    key_low = matmul(inputs, w_k).astype(jnp.bfloat16)
    value_low = (matmul(inputs, w_v) + b_v).astype(jnp.bfloat16)
    context, self_top = attend(
        heads(query_low, items), heads(key_low, items), heads(value_low, items), allowed
    )
    context_low = context.reshape(-1, width).astype(jnp.bfloat16)
    summed_one = inputs.astype(jnp.float32) + (matmul(context_low, w_o) + b_o)
    first = layer_norm(summed_one, gain_one.astype(jnp.float32), shift_one.astype(jnp.float32))
    first_items = first.reshape(items, seq, width)
    query_rows = first_items[:, :NQ].reshape(-1, width)
    text_rows = first_items[:, NQ:].reshape(-1, width)
    cross_full = lax.all_gather(cross_params, "fsdp", axis=0, tiled=True)
    cross_parts = split_flat(cross_full, cross_layout())
    cross_wq, cross_wk, cross_wv, cross_wo, cross_bq, cross_bv, cross_bo, gain_two, shift_two = (
        cross_parts
    )
    query_in = query_rows.astype(jnp.bfloat16)
    image_rows = features.reshape(-1, features.shape[-1])
    cross_query = (matmul(query_in, cross_wq) + cross_bq).astype(jnp.bfloat16)
    cross_key = matmul(image_rows, cross_wk).astype(jnp.bfloat16)
    cross_value = (matmul(image_rows, cross_wv) + cross_bv).astype(jnp.bfloat16)
    cross_context, cross_top = attend(
        heads(cross_query, items), heads(cross_key, items), heads(cross_value, items), None
    )
    cross_low = cross_context.reshape(-1, width).astype(jnp.bfloat16)
    summed_two = query_rows + (matmul(cross_low, cross_wo) + cross_bo)
    second = layer_norm(summed_two, gain_two.astype(jnp.float32), shift_two.astype(jnp.float32))
    ffn_full = lax.all_gather(ffn_params, "fsdp", axis=0, tiled=True)
    ffn_parts = split_flat(ffn_full, ffn_layout())
    query_final, query_kept = ffn_forward(second, ffn_parts[:6])
    text_final, text_kept = ffn_forward(text_rows, ffn_parts[6:])
    mixed = jnp.concatenate(
        [query_final.reshape(items, NQ, width), text_final.reshape(items, -1, width)], 1
    ).astype(jnp.bfloat16)
    grad_items = cotangent.astype(jnp.float32)
    grad_query_final = grad_items[:, :NQ].reshape(-1, width)
    grad_text_final = grad_items[:, NQ:].reshape(-1, width)
    ffn_back = split_flat(lax.all_gather(ffn_params, "fsdp", axis=0, tiled=True), ffn_layout())
    grad_second, query_grads = ffn_backward(grad_query_final, query_kept, ffn_back[:6])
    grad_text, text_grads = ffn_backward(grad_text_final, text_kept, ffn_back[6:])
    ffn_flat_grad = join_flat(query_grads + text_grads, ffn_full.shape[0])
    ffn_grad = lax.psum_scatter(
        regroup(ffn_flat_grad), ("dp", "fsdp"), scatter_dimension=0, tiled=True
    )
    cross_back = split_flat(
        lax.all_gather(cross_params, "fsdp", axis=0, tiled=True), cross_layout()
    )
    grad_summed_two, grad_gain_two, grad_shift_two = norm_backward(
        summed_two, cross_back[7], cross_back[8], grad_second
    )
    grad_cross_out = grad_summed_two.astype(jnp.bfloat16)
    grad_cross_wo, grad_cross_bo, grad_cross_ctx = linear_back(
        cross_low, cross_back[3], grad_cross_out
    )
    grad_cq, grad_ck, grad_cv = attend_back(
        heads(cross_query, items),
        heads(cross_key, items),
        heads(cross_value, items),
        None,
        cross_top,
        heads(grad_cross_ctx.astype(jnp.bfloat16), items),
    )
    grad_cq = grad_cq.reshape(-1, width).astype(jnp.bfloat16)
    grad_ck = grad_ck.reshape(-1, width).astype(jnp.bfloat16)
    grad_cv = grad_cv.reshape(-1, width).astype(jnp.bfloat16)
    grad_cross_wq, grad_cross_bq, grad_query_in = linear_back(query_in, cross_back[0], grad_cq)
    grad_cross_wk = matmul_left(image_rows, grad_ck)
    grad_cross_wv = matmul_left(image_rows, grad_cv)
    grad_cross_bv = column_sum(grad_cv)
    grad_query_rows = grad_summed_two + grad_query_in
    cross_list = [
        grad_cross_wq,
        grad_cross_wk,
        grad_cross_wv,
        grad_cross_wo,
        grad_cross_bq,
        grad_cross_bv,
        grad_cross_bo,
        grad_gain_two,
        grad_shift_two,
    ]
    cross_flat_grad = join_flat(cross_list, cross_full.shape[0])
    cross_grad = lax.psum_scatter(
        regroup(cross_flat_grad), ("dp", "fsdp"), scatter_dimension=0, tiled=True
    )
    self_back = split_flat(lax.all_gather(self_params, "fsdp", axis=0, tiled=True), self_layout())
    grad_first = jnp.concatenate(
        [grad_query_rows.reshape(items, NQ, width), grad_text.reshape(items, -1, width)], 1
    ).reshape(-1, width)
    grad_summed_one, grad_gain_one, grad_shift_one = norm_backward(
        summed_one, self_back[7], self_back[8], grad_first
    )
    grad_attn = grad_summed_one.astype(jnp.bfloat16)
    grad_w_o, grad_b_o, grad_ctx = linear_back(context_low, self_back[3], grad_attn)
    grad_q, grad_k, grad_v = attend_back(
        heads(query_low, items),
        heads(key_low, items),
        heads(value_low, items),
        allowed,
        self_top,
        heads(grad_ctx.astype(jnp.bfloat16), items),
    )
    grad_q = grad_q.reshape(-1, width).astype(jnp.bfloat16)
    grad_k = grad_k.reshape(-1, width).astype(jnp.bfloat16)
    grad_v = grad_v.reshape(-1, width).astype(jnp.bfloat16)
    grad_w_q, grad_b_q, input_from_q = linear_back(inputs, self_back[0], grad_q)
    grad_w_k = matmul_left(inputs, grad_k)
    input_from_k = matmul_right(grad_k, self_back[1])
    grad_w_v, grad_b_v, input_from_v = linear_back(inputs, self_back[2], grad_v)
    hidden_grad = (
        (grad_summed_one + input_from_q + input_from_k + input_from_v)
        .reshape(items, seq, width)
        .astype(jnp.bfloat16)
    )
    self_list = [
        grad_w_q,
        grad_w_k,
        grad_w_v,
        grad_w_o,
        grad_b_q,
        grad_b_v,
        grad_b_o,
        grad_gain_one,
        grad_shift_one,
    ]
    self_flat_grad = join_flat(self_list, self_full.shape[0])
    self_grad = lax.psum_scatter(
        regroup(self_flat_grad), ("dp", "fsdp"), scatter_dimension=0, tiled=True
    )
    self_grad, cross_grad, ffn_grad = (
        lax.all_gather(self_grad.astype(jnp.bfloat16), "dp", axis=0, tiled=True).astype(
            self_grad.dtype
        ),
        lax.all_gather(cross_grad.astype(jnp.bfloat16), "dp", axis=0, tiled=True).astype(
            cross_grad.dtype
        ),
        lax.all_gather(ffn_grad.astype(jnp.bfloat16), "dp", axis=0, tiled=True).astype(
            ffn_grad.dtype
        ),
    )
    return (mixed, hidden_grad, self_grad, cross_grad, ffn_grad)


MESH = pl.DeviceIdType.MESH
BF = jnp.bfloat16
F32 = jnp.float32
VMEM_BYTES = 62 * 2**20


def place():
    f = lax.axis_index("fsdp")
    return lax.axis_index("dp"), f // 4, (f // 2) % 2, f % 2


def device(x, z, y, c):
    return (x, (z * 2 + y) * 2 + c)


def shift_back():
    f = lax.axis_index("fsdp")
    return 2 * f, 2 * f, 6 * (f % 4) + jnp.where(f >= 8, 6, 0)


def meet(devices):
    barrier = pltpu.get_barrier_semaphore()
    for d in devices:
        pl.semaphore_signal(barrier, inc=1, device_id=d, device_id_type=MESH)
    pl.semaphore_wait(barrier, len(devices))


def remote(src, dst, send, recv, target):
    return pltpu.make_async_remote_copy(
        src_ref=src,
        dst_ref=dst,
        send_sem=send,
        recv_sem=recv,
        device_id=target,
        device_id_type=MESH,
    )


def mm(a, b):
    return jnp.dot(a, b, preferred_element_type=F32)


def mm_nt(a, b):
    return lax.dot_general(a, b, (((1,), (1,)), ((), ())), preferred_element_type=F32)


def mm_tn(a, b):
    return lax.dot_general(a, b, (((0,), (0,)), ((), ())), preferred_element_type=F32)


def rows_sum(v):
    return jnp.sum(v.astype(F32), 0, keepdims=True)


def add(a, b):
    return (a.astype(F32) + b.astype(F32)).astype(BF)


def normed(v):
    centered = v - jnp.mean(v, -1, keepdims=True)
    r = lax.rsqrt(jnp.mean(centered * centered, -1, keepdims=True) + EPS)
    return centered * r, r


def norm_back(v, gain, g_out):
    xh, r = normed(v)
    gg = g_out * gain
    dv = r * (gg - jnp.mean(gg, -1, keepdims=True) - xh * jnp.mean(gg * xh, -1, keepdims=True))
    return dv, rows_sum(g_out * xh), rows_sum(g_out)


GELU_A = math.sqrt(2.0 / math.pi)
GELU_B = 0.044715


def gelu(v):
    return 0.5 * v * (1.0 + jnp.tanh(GELU_A * (v + GELU_B * (v * v * v))))


def gelu_slope(v):
    t = jnp.tanh(GELU_A * (v + GELU_B * (v * v * v)))
    return 0.5 * (1.0 + t) + 0.5 * v * (1.0 - t * t) * (GELU_A * (1.0 + 3.0 * GELU_B * (v * v)))


def head_mask(h):
    lane = lax.broadcasted_iota(jnp.int32, (1, 256), 1)
    return jnp.where(lane // HDIM == h, 1.0, 0.0)


def spread(rows):
    wide = rows.astype(F32)
    return jnp.concatenate([(wide * head_mask(h)).astype(BF) for h in range(4)], 0)


def fold(stacked):
    n = stacked.shape[0] // 4
    total = stacked[:n] * head_mask(0)
    for h in range(1, 4):
        total = total + stacked[h * n : (h + 1) * n] * head_mask(h)
    return total


def attend_block(q, k, v, allowed):
    s = mm_nt(spread(q), k) * SCALE
    s = jnp.where(allowed > 0.5, s, -1e30)
    e = jnp.exp(s - jnp.max(s, -1, keepdims=True))
    p = e / jnp.sum(e, -1, keepdims=True)
    return p, fold(mm(p.astype(BF), v)).astype(BF)


def attend_block_back(q, k, v, p, da):
    dax = spread(da)
    dp = mm_nt(dax, v)
    ds = (p * (dp - jnp.sum(p * dp, -1, keepdims=True))).astype(BF)
    dq = (fold(mm(ds, k)) * SCALE).astype(BF)
    dk = (mm_tn(ds, spread(q)) * SCALE).astype(BF)
    dv = mm_tn(p.astype(BF), dax).astype(BF)
    return dq, dk, dv


def rows_of(ref, first):
    return jnp.concatenate([ref[first : first + 32], ref[64 + first : 96 + first]], 0)


SPLIT = 240
REST = 384 - SPLIT
X_FIRST = (False, True)
SIDE = tuple((2, 4) if first else (4,) for first in X_FIRST)
WIDTH = tuple(384 if first else 768 for first in X_FIRST)
STREAMS = ((192, 384), (272, 384), (SPLIT, D), (REST, D), (REST, D))


def scratch():
    dma = lambda *s: pltpu.SemaphoreType.DMA(s)
    b = lambda *s: pltpu.VMEM(s, BF)
    f = lambda *s: pltpu.VMEM(s, F32)
    return dict(
        ws=b(4, D, D), wc=b(4352, D), wf=b(4, D, D), theirs=b(192, D), own_t=b(16, D), tb=b(4, 16, D), before=b(96, 128),
        tv=f(4, 16, D), vg=f(4, 16, D),
        q=b(128, D), k=b(128, D), v=b(128, D), a=b(128, D), p=f(2, 3, 256, 64),
        sum1=f(128, D), first=f(128, D), cq=b(64, D), ck=b(544, D), cv=b(544, D), ca=b(64, D),
        pc=f(2, 3, 128, 272), sum2=f(64, D), second=f(64, D),
        xg=b(2, 2, 4, 64, D), pre=f(2, 256, D), act=b(2, 256, D), part=f(2, 4, 64, D),
        send_p=b(2, 2, 2, 64, D), recv_p=b(2, 2, 2, 64, D), send_x=b(2, 2, 64, D), recv_x=b(2, 2, 64, D),
        sum3=f(2, 64, D), dpre=b(2, 256, D), dsum3=f(2, 64, D), dfirst=f(128, D),
        core_s=b(2, 4, 192, D), core_c=b(2, 4, 272, D), xs=b(*SIDE[0], 192, 384), xc=b(*SIDE[1], 272, 384),
        ys=b(4, 192, WIDTH[0]), yc=b(4, 272, WIDTH[1]), yf=b(4, SPLIT, D), yf2=b(REST, D), of=b(REST, D),
        fin_s=b(192, 384), fin_c=b(272, 384), fin_f=b(384, D),
        **{f"{n}{i}": b(*lead, *shape) for i, shape in enumerate(STREAMS) for n, lead in (("zb", (3,)), ("zr", ()))},
        v_send=b(4, 16, D), v_in=b(3, 4, 16, D), v_z=b(4, 16, D), v_zin=b(3, 16, D), v_x=b(16, D), v_xin=b(16, D),
        nice_s=b(192, D), nice_c=b(272, D), nice_f=b(4, 192, D), total_v=b(16, D), heads=b(3, 32, 128), after=b(3, 32, 128),
        loc=dma(1), tail_s=dma(1), tail_r=dma(1), head_s=dma(3), head_r=dma(3), gz_s=dma(7, 4), gz_r=dma(7, 4), gy_s=dma(7, 4), gy_r=dma(7, 4), gx_s=dma(2, 7), gx_r=dma(2, 7),
        gc_s=dma(3, 15), gc_r=dma(3, 15), t_s=dma(6), t_r=dma(4),
        ex_s=dma(2, 2, 3), ex_r=dma(2, 2, 3), rs_s=dma(2, 2, 3), rs_r=dma(2, 2, 3),
        co_s=dma(2, 2, 4), co_r=dma(2, 2, 4), xx_s=dma(2, 2, 4), xx_r=dma(2, 2, 4), yy_s=dma(4, 4), yy_r=dma(4, 4),
        zz_s=dma(5, 4), zz_r=dma(5, 4), zq_s=dma(5), zq_r=dma(5), fi_s=dma(5), fi_r=dma(5), vv_s=dma(5), vv_r=dma(7),
    )


def layer_kernel(*refs):
    names = [
        "flat_s", "flat_c", "flat_f", "tails", "lens", "hid", "feat", "cot",
        "mixed", "hgrad", "out_s", "out_c", "out_f",
    ] + list(scratch())
    r = SimpleNamespace(**dict(zip(names, refs)))
    x, z, y, c = place()
    core, xn, yn = device(x, z, y, 1 - c), device(1 - x, z, y, c), device(x, z, 1 - y, c)
    diag = device(1 - x, z, y, 1 - c)
    zdev = lambda d: device(x, (z + d) % 4, y, c)
    f = lax.axis_index("fsdp")
    following, preceding = (x, (f + 1) % 16), (x, (f + 15) % 16)
    meet([core, xn, yn, diag, device(x, z, 1 - y, 1 - c), zdev(1), zdev(2), zdev(3), following, preceding])
    me = 2 * c + x
    cols = lambda h: pl.ds(pl.multiple_of(384 * h, 384), 384)
    root = jnp.logical_and(y == 1, c == 1)
    w1 = z % 2 == 0

    inner = jnp.logical_and(z > 0, z < 3)
    outer = jnp.logical_not(inner)

    def when(cond, what):
        if cond is None:
            what()
        else:
            pl.when(cond)(what)

    def go(sent, src, dst, send, recv, target, cond=None):
        make = lambda: remote(src, dst, send, recv, target)
        when(cond, lambda: make().start())
        sent.append((make, cond))

    def arrived(view, recv):
        remote(view, view, recv, recv, core).wait_recv()

    def drain(sent):
        for make, cond in sent:
            when(cond, lambda: make().wait_send())

    def shard_s(zz, yy, cc):
        return r.ws.at[zz, pl.ds(pl.multiple_of(192 * (2 * yy + cc), 192), 192)]

    def shard_c(zz, yy, cc):
        return r.wc.at[pl.ds(pl.multiple_of(272 * ((zz * 2 + yy) * 2 + cc), 16), 272)]

    def part_f(zz, yy, lo=0, n=384):
        return r.wf.at[zz, pl.ds(pl.multiple_of(384 * yy + lo, 16), n)]

    shards = (shard_s, shard_c)
    sent_w = ([], [], [])
    steps = [jnp.where(z == 0, 3 - i, jnp.where(z == 3, 1 + i, (2, 1, 3)[i])) for i in range(3)]

    def part(g, zz, yy, cc, h):
        if g >= 2:
            return part_f(zz, yy, 96 * (g - 2), 96)
        view = shards[g](zz, yy, cc)
        return view if h is None else view.at[:, cols(h)]

    def own_part(g):
        return part(g, z, y, c, x)

    def z_out(src, dst, g, i):
        for k in (2, 1, 3):
            cond = {1: z != 3, 2: None, 3: z != 0}[k]
            go(sent_w[min(g, 2)], src, dst, r.gz_s.at[i, k], r.gz_r.at[i, k], zdev(k), cond)

    def z_on(view, g, i, k):
        cond = jnp.logical_and(inner, k == 2)
        go(sent_w[min(g, 2)], view, view, r.gz_s.at[i, 0], r.gz_r.at[i, 2 * z - 1], device(x, 3 * (z - 1), y, c), cond)

    def own_z(g):
        z_out(own_part(g), part(g, z, y, c, x), g, g)

    def own_y(g):
        go(sent_w[min(g, 2)], own_part(g), part(g, z, y, c, x), r.gy_s.at[g, 0], r.gy_r.at[g, 0], yn)

    def own_core(g):
        own = part(g, z, y, c, None)
        go(sent_w[g], own, own, r.gc_s.at[g, 0], r.gc_r.at[g, 0], core)

    def gather_z(g, last=False):
        for k in steps:
            view = part(g, (z - k) % 4, y, c, x)
            arrived(view, r.gz_r.at[g, k])
            z_on(view, g, g, k)
            if not last:
                go(sent_w[min(g, 2)], view, view, r.gy_s.at[g, k], r.gy_r.at[g, k], yn)
            if g < 2:
                go(sent_w[g], view, view, r.gx_s.at[g, k - 1], r.gx_r.at[g, k - 1], xn)
                go(sent_w[g], view, view, r.gc_s.at[g, k], r.gc_r.at[g, k], core)

    def gather_y(g, which=(0, 1, 2, 3)):
        for j in which:
            view = part(g, (z - j) % 4, 1 - y, c, x)
            arrived(view, r.gy_r.at[g, j])
            if g < 2:
                go(sent_w[g], view, view, r.gx_s.at[g, 3 + j], r.gx_r.at[g, 3 + j], xn)
                go(sent_w[g], view, view, r.gc_s.at[g, 4 + j], r.gc_r.at[g, 4 + j], core)

    def other_z():
        view = part(5, z, 1 - y, c, x)
        arrived(view, r.gy_r.at[5, 0])
        z_out(view, view, 5, 6)

    def other_arrivals():
        for k in steps:
            view = part(5, (z - k) % 4, 1 - y, c, x)
            arrived(view, r.gz_r.at[6, k])
            z_on(view, 5, 6, k)

    def gather_x(g):
        for j in range(7):
            view = part(g, (z - j - 1) % 4, y, c, 1 - x) if j < 3 else part(g, (z - j + 3) % 4, 1 - y, c, 1 - x)
            arrived(view, r.gx_r.at[g, j])
            go(sent_w[g], view, view, r.gc_s.at[g, 8 + j], r.gc_r.at[g, 8 + j], core)

    def gather_core(g, which):
        for j in which:
            if j == 0:
                view = part(g, z, y, 1 - c, None)
            elif j < 4:
                view = part(g, (z - j) % 4, y, 1 - c, x)
            elif j < 8:
                view = part(g, (z - j + 4) % 4, 1 - y, 1 - c, x)
            elif j < 11:
                view = part(g, (z - j + 7) % 4, y, 1 - c, 1 - x)
            else:
                view = part(g, (z - j + 11) % 4, 1 - y, 1 - c, 1 - x)
            arrived(view, r.gc_r.at[g, j])

    tail = remote(r.tails, r.before, r.tail_s.at[0], r.tail_r.at[0], following)
    tail.start()
    back = shift_back()

    def one_hot(shape, pick):
        row = lax.broadcasted_iota(jnp.int32, shape, 0)
        col = lax.broadcasted_iota(jnp.int32, shape, 1)
        return jnp.where(col == pick(row), 1.0, 0.0).astype(BF)

    def to_rows(g):
        return one_hot((96, 128), lambda i: 32 - back[g] + 6 * (i % 16) + i // 16)

    def store_rows(dst, row, tiles, n=6):
        for j in range(n):
            dst[pl.ds(pl.multiple_of(row, 16), 16), 128 * j : 128 * j + 128] = tiles[16 * j : 16 * j + 16]

    def first_window(g, flat, n):
        return jnp.concatenate([r.before[32 * g : 32 * g + 32], flat[0:n]], 0)

    def lay_rows(g, flat, dst, n):
        perm = to_rows(g)

        def body(i, carry):
            window = flat[pl.ds(pl.multiple_of(96 * i - 32, 32), 128)]
            store_rows(dst, 16 * i, mm(perm, window).astype(BF))
            return carry

        lax.fori_loop(1, n, body, 0)
        return perm

    tail_v = one_hot(
        (96, 96),
        lambda i: jnp.where(
            i % 16 < 5,
            6 * (i % 16) + i // 16,
            jnp.where(
                i % 16 < 10,
                32 + 6 * (i % 16 - 5) + i // 16,
                jnp.where(z < 2, 72, 66)
                + jnp.where(
                    z % 2 == 0,
                    12 * (i // 48) + 3 * (i % 16 - 10) + (i // 16) % 3,
                    6 * (i % 16 - 10) + i // 16,
                ),
            ),
        ),
    )
    store_rows(r.own_t, 0, mm(tail_v, r.tails[...]).astype(BF))
    mine_s, mine_c = part(0, z, y, c, None), part(1, z, y, c, None)
    perm = lay_rows(0, r.flat_s, mine_s, 12)
    tail.wait_recv()
    store_rows(mine_s, 0, mm(perm, first_window(0, r.flat_s, 96)).astype(BF))
    own_z(0)
    own_y(0)
    own_core(0)

    @pl.when(root)
    def _():
        mine = pltpu.make_async_copy(r.own_t, r.tb.at[z], r.loc.at[0])
        mine.start()
        out = []
        for k in (1, 2, 3):
            go(out, r.own_t, r.tb.at[z], r.t_s.at[k - 1], r.t_r.at[k], zdev(k))
        mine.wait()
        for k in (1, 2, 3):
            arrived(r.tb.at[(z - k) % 4], r.t_r.at[k])
        for i, (yy, cc) in enumerate(((0, 0), (0, 1), (1, 0))):
            go(out, r.tb, r.tb, r.t_s.at[3 + i], r.t_r.at[0], device(x, z, yy, cc))
        drain(out)

    perm = lay_rows(1, r.flat_c, mine_c, 17)
    store_rows(mine_c, 0, mm(perm, first_window(1, r.flat_c, 96)).astype(BF))
    own_z(1)
    own_y(1)
    own_core(1)

    @pl.when(w1)
    def _():
        def pick(i):
            m, j = i % 16, i // 16
            q = 2 * jnp.where(j < 6, c, 1 - c) + x
            j = j % 6
            return 32 - back[2] + 24 * m + 12 * (j // 3) + 3 * q + j % 3

        perm = one_hot((192, 416), pick)
        mine = part_f(z, y, 192 * c, 192)

        def put(i, window):
            tiles = mm(perm, window).astype(BF)
            store_rows(r.theirs, 16 * i, tiles[96:192])
            store_rows(mine, 16 * i, tiles[0:96])

        def body(i, carry):
            put(i, r.flat_f[pl.ds(pl.multiple_of(384 * i - 32, 32), 416)])
            return carry

        put(0, first_window(2, r.flat_f, 384))
        lax.fori_loop(1, 12, body, 0)
        swap = remote(r.theirs, mine, r.gc_s.at[2, 0], r.gc_r.at[2, 0], core)
        swap.start()
        swap.wait()

    @pl.when(jnp.logical_not(w1))
    def _():
        perm = to_rows(2)
        mine = part_f(z, y)

        def body(i, carry):
            window = r.flat_f[pl.ds(pl.multiple_of(2304 * x + 96 * i - 32, 32), 128)]
            store_rows(mine, 16 * i, mm(perm, window).astype(BF))
            return carry

        lax.fori_loop(1, 24, body, 0)
        lead = jnp.where(x == 0, r.before[64:96], r.flat_f[2304 - 32 : 2304])
        rest = r.flat_f[pl.ds(pl.multiple_of(2304 * x, 32), 96)]
        store_rows(mine, 0, mm(perm, jnp.concatenate([lead, rest], 0)).astype(BF))

    tail.wait_send()
    r.vg[...] = jnp.zeros_like(r.vg)

    own_y(5)
    gather_z(0)
    own_z(2)
    for g in (2, 3, 4):
        own_y(g)
    gather_y(0)
    own_z(3)
    gather_z(1)
    own_z(4)
    own_z(5)
    other_z()
    gather_y(1, (0,))
    gather_x(0)
    @pl.when(jnp.logical_not(root))
    def _():
        arrived(r.tb, r.t_r.at[0])

    r.tv[...] = r.tb[...].astype(F32)
    gather_core(0, range(15))

    self_v = lambda j: r.tv[3, j : j + 1]
    cross_v = lambda j: r.tv[3, 5 + j : 6 + j]
    ffn_b1 = lambda b: r.tv[2 * b, pl.ds(10 + me, 1)]
    ffn_v = lambda b, j: r.tv[2 * b + 1, 10 + j : 11 + j]

    def slot(xx, cc):
        return 2 * cc + xx

    def ag_copy(ph, b, i):
        buf = r.xg.at[ph, b]
        pair = [(me, xn), (me, core), (slot(1 - x, c), core)]
        s, t = pair[i]
        return remote(buf.at[s], buf.at[s], r.ex_s.at[ph, b, i], r.ex_r.at[ph, b, i], t)

    def ag_start(ph, b):
        ag_copy(ph, b, 0).start()
        ag_copy(ph, b, 1).start()

    def ag_mid(ph, b):
        ag_copy(ph, b, 0).wait_recv()
        ag_copy(ph, b, 2).start()

    def ag_end(ph, b):
        ag_copy(ph, b, 1).wait_recv()
        ag_copy(ph, b, 2).wait_recv()
        for i in range(3):
            ag_copy(ph, b, i).wait_send()

    def rs_copy(ph, b, i):
        src = r.send_x.at[ph, b] if i == 2 else r.send_p.at[ph, b, i]
        dst = r.recv_x.at[ph, b] if i == 2 else r.recv_p.at[ph, b, i]
        return remote(src, dst, r.rs_s.at[ph, b, i], r.rs_r.at[ph, b, i], xn if i == 2 else core)

    def rs_start(ph, b):
        r.send_p[ph, b, 0] = r.part[b, slot(1 - x, 1 - c)].astype(BF)
        rs_copy(ph, b, 0).start()
        r.send_p[ph, b, 1] = r.part[b, slot(x, 1 - c)].astype(BF)
        rs_copy(ph, b, 1).start()

    def rs_mid(ph, b):
        rs_copy(ph, b, 0).wait_recv()
        r.send_x[ph, b] = (r.part[b, slot(1 - x, c)] + r.recv_p[ph, b, 0].astype(F32)).astype(BF)
        rs_copy(ph, b, 2).start()

    def rs_end(ph, b):
        rs_copy(ph, b, 1).wait_recv()
        rs_copy(ph, b, 2).wait_recv()
        for i in range(3):
            rs_copy(ph, b, i).wait_send()
        return r.part[b, me] + r.recv_p[ph, b, 1].astype(F32) + r.recv_x[ph, b].astype(F32)

    h = r.hid[...]
    r.q[...] = (mm(h, r.ws[0]) + self_v(0)).astype(BF)
    r.k[...] = mm(h, r.ws[1]).astype(BF)
    r.v[...] = (mm(h, r.ws[2]) + self_v(1)).astype(BF)
    for i in range(2):
        rows = slice(64 * i, 64 * i + 64)
        at = lax.broadcasted_iota(jnp.int32, (256, 64), 0) % 64
        key = lax.broadcasted_iota(jnp.int32, (256, 64), 1)
        caption = jnp.where(at >= NQ, 1.0, 0.0) * jnp.where(key <= at, 1.0, 0.0)
        ok = jnp.where(key < NQ, 1.0, caption * jnp.where(key < NQ + r.lens[i], 1.0, 0.0))
        for g in range(3):
            lanes = slice(256 * g, 256 * g + 256)
            p, a = attend_block(r.q[rows, lanes], r.k[rows, lanes], r.v[rows, lanes], ok)
            r.p[i, g] = p
            r.a[rows, lanes] = a
    r.sum1[...] = h.astype(F32) + (mm(r.a[...], r.ws[3]) + self_v(2))
    xh, _ = normed(r.sum1[...])
    r.first[...] = xh * self_v(3) + self_v(4)
    r.xg[0, 1, me] = rows_of(r.first, 32).astype(BF)
    ag_start(0, 1)
    gather_z(2)
    gather_y(1, (1, 2, 3))
    gather_z(3)

    for i in range(2):
        r.ck[272 * i + 256 : 272 * i + 272] = jnp.zeros((16, D), BF)
        r.cv[272 * i + 256 : 272 * i + 272] = jnp.zeros((16, D), BF)
    gather_core(1, range(8))
    for i in range(2):
        rows = slice(272 * i, 272 * i + 257)
        r.ck[rows, cols(x)] = mm(r.feat[i], r.wc[768:2176, cols(x)]).astype(BF)
        bias = r.tv[3, 6:7, cols(x)]
        r.cv[rows, cols(x)] = (mm(r.feat[i], r.wc[2176:3584, cols(x)]) + bias).astype(BF)
    ag_mid(0, 1)
    gather_z(4)
    gather_x(1)
    gather_core(1, range(8, 15))
    far_cols = cols(1 - x)
    for i in range(2):
        rows = slice(272 * i, 272 * i + 257)
        r.ck[rows, far_cols] = mm(r.feat[i], r.wc[768:2176, far_cols]).astype(BF)
        bias = r.tv[3, 6:7, far_cols]
        r.cv[rows, far_cols] = (mm(r.feat[i], r.wc[2176:3584, far_cols]) + bias).astype(BF)
    u = rows_of(r.first, 0)
    r.cq[...] = (mm(u.astype(BF), r.wc[0:768]) + cross_v(0)).astype(BF)
    ok = jnp.where(lax.broadcasted_iota(jnp.int32, (128, 272), 1) < 257, 1.0, 0.0)
    for i in range(2):
        rows = slice(272 * i, 272 * i + 272)
        mine = slice(32 * i, 32 * i + 32)
        for g in range(3):
            lanes = slice(256 * g, 256 * g + 256)
            p, a = attend_block(r.cq[mine, lanes], r.ck[rows, lanes], r.cv[rows, lanes], ok)
            r.pc[i, g] = p
            r.ca[mine, lanes] = a
        if i == 0:
            gather_z(5, last=True)
    r.sum2[...] = u + (mm(r.ca[...], r.wc[3584:4352]) + cross_v(2))
    xh, _ = normed(r.sum2[...])
    r.second[...] = xh * cross_v(3) + cross_v(4)
    r.xg[0, 0, me] = r.second[...].astype(BF)
    ag_start(0, 0)

    other_arrivals()
    for g in (2, 3, 4):
        gather_y(g)

    def ffn_forward_part(b):
        rows = r.xg[0, b].reshape(256, D)
        r.pre[b] = mm(rows, r.wf[2 * b]) + ffn_b1(b)
        r.act[b] = gelu(r.pre[b]).astype(BF)
        r.part[b] = mm(r.act[b], r.wf[2 * b + 1]).reshape(4, 64, D)

    def ffn_turn(b):
        rows = r.second[...] if b == 0 else rows_of(r.first, 32)
        s3 = rows + (rs_end(0, b) + ffn_v(b, 0))
        xh, _ = normed(s3)
        done = (xh * ffn_v(b, 1) + ffn_v(b, 2)).astype(BF)
        for i in range(2):
            r.mixed[64 * i + 32 * b : 64 * i + 32 * b + 32] = done[32 * i : 32 * i + 32]
        g_out = rows_of(r.cot, 32 * b).astype(F32)
        dsum, dgain, dshift = norm_back(s3, ffn_v(b, 1), g_out)
        r.dsum3[b] = dsum
        low = dsum.astype(BF)
        r.xg[1, b, me] = low
        r.vg[2 * b + 1, 10:11] = rows_sum(low)
        r.vg[2 * b + 1, 11:12] = dgain
        r.vg[2 * b + 1, 12:13] = dshift

    def ffn_backward_part(b):
        up = r.xg[1, b].reshape(256, D)
        r.dpre[b] = (mm_nt(up, r.wf[2 * b + 1]) * gelu_slope(r.pre[b])).astype(BF)
        r.part[b] = mm_nt(r.dpre[b], r.wf[2 * b]).reshape(4, 64, D)
        db1 = rows_sum(r.dpre[b])
        for j in range(4):
            r.vg[2 * b, 10 + j : 11 + j] = jnp.where(j == me, db1, 0.0)

    sent = []

    def ffn_weight_grads(b):
        rows = r.xg[0, b].reshape(256, D)
        up = r.xg[1, b].reshape(256, D)
        r.wf[2 * b] = mm_tn(rows, r.dpre[b]).astype(BF)
        r.wf[2 * b + 1] = mm_tn(r.act[b], up).astype(BF)
        for p in (2 * b, 2 * b + 1):
            go(sent, part_f(p, 1 - y, 0, SPLIT), r.yf.at[p], r.yy_s.at[2, p], r.yy_r.at[2, p], yn)
        for p in (2 * b, 2 * b + 1):
            for i, yy in ((4, 1 - y), (3, y)):
                z_out_sum(i, part_f(p, yy, SPLIT, REST), p)

    hop = jnp.where(z < 2, 1, 2)

    def z_out_sum(i, src, p):
        zb, zr = getattr(r, f"zb{i}"), getattr(r, f"zr{i}")
        d = (p - z) % 4
        far = {0: z == 3, 3: z == 0}.get(p)
        later = {0: z == 2, 3: z == 1}.get(p)
        direct = z != p
        if far is not None:
            go(sent, src, zr, r.zq_s.at[i], r.zq_r.at[i], device(x, hop, y, c), far)
            direct = jnp.logical_and(direct, jnp.logical_not(jnp.logical_or(far, later)))
        go(sent, src, zb.at[d - 1], r.zz_s.at[i, p], r.zz_r.at[i, d], device(x, p, y, c), direct)

    def z_add_sum(i, src, p):
        later = {0: z == 2, 3: z == 1}.get(p)
        if later is None:
            return
        zb, zr = getattr(r, f"zb{i}"), getattr(r, f"zr{i}")

        @pl.when(later)
        def _():
            arrived(zr, r.zq_r.at[i])
            zr[...] = add(zr[...], src[...])

        go(sent, zr, zb.at[1], r.zz_s.at[i, p], r.zz_r.at[i, 2], device(x, p, y, c), later)

    def z_total(i, own, out):
        zb = getattr(r, f"zb{i}")
        arrived(zb.at[1], r.zz_r.at[i, 2])
        out[...] = add(own, zb[1])
        for d, without in ((1, 0), (3, 3)):

            @pl.when(z != without)
            def _():
                arrived(zb.at[d - 1], r.zz_r.at[i, d])
                out[...] = add(out[...], zb[d - 1])

    def ffn_sum_y(p):
        arrived(r.yf.at[p], r.yy_r.at[2, p])
        r.yf[p] = add(r.yf[p], part_f(p, y, 0, SPLIT)[...])
        z_out_sum(2, r.yf.at[p], p)

    def ffn_add(p):
        for i, yy in ((4, 1 - y), (3, y)):
            z_add_sum(i, part_f(p, yy, SPLIT, REST), p)

    def ffn_sum_other():
        z_total(4, part_f(z, 1 - y, SPLIT, REST)[...], r.of)
        go(sent, r.of, r.yf2, r.yy_s.at[3, 0], r.yy_r.at[3, 0], yn)

    ag_end(0, 1)
    ffn_forward_part(1)
    rs_start(0, 1)
    ag_mid(0, 0)
    ag_end(0, 0)
    rs_mid(0, 1)
    ffn_forward_part(0)
    rs_start(0, 0)
    ffn_turn(1)
    ag_start(1, 1)
    rs_mid(0, 0)
    ag_mid(1, 1)
    ag_end(1, 1)
    ffn_backward_part(1)
    rs_start(1, 1)
    ffn_turn(0)
    ag_start(1, 0)
    rs_mid(1, 1)
    drain(sent_w[2])
    ffn_weight_grads(1)
    ag_mid(1, 0)
    ag_end(1, 0)
    ffn_backward_part(0)
    rs_start(1, 0)
    d_text = r.dsum3[1] + rs_end(1, 1)
    for i in range(2):
        r.dfirst[64 * i + 32 : 64 * i + 64] = d_text[32 * i : 32 * i + 32]
    rs_mid(1, 0)
    ffn_weight_grads(0)
    d_second = r.dsum3[0] + rs_end(1, 0)

    groups = (
        (shard_s, r.core_s, r.xs, r.ys, r.fin_s, r.nice_s),
        (shard_c, r.core_c, r.xc, r.yc, r.fin_c, r.nice_c),
    )
    order = (3, 1, 2, 0)

    def sum_start(g):
        view, cb = groups[g][:2]
        for far in range(2):
            for d in order:
                zz = (z + d) % 4
                go(sent, view(zz, y if far else 1 - y, 1 - c), cb.at[far, zz], r.co_s.at[g, far, d], r.co_r.at[g, far, d], core)

    def sum_core(g, fars=(0, 1)):
        view, cb, xb, yb = groups[g][:4]
        for far in fars:
            for d in order:
                zz = (z + d) % 4
                arrived(cb.at[far, zz], r.co_r.at[g, far, d])
                cb[far, zz] = add(cb[far, zz], view(zz, y if far else 1 - y, c)[...])
                if X_FIRST[g]:
                    go(sent, cb.at[far, zz, :, cols(1 - x)], xb.at[far, zz], r.xx_s.at[g, far, d], r.xx_r.at[g, far, d], xn)
                elif far == 0:
                    go(sent, cb.at[0, zz], yb.at[zz], r.yy_s.at[g, d], r.yy_r.at[g, d], yn)

    def sum_mid(g, fars=(0, 1)):
        view, cb, xb, yb = groups[g][:4]
        for far in fars if X_FIRST[g] else (0,):
            for d in order:
                zz = (z + d) % 4
                if X_FIRST[g]:
                    arrived(xb.at[far, zz], r.xx_r.at[g, far, d])
                    xb[far, zz] = add(xb[far, zz], cb[far, zz, :, cols(x)])
                    if far == 0:
                        go(sent, xb.at[0, zz], yb.at[zz], r.yy_s.at[g, d], r.yy_r.at[g, d], yn)
                else:
                    arrived(yb.at[zz], r.yy_r.at[g, d])
                    yb[zz] = add(yb[zz], cb[1, zz])
                    go(sent, yb.at[zz, :, cols(1 - x)], xb.at[zz], r.xx_s.at[g, 0, d], r.xx_r.at[g, 0, d], xn)

    def to_z(g, mine, d):
        zb, zr = getattr(r, f"zb{g}"), getattr(r, f"zr{g}")
        if d == 2:

            @pl.when(inner)
            def _():
                arrived(zr, r.zq_r.at[g])
                zr[...] = add(zr[...], mine[...])

            go(sent, zr, zb.at[1], r.zz_s.at[g, 2], r.zz_r.at[g, 2], zdev(2), inner)
            go(sent, mine, zb.at[1], r.zz_s.at[g, 2], r.zz_r.at[g, 2], zdev(2), outer)
        elif d:
            far = z == (0 if d == 3 else 3)
            go(sent, mine, zr, r.zq_s.at[g], r.zq_r.at[g], device(x, hop, y, c), far)
            go(sent, mine, zb.at[d - 1], r.zz_s.at[g, d], r.zz_r.at[g, d], zdev(d), jnp.logical_not(far))

    def sum_last(g):
        view, cb, xb, yb = groups[g][:4]
        for d in order:
            zz = (z + d) % 4
            if X_FIRST[g]:
                arrived(yb.at[zz], r.yy_r.at[g, d])
                yb[zz] = add(yb[zz], xb[1, zz])
                to_z(g, yb.at[zz], d)
            else:
                arrived(xb.at[zz], r.xx_r.at[g, 0, d])
                xb[zz] = add(xb[zz], yb[zz, :, cols(x)])
                to_z(g, xb.at[zz], d)

    def sum_z(g):
        view, cb, xb, yb, fin, out = groups[g]
        z_total(g, yb[z] if X_FIRST[g] else xb[z], fin)
        out[:, cols(x)] = fin[...]
        go(sent, fin, out.at[:, cols(x)], r.fi_s.at[g], r.fi_r.at[g], xn)

    def ffn_sum_z():
        z_total(2, r.yf[z], r.fin_f.at[0:SPLIT])
        last = r.fin_f.at[SPLIT:384]
        z_total(3, part_f(z, y, SPLIT, REST)[...], last)
        arrived(r.yf2, r.yy_r.at[3, 0])
        last[...] = add(last[...], r.yf2[...])
        half = lambda j: r.fin_f.at[pl.ds(pl.multiple_of(192 * j, 192), 192)]

        @pl.when(w1)
        def _():
            r.nice_f[me] = half(c)[...]
            remote(half(c), r.nice_f.at[me], r.fi_s.at[2], r.fi_r.at[2], xn).start()
            remote(half(1 - c), r.nice_f.at[me], r.fi_s.at[3], r.fi_r.at[3], core).start()
            remote(half(1 - c), r.nice_f.at[me], r.fi_s.at[4], r.fi_r.at[4], diag).start()

        @pl.when(jnp.logical_not(w1))
        def _():
            for j in range(2):
                r.nice_f[2 * x + j] = half(j)[...]
                remote(half(j), r.nice_f.at[2 * x + j], r.fi_s.at[2 + j], r.fi_r.at[2 + j], xn).start()

    def ffn_end():
        def ends(n):
            for j in range(n):
                remote(r.fin_f.at[0:192], r.nice_f.at[0], r.fi_s.at[2 + j], r.fi_r.at[2 + j], xn).wait()

        pl.when(w1)(lambda: ends(3))
        pl.when(jnp.logical_not(w1))(lambda: ends(2))

    du2, dgain, dshift = norm_back(r.sum2[...], cross_v(3), d_second)
    r.vg[3, 8:9] = dgain
    r.vg[3, 9:10] = dshift
    low = du2.astype(BF)
    r.vg[3, 7:8] = rows_sum(low)
    dca = mm_nt(low, r.wc[3584:4352]).astype(BF)
    drain(sent_w[1])
    r.wc[3584:4352] = mm_tn(r.ca[...], low).astype(BF)
    dcq = []
    for i in range(2):
        rows = slice(272 * i, 272 * i + 272)
        mine = slice(32 * i, 32 * i + 32)
        blocks = []
        for g in range(3):
            lanes = slice(256 * g, 256 * g + 256)
            dq, dk, dv = attend_block_back(
                r.cq[mine, lanes], r.ck[rows, lanes], r.cv[rows, lanes], r.pc[i, g], dca[mine, lanes]
            )
            blocks.append(dq)
            r.ck[rows, lanes] = dk
            r.cv[rows, lanes] = dv
        dcq.append(jnp.concatenate(blocks, 1))
    dcq = jnp.concatenate(dcq, 0)
    r.vg[3, 5:6] = rows_sum(dcq)
    r.vg[3, 6:7] = rows_sum(r.cv[...])
    du = du2 + mm_nt(dcq, r.wc[0:768])
    for i in range(2):
        r.dfirst[64 * i : 64 * i + 32] = du[32 * i : 32 * i + 32]
    r.wc[0:768] = mm_tn(rows_of(r.first, 0).astype(BF), dcq).astype(BF)
    for j in range(11):
        block = [r.feat[i, :, 128 * j : 128 * j + 128] for i in range(2)]
        both = lambda d: mm_tn(block[0], d[0:257]) + mm_tn(block[1], d[272:529])
        r.wc[768 + 128 * j : 896 + 128 * j] = both(r.ck).astype(BF)
        r.wc[2176 + 128 * j : 2304 + 128 * j] = both(r.cv).astype(BF)
    sum_start(1)
    ffn_add(3)
    ffn_sum_y(2)
    ffn_sum_y(3)

    dsum1, dgain, dshift = norm_back(r.sum1[...], self_v(3), r.dfirst[...])
    r.vg[3, 3:4] = dgain
    r.vg[3, 4:5] = dshift
    low = dsum1.astype(BF)
    r.vg[3, 2:3] = rows_sum(low)
    da = mm_nt(low, r.ws[3]).astype(BF)
    drain(sent_w[0])
    r.ws[3] = mm_tn(r.a[...], low).astype(BF)
    for i in range(2):
        rows = slice(64 * i, 64 * i + 64)
        for g in range(3):
            lanes = slice(256 * g, 256 * g + 256)
            dq, dk, dv = attend_block_back(
                r.q[rows, lanes], r.k[rows, lanes], r.v[rows, lanes], r.p[i, g], da[rows, lanes]
            )
            r.q[rows, lanes] = dq
            r.k[rows, lanes] = dk
            r.v[rows, lanes] = dv
    sum_core(1, (0,))
    r.vg[3, 0:1] = rows_sum(r.q[...])
    r.vg[3, 1:2] = rows_sum(r.v[...])
    total = dsum1 + mm_nt(r.q[...], r.ws[0]) + mm_nt(r.k[...], r.ws[1]) + mm_nt(r.v[...], r.ws[2])
    r.hgrad[...] = total.astype(BF)
    r.ws[0] = mm_tn(r.hid[...], r.q[...]).astype(BF)
    r.ws[1] = mm_tn(r.hid[...], r.k[...]).astype(BF)
    r.ws[2] = mm_tn(r.hid[...], r.v[...]).astype(BF)
    sum_start(0)
    sum_core(1, (1,))
    sum_core(0)

    r.v_send[...] = r.vg[...].astype(BF)
    index = 2 * y + c
    home = device(x, z, 1, 1)

    @pl.when(jnp.logical_not(root))
    def _():
        remote(r.v_send, r.v_in.at[index], r.vv_s.at[0], r.vv_r.at[index], home).start()

    ffn_add(0)
    ffn_sum_y(0)
    ffn_sum_y(1)
    z_add_sum(2, r.yf.at[0], 0)
    z_add_sum(2, r.yf.at[3], 3)
    sum_mid(1, (0,))

    @pl.when(root)
    def _():
        total = r.vg[...]
        for i in range(3):
            arrived(r.v_in.at[i], r.vv_r.at[i])
            total = total + r.v_in[i].astype(F32)
        r.v_z[...] = total.astype(BF)
        for k in (1, 2, 3):
            zz = (z + k) % 4
            remote(r.v_z.at[zz], r.v_zin.at[k - 1], r.vv_s.at[k], r.vv_r.at[2 + k], device(x, zz, y, c)).start()

    sum_mid(0)
    sum_mid(1, (1,))
    ffn_sum_other()
    sum_last(1)

    @pl.when(root)
    def _():
        total = r.v_z[z].astype(F32)
        for k in (1, 2, 3):
            arrived(r.v_zin.at[k - 1], r.vv_r.at[2 + k])
            total = total + r.v_zin[k - 1].astype(F32)
        r.v_x[...] = total.astype(BF)
        remote(r.v_x, r.v_xin, r.vv_s.at[4], r.vv_r.at[6], xn).start()

    ffn_sum_z()
    sum_last(0)
    sum_z(1)
    sum_z(0)

    @pl.when(root)
    def _():
        arrived(r.v_xin, r.vv_r.at[6])
        r.total_v[...] = add(r.v_x[...], r.v_xin[...])
        for k in (1, 2, 3):
            zz = (z + k) % 4
            remote(r.v_z.at[zz], r.v_zin.at[k - 1], r.vv_s.at[k], r.vv_r.at[2 + k], device(x, zz, y, c)).wait_send()
        remote(r.v_x, r.v_xin, r.vv_s.at[4], r.vv_r.at[6], xn).wait_send()

    @pl.when(jnp.logical_not(root))
    def _():
        r.total_v[...] = jnp.zeros_like(r.total_v)
        remote(r.v_send, r.v_in.at[index], r.vv_s.at[0], r.vv_r.at[index], home).wait_send()

    ffn_end()

    def stack(src, row, n=6):
        return jnp.concatenate(
            [src[pl.ds(pl.multiple_of(row, 16), 16), 128 * j : 128 * j + 128] for j in range(n)], 0
        )

    to_flat = one_hot((96, 96), lambda i: 16 * (i % 6) + i // 6)

    def lay_flat(src, dst, n, base=0):
        def body(i, carry):
            dst[pl.ds(pl.multiple_of(base + 96 * i, 32), 96)] = mm(to_flat, stack(src, 16 * i)).astype(BF)
            return carry

        lax.fori_loop(0, n, body, 0)

    def head_out(g, fl):
        r.heads[g] = fl[0:32]
        go(sent, r.heads.at[g], r.after.at[g], r.head_s.at[g], r.head_r.at[g], preceding)

    @pl.when(w1)
    def _():
        def pick(i):
            m, t = i // 24, i % 24
            return 96 * ((t % 12) // 3) + 16 * (3 * (t // 12) + t % 3) + m

        perm = one_hot((384, 384), pick)

        def body(i, carry):
            tiles = jnp.concatenate([stack(r.nice_f.at[q], 16 * i) for q in range(4)], 0)
            r.out_f[pl.ds(pl.multiple_of(384 * i, 128), 384)] = mm(perm, tiles).astype(BF)
            return carry

        lax.fori_loop(0, 12, body, 0)

    @pl.when(jnp.logical_not(w1))
    def _():
        for q in range(4):
            lay_flat(r.nice_f.at[q], r.out_f, 12, 1152 * q)

    head_out(2, r.out_f)
    arrived(groups[1][5].at[:, cols(1 - x)], r.fi_r.at[1])
    lay_flat(r.nice_c, r.out_c, 17)
    head_out(1, r.out_c)
    arrived(groups[0][5].at[:, cols(1 - x)], r.fi_r.at[0])
    lay_flat(r.nice_s, r.out_s, 12)
    head_out(0, r.out_s)

    vectors = stack(r.total_v, 0)
    end = (f == 15, f == 15, f % 4 == 3)
    plain = lambda first: lambda i: 16 * (i % 6) + first + i // 6
    hidden = lambda i: 16 * (3 * (i // 12) + i % 3) + 10 + (i % 12) // 3
    none = -1
    count = jnp.where(w1, 24, 18)

    def from_vectors(g):
        if g < 2:
            return lambda i: jnp.where(jnp.logical_and(end[g], i < 30), plain(5 * g)(i), none)
        pick = lambda i: jnp.where(w1, hidden(i), plain(10)(i))
        return lambda i: jnp.where(jnp.logical_and(end[2], i < count), pick(i), none)

    def from_next(g):
        if g < 2:
            return lambda i: jnp.where(end[g], none, i)
        inside = jnp.logical_or(z == 1, z == 2)
        return lambda i: jnp.where(
            end[2], jnp.where(jnp.logical_and(inside, i >= count), i - count, none), i
        )

    for g, (fl, rows) in enumerate(((r.out_s, 1152), (r.out_c, 1632), (r.out_f, 4608))):
        arrived(r.after.at[g], r.head_r.at[g])
        tail = mm(one_hot((32, 96), from_vectors(g)), vectors) + mm(one_hot((32, 32), from_next(g)), r.after[g])
        fl[rows : rows + 32] = tail.astype(BF)

    drain(sent)


def layer(flat_s, flat_c, flat_f, tails, lens, hid, feat, cot):
    vm = pl.BlockSpec(memory_space=pltpu.VMEM)
    return pl.pallas_call(
        layer_kernel,
        out_shape=(
            jax.ShapeDtypeStruct((128, D), BF),
            jax.ShapeDtypeStruct((128, D), BF),
            *[jax.ShapeDtypeStruct((n, 128), BF) for n in (1184, 1664, 4640)],
        ),
        in_specs=[vm] * 4 + [pl.BlockSpec(memory_space=pltpu.SMEM)] + [vm] * 3,
        out_specs=[vm] * 5,
        scratch_shapes=list(scratch().values()),
        compiler_params=pltpu.CompilerParams(
            collective_id=0, has_side_effects=True, vmem_limit_bytes=VMEM_BYTES
        ),
    )(flat_s, flat_c, flat_f, tails, lens, hid, feat, cot)


def per_device_fast(hidden, lengths, features, cotangent, self_params, cross_params, ffn_params):
    flats = [v.reshape(-1, 128) for v in (self_params, cross_params, ffn_params)]
    tails = jnp.concatenate([v[-32:] for v in flats])
    mixed, hgrad, *grads = layer(
        *flats, tails, lengths, hidden.reshape(128, D), features, cotangent.reshape(128, D)
    )
    outs = [
        lax.dynamic_slice_in_dim(rows, back, flat.shape[0]).astype(F32).reshape(-1)
        for rows, back, flat in zip(grads, shift_back(), flats)
    ]
    return (mixed.reshape(2, 64, D), hgrad.reshape(2, 64, D), *outs)


def solution(mesh):
    fast = mesh.shape["dp"] == 2 and mesh.shape["fsdp"] == 16
    return jax.shard_map(
        per_device_fast if fast else per_device,
        mesh=mesh,
        in_specs=(
            P(("dp", "fsdp"), None, None),
            P(("dp", "fsdp")),
            P(("dp", "fsdp"), None, None),
            P(("dp", "fsdp"), None, None),
            P("fsdp"),
            P("fsdp"),
            P("fsdp"),
        ),
        out_specs=(
            P(("dp", "fsdp"), None, None),
            P(("dp", "fsdp"), None, None),
            P("fsdp"),
            P("fsdp"),
            P("fsdp"),
        ),
        check_vma=False,
    )
```

```python
from functools import partial
import math
from types import SimpleNamespace

import jax
import jax.numpy as jnp
from jax import lax
from jax.experimental import pallas as pl
from jax.experimental.pallas import tpu as pltpu
from jax.sharding import PartitionSpec as P

D = 768
HEADS = 12
HDIM = 64
F = 3072
E = 1408
NQ = 32


EPS = 1e-06
SCALE = 0.125


def self_layout():
    return [(D, D)] * 4 + [(D,)] * 5


def cross_layout():
    return [(D, D), (E, D), (E, D), (D, D)] + [(D,)] * 5


def ffn_layout():
    return [(D, F), (F,), (F, D), (D,), (D,), (D,)] * 2


def split_flat(flat_vec, layouts):
    pieces = []
    offset = 0
    for layout in layouts:
        amount = math.prod(layout)
        pieces.append(flat_vec[offset : offset + amount].reshape(layout))
        offset = offset + amount
    return pieces


def join_flat(pieces, length):
    flat_vec = jnp.concatenate([piece.reshape(-1) for piece in pieces])
    return jnp.pad(flat_vec, (0, length - flat_vec.shape[0]))


def regroup(flat_vec):
    groups = lax.axis_size("fsdp")
    replicas = lax.axis_size("dp")
    return flat_vec.reshape(groups, replicas, -1).transpose(1, 0, 2).reshape(-1)


def matmul(left, right):
    return jnp.dot(left, right, preferred_element_type=jnp.float32)


def matmul_left(left, right):
    return lax.dot_general(
        left, right, (((0,), (0,)), ((), ())), preferred_element_type=jnp.float32
    )


def matmul_right(left, right):
    return lax.dot_general(
        left, right, (((1,), (1,)), ((), ())), preferred_element_type=jnp.float32
    )


def column_sum(values):
    return jnp.sum(values.astype(jnp.float32), 0)


def layer_norm(values, gain, shift):
    average = jnp.mean(values, -1, keepdims=True)
    centered = values - average
    variance = jnp.mean(centered * centered, -1, keepdims=True)
    return centered * lax.rsqrt(variance + EPS) * gain + shift


def norm_backward(summed, gain, shift, grad_out):
    _, norm_pull = jax.vjp(layer_norm, summed, gain.astype(jnp.float32), shift.astype(jnp.float32))
    return norm_pull(grad_out)


def heads(rows, items):
    return rows.reshape(items, -1, HEADS, HDIM)


def score_block(query, keys, mask):
    scores = jnp.einsum("iqhd,ikhd->ihqk", query, keys, preferred_element_type=jnp.float32) * SCALE
    if mask is not None:
        scores = jnp.where(mask, scores, -1e30)
    return scores


def attend(query, keys, values, mask):
    scores = score_block(query, keys, mask)
    top_sum = jax.nn.logsumexp(scores, axis=-1)
    probs = jnp.exp(scores - top_sum[..., None]).astype(jnp.bfloat16)
    context = jnp.einsum("ihqk,ikhd->iqhd", probs, values, preferred_element_type=jnp.float32)
    return (context, top_sum)


def attend_back(query, keys, values, mask, top_sum, grad_context):
    probs = jnp.exp(score_block(query, keys, mask) - top_sum[..., None])
    grad_probs = jnp.einsum(
        "iqhd,ikhd->ihqk", grad_context, values, preferred_element_type=jnp.float32
    )
    inner = jnp.sum(probs * grad_probs, -1, keepdims=True)
    grad_scores = (probs * (grad_probs - inner)).astype(jnp.bfloat16)
    grad_query = (
        jnp.einsum("ihqk,ikhd->iqhd", grad_scores, keys, preferred_element_type=jnp.float32) * SCALE
    )
    grad_keys = (
        jnp.einsum("ihqk,iqhd->ikhd", grad_scores, query, preferred_element_type=jnp.float32)
        * SCALE
    )
    grad_values = jnp.einsum(
        "ihqk,iqhd->ikhd",
        probs.astype(jnp.bfloat16),
        grad_context,
        preferred_element_type=jnp.float32,
    )
    return (grad_query, grad_keys, grad_values)


def linear_back(inputs, weight, grad_out):
    return (matmul_left(inputs, grad_out), column_sum(grad_out), matmul_right(grad_out, weight))


def ffn_forward(rows, params):
    w_in, b_in, w_out, b_out, gain, shift = params
    rows_low = rows.astype(jnp.bfloat16)
    hidden_pre = matmul(rows_low, w_in) + b_in
    activated = jax.nn.gelu(hidden_pre, approximate=True).astype(jnp.bfloat16)
    summed = rows + (matmul(activated, w_out) + b_out)
    final = layer_norm(summed, gain.astype(jnp.float32), shift.astype(jnp.float32))
    return (final, (rows_low, hidden_pre, activated, summed))


def ffn_backward(grad_out, kept, params):
    w_in, b_in, w_out, b_out, gain, shift = params
    rows_low, hidden_pre, activated, summed = kept
    grad_sum, grad_gain, grad_shift = norm_backward(summed, gain, shift, grad_out)
    grad_branch = grad_sum.astype(jnp.bfloat16)
    grad_w_out, grad_b_out, grad_act = linear_back(activated, w_out, grad_branch)
    _, gelu_pull = jax.vjp(partial(jax.nn.gelu, approximate=True), hidden_pre)
    grad_pre = gelu_pull(grad_act)[0].astype(jnp.bfloat16)
    grad_w_in, grad_b_in, grad_rows = linear_back(rows_low, w_in, grad_pre)
    return (
        grad_sum + grad_rows,
        [grad_w_in, grad_b_in, grad_w_out, grad_b_out, grad_gain, grad_shift],
    )


def per_device(hidden, lengths, features, cotangent, self_params, cross_params, ffn_params):
    items, seq, width = hidden.shape
    self_full = lax.all_gather(self_params, "fsdp", axis=0, tiled=True)
    self_parts = split_flat(self_full, self_layout())
    w_q, w_k, w_v, w_o, b_q, b_v, b_o, gain_one, shift_one = self_parts
    positions = jnp.arange(seq)
    rows_at = positions[:, None]
    cols_at = positions[None, :]
    allowed = (cols_at < NQ)[None] | ((rows_at >= NQ) & (cols_at <= rows_at))[None] & (
        cols_at[None] < NQ + lengths[:, None, None]
    )
    allowed = allowed[:, None]
    inputs = hidden.reshape(-1, width)
    query_low = (matmul(inputs, w_q) + b_q).astype(jnp.bfloat16)
    key_low = matmul(inputs, w_k).astype(jnp.bfloat16)
    value_low = (matmul(inputs, w_v) + b_v).astype(jnp.bfloat16)
    context, self_top = attend(
        heads(query_low, items), heads(key_low, items), heads(value_low, items), allowed
    )
    context_low = context.reshape(-1, width).astype(jnp.bfloat16)
    summed_one = inputs.astype(jnp.float32) + (matmul(context_low, w_o) + b_o)
    first = layer_norm(summed_one, gain_one.astype(jnp.float32), shift_one.astype(jnp.float32))
    first_items = first.reshape(items, seq, width)
    query_rows = first_items[:, :NQ].reshape(-1, width)
    text_rows = first_items[:, NQ:].reshape(-1, width)
    cross_full = lax.all_gather(cross_params, "fsdp", axis=0, tiled=True)
    cross_parts = split_flat(cross_full, cross_layout())
    cross_wq, cross_wk, cross_wv, cross_wo, cross_bq, cross_bv, cross_bo, gain_two, shift_two = (
        cross_parts
    )
    query_in = query_rows.astype(jnp.bfloat16)
    image_rows = features.reshape(-1, features.shape[-1])
    cross_query = (matmul(query_in, cross_wq) + cross_bq).astype(jnp.bfloat16)
    cross_key = matmul(image_rows, cross_wk).astype(jnp.bfloat16)
    cross_value = (matmul(image_rows, cross_wv) + cross_bv).astype(jnp.bfloat16)
    cross_context, cross_top = attend(
        heads(cross_query, items), heads(cross_key, items), heads(cross_value, items), None
    )
    cross_low = cross_context.reshape(-1, width).astype(jnp.bfloat16)
    summed_two = query_rows + (matmul(cross_low, cross_wo) + cross_bo)
    second = layer_norm(summed_two, gain_two.astype(jnp.float32), shift_two.astype(jnp.float32))
    ffn_full = lax.all_gather(ffn_params, "fsdp", axis=0, tiled=True)
    ffn_parts = split_flat(ffn_full, ffn_layout())
    query_final, query_kept = ffn_forward(second, ffn_parts[:6])
    text_final, text_kept = ffn_forward(text_rows, ffn_parts[6:])
    mixed = jnp.concatenate(
        [query_final.reshape(items, NQ, width), text_final.reshape(items, -1, width)], 1
    ).astype(jnp.bfloat16)
    grad_items = cotangent.astype(jnp.float32)
    grad_query_final = grad_items[:, :NQ].reshape(-1, width)
    grad_text_final = grad_items[:, NQ:].reshape(-1, width)
    ffn_back = split_flat(lax.all_gather(ffn_params, "fsdp", axis=0, tiled=True), ffn_layout())
    grad_second, query_grads = ffn_backward(grad_query_final, query_kept, ffn_back[:6])
    grad_text, text_grads = ffn_backward(grad_text_final, text_kept, ffn_back[6:])
    ffn_flat_grad = join_flat(query_grads + text_grads, ffn_full.shape[0])
    ffn_grad = lax.psum_scatter(
        regroup(ffn_flat_grad), ("dp", "fsdp"), scatter_dimension=0, tiled=True
    )
    cross_back = split_flat(
        lax.all_gather(cross_params, "fsdp", axis=0, tiled=True), cross_layout()
    )
    grad_summed_two, grad_gain_two, grad_shift_two = norm_backward(
        summed_two, cross_back[7], cross_back[8], grad_second
    )
    grad_cross_out = grad_summed_two.astype(jnp.bfloat16)
    grad_cross_wo, grad_cross_bo, grad_cross_ctx = linear_back(
        cross_low, cross_back[3], grad_cross_out
    )
    grad_cq, grad_ck, grad_cv = attend_back(
        heads(cross_query, items),
        heads(cross_key, items),
        heads(cross_value, items),
        None,
        cross_top,
        heads(grad_cross_ctx.astype(jnp.bfloat16), items),
    )
    grad_cq = grad_cq.reshape(-1, width).astype(jnp.bfloat16)
    grad_ck = grad_ck.reshape(-1, width).astype(jnp.bfloat16)
    grad_cv = grad_cv.reshape(-1, width).astype(jnp.bfloat16)
    grad_cross_wq, grad_cross_bq, grad_query_in = linear_back(query_in, cross_back[0], grad_cq)
    grad_cross_wk = matmul_left(image_rows, grad_ck)
    grad_cross_wv = matmul_left(image_rows, grad_cv)
    grad_cross_bv = column_sum(grad_cv)
    grad_query_rows = grad_summed_two + grad_query_in
    cross_list = [
        grad_cross_wq,
        grad_cross_wk,
        grad_cross_wv,
        grad_cross_wo,
        grad_cross_bq,
        grad_cross_bv,
        grad_cross_bo,
        grad_gain_two,
        grad_shift_two,
    ]
    cross_flat_grad = join_flat(cross_list, cross_full.shape[0])
    cross_grad = lax.psum_scatter(
        regroup(cross_flat_grad), ("dp", "fsdp"), scatter_dimension=0, tiled=True
    )
    self_back = split_flat(lax.all_gather(self_params, "fsdp", axis=0, tiled=True), self_layout())
    grad_first = jnp.concatenate(
        [grad_query_rows.reshape(items, NQ, width), grad_text.reshape(items, -1, width)], 1
    ).reshape(-1, width)
    grad_summed_one, grad_gain_one, grad_shift_one = norm_backward(
        summed_one, self_back[7], self_back[8], grad_first
    )
    grad_attn = grad_summed_one.astype(jnp.bfloat16)
    grad_w_o, grad_b_o, grad_ctx = linear_back(context_low, self_back[3], grad_attn)
    grad_q, grad_k, grad_v = attend_back(
        heads(query_low, items),
        heads(key_low, items),
        heads(value_low, items),
        allowed,
        self_top,
        heads(grad_ctx.astype(jnp.bfloat16), items),
    )
    grad_q = grad_q.reshape(-1, width).astype(jnp.bfloat16)
    grad_k = grad_k.reshape(-1, width).astype(jnp.bfloat16)
    grad_v = grad_v.reshape(-1, width).astype(jnp.bfloat16)
    grad_w_q, grad_b_q, input_from_q = linear_back(inputs, self_back[0], grad_q)
    grad_w_k = matmul_left(inputs, grad_k)
    input_from_k = matmul_right(grad_k, self_back[1])
    grad_w_v, grad_b_v, input_from_v = linear_back(inputs, self_back[2], grad_v)
    hidden_grad = (
        (grad_summed_one + input_from_q + input_from_k + input_from_v)
        .reshape(items, seq, width)
        .astype(jnp.bfloat16)
    )
    self_list = [
        grad_w_q,
        grad_w_k,
        grad_w_v,
        grad_w_o,
        grad_b_q,
        grad_b_v,
        grad_b_o,
        grad_gain_one,
        grad_shift_one,
    ]
    self_flat_grad = join_flat(self_list, self_full.shape[0])
    self_grad = lax.psum_scatter(
        regroup(self_flat_grad), ("dp", "fsdp"), scatter_dimension=0, tiled=True
    )
    self_grad, cross_grad, ffn_grad = (
        lax.all_gather(self_grad.astype(jnp.bfloat16), "dp", axis=0, tiled=True).astype(
            self_grad.dtype
        ),
        lax.all_gather(cross_grad.astype(jnp.bfloat16), "dp", axis=0, tiled=True).astype(
            cross_grad.dtype
        ),
        lax.all_gather(ffn_grad.astype(jnp.bfloat16), "dp", axis=0, tiled=True).astype(
            ffn_grad.dtype
        ),
    )
    return (mixed, hidden_grad, self_grad, cross_grad, ffn_grad)


MESH = pl.DeviceIdType.MESH
BF = jnp.bfloat16
F32 = jnp.float32
VMEM_BYTES = 62 * 2**20


def place():
    f = lax.axis_index("fsdp")
    return lax.axis_index("dp"), f // 4, (f // 2) % 2, f % 2


def device(x, z, y, c):
    return (x, (z * 2 + y) * 2 + c)


def shift_back():
    f = lax.axis_index("fsdp")
    return 2 * f, 2 * f, 6 * (f % 4) + jnp.where(f >= 8, 6, 0)


def meet(devices):
    barrier = pltpu.get_barrier_semaphore()
    for d in devices:
        pl.semaphore_signal(barrier, inc=1, device_id=d, device_id_type=MESH)
    pl.semaphore_wait(barrier, len(devices))


def remote(src, dst, send, recv, target):
    return pltpu.make_async_remote_copy(
        src_ref=src,
        dst_ref=dst,
        send_sem=send,
        recv_sem=recv,
        device_id=target,
        device_id_type=MESH,
    )


def mm(a, b):
    return jnp.dot(a, b, preferred_element_type=F32)


def mm_nt(a, b):
    return lax.dot_general(a, b, (((1,), (1,)), ((), ())), preferred_element_type=F32)


def mm_tn(a, b):
    return lax.dot_general(a, b, (((0,), (0,)), ((), ())), preferred_element_type=F32)


def rows_sum(v):
    return jnp.sum(v.astype(F32), 0, keepdims=True)


def add(a, b):
    return (a.astype(F32) + b.astype(F32)).astype(BF)


def normed(v):
    centered = v - jnp.mean(v, -1, keepdims=True)
    r = lax.rsqrt(jnp.mean(centered * centered, -1, keepdims=True) + EPS)
    return centered * r, r


def norm_back(v, gain, g_out):
    xh, r = normed(v)
    gg = g_out * gain
    dv = r * (gg - jnp.mean(gg, -1, keepdims=True) - xh * jnp.mean(gg * xh, -1, keepdims=True))
    return dv, rows_sum(g_out * xh), rows_sum(g_out)


GELU_A = math.sqrt(2.0 / math.pi)
GELU_B = 0.044715


def gelu(v):
    return 0.5 * v * (1.0 + jnp.tanh(GELU_A * (v + GELU_B * (v * v * v))))


def gelu_slope(v):
    t = jnp.tanh(GELU_A * (v + GELU_B * (v * v * v)))
    return 0.5 * (1.0 + t) + 0.5 * v * (1.0 - t * t) * (GELU_A * (1.0 + 3.0 * GELU_B * (v * v)))


def head_mask(h):
    lane = lax.broadcasted_iota(jnp.int32, (1, 256), 1)
    return jnp.where(lane // HDIM == h, 1.0, 0.0)


def spread(rows):
    wide = rows.astype(F32)
    return jnp.concatenate([(wide * head_mask(h)).astype(BF) for h in range(4)], 0)


def fold(stacked):
    n = stacked.shape[0] // 4
    total = stacked[:n] * head_mask(0)
    for h in range(1, 4):
        total = total + stacked[h * n : (h + 1) * n] * head_mask(h)
    return total


def attend_block(q, k, v, allowed):
    s = mm_nt(spread(q), k) * SCALE
    s = jnp.where(allowed > 0.5, s, -1e30)
    e = jnp.exp(s - jnp.max(s, -1, keepdims=True))
    p = e / jnp.sum(e, -1, keepdims=True)
    return p, fold(mm(p.astype(BF), v)).astype(BF)


def attend_block_back(q, k, v, p, da):
    dax = spread(da)
    dp = mm_nt(dax, v)
    ds = (p * (dp - jnp.sum(p * dp, -1, keepdims=True))).astype(BF)
    dq = (fold(mm(ds, k)) * SCALE).astype(BF)
    dk = (mm_tn(ds, spread(q)) * SCALE).astype(BF)
    dv = mm_tn(p.astype(BF), dax).astype(BF)
    return dq, dk, dv


def rows_of(ref, first):
    return jnp.concatenate([ref[first : first + 32], ref[64 + first : 96 + first]], 0)


SPLIT = 240
REST = 384 - SPLIT
X_FIRST = (False, True)
SIDE = tuple((2, 4) if first else (4,) for first in X_FIRST)
WIDTH = tuple(384 if first else 768 for first in X_FIRST)
STREAMS = ((192, 384), (272, 384), (SPLIT, D), (REST, D), (REST, D))


def scratch():
    dma = lambda *s: pltpu.SemaphoreType.DMA(s)
    b = lambda *s: pltpu.VMEM(s, BF)
    f = lambda *s: pltpu.VMEM(s, F32)
    return dict(
        ws=b(4, D, D), wc=b(4352, D), wf=b(4, D, D), theirs=b(192, D), own_t=b(16, D), tb=b(4, 16, D), before=b(96, 128),
        tv=f(4, 16, D), vg=f(4, 16, D),
        q=b(128, D), k=b(128, D), v=b(128, D), a=b(128, D), p=f(2, 3, 256, 64),
        sum1=f(128, D), first=f(128, D), cq=b(64, D), ck=b(544, D), cv=b(544, D), ca=b(64, D),
        pc=f(2, 3, 128, 272), sum2=f(64, D), second=f(64, D),
        xg=b(2, 2, 4, 64, D), pre=f(2, 256, D), act=b(2, 256, D), part=f(2, 4, 64, D),
        send_p=b(2, 2, 2, 64, D), recv_p=b(2, 2, 2, 64, D), send_x=b(2, 2, 64, D), recv_x=b(2, 2, 64, D),
        sum3=f(2, 64, D), dpre=b(2, 256, D), dsum3=f(2, 64, D), dfirst=f(128, D),
        core_s=b(2, 4, 192, D), core_c=b(2, 4, 272, D), xs=b(*SIDE[0], 192, 384), xc=b(*SIDE[1], 272, 384),
        ys=b(4, 192, WIDTH[0]), yc=b(4, 272, WIDTH[1]), yf=b(4, SPLIT, D), yf2=b(REST, D), of=b(REST, D),
        fin_s=b(192, 384), fin_c=b(272, 384), fin_f=b(384, D),
        **{f"{n}{i}": b(*lead, *shape) for i, shape in enumerate(STREAMS) for n, lead in (("zb", (3,)), ("zr", ()))},
        v_send=b(4, 16, D), v_in=b(3, 4, 16, D), v_z=b(4, 16, D), v_zin=b(3, 16, D), v_x=b(16, D), v_xin=b(16, D),
        nice_s=b(192, D), nice_c=b(272, D), nice_f=b(4, 192, D), total_v=b(16, D), heads=b(3, 32, 128), after=b(3, 32, 128),
        loc=dma(1), tail_s=dma(1), tail_r=dma(1), head_s=dma(3), head_r=dma(3), gz_s=dma(7, 4), gz_r=dma(7, 4), gy_s=dma(7, 4), gy_r=dma(7, 4), gx_s=dma(2, 7), gx_r=dma(2, 7),
        gc_s=dma(3, 15), gc_r=dma(3, 15), t_s=dma(6), t_r=dma(4),
        ex_s=dma(2, 2, 3), ex_r=dma(2, 2, 3), rs_s=dma(2, 2, 3), rs_r=dma(2, 2, 3),
        co_s=dma(2, 2, 4), co_r=dma(2, 2, 4), xx_s=dma(2, 2, 4), xx_r=dma(2, 2, 4), yy_s=dma(4, 4), yy_r=dma(4, 4),
        zz_s=dma(5, 4), zz_r=dma(5, 4), zq_s=dma(5), zq_r=dma(5), fi_s=dma(5), fi_r=dma(5), vv_s=dma(5), vv_r=dma(7),
    )


def layer_kernel(*refs):
    names = [
        "flat_s", "flat_c", "flat_f", "tails", "lens", "hid", "feat", "cot",
        "mixed", "hgrad", "out_s", "out_c", "out_f",
    ] + list(scratch())
    r = SimpleNamespace(**dict(zip(names, refs)))
    x, z, y, c = place()
    core, xn, yn = device(x, z, y, 1 - c), device(1 - x, z, y, c), device(x, z, 1 - y, c)
    diag = device(1 - x, z, y, 1 - c)
    zdev = lambda d: device(x, (z + d) % 4, y, c)
    f = lax.axis_index("fsdp")
    following, preceding = (x, (f + 1) % 16), (x, (f + 15) % 16)
    meet([core, xn, yn, diag, device(x, z, 1 - y, 1 - c), zdev(1), zdev(2), zdev(3), following, preceding])
    me = 2 * c + x
    cols = lambda h: pl.ds(pl.multiple_of(384 * h, 384), 384)
    root = jnp.logical_and(y == 1, c == 1)
    w1 = z % 2 == 0

    inner = jnp.logical_and(z > 0, z < 3)
    outer = jnp.logical_not(inner)

    def when(cond, what):
        if cond is None:
            what()
        else:
            pl.when(cond)(what)

    def go(sent, src, dst, send, recv, target, cond=None):
        make = lambda: remote(src, dst, send, recv, target)
        when(cond, lambda: make().start())
        sent.append((make, cond))

    def arrived(view, recv):
        remote(view, view, recv, recv, core).wait_recv()

    def drain(sent):
        for make, cond in sent:
            when(cond, lambda: make().wait_send())

    def shard_s(zz, yy, cc):
        return r.ws.at[zz, pl.ds(pl.multiple_of(192 * (2 * yy + cc), 192), 192)]

    def shard_c(zz, yy, cc):
        return r.wc.at[pl.ds(pl.multiple_of(272 * ((zz * 2 + yy) * 2 + cc), 16), 272)]

    def part_f(zz, yy, lo=0, n=384):
        return r.wf.at[zz, pl.ds(pl.multiple_of(384 * yy + lo, 16), n)]

    shards = (shard_s, shard_c)
    sent_w, sent_f = ([], []), ([], [])
    steps = [jnp.where(z == 0, 3 - i, jnp.where(z == 3, 1 + i, (2, 1, 3)[i])) for i in range(3)]

    def part(g, zz, yy, cc, h):
        if g >= 2:
            return part_f(zz, yy, 96 * (g - 2), 96)
        view = shards[g](zz, yy, cc)
        return view if h is None else view.at[:, cols(h)]

    def own_part(g):
        return part(g, z, y, c, x)

    def both(a, b):
        return a if b is None else b if a is None else jnp.logical_and(a, b)

    branch = (z < 2, z >= 2)

    def sent_of(g, b):
        return sent_w[g] if g < 2 else sent_f[b]

    def z_out(src, dst, g, i, b=None):
        for k in (2, 1, 3):
            cond = both({1: z != 3, 2: None, 3: z != 0}[k], None if b is None else branch[b])
            go(sent_of(g, b), src, dst, r.gz_s.at[i, k], r.gz_r.at[i, k], zdev(k), cond)

    def z_on(view, g, k):
        cond = jnp.logical_and(inner, k == 2)
        go(sent_w[g], view, view, r.gz_s.at[g, 0], r.gz_r.at[g, 2 * z - 1], device(x, 3 * (z - 1), y, c), cond)

    def own_z(g, b=None):
        z_out(own_part(g), part(g, z, y, c, x), g, g, b)

    def own_y(g, b=None):
        cond = None if b is None else branch[b]
        go(sent_of(g, b), own_part(g), part(g, z, y, c, x), r.gy_s.at[g, 0], r.gy_r.at[g, 0], yn, cond)

    def own_core(g):
        own = part(g, z, y, c, None)
        go(sent_w[g], own, own, r.gc_s.at[g, 0], r.gc_r.at[g, 0], core)

    def gather_z(g, i):
        k = steps[i]
        view = part(g, (z - k) % 4, y, c, x)
        arrived(view, r.gz_r.at[g, k])
        z_on(view, g, k)
        go(sent_w[g], view, view, r.gy_s.at[g, k], r.gy_r.at[g, k], yn)
        go(sent_w[g], view, view, r.gx_s.at[g, k - 1], r.gx_r.at[g, k - 1], xn)
        go(sent_w[g], view, view, r.gc_s.at[g, k], r.gc_r.at[g, k], core)

    def gather_y(g, j):
        view = part(g, (z - j) % 4, 1 - y, c, x)
        arrived(view, r.gy_r.at[g, j])
        go(sent_w[g], view, view, r.gx_s.at[g, 3 + j], r.gx_r.at[g, 3 + j], xn)
        go(sent_w[g], view, view, r.gc_s.at[g, 4 + j], r.gc_r.at[g, 4 + j], core)

    def ffn_z(g, p, other=False):
        i = 6 if other else g
        view = part(g, p, 1 - y if other else y, c, x)
        b = p // 2
        k = (z - p) % 4

        @pl.when(z != p)
        def _():
            arrived(view, r.gz_r.at[i, k])

        if p in (0, 3):
            at, to, slot_at = (2, 3, 3) if p == 0 else (1, 0, 1)
            go(sent_f[b], view, view, r.gz_s.at[i, 0], r.gz_r.at[i, slot_at], device(x, to, y, c), z == at)
        if g < 5:
            go(sent_f[b], view, view, r.gy_s.at[g, k], r.gy_r.at[g, k], yn, z != p)

    def ffn_y(g, p):
        arrived(part(g, p, 1 - y, c, x), r.gy_r.at[g, (z - p) % 4])

    def other_z(b):
        view = part(5, z, 1 - y, c, x)

        @pl.when(branch[b])
        def _():
            arrived(view, r.gy_r.at[5, 0])

        z_out(view, view, 5, 6, b)

    def gather_x(g):
        for j in range(7):
            view = part(g, (z - j - 1) % 4, y, c, 1 - x) if j < 3 else part(g, (z - j + 3) % 4, 1 - y, c, 1 - x)
            arrived(view, r.gx_r.at[g, j])
            go(sent_w[g], view, view, r.gc_s.at[g, 8 + j], r.gc_r.at[g, 8 + j], core)

    def gather_core(g, which):
        for j in which:
            if j == 0:
                view = part(g, z, y, 1 - c, None)
            elif j < 4:
                view = part(g, (z - j) % 4, y, 1 - c, x)
            elif j < 8:
                view = part(g, (z - j + 4) % 4, 1 - y, 1 - c, x)
            elif j < 11:
                view = part(g, (z - j + 7) % 4, y, 1 - c, 1 - x)
            else:
                view = part(g, (z - j + 11) % 4, 1 - y, 1 - c, 1 - x)
            arrived(view, r.gc_r.at[g, j])

    tail = remote(r.tails, r.before, r.tail_s.at[0], r.tail_r.at[0], following)
    back = shift_back()

    def one_hot(shape, pick):
        row = lax.broadcasted_iota(jnp.int32, shape, 0)
        col = lax.broadcasted_iota(jnp.int32, shape, 1)
        return jnp.where(col == pick(row), 1.0, 0.0).astype(BF)

    def to_rows(g):
        return one_hot((96, 128), lambda i: 32 - back[g] + 6 * (i % 16) + i // 16)

    def store_rows(dst, row, tiles, n=6):
        for j in range(n):
            dst[pl.ds(pl.multiple_of(row, 16), 16), 128 * j : 128 * j + 128] = tiles[16 * j : 16 * j + 16]

    def first_window(g, flat, n):
        return jnp.concatenate([r.before[32 * g : 32 * g + 32], flat[0:n]], 0)

    def lay_rows(g, flat, dst, n):
        perm = to_rows(g)

        def body(i, carry):
            window = flat[pl.ds(pl.multiple_of(96 * i - 32, 32), 128)]
            store_rows(dst, 16 * i, mm(perm, window).astype(BF))
            return carry

        lax.fori_loop(1, n, body, 0)
        return perm

    tail_v = one_hot(
        (96, 96),
        lambda i: jnp.where(
            i % 16 < 5,
            6 * (i % 16) + i // 16,
            jnp.where(
                i % 16 < 10,
                32 + 6 * (i % 16 - 5) + i // 16,
                jnp.where(z < 2, 72, 66)
                + jnp.where(
                    z % 2 == 0,
                    12 * (i // 48) + 3 * (i % 16 - 10) + (i // 16) % 3,
                    6 * (i % 16 - 10) + i // 16,
                ),
            ),
        ),
    )
    mine_s, mine_c = part(0, z, y, c, None), part(1, z, y, c, None)

    def rows_s():
        store_rows(r.own_t, 0, mm(tail_v, r.tails[...]).astype(BF))
        perm = lay_rows(0, r.flat_s, mine_s, 12)
        tail.wait_recv()
        store_rows(mine_s, 0, mm(perm, first_window(0, r.flat_s, 96)).astype(BF))

    def rows_c():
        perm = lay_rows(1, r.flat_c, mine_c, 17)
        store_rows(mine_c, 0, mm(perm, first_window(1, r.flat_c, 96)).astype(BF))

    def rows_f():
        @pl.when(w1)
        def _():
            def pick(i):
                m, j = i % 16, i // 16
                q = 2 * jnp.where(j < 6, c, 1 - c) + x
                j = j % 6
                return 32 - back[2] + 24 * m + 12 * (j // 3) + 3 * q + j % 3

            perm = one_hot((192, 416), pick)
            mine = part_f(z, y, 192 * c, 192)

            def put(i, window):
                tiles = mm(perm, window).astype(BF)
                store_rows(r.theirs, 16 * i, tiles[96:192])
                store_rows(mine, 16 * i, tiles[0:96])

            def body(i, carry):
                put(i, r.flat_f[pl.ds(pl.multiple_of(384 * i - 32, 32), 416)])
                return carry

            put(0, first_window(2, r.flat_f, 384))
            lax.fori_loop(1, 12, body, 0)
            swap = remote(r.theirs, mine, r.gc_s.at[2, 0], r.gc_r.at[2, 0], core)
            swap.start()
            swap.wait()

        @pl.when(jnp.logical_not(w1))
        def _():
            perm = to_rows(2)
            mine = part_f(z, y)

            def body(i, carry):
                window = r.flat_f[pl.ds(pl.multiple_of(2304 * x + 96 * i - 32, 32), 128)]
                store_rows(mine, 16 * i, mm(perm, window).astype(BF))
                return carry

            lax.fori_loop(1, 24, body, 0)
            lead = jnp.where(x == 0, r.before[64:96], r.flat_f[2304 - 32 : 2304])
            rest = r.flat_f[pl.ds(pl.multiple_of(2304 * x, 32), 96)]
            store_rows(mine, 0, mm(perm, jnp.concatenate([lead, rest], 0)).astype(BF))

    def vectors_out():
        @pl.when(root)
        def _():
            own = pltpu.make_async_copy(r.own_t, r.tb.at[z], r.loc.at[0])
            own.start()
            for k in (1, 2, 3):
                remote(r.own_t, r.tb.at[z], r.t_s.at[k - 1], r.t_r.at[k], zdev(k)).start()
            own.wait()

    def vectors_on():
        @pl.when(root)
        def _():
            for k in (1, 2, 3):
                arrived(r.tb.at[(z - k) % 4], r.t_r.at[k])
            out = []
            for i, (yy, cc) in enumerate(((0, 0), (0, 1), (1, 0))):
                go(out, r.tb, r.tb, r.t_s.at[3 + i], r.t_r.at[0], device(x, z, yy, cc))
            drain(out)
            for k in (1, 2, 3):
                remote(r.own_t, r.tb.at[z], r.t_s.at[k - 1], r.t_r.at[k], zdev(k)).wait_send()

    def vectors_in():
        @pl.when(jnp.logical_not(root))
        def _():
            arrived(r.tb, r.t_r.at[0])

        r.tv[...] = r.tb[...].astype(F32)
        r.vg[...] = jnp.zeros_like(r.vg)

    self_v = lambda j: r.tv[3, j : j + 1]
    cross_v = lambda j: r.tv[3, 5 + j : 6 + j]
    ffn_b1 = lambda b: r.tv[2 * b, pl.ds(10 + me, 1)]
    ffn_v = lambda b, j: r.tv[2 * b + 1, 10 + j : 11 + j]

    def slot(xx, cc):
        return 2 * cc + xx

    def ag_copy(ph, b, i):
        buf = r.xg.at[ph, b]
        pair = [(me, xn), (me, core), (slot(1 - x, c), core)]
        s, t = pair[i]
        return remote(buf.at[s], buf.at[s], r.ex_s.at[ph, b, i], r.ex_r.at[ph, b, i], t)

    def ag_start(ph, b):
        ag_copy(ph, b, 0).start()
        ag_copy(ph, b, 1).start()

    def ag_mid(ph, b):
        ag_copy(ph, b, 0).wait_recv()
        ag_copy(ph, b, 2).start()

    def ag_end(ph, b):
        ag_copy(ph, b, 1).wait_recv()
        ag_copy(ph, b, 2).wait_recv()
        for i in range(3):
            ag_copy(ph, b, i).wait_send()

    def rs_copy(ph, b, i):
        src = r.send_x.at[ph, b] if i == 2 else r.send_p.at[ph, b, i]
        dst = r.recv_x.at[ph, b] if i == 2 else r.recv_p.at[ph, b, i]
        return remote(src, dst, r.rs_s.at[ph, b, i], r.rs_r.at[ph, b, i], xn if i == 2 else core)

    def rs_start(ph, b):
        r.send_p[ph, b, 0] = r.part[b, slot(1 - x, 1 - c)].astype(BF)
        rs_copy(ph, b, 0).start()
        r.send_p[ph, b, 1] = r.part[b, slot(x, 1 - c)].astype(BF)
        rs_copy(ph, b, 1).start()

    def rs_mid(ph, b):
        rs_copy(ph, b, 0).wait_recv()
        r.send_x[ph, b] = (r.part[b, slot(1 - x, c)] + r.recv_p[ph, b, 0].astype(F32)).astype(BF)
        rs_copy(ph, b, 2).start()

    def rs_end(ph, b):
        rs_copy(ph, b, 1).wait_recv()
        rs_copy(ph, b, 2).wait_recv()
        for i in range(3):
            rs_copy(ph, b, i).wait_send()
        return r.part[b, me] + r.recv_p[ph, b, 1].astype(F32) + r.recv_x[ph, b].astype(F32)

    keep = SimpleNamespace()

    def self_attention():
        h = r.hid[...]
        r.q[...] = (mm(h, r.ws[0]) + self_v(0)).astype(BF)
        r.k[...] = mm(h, r.ws[1]).astype(BF)
        r.v[...] = (mm(h, r.ws[2]) + self_v(1)).astype(BF)
        for i in range(2):
            rows = slice(64 * i, 64 * i + 64)
            at = lax.broadcasted_iota(jnp.int32, (256, 64), 0) % 64
            key = lax.broadcasted_iota(jnp.int32, (256, 64), 1)
            caption = jnp.where(at >= NQ, 1.0, 0.0) * jnp.where(key <= at, 1.0, 0.0)
            ok = jnp.where(key < NQ, 1.0, caption * jnp.where(key < NQ + r.lens[i], 1.0, 0.0))
            for g in range(3):
                lanes = slice(256 * g, 256 * g + 256)
                p, a = attend_block(r.q[rows, lanes], r.k[rows, lanes], r.v[rows, lanes], ok)
                r.p[i, g] = p
                r.a[rows, lanes] = a
        r.sum1[...] = h.astype(F32) + (mm(r.a[...], r.ws[3]) + self_v(2))
        xh, _ = normed(r.sum1[...])
        r.first[...] = xh * self_v(3) + self_v(4)
        r.xg[0, 1, me] = rows_of(r.first, 32).astype(BF)

    def image_rows(lanes):
        for i in range(2):
            rows = slice(272 * i, 272 * i + 257)
            r.ck[rows, lanes] = mm(r.feat[i], r.wc[768:2176, lanes]).astype(BF)
            bias = r.tv[3, 6:7, lanes]
            r.cv[rows, lanes] = (mm(r.feat[i], r.wc[2176:3584, lanes]) + bias).astype(BF)

    def pad_rows():
        for i in range(2):
            r.ck[272 * i + 256 : 272 * i + 272] = jnp.zeros((16, D), BF)
            r.cv[272 * i + 256 : 272 * i + 272] = jnp.zeros((16, D), BF)

    def cross_start():
        keep.u = rows_of(r.first, 0)
        r.cq[...] = (mm(keep.u.astype(BF), r.wc[0:768]) + cross_v(0)).astype(BF)

    def cross_attention(i):
        ok = jnp.where(lax.broadcasted_iota(jnp.int32, (128, 272), 1) < 257, 1.0, 0.0)
        rows = slice(272 * i, 272 * i + 272)
        mine = slice(32 * i, 32 * i + 32)
        for g in range(3):
            lanes = slice(256 * g, 256 * g + 256)
            p, a = attend_block(r.cq[mine, lanes], r.ck[rows, lanes], r.cv[rows, lanes], ok)
            r.pc[i, g] = p
            r.ca[mine, lanes] = a

    def cross_end():
        r.sum2[...] = keep.u + (mm(r.ca[...], r.wc[3584:4352]) + cross_v(2))
        xh, _ = normed(r.sum2[...])
        r.second[...] = xh * cross_v(3) + cross_v(4)
        r.xg[0, 0, me] = r.second[...].astype(BF)

    sent = []

    def ffn_forward_part(b):
        rows = r.xg[0, b].reshape(256, D)
        r.pre[b] = mm(rows, r.wf[2 * b]) + ffn_b1(b)
        r.act[b] = gelu(r.pre[b]).astype(BF)
        r.part[b] = mm(r.act[b], r.wf[2 * b + 1]).reshape(4, 64, D)

    def ffn_turn(b):
        rows = r.second[...] if b == 0 else rows_of(r.first, 32)
        s3 = rows + (rs_end(0, b) + ffn_v(b, 0))
        xh, _ = normed(s3)
        done = (xh * ffn_v(b, 1) + ffn_v(b, 2)).astype(BF)
        for i in range(2):
            r.mixed[64 * i + 32 * b : 64 * i + 32 * b + 32] = done[32 * i : 32 * i + 32]
        g_out = rows_of(r.cot, 32 * b).astype(F32)
        dsum, dgain, dshift = norm_back(s3, ffn_v(b, 1), g_out)
        r.dsum3[b] = dsum
        low = dsum.astype(BF)
        r.xg[1, b, me] = low
        r.vg[2 * b + 1, 10:11] = rows_sum(low)
        r.vg[2 * b + 1, 11:12] = dgain
        r.vg[2 * b + 1, 12:13] = dshift

    def ffn_backward_part(b):
        up = r.xg[1, b].reshape(256, D)
        r.dpre[b] = (mm_nt(up, r.wf[2 * b + 1]) * gelu_slope(r.pre[b])).astype(BF)
        r.part[b] = mm_nt(r.dpre[b], r.wf[2 * b]).reshape(4, 64, D)
        db1 = rows_sum(r.dpre[b])
        for j in range(4):
            r.vg[2 * b, 10 + j : 11 + j] = jnp.where(j == me, db1, 0.0)

    def ffn_weight_grads(b):
        drain(sent_f[b])
        rows = r.xg[0, b].reshape(256, D)
        up = r.xg[1, b].reshape(256, D)
        r.wf[2 * b] = mm_tn(rows, r.dpre[b]).astype(BF)
        r.wf[2 * b + 1] = mm_tn(r.act[b], up).astype(BF)

    def ffn_sum_start(b):
        for p in (2 * b, 2 * b + 1):
            go(sent, part_f(p, 1 - y, 0, SPLIT), r.yf.at[p], r.yy_s.at[2, p], r.yy_r.at[2, p], yn)
        for p in (2 * b, 2 * b + 1):
            for i, yy in ((4, 1 - y), (3, y)):
                z_out_sum(i, part_f(p, yy, SPLIT, REST), p)

    hop = jnp.where(z < 2, 1, 2)

    def z_out_sum(i, src, p):
        zb, zr = getattr(r, f"zb{i}"), getattr(r, f"zr{i}")
        d = (p - z) % 4
        far = {0: z == 3, 3: z == 0}.get(p)
        later = {0: z == 2, 3: z == 1}.get(p)
        direct = z != p
        if far is not None:
            go(sent, src, zr, r.zq_s.at[i], r.zq_r.at[i], device(x, hop, y, c), far)
            direct = jnp.logical_and(direct, jnp.logical_not(jnp.logical_or(far, later)))
        go(sent, src, zb.at[d - 1], r.zz_s.at[i, p], r.zz_r.at[i, d], device(x, p, y, c), direct)

    def z_add_sum(i, src, p):
        later = {0: z == 2, 3: z == 1}.get(p)
        if later is None:
            return
        zb, zr = getattr(r, f"zb{i}"), getattr(r, f"zr{i}")

        @pl.when(later)
        def _():
            arrived(zr, r.zq_r.at[i])
            zr[...] = add(zr[...], src[...])

        go(sent, zr, zb.at[1], r.zz_s.at[i, p], r.zz_r.at[i, 2], device(x, p, y, c), later)

    def z_total(i, own, out):
        zb = getattr(r, f"zb{i}")
        arrived(zb.at[1], r.zz_r.at[i, 2])
        out[...] = add(own, zb[1])
        for d, without in ((1, 0), (3, 3)):

            @pl.when(z != without)
            def _():
                arrived(zb.at[d - 1], r.zz_r.at[i, d])
                out[...] = add(out[...], zb[d - 1])

    def ffn_sum_y(p):
        arrived(r.yf.at[p], r.yy_r.at[2, p])
        r.yf[p] = add(r.yf[p], part_f(p, y, 0, SPLIT)[...])
        z_out_sum(2, r.yf.at[p], p)

    def ffn_add(p):
        for i, yy in ((4, 1 - y), (3, y)):
            z_add_sum(i, part_f(p, yy, SPLIT, REST), p)

    def ffn_sum_other():
        z_total(4, part_f(z, 1 - y, SPLIT, REST)[...], r.of)
        go(sent, r.of, r.yf2, r.yy_s.at[3, 0], r.yy_r.at[3, 0], yn)

    groups = (
        (shard_s, r.core_s, r.xs, r.ys, r.fin_s, r.nice_s),
        (shard_c, r.core_c, r.xc, r.yc, r.fin_c, r.nice_c),
    )
    order = (3, 1, 2, 0)

    def sum_start(g, far):
        view, cb = groups[g][:2]
        for d in order:
            zz = (z + d) % 4
            go(sent, view(zz, y if far else 1 - y, 1 - c), cb.at[far, zz], r.co_s.at[g, far, d], r.co_r.at[g, far, d], core)

    def sum_core(g, fars=(0, 1)):
        view, cb, xb, yb = groups[g][:4]
        for far in fars:
            for d in order:
                zz = (z + d) % 4
                arrived(cb.at[far, zz], r.co_r.at[g, far, d])
                cb[far, zz] = add(cb[far, zz], view(zz, y if far else 1 - y, c)[...])
                if X_FIRST[g]:
                    go(sent, cb.at[far, zz, :, cols(1 - x)], xb.at[far, zz], r.xx_s.at[g, far, d], r.xx_r.at[g, far, d], xn)
                elif far == 0:
                    go(sent, cb.at[0, zz], yb.at[zz], r.yy_s.at[g, d], r.yy_r.at[g, d], yn)

    def sum_mid(g, fars=(0, 1)):
        view, cb, xb, yb = groups[g][:4]
        for far in fars if X_FIRST[g] else (0,):
            for d in order:
                zz = (z + d) % 4
                if X_FIRST[g]:
                    arrived(xb.at[far, zz], r.xx_r.at[g, far, d])
                    xb[far, zz] = add(xb[far, zz], cb[far, zz, :, cols(x)])
                    if far == 0:
                        go(sent, xb.at[0, zz], yb.at[zz], r.yy_s.at[g, d], r.yy_r.at[g, d], yn)
                else:
                    arrived(yb.at[zz], r.yy_r.at[g, d])
                    yb[zz] = add(yb[zz], cb[1, zz])
                    go(sent, yb.at[zz, :, cols(1 - x)], xb.at[zz], r.xx_s.at[g, 0, d], r.xx_r.at[g, 0, d], xn)

    def to_z(g, mine, d):
        zb, zr = getattr(r, f"zb{g}"), getattr(r, f"zr{g}")
        if d == 2:

            @pl.when(inner)
            def _():
                arrived(zr, r.zq_r.at[g])
                zr[...] = add(zr[...], mine[...])

            go(sent, zr, zb.at[1], r.zz_s.at[g, 2], r.zz_r.at[g, 2], zdev(2), inner)
            go(sent, mine, zb.at[1], r.zz_s.at[g, 2], r.zz_r.at[g, 2], zdev(2), outer)
        elif d:
            far = z == (0 if d == 3 else 3)
            go(sent, mine, zr, r.zq_s.at[g], r.zq_r.at[g], device(x, hop, y, c), far)
            go(sent, mine, zb.at[d - 1], r.zz_s.at[g, d], r.zz_r.at[g, d], zdev(d), jnp.logical_not(far))

    def sum_last(g):
        view, cb, xb, yb = groups[g][:4]
        for d in order:
            zz = (z + d) % 4
            if X_FIRST[g]:
                arrived(yb.at[zz], r.yy_r.at[g, d])
                yb[zz] = add(yb[zz], xb[1, zz])
                to_z(g, yb.at[zz], d)
            else:
                arrived(xb.at[zz], r.xx_r.at[g, 0, d])
                xb[zz] = add(xb[zz], yb[zz, :, cols(x)])
                to_z(g, xb.at[zz], d)

    def sum_z(g):
        view, cb, xb, yb, fin, out = groups[g]
        z_total(g, yb[z] if X_FIRST[g] else xb[z], fin)
        out[:, cols(x)] = fin[...]
        go(sent, fin, out.at[:, cols(x)], r.fi_s.at[g], r.fi_r.at[g], xn)

    def ffn_sum_z():
        z_total(2, r.yf[z], r.fin_f.at[0:SPLIT])
        last = r.fin_f.at[SPLIT:384]
        z_total(3, part_f(z, y, SPLIT, REST)[...], last)
        arrived(r.yf2, r.yy_r.at[3, 0])
        last[...] = add(last[...], r.yf2[...])
        half = lambda j: r.fin_f.at[pl.ds(pl.multiple_of(192 * j, 192), 192)]

        @pl.when(w1)
        def _():
            r.nice_f[me] = half(c)[...]
            remote(half(c), r.nice_f.at[me], r.fi_s.at[2], r.fi_r.at[2], xn).start()
            remote(half(1 - c), r.nice_f.at[me], r.fi_s.at[3], r.fi_r.at[3], core).start()
            remote(half(1 - c), r.nice_f.at[me], r.fi_s.at[4], r.fi_r.at[4], diag).start()

        @pl.when(jnp.logical_not(w1))
        def _():
            for j in range(2):
                r.nice_f[2 * x + j] = half(j)[...]
                remote(half(j), r.nice_f.at[2 * x + j], r.fi_s.at[2 + j], r.fi_r.at[2 + j], xn).start()

    def ffn_end():
        def ends(n):
            for j in range(n):
                remote(r.fin_f.at[0:192], r.nice_f.at[0], r.fi_s.at[2 + j], r.fi_r.at[2 + j], xn).wait()

        pl.when(w1)(lambda: ends(3))
        pl.when(jnp.logical_not(w1))(lambda: ends(2))

    def stack(src, row, n=6):
        return jnp.concatenate(
            [src[pl.ds(pl.multiple_of(row, 16), 16), 128 * j : 128 * j + 128] for j in range(n)], 0
        )

    to_flat = one_hot((96, 96), lambda i: 16 * (i % 6) + i // 6)

    def lay_flat(src, dst, n, base=0):
        def body(i, carry):
            dst[pl.ds(pl.multiple_of(base + 96 * i, 32), 96)] = mm(to_flat, stack(src, 16 * i)).astype(BF)
            return carry

        lax.fori_loop(0, n, body, 0)

    def head_out(g, fl):
        r.heads[g] = fl[0:32]
        go(sent, r.heads.at[g], r.after.at[g], r.head_s.at[g], r.head_r.at[g], preceding)

    def text_end():
        d_text = r.dsum3[1] + rs_end(1, 1)
        for i in range(2):
            r.dfirst[64 * i + 32 : 64 * i + 64] = d_text[32 * i : 32 * i + 32]

    def query_end():
        keep.d_second = r.dsum3[0] + rs_end(1, 0)

    def cross_back():
        du2, dgain, dshift = norm_back(r.sum2[...], cross_v(3), keep.d_second)
        r.vg[3, 8:9] = dgain
        r.vg[3, 9:10] = dshift
        low = keep.low2 = du2.astype(BF)
        r.vg[3, 7:8] = rows_sum(low)
        dca = mm_nt(low, r.wc[3584:4352]).astype(BF)
        dcq = []
        for i in range(2):
            rows = slice(272 * i, 272 * i + 272)
            mine = slice(32 * i, 32 * i + 32)
            blocks = []
            for g in range(3):
                lanes = slice(256 * g, 256 * g + 256)
                dq, dk, dv = attend_block_back(
                    r.cq[mine, lanes], r.ck[rows, lanes], r.cv[rows, lanes], r.pc[i, g], dca[mine, lanes]
                )
                blocks.append(dq)
                r.ck[rows, lanes] = dk
                r.cv[rows, lanes] = dv
            dcq.append(jnp.concatenate(blocks, 1))
        dcq = keep.dcq = jnp.concatenate(dcq, 0)
        r.vg[3, 5:6] = rows_sum(dcq)
        r.vg[3, 6:7] = rows_sum(r.cv[...])
        du = du2 + mm_nt(dcq, r.wc[0:768])
        for i in range(2):
            r.dfirst[64 * i : 64 * i + 32] = du[32 * i : 32 * i + 32]

    def cross_grads():
        drain(sent_w[1])
        r.wc[3584:4352] = mm_tn(r.ca[...], keep.low2).astype(BF)
        r.wc[0:768] = mm_tn(rows_of(r.first, 0).astype(BF), keep.dcq).astype(BF)
        for j in range(11):
            block = [r.feat[i, :, 128 * j : 128 * j + 128] for i in range(2)]
            both = lambda d: mm_tn(block[0], d[0:257]) + mm_tn(block[1], d[272:529])
            r.wc[768 + 128 * j : 896 + 128 * j] = both(r.ck).astype(BF)
            r.wc[2176 + 128 * j : 2304 + 128 * j] = both(r.cv).astype(BF)

    def self_back():
        dsum1, dgain, dshift = norm_back(r.sum1[...], self_v(3), r.dfirst[...])
        r.vg[3, 3:4] = dgain
        r.vg[3, 4:5] = dshift
        keep.dsum1 = dsum1
        low = keep.low1 = dsum1.astype(BF)
        r.vg[3, 2:3] = rows_sum(low)
        da = mm_nt(low, r.ws[3]).astype(BF)
        for i in range(2):
            rows = slice(64 * i, 64 * i + 64)
            for g in range(3):
                lanes = slice(256 * g, 256 * g + 256)
                dq, dk, dv = attend_block_back(
                    r.q[rows, lanes], r.k[rows, lanes], r.v[rows, lanes], r.p[i, g], da[rows, lanes]
                )
                r.q[rows, lanes] = dq
                r.k[rows, lanes] = dk
                r.v[rows, lanes] = dv

    def self_grads():
        drain(sent_w[0])
        r.vg[3, 0:1] = rows_sum(r.q[...])
        r.vg[3, 1:2] = rows_sum(r.v[...])
        total = keep.dsum1 + mm_nt(r.q[...], r.ws[0]) + mm_nt(r.k[...], r.ws[1]) + mm_nt(r.v[...], r.ws[2])
        r.hgrad[...] = total.astype(BF)
        r.ws[0] = mm_tn(r.hid[...], r.q[...]).astype(BF)
        r.ws[1] = mm_tn(r.hid[...], r.k[...]).astype(BF)
        r.ws[2] = mm_tn(r.hid[...], r.v[...]).astype(BF)
        r.ws[3] = mm_tn(r.a[...], keep.low1).astype(BF)

    index = 2 * y + c
    home = device(x, z, 1, 1)

    def vector_sums_out():
        r.v_send[...] = r.vg[...].astype(BF)

        @pl.when(jnp.logical_not(root))
        def _():
            remote(r.v_send, r.v_in.at[index], r.vv_s.at[0], r.vv_r.at[index], home).start()

    def vector_sums_z():
        @pl.when(root)
        def _():
            total = r.vg[...]
            for i in range(3):
                arrived(r.v_in.at[i], r.vv_r.at[i])
                total = total + r.v_in[i].astype(F32)
            r.v_z[...] = total.astype(BF)
            for k in (1, 2, 3):
                zz = (z + k) % 4
                remote(r.v_z.at[zz], r.v_zin.at[k - 1], r.vv_s.at[k], r.vv_r.at[2 + k], device(x, zz, y, c)).start()

    def vector_sums_x():
        @pl.when(root)
        def _():
            total = r.v_z[z].astype(F32)
            for k in (1, 2, 3):
                arrived(r.v_zin.at[k - 1], r.vv_r.at[2 + k])
                total = total + r.v_zin[k - 1].astype(F32)
            r.v_x[...] = total.astype(BF)
            remote(r.v_x, r.v_xin, r.vv_s.at[4], r.vv_r.at[6], xn).start()

    def vector_sums_end():
        @pl.when(root)
        def _():
            arrived(r.v_xin, r.vv_r.at[6])
            r.total_v[...] = add(r.v_x[...], r.v_xin[...])
            for k in (1, 2, 3):
                zz = (z + k) % 4
                remote(r.v_z.at[zz], r.v_zin.at[k - 1], r.vv_s.at[k], r.vv_r.at[2 + k], device(x, zz, y, c)).wait_send()
            remote(r.v_x, r.v_xin, r.vv_s.at[4], r.vv_r.at[6], xn).wait_send()

        @pl.when(jnp.logical_not(root))
        def _():
            r.total_v[...] = jnp.zeros_like(r.total_v)
            remote(r.v_send, r.v_in.at[index], r.vv_s.at[0], r.vv_r.at[index], home).wait_send()

    def flat_f():
        @pl.when(w1)
        def _():
            def pick(i):
                m, t = i // 24, i % 24
                return 96 * ((t % 12) // 3) + 16 * (3 * (t // 12) + t % 3) + m

            perm = one_hot((384, 384), pick)

            def body(i, carry):
                tiles = jnp.concatenate([stack(r.nice_f.at[q], 16 * i) for q in range(4)], 0)
                r.out_f[pl.ds(pl.multiple_of(384 * i, 128), 384)] = mm(perm, tiles).astype(BF)
                return carry

            lax.fori_loop(0, 12, body, 0)

        @pl.when(jnp.logical_not(w1))
        def _():
            for q in range(4):
                lay_flat(r.nice_f.at[q], r.out_f, 12, 1152 * q)

        head_out(2, r.out_f)

    tail.start()
    rows_s()
    own_z(0)
    own_y(0)
    own_core(0)
    vectors_out()
    pad_rows()
    rows_f()
    gather_y(0, 0)
    rows_c()
    vectors_on()
    own_y(1)
    own_z(1)
    gather_z(0, 0)
    gather_z(0, 1)
    own_y(2, 1)
    gather_y(1, 0)
    gather_z(0, 2)
    gather_z(1, 1)
    gather_y(0, 1)
    own_core(1)
    own_y(3, 0)
    gather_y(0, 2)
    own_y(5, 0)
    own_z(2, 1)
    own_y(5, 1)
    own_z(3, 0)
    gather_y(0, 3)
    gather_z(1, 0)
    own_z(4, 0)
    other_z(0)
    own_z(4, 1)
    ffn_z(2, 2)
    gather_z(1, 2)
    gather_x(0)
    own_y(3, 1)
    gather_core(0, range(15))
    gather_y(1, 2)
    own_y(4, 0)
    own_z(3, 1)
    gather_y(1, 1)
    vectors_in()
    self_attention()
    ffn_z(3, 1)
    ffn_z(2, 3)
    gather_y(1, 3)
    gather_core(1, range(8))
    ffn_z(4, 3)
    ffn_z(4, 0)
    other_z(1)
    ffn_z(4, 1)
    ffn_z(3, 2)
    ffn_z(3, 3)
    own_z(2, 0)
    ffn_y(2, 3)
    own_z(5, 1)
    ag_start(0, 1)
    own_y(4, 1)
    image_rows(cols(x))
    gather_x(1)
    ffn_z(4, 2)
    ffn_z(2, 1)
    ffn_z(5, 0, other=True)
    gather_core(1, range(8, 15))
    own_z(5, 0)
    image_rows(cols(1 - x))
    ag_mid(0, 1)
    cross_start()
    cross_attention(0)
    ffn_y(4, 3)
    ffn_z(5, 3, other=True)
    ffn_y(3, 3)
    cross_attention(1)
    cross_end()
    ffn_z(5, 3)
    ffn_z(5, 2)
    ffn_z(5, 2, other=True)
    own_y(2, 0)
    ffn_y(3, 1)
    ffn_y(4, 0)
    ag_end(0, 1)
    ag_start(0, 0)
    ffn_y(2, 2)
    ffn_z(3, 0)
    ffn_y(4, 2)
    ffn_y(3, 2)
    ffn_forward_part(1)
    rs_start(0, 1)
    ffn_z(2, 0)
    ag_mid(0, 0)
    rs_mid(0, 1)
    ffn_z(5, 1, other=True)
    ffn_y(2, 1)
    ffn_z(5, 0)
    ffn_turn(1)
    ag_start(1, 1)
    ffn_y(3, 0)
    ffn_y(4, 1)
    ag_end(0, 0)
    ffn_z(5, 1)
    ffn_y(2, 0)
    ffn_forward_part(0)
    rs_start(0, 0)
    ag_mid(1, 1)
    rs_mid(0, 0)
    ag_end(1, 1)
    ffn_backward_part(1)
    ffn_weight_grads(1)
    ffn_sum_start(1)
    ffn_turn(0)
    ag_start(1, 0)
    rs_start(1, 1)
    ag_mid(1, 0)
    rs_mid(1, 1)
    ag_end(1, 0)
    ffn_backward_part(0)
    rs_start(1, 0)
    ffn_weight_grads(0)
    ffn_sum_start(0)
    rs_mid(1, 0)
    text_end()
    query_end()
    cross_back()
    cross_grads()
    sum_start(1, 0)
    self_back()
    self_grads()
    vector_sums_out()
    ffn_add(0)
    ffn_add(3)
    sum_start(0, 0)
    sum_core(1, (0,))
    ffn_sum_y(3)
    ffn_sum_y(0)
    sum_start(0, 1)
    ffn_sum_y(2)
    sum_core(0, (0,))
    sum_start(1, 1)
    ffn_sum_other()
    vector_sums_z()
    sum_core(1, (1,))
    ffn_sum_y(1)
    z_add_sum(2, r.yf.at[0], 0)
    sum_core(0, (1,))
    z_add_sum(2, r.yf.at[3], 3)
    sum_mid(1, (0,))
    ffn_sum_z()
    sum_mid(0, (0,))
    sum_mid(1, (1,))
    sum_last(1)
    sum_last(0)
    vector_sums_x()
    sum_z(1)
    sum_z(0)
    ffn_end()
    flat_f()
    vector_sums_end()
    tail.wait_send()

    arrived(groups[1][5].at[:, cols(1 - x)], r.fi_r.at[1])
    lay_flat(r.nice_c, r.out_c, 17)
    head_out(1, r.out_c)
    arrived(groups[0][5].at[:, cols(1 - x)], r.fi_r.at[0])
    lay_flat(r.nice_s, r.out_s, 12)
    head_out(0, r.out_s)

    vectors = stack(r.total_v, 0)
    end = (f == 15, f == 15, f % 4 == 3)
    plain = lambda first: lambda i: 16 * (i % 6) + first + i // 6
    hidden = lambda i: 16 * (3 * (i // 12) + i % 3) + 10 + (i % 12) // 3
    none = -1
    count = jnp.where(w1, 24, 18)

    def from_vectors(g):
        if g < 2:
            return lambda i: jnp.where(jnp.logical_and(end[g], i < 30), plain(5 * g)(i), none)
        pick = lambda i: jnp.where(w1, hidden(i), plain(10)(i))
        return lambda i: jnp.where(jnp.logical_and(end[2], i < count), pick(i), none)

    def from_next(g):
        if g < 2:
            return lambda i: jnp.where(end[g], none, i)
        inside = jnp.logical_or(z == 1, z == 2)
        return lambda i: jnp.where(
            end[2], jnp.where(jnp.logical_and(inside, i >= count), i - count, none), i
        )

    for g, (fl, rows) in enumerate(((r.out_s, 1152), (r.out_c, 1632), (r.out_f, 4608))):
        arrived(r.after.at[g], r.head_r.at[g])
        tail = mm(one_hot((32, 96), from_vectors(g)), vectors) + mm(one_hot((32, 32), from_next(g)), r.after[g])
        fl[rows : rows + 32] = tail.astype(BF)

    drain(sent)


def layer(flat_s, flat_c, flat_f, tails, lens, hid, feat, cot):
    vm = pl.BlockSpec(memory_space=pltpu.VMEM)
    return pl.pallas_call(
        layer_kernel,
        out_shape=(
            jax.ShapeDtypeStruct((128, D), BF),
            jax.ShapeDtypeStruct((128, D), BF),
            *[jax.ShapeDtypeStruct((n, 128), BF) for n in (1184, 1664, 4640)],
        ),
        in_specs=[vm] * 4 + [pl.BlockSpec(memory_space=pltpu.SMEM)] + [vm] * 3,
        out_specs=[vm] * 5,
        scratch_shapes=list(scratch().values()),
        compiler_params=pltpu.CompilerParams(
            collective_id=0, has_side_effects=True, vmem_limit_bytes=VMEM_BYTES
        ),
    )(flat_s, flat_c, flat_f, tails, lens, hid, feat, cot)


def per_device_fast(hidden, lengths, features, cotangent, self_params, cross_params, ffn_params):
    flats = [v.reshape(-1, 128) for v in (self_params, cross_params, ffn_params)]
    tails = jnp.concatenate([v[-32:] for v in flats])
    mixed, hgrad, *grads = layer(
        *flats, tails, lengths, hidden.reshape(128, D), features, cotangent.reshape(128, D)
    )
    outs = [
        lax.dynamic_slice_in_dim(rows, back, flat.shape[0]).astype(F32).reshape(-1)
        for rows, back, flat in zip(grads, shift_back(), flats)
    ]
    return (mixed.reshape(2, 64, D), hgrad.reshape(2, 64, D), *outs)


def solution(mesh):
    fast = mesh.shape["dp"] == 2 and mesh.shape["fsdp"] == 16
    return jax.shard_map(
        per_device_fast if fast else per_device,
        mesh=mesh,
        in_specs=(
            P(("dp", "fsdp"), None, None),
            P(("dp", "fsdp")),
            P(("dp", "fsdp"), None, None),
            P(("dp", "fsdp"), None, None),
            P("fsdp"),
            P("fsdp"),
            P("fsdp"),
        ),
        out_specs=(
            P(("dp", "fsdp"), None, None),
            P(("dp", "fsdp"), None, None),
            P("fsdp"),
            P("fsdp"),
            P("fsdp"),
        ),
        check_vma=False,
    )
```

```python
from functools import partial
import math
from types import SimpleNamespace

import jax
import jax.numpy as jnp
from jax import lax
from jax.experimental import pallas as pl
from jax.experimental.pallas import tpu as pltpu
from jax.sharding import PartitionSpec as P

D = 768
HEADS = 12
HDIM = 64
F = 3072
E = 1408
NQ = 32


EPS = 1e-06
SCALE = 0.125


def self_layout():
    return [(D, D)] * 4 + [(D,)] * 5


def cross_layout():
    return [(D, D), (E, D), (E, D), (D, D)] + [(D,)] * 5


def ffn_layout():
    return [(D, F), (F,), (F, D), (D,), (D,), (D,)] * 2


def split_flat(flat_vec, layouts):
    pieces = []
    offset = 0
    for layout in layouts:
        amount = math.prod(layout)
        pieces.append(flat_vec[offset : offset + amount].reshape(layout))
        offset = offset + amount
    return pieces


def join_flat(pieces, length):
    flat_vec = jnp.concatenate([piece.reshape(-1) for piece in pieces])
    return jnp.pad(flat_vec, (0, length - flat_vec.shape[0]))


def regroup(flat_vec):
    groups = lax.axis_size("fsdp")
    replicas = lax.axis_size("dp")
    return flat_vec.reshape(groups, replicas, -1).transpose(1, 0, 2).reshape(-1)


def matmul(left, right):
    return jnp.dot(left, right, preferred_element_type=jnp.float32)


def matmul_left(left, right):
    return lax.dot_general(
        left, right, (((0,), (0,)), ((), ())), preferred_element_type=jnp.float32
    )


def matmul_right(left, right):
    return lax.dot_general(
        left, right, (((1,), (1,)), ((), ())), preferred_element_type=jnp.float32
    )


def column_sum(values):
    return jnp.sum(values.astype(jnp.float32), 0)


def layer_norm(values, gain, shift):
    average = jnp.mean(values, -1, keepdims=True)
    centered = values - average
    variance = jnp.mean(centered * centered, -1, keepdims=True)
    return centered * lax.rsqrt(variance + EPS) * gain + shift


def norm_backward(summed, gain, shift, grad_out):
    _, norm_pull = jax.vjp(layer_norm, summed, gain.astype(jnp.float32), shift.astype(jnp.float32))
    return norm_pull(grad_out)


def heads(rows, items):
    return rows.reshape(items, -1, HEADS, HDIM)


def score_block(query, keys, mask):
    scores = jnp.einsum("iqhd,ikhd->ihqk", query, keys, preferred_element_type=jnp.float32) * SCALE
    if mask is not None:
        scores = jnp.where(mask, scores, -1e30)
    return scores


def attend(query, keys, values, mask):
    scores = score_block(query, keys, mask)
    top_sum = jax.nn.logsumexp(scores, axis=-1)
    probs = jnp.exp(scores - top_sum[..., None]).astype(jnp.bfloat16)
    context = jnp.einsum("ihqk,ikhd->iqhd", probs, values, preferred_element_type=jnp.float32)
    return (context, top_sum)


def attend_back(query, keys, values, mask, top_sum, grad_context):
    probs = jnp.exp(score_block(query, keys, mask) - top_sum[..., None])
    grad_probs = jnp.einsum(
        "iqhd,ikhd->ihqk", grad_context, values, preferred_element_type=jnp.float32
    )
    inner = jnp.sum(probs * grad_probs, -1, keepdims=True)
    grad_scores = (probs * (grad_probs - inner)).astype(jnp.bfloat16)
    grad_query = (
        jnp.einsum("ihqk,ikhd->iqhd", grad_scores, keys, preferred_element_type=jnp.float32) * SCALE
    )
    grad_keys = (
        jnp.einsum("ihqk,iqhd->ikhd", grad_scores, query, preferred_element_type=jnp.float32)
        * SCALE
    )
    grad_values = jnp.einsum(
        "ihqk,iqhd->ikhd",
        probs.astype(jnp.bfloat16),
        grad_context,
        preferred_element_type=jnp.float32,
    )
    return (grad_query, grad_keys, grad_values)


def linear_back(inputs, weight, grad_out):
    return (matmul_left(inputs, grad_out), column_sum(grad_out), matmul_right(grad_out, weight))


def ffn_forward(rows, params):
    w_in, b_in, w_out, b_out, gain, shift = params
    rows_low = rows.astype(jnp.bfloat16)
    hidden_pre = matmul(rows_low, w_in) + b_in
    activated = jax.nn.gelu(hidden_pre, approximate=True).astype(jnp.bfloat16)
    summed = rows + (matmul(activated, w_out) + b_out)
    final = layer_norm(summed, gain.astype(jnp.float32), shift.astype(jnp.float32))
    return (final, (rows_low, hidden_pre, activated, summed))


def ffn_backward(grad_out, kept, params):
    w_in, b_in, w_out, b_out, gain, shift = params
    rows_low, hidden_pre, activated, summed = kept
    grad_sum, grad_gain, grad_shift = norm_backward(summed, gain, shift, grad_out)
    grad_branch = grad_sum.astype(jnp.bfloat16)
    grad_w_out, grad_b_out, grad_act = linear_back(activated, w_out, grad_branch)
    _, gelu_pull = jax.vjp(partial(jax.nn.gelu, approximate=True), hidden_pre)
    grad_pre = gelu_pull(grad_act)[0].astype(jnp.bfloat16)
    grad_w_in, grad_b_in, grad_rows = linear_back(rows_low, w_in, grad_pre)
    return (
        grad_sum + grad_rows,
        [grad_w_in, grad_b_in, grad_w_out, grad_b_out, grad_gain, grad_shift],
    )


def per_device(hidden, lengths, features, cotangent, self_params, cross_params, ffn_params):
    items, seq, width = hidden.shape
    self_full = lax.all_gather(self_params, "fsdp", axis=0, tiled=True)
    self_parts = split_flat(self_full, self_layout())
    w_q, w_k, w_v, w_o, b_q, b_v, b_o, gain_one, shift_one = self_parts
    positions = jnp.arange(seq)
    rows_at = positions[:, None]
    cols_at = positions[None, :]
    allowed = (cols_at < NQ)[None] | ((rows_at >= NQ) & (cols_at <= rows_at))[None] & (
        cols_at[None] < NQ + lengths[:, None, None]
    )
    allowed = allowed[:, None]
    inputs = hidden.reshape(-1, width)
    query_low = (matmul(inputs, w_q) + b_q).astype(jnp.bfloat16)
    key_low = matmul(inputs, w_k).astype(jnp.bfloat16)
    value_low = (matmul(inputs, w_v) + b_v).astype(jnp.bfloat16)
    context, self_top = attend(
        heads(query_low, items), heads(key_low, items), heads(value_low, items), allowed
    )
    context_low = context.reshape(-1, width).astype(jnp.bfloat16)
    summed_one = inputs.astype(jnp.float32) + (matmul(context_low, w_o) + b_o)
    first = layer_norm(summed_one, gain_one.astype(jnp.float32), shift_one.astype(jnp.float32))
    first_items = first.reshape(items, seq, width)
    query_rows = first_items[:, :NQ].reshape(-1, width)
    text_rows = first_items[:, NQ:].reshape(-1, width)
    cross_full = lax.all_gather(cross_params, "fsdp", axis=0, tiled=True)
    cross_parts = split_flat(cross_full, cross_layout())
    cross_wq, cross_wk, cross_wv, cross_wo, cross_bq, cross_bv, cross_bo, gain_two, shift_two = (
        cross_parts
    )
    query_in = query_rows.astype(jnp.bfloat16)
    image_rows = features.reshape(-1, features.shape[-1])
    cross_query = (matmul(query_in, cross_wq) + cross_bq).astype(jnp.bfloat16)
    cross_key = matmul(image_rows, cross_wk).astype(jnp.bfloat16)
    cross_value = (matmul(image_rows, cross_wv) + cross_bv).astype(jnp.bfloat16)
    cross_context, cross_top = attend(
        heads(cross_query, items), heads(cross_key, items), heads(cross_value, items), None
    )
    cross_low = cross_context.reshape(-1, width).astype(jnp.bfloat16)
    summed_two = query_rows + (matmul(cross_low, cross_wo) + cross_bo)
    second = layer_norm(summed_two, gain_two.astype(jnp.float32), shift_two.astype(jnp.float32))
    ffn_full = lax.all_gather(ffn_params, "fsdp", axis=0, tiled=True)
    ffn_parts = split_flat(ffn_full, ffn_layout())
    query_final, query_kept = ffn_forward(second, ffn_parts[:6])
    text_final, text_kept = ffn_forward(text_rows, ffn_parts[6:])
    mixed = jnp.concatenate(
        [query_final.reshape(items, NQ, width), text_final.reshape(items, -1, width)], 1
    ).astype(jnp.bfloat16)
    grad_items = cotangent.astype(jnp.float32)
    grad_query_final = grad_items[:, :NQ].reshape(-1, width)
    grad_text_final = grad_items[:, NQ:].reshape(-1, width)
    ffn_back = split_flat(lax.all_gather(ffn_params, "fsdp", axis=0, tiled=True), ffn_layout())
    grad_second, query_grads = ffn_backward(grad_query_final, query_kept, ffn_back[:6])
    grad_text, text_grads = ffn_backward(grad_text_final, text_kept, ffn_back[6:])
    ffn_flat_grad = join_flat(query_grads + text_grads, ffn_full.shape[0])
    ffn_grad = lax.psum_scatter(
        regroup(ffn_flat_grad), ("dp", "fsdp"), scatter_dimension=0, tiled=True
    )
    cross_back = split_flat(
        lax.all_gather(cross_params, "fsdp", axis=0, tiled=True), cross_layout()
    )
    grad_summed_two, grad_gain_two, grad_shift_two = norm_backward(
        summed_two, cross_back[7], cross_back[8], grad_second
    )
    grad_cross_out = grad_summed_two.astype(jnp.bfloat16)
    grad_cross_wo, grad_cross_bo, grad_cross_ctx = linear_back(
        cross_low, cross_back[3], grad_cross_out
    )
    grad_cq, grad_ck, grad_cv = attend_back(
        heads(cross_query, items),
        heads(cross_key, items),
        heads(cross_value, items),
        None,
        cross_top,
        heads(grad_cross_ctx.astype(jnp.bfloat16), items),
    )
    grad_cq = grad_cq.reshape(-1, width).astype(jnp.bfloat16)
    grad_ck = grad_ck.reshape(-1, width).astype(jnp.bfloat16)
    grad_cv = grad_cv.reshape(-1, width).astype(jnp.bfloat16)
    grad_cross_wq, grad_cross_bq, grad_query_in = linear_back(query_in, cross_back[0], grad_cq)
    grad_cross_wk = matmul_left(image_rows, grad_ck)
    grad_cross_wv = matmul_left(image_rows, grad_cv)
    grad_cross_bv = column_sum(grad_cv)
    grad_query_rows = grad_summed_two + grad_query_in
    cross_list = [
        grad_cross_wq,
        grad_cross_wk,
        grad_cross_wv,
        grad_cross_wo,
        grad_cross_bq,
        grad_cross_bv,
        grad_cross_bo,
        grad_gain_two,
        grad_shift_two,
    ]
    cross_flat_grad = join_flat(cross_list, cross_full.shape[0])
    cross_grad = lax.psum_scatter(
        regroup(cross_flat_grad), ("dp", "fsdp"), scatter_dimension=0, tiled=True
    )
    self_back = split_flat(lax.all_gather(self_params, "fsdp", axis=0, tiled=True), self_layout())
    grad_first = jnp.concatenate(
        [grad_query_rows.reshape(items, NQ, width), grad_text.reshape(items, -1, width)], 1
    ).reshape(-1, width)
    grad_summed_one, grad_gain_one, grad_shift_one = norm_backward(
        summed_one, self_back[7], self_back[8], grad_first
    )
    grad_attn = grad_summed_one.astype(jnp.bfloat16)
    grad_w_o, grad_b_o, grad_ctx = linear_back(context_low, self_back[3], grad_attn)
    grad_q, grad_k, grad_v = attend_back(
        heads(query_low, items),
        heads(key_low, items),
        heads(value_low, items),
        allowed,
        self_top,
        heads(grad_ctx.astype(jnp.bfloat16), items),
    )
    grad_q = grad_q.reshape(-1, width).astype(jnp.bfloat16)
    grad_k = grad_k.reshape(-1, width).astype(jnp.bfloat16)
    grad_v = grad_v.reshape(-1, width).astype(jnp.bfloat16)
    grad_w_q, grad_b_q, input_from_q = linear_back(inputs, self_back[0], grad_q)
    grad_w_k = matmul_left(inputs, grad_k)
    input_from_k = matmul_right(grad_k, self_back[1])
    grad_w_v, grad_b_v, input_from_v = linear_back(inputs, self_back[2], grad_v)
    hidden_grad = (
        (grad_summed_one + input_from_q + input_from_k + input_from_v)
        .reshape(items, seq, width)
        .astype(jnp.bfloat16)
    )
    self_list = [
        grad_w_q,
        grad_w_k,
        grad_w_v,
        grad_w_o,
        grad_b_q,
        grad_b_v,
        grad_b_o,
        grad_gain_one,
        grad_shift_one,
    ]
    self_flat_grad = join_flat(self_list, self_full.shape[0])
    self_grad = lax.psum_scatter(
        regroup(self_flat_grad), ("dp", "fsdp"), scatter_dimension=0, tiled=True
    )
    self_grad, cross_grad, ffn_grad = (
        lax.all_gather(self_grad.astype(jnp.bfloat16), "dp", axis=0, tiled=True).astype(
            self_grad.dtype
        ),
        lax.all_gather(cross_grad.astype(jnp.bfloat16), "dp", axis=0, tiled=True).astype(
            cross_grad.dtype
        ),
        lax.all_gather(ffn_grad.astype(jnp.bfloat16), "dp", axis=0, tiled=True).astype(
            ffn_grad.dtype
        ),
    )
    return (mixed, hidden_grad, self_grad, cross_grad, ffn_grad)


MESH = pl.DeviceIdType.MESH
BF = jnp.bfloat16
F32 = jnp.float32
VMEM_BYTES = 62 * 2**20


def place():
    f = lax.axis_index("fsdp")
    return lax.axis_index("dp"), f // 4, (f // 2) % 2, f % 2


def device(x, z, y, c):
    return (x, (z * 2 + y) * 2 + c)


def shift_back():
    f = lax.axis_index("fsdp")
    return 2 * f, 2 * f, 6 * (f % 4) + jnp.where(f >= 8, 6, 0)


def remote(src, dst, send, recv, target):
    return pltpu.make_async_remote_copy(
        src_ref=src,
        dst_ref=dst,
        send_sem=send,
        recv_sem=recv,
        device_id=target,
        device_id_type=MESH,
    )


def mm(a, b):
    return jnp.dot(a, b, preferred_element_type=F32)


def mm_nt(a, b):
    return lax.dot_general(a, b, (((1,), (1,)), ((), ())), preferred_element_type=F32)


def mm_tn(a, b):
    return lax.dot_general(a, b, (((0,), (0,)), ((), ())), preferred_element_type=F32)


def rows_sum(v):
    return jnp.sum(v.astype(F32), 0, keepdims=True)


def add(a, b):
    return (a.astype(F32) + b.astype(F32)).astype(BF)


def normed(v):
    centered = v - jnp.mean(v, -1, keepdims=True)
    r = lax.rsqrt(jnp.mean(centered * centered, -1, keepdims=True) + EPS)
    return centered * r, r


def norm_back(v, gain, g_out):
    xh, r = normed(v)
    gg = g_out * gain
    dv = r * (gg - jnp.mean(gg, -1, keepdims=True) - xh * jnp.mean(gg * xh, -1, keepdims=True))
    return dv, rows_sum(g_out * xh), rows_sum(g_out)


GELU_A = math.sqrt(2.0 / math.pi)
GELU_B = 0.044715


def gelu(v):
    return 0.5 * v * (1.0 + jnp.tanh(GELU_A * (v + GELU_B * (v * v * v))))


def gelu_slope(v):
    t = jnp.tanh(GELU_A * (v + GELU_B * (v * v * v)))
    return 0.5 * (1.0 + t) + 0.5 * v * (1.0 - t * t) * (GELU_A * (1.0 + 3.0 * GELU_B * (v * v)))


def head_mask(h):
    lane = lax.broadcasted_iota(jnp.int32, (1, 256), 1)
    return jnp.where(lane // HDIM == h, 1.0, 0.0)


def spread(rows):
    wide = rows.astype(F32)
    return jnp.concatenate([(wide * head_mask(h)).astype(BF) for h in range(4)], 0)


def fold(stacked):
    n = stacked.shape[0] // 4
    total = stacked[:n] * head_mask(0)
    for h in range(1, 4):
        total = total + stacked[h * n : (h + 1) * n] * head_mask(h)
    return total


def attend_block(q, k, v, allowed):
    s = mm_nt(spread(q), k) * SCALE
    s = jnp.where(allowed > 0.5, s, -1e30)
    e = jnp.exp(s - jnp.max(s, -1, keepdims=True))
    p = e / jnp.sum(e, -1, keepdims=True)
    return p, fold(mm(p.astype(BF), v)).astype(BF)


def attend_block_back(q, k, v, p, da):
    dax = spread(da)
    dp = mm_nt(dax, v)
    ds = (p * (dp - jnp.sum(p * dp, -1, keepdims=True))).astype(BF)
    dq = (fold(mm(ds, k)) * SCALE).astype(BF)
    dk = (mm_tn(ds, spread(q)) * SCALE).astype(BF)
    dv = mm_tn(p.astype(BF), dax).astype(BF)
    return dq, dk, dv


def rows_of(ref, first):
    return jnp.concatenate([ref[first : first + 32], ref[64 + first : 96 + first]], 0)


SPLIT = 192
REST = 384 - SPLIT
X_FIRST = (True, False)
SIDE = tuple((2, 4) if first else (4,) for first in X_FIRST)
WIDTH = tuple(384 if first else 768 for first in X_FIRST)
STREAMS = ((192, 384), (272, 384), (SPLIT, D), (REST, D), (REST, D))


def scratch():
    dma = lambda *s: pltpu.SemaphoreType.DMA(s)
    b = lambda *s: pltpu.VMEM(s, BF)
    f = lambda *s: pltpu.VMEM(s, F32)
    return dict(
        ws=b(4, D, D), wc=b(4352, D), wf=b(4, D, D), theirs=b(192, D), own_t=b(16, D), tb=b(4, 16, D), before=b(96, 128),
        tv=f(4, 16, D), vg=f(4, 16, D),
        flat_c=b(1634, 128), flat_f=b(4614, 128), hid=b(128, D), feat=b(2, 257, E), cot=b(128, D), in_sem=dma(5),
        tails=b(96, 128),
        q=b(128, D), k=b(128, D), v=b(128, D), a=b(128, D), p=f(2, 3, 256, 64),
        sum1=f(128, D), first=f(128, D), cq=b(64, D), ck=b(544, D), cv=b(544, D), ca=b(64, D),
        pc=f(2, 3, 128, 272), sum2=f(64, D), second=f(64, D),
        xg=b(2, 2, 4, 64, D), pre=f(2, 256, D), act=b(2, 256, D), part=f(2, 4, 64, D),
        send_p=b(2, 2, 2, 64, D), recv_p=b(2, 2, 2, 64, D), send_x=b(2, 2, 64, D), recv_x=b(2, 2, 64, D),
        sum3=f(2, 64, D), dpre=b(2, 256, D), dsum3=f(2, 64, D), dfirst=f(128, D),
        core_s=b(2, 4, 192, D), core_c=b(2, 4, 272, D), xs=b(*SIDE[0], 192, 384), xc=b(*SIDE[1], 272, 384),
        ys=b(4, 192, WIDTH[0]), yc=b(4, 272, WIDTH[1]), yf=b(4, SPLIT, D), yf2=b(REST, D), of=b(REST, D),
        fin_s=b(192, 384), fin_c=b(272, 384), fin_f=b(384, D),
        **{f"{n}{i}": b(*lead, *shape) for i, shape in enumerate(STREAMS) for n, lead in (("zb", (3,)), ("zr", ()))},
        v_send=b(4, 16, D), v_in=b(3, 4, 16, D), v_z=b(4, 16, D), v_zin=b(3, 16, D), v_x=b(16, D), v_xin=b(16, D),
        nice_s=b(192, D), nice_c=b(272, D), nice_f=b(4, 192, D), total_v=b(16, D), heads=b(3, 32, 128), after=b(3, 32, 128),
        loc=dma(1), tail_s=dma(1), tail_r=dma(1), head_s=dma(3), head_r=dma(3), gz_s=dma(7, 4), gz_r=dma(7, 4), gy_s=dma(7, 4), gy_r=dma(7, 4), gx_s=dma(2, 7), gx_r=dma(2, 7),
        gc_s=dma(3, 15), gc_r=dma(3, 15), t_s=dma(6), t_r=dma(4),
        ex_s=dma(2, 2, 3), ex_r=dma(2, 2, 3), rs_s=dma(2, 2, 3), rs_r=dma(2, 2, 3),
        co_s=dma(2, 2, 4), co_r=dma(2, 2, 4), xx_s=dma(2, 2, 4), xx_r=dma(2, 2, 4), yy_s=dma(4, 4), yy_r=dma(4, 4),
        zz_s=dma(5, 4), zz_r=dma(5, 4), zq_s=dma(5), zq_r=dma(5), fi_s=dma(5), fi_r=dma(5), vv_s=dma(5), vv_r=dma(7),
    )


def layer_kernel(*refs):
    names = [
        "flat_s", "in_c", "in_f", "lens", "in_hid", "in_feat", "in_cot",
        "mixed", "hgrad", "out_s", "out_c", "out_f",
    ] + list(scratch())
    r = SimpleNamespace(**dict(zip(names, refs)))
    x, z, y, c = place()
    core, xn, yn = device(x, z, y, 1 - c), device(1 - x, z, y, c), device(x, z, 1 - y, c)
    diag = device(1 - x, z, y, 1 - c)
    zdev = lambda d: device(x, (z + d) % 4, y, c)
    f = lax.axis_index("fsdp")
    following, preceding = (x, (f + 1) % 16), (x, (f + 15) % 16)
    loads = SimpleNamespace(**{
        n: pltpu.make_async_copy(getattr(r, f"in_{n[-1]}" if n[:4] == "flat" else f"in_{n}"), getattr(r, n), r.in_sem.at[i])
        for i, n in enumerate(("flat_c", "flat_f", "hid", "feat", "cot"))
    })
    for load in vars(loads).values():
        load.start()
    near = [core, xn, yn, diag, device(x, z, 1 - y, 1 - c), zdev(1), zdev(2), zdev(3), following, preceding]
    barrier = pltpu.get_barrier_semaphore()
    for d in near:
        pl.semaphore_signal(barrier, inc=1, device_id=d, device_id_type=MESH)
    me = 2 * c + x
    cols = lambda h: pl.ds(pl.multiple_of(384 * h, 384), 384)
    root = jnp.logical_and(y == 1, c == 1)
    w1 = z % 2 == 0

    inner = jnp.logical_and(z > 0, z < 3)
    outer = jnp.logical_not(inner)

    def when(cond, what):
        if cond is None:
            what()
        else:
            pl.when(cond)(what)

    def go(sent, src, dst, send, recv, target, cond=None):
        make = lambda: remote(src, dst, send, recv, target)
        when(cond, lambda: make().start())
        sent.append((make, cond))

    def arrived(view, recv):
        remote(view, view, recv, recv, core).wait_recv()

    def drain(sent):
        for make, cond in sent:
            when(cond, lambda: make().wait_send())

    def shard_s(zz, yy, cc):
        return r.ws.at[zz, pl.ds(pl.multiple_of(192 * (2 * yy + cc), 192), 192)]

    def shard_c(zz, yy, cc):
        return r.wc.at[pl.ds(pl.multiple_of(272 * ((zz * 2 + yy) * 2 + cc), 16), 272)]

    def part_f(zz, yy, lo=0, n=384):
        return r.wf.at[zz, pl.ds(pl.multiple_of(384 * yy + lo, 16), n)]

    shards = (shard_s, shard_c)
    sent_w, sent_f = ([], []), ([], [])
    steps = [jnp.where(z == 0, 3 - i, jnp.where(z == 3, 1 + i, (2, 1, 3)[i])) for i in range(3)]

    def part(g, zz, yy, cc, h):
        if g >= 2:
            return part_f(zz, yy, 96 * (g - 2), 96)
        view = shards[g](zz, yy, cc)
        return view if h is None else view.at[:, cols(h)]

    def own_part(g):
        return part(g, z, y, c, x)

    def both(a, b):
        return a if b is None else b if a is None else jnp.logical_and(a, b)

    branch = (z < 2, z >= 2)

    def sent_of(g, b):
        return sent_w[g] if g < 2 else sent_f[b]

    def z_out(src, dst, g, i, b=None):
        for k in (2, 1, 3):
            cond = both({1: z != 3, 2: None, 3: z != 0}[k], None if b is None else branch[b])
            go(sent_of(g, b), src, dst, r.gz_s.at[i, k], r.gz_r.at[i, k], zdev(k), cond)

    def z_on(view, g, k):
        cond = jnp.logical_and(inner, k == 2)
        go(sent_w[g], view, view, r.gz_s.at[g, 0], r.gz_r.at[g, 2 * z - 1], device(x, 3 * (z - 1), y, c), cond)

    def own_z(g, b=None):
        z_out(own_part(g), part(g, z, y, c, x), g, g, b)

    def own_y(g, b=None):
        cond = None if b is None else branch[b]
        go(sent_of(g, b), own_part(g), part(g, z, y, c, x), r.gy_s.at[g, 0], r.gy_r.at[g, 0], yn, cond)

    def own_core(g):
        own = part(g, z, y, c, None)
        go(sent_w[g], own, own, r.gc_s.at[g, 0], r.gc_r.at[g, 0], core)

    def gather_z(g, i):
        k = steps[i]
        view = part(g, (z - k) % 4, y, c, x)
        arrived(view, r.gz_r.at[g, k])
        z_on(view, g, k)
        go(sent_w[g], view, view, r.gy_s.at[g, k], r.gy_r.at[g, k], yn)
        go(sent_w[g], view, view, r.gx_s.at[g, k - 1], r.gx_r.at[g, k - 1], xn)
        go(sent_w[g], view, view, r.gc_s.at[g, k], r.gc_r.at[g, k], core)

    def gather_y(g, j):
        view = part(g, (z - j) % 4, 1 - y, c, x)
        arrived(view, r.gy_r.at[g, j])
        go(sent_w[g], view, view, r.gx_s.at[g, 3 + j], r.gx_r.at[g, 3 + j], xn)
        go(sent_w[g], view, view, r.gc_s.at[g, 4 + j], r.gc_r.at[g, 4 + j], core)

    def ffn_z(g, p, other=False):
        i = 6 if other else g
        view = part(g, p, 1 - y if other else y, c, x)
        b = p // 2
        k = (z - p) % 4

        @pl.when(z != p)
        def _():
            arrived(view, r.gz_r.at[i, k])

        if p in (0, 3):
            at, to, slot_at = (2, 3, 3) if p == 0 else (1, 0, 1)
            go(sent_f[b], view, view, r.gz_s.at[i, 0], r.gz_r.at[i, slot_at], device(x, to, y, c), z == at)
        if g < 5:
            go(sent_f[b], view, view, r.gy_s.at[g, k], r.gy_r.at[g, k], yn, z != p)

    def ffn_y(g, p):
        arrived(part(g, p, 1 - y, c, x), r.gy_r.at[g, (z - p) % 4])

    def other_z(b):
        view = part(5, z, 1 - y, c, x)

        @pl.when(branch[b])
        def _():
            arrived(view, r.gy_r.at[5, 0])

        z_out(view, view, 5, 6, b)

    def gather_x(g):
        for j in range(7):
            view = part(g, (z - j - 1) % 4, y, c, 1 - x) if j < 3 else part(g, (z - j + 3) % 4, 1 - y, c, 1 - x)
            arrived(view, r.gx_r.at[g, j])
            go(sent_w[g], view, view, r.gc_s.at[g, 8 + j], r.gc_r.at[g, 8 + j], core)

    def gather_core(g, which):
        for j in which:
            if j == 0:
                view = part(g, z, y, 1 - c, None)
            elif j < 4:
                view = part(g, (z - j) % 4, y, 1 - c, x)
            elif j < 8:
                view = part(g, (z - j + 4) % 4, 1 - y, 1 - c, x)
            elif j < 11:
                view = part(g, (z - j + 7) % 4, y, 1 - c, 1 - x)
            else:
                view = part(g, (z - j + 11) % 4, 1 - y, 1 - c, 1 - x)
            arrived(view, r.gc_r.at[g, j])

    tail = remote(r.tails, r.before, r.tail_s.at[0], r.tail_r.at[0], following)
    back = shift_back()

    def one_hot(shape, pick):
        row = lax.broadcasted_iota(jnp.int32, shape, 0)
        col = lax.broadcasted_iota(jnp.int32, shape, 1)
        return jnp.where(col == pick(row), 1.0, 0.0).astype(BF)

    def to_rows(g):
        return one_hot((96, 128), lambda i: 32 - back[g] + 6 * (i % 16) + i // 16)

    def store_rows(dst, row, tiles, n=6):
        for j in range(n):
            dst[pl.ds(pl.multiple_of(row, 16), 16), 128 * j : 128 * j + 128] = tiles[16 * j : 16 * j + 16]

    def first_window(g, flat, n):
        return jnp.concatenate([r.before[32 * g : 32 * g + 32], flat[0:n]], 0)

    def lay_rows(perm, flat, dst, n):
        def body(i, carry):
            window = flat[pl.ds(pl.multiple_of(96 * i - 32, 32), 128)]
            store_rows(dst, 16 * i, mm(perm, window).astype(BF))
            return carry

        lax.fori_loop(1, n, body, 0)

    tail_v = one_hot(
        (96, 96),
        lambda i: jnp.where(
            i % 16 < 5,
            6 * (i % 16) + i // 16,
            jnp.where(
                i % 16 < 10,
                32 + 6 * (i % 16 - 5) + i // 16,
                jnp.where(z < 2, 72, 66)
                + jnp.where(
                    z % 2 == 0,
                    12 * (i // 48) + 3 * (i % 16 - 10) + (i // 16) % 3,
                    6 * (i % 16 - 10) + i // 16,
                ),
            ),
        ),
    )
    mine_s, mine_c = part(0, z, y, c, None), part(1, z, y, c, None)

    perm_sc = to_rows(0)

    def rows_first(g, flat, dst):
        store_rows(dst, 0, mm(perm_sc, first_window(g, flat, 96)).astype(BF))

    def rows_f():
        @pl.when(w1)
        def _():
            def pick(i):
                m, j = i % 16, i // 16
                q = 2 * jnp.where(j < 6, c, 1 - c) + x
                j = j % 6
                return 32 - back[2] + 24 * m + 12 * (j // 3) + 3 * q + j % 3

            perm = one_hot((192, 416), pick)
            mine = part_f(z, y, 192 * c, 192)

            def put(i, window):
                tiles = mm(perm, window).astype(BF)
                store_rows(r.theirs, 16 * i, tiles[96:192])
                store_rows(mine, 16 * i, tiles[0:96])

            def body(i, carry):
                put(i, r.flat_f[pl.ds(pl.multiple_of(384 * i - 32, 32), 416)])
                return carry

            put(0, first_window(2, r.flat_f, 384))
            lax.fori_loop(1, 12, body, 0)
            swap = remote(r.theirs, mine, r.gc_s.at[2, 0], r.gc_r.at[2, 0], core)
            swap.start()
            swap.wait()

        @pl.when(jnp.logical_not(w1))
        def _():
            perm = to_rows(2)
            mine = part_f(z, y)

            def body(i, carry):
                window = r.flat_f[pl.ds(pl.multiple_of(2304 * x + 96 * i - 32, 32), 128)]
                store_rows(mine, 16 * i, mm(perm, window).astype(BF))
                return carry

            lax.fori_loop(1, 24, body, 0)
            lead = jnp.where(x == 0, r.before[64:96], r.flat_f[2304 - 32 : 2304])
            rest = r.flat_f[pl.ds(pl.multiple_of(2304 * x, 32), 96)]
            store_rows(mine, 0, mm(perm, jnp.concatenate([lead, rest], 0)).astype(BF))

    def vectors_out():
        @pl.when(root)
        def _():
            own = pltpu.make_async_copy(r.own_t, r.tb.at[z], r.loc.at[0])
            own.start()
            for k in (1, 2, 3):
                remote(r.own_t, r.tb.at[z], r.t_s.at[k - 1], r.t_r.at[k], zdev(k)).start()
            own.wait()

    def vectors_on():
        @pl.when(root)
        def _():
            for k in (1, 2, 3):
                arrived(r.tb.at[(z - k) % 4], r.t_r.at[k])
            out = []
            for i, (yy, cc) in enumerate(((0, 0), (0, 1), (1, 0))):
                go(out, r.tb, r.tb, r.t_s.at[3 + i], r.t_r.at[0], device(x, z, yy, cc))
            drain(out)
            for k in (1, 2, 3):
                remote(r.own_t, r.tb.at[z], r.t_s.at[k - 1], r.t_r.at[k], zdev(k)).wait_send()

    def vectors_in():
        @pl.when(jnp.logical_not(root))
        def _():
            arrived(r.tb, r.t_r.at[0])

        r.tv[...] = r.tb[...].astype(F32)
        r.vg[...] = jnp.zeros_like(r.vg)

    self_v = lambda j: r.tv[3, j : j + 1]
    cross_v = lambda j: r.tv[3, 5 + j : 6 + j]
    ffn_b1 = lambda b: r.tv[2 * b, pl.ds(10 + me, 1)]
    ffn_v = lambda b, j: r.tv[2 * b + 1, 10 + j : 11 + j]

    def slot(xx, cc):
        return 2 * cc + xx

    def ag_copy(ph, b, i):
        buf = r.xg.at[ph, b]
        pair = [(me, xn), (me, core), (slot(1 - x, c), core)]
        s, t = pair[i]
        return remote(buf.at[s], buf.at[s], r.ex_s.at[ph, b, i], r.ex_r.at[ph, b, i], t)

    def ag_start(ph, b):
        ag_copy(ph, b, 0).start()
        ag_copy(ph, b, 1).start()

    def ag_mid(ph, b):
        ag_copy(ph, b, 0).wait_recv()
        ag_copy(ph, b, 2).start()

    def ag_end(ph, b):
        ag_copy(ph, b, 1).wait_recv()
        ag_copy(ph, b, 2).wait_recv()
        for i in range(3):
            ag_copy(ph, b, i).wait_send()

    def rs_copy(ph, b, i):
        src = r.send_x.at[ph, b] if i == 2 else r.send_p.at[ph, b, i]
        dst = r.recv_x.at[ph, b] if i == 2 else r.recv_p.at[ph, b, i]
        return remote(src, dst, r.rs_s.at[ph, b, i], r.rs_r.at[ph, b, i], xn if i == 2 else core)

    def rs_start(ph, b):
        r.send_p[ph, b, 0] = r.part[b, slot(1 - x, 1 - c)].astype(BF)
        rs_copy(ph, b, 0).start()
        r.send_p[ph, b, 1] = r.part[b, slot(x, 1 - c)].astype(BF)
        rs_copy(ph, b, 1).start()

    def rs_mid(ph, b):
        rs_copy(ph, b, 0).wait_recv()
        r.send_x[ph, b] = (r.part[b, slot(1 - x, c)] + r.recv_p[ph, b, 0].astype(F32)).astype(BF)
        rs_copy(ph, b, 2).start()

    def rs_end(ph, b):
        rs_copy(ph, b, 1).wait_recv()
        rs_copy(ph, b, 2).wait_recv()
        for i in range(3):
            rs_copy(ph, b, i).wait_send()
        return r.part[b, me] + r.recv_p[ph, b, 1].astype(F32) + r.recv_x[ph, b].astype(F32)

    keep = SimpleNamespace()

    def self_attention():
        h = r.hid[...]
        r.q[...] = (mm(h, r.ws[0]) + self_v(0)).astype(BF)
        r.k[...] = mm(h, r.ws[1]).astype(BF)
        r.v[...] = (mm(h, r.ws[2]) + self_v(1)).astype(BF)
        for i in range(2):
            rows = slice(64 * i, 64 * i + 64)
            at = lax.broadcasted_iota(jnp.int32, (256, 64), 0) % 64
            key = lax.broadcasted_iota(jnp.int32, (256, 64), 1)
            caption = jnp.where(at >= NQ, 1.0, 0.0) * jnp.where(key <= at, 1.0, 0.0)
            ok = jnp.where(key < NQ, 1.0, caption * jnp.where(key < NQ + r.lens[i], 1.0, 0.0))
            for g in range(3):
                lanes = slice(256 * g, 256 * g + 256)
                p, a = attend_block(r.q[rows, lanes], r.k[rows, lanes], r.v[rows, lanes], ok)
                r.p[i, g] = p
                r.a[rows, lanes] = a
        r.sum1[...] = h.astype(F32) + (mm(r.a[...], r.ws[3]) + self_v(2))
        xh, _ = normed(r.sum1[...])
        r.first[...] = xh * self_v(3) + self_v(4)
        r.xg[0, 1, me] = rows_of(r.first, 32).astype(BF)

    def image_rows(lanes):
        for i in range(2):
            rows = slice(272 * i, 272 * i + 257)
            r.ck[rows, lanes] = mm(r.feat[i], r.wc[768:2176, lanes]).astype(BF)
            bias = r.tv[3, 6:7, lanes]
            r.cv[rows, lanes] = (mm(r.feat[i], r.wc[2176:3584, lanes]) + bias).astype(BF)

    def pad_rows():
        for i in range(2):
            r.ck[272 * i + 256 : 272 * i + 272] = jnp.zeros((16, D), BF)
            r.cv[272 * i + 256 : 272 * i + 272] = jnp.zeros((16, D), BF)

    def cross_start():
        keep.u = rows_of(r.first, 0)
        r.cq[...] = (mm(keep.u.astype(BF), r.wc[0:768]) + cross_v(0)).astype(BF)

    def cross_attention(i):
        ok = jnp.where(lax.broadcasted_iota(jnp.int32, (128, 272), 1) < 257, 1.0, 0.0)
        rows = slice(272 * i, 272 * i + 272)
        mine = slice(32 * i, 32 * i + 32)
        for g in range(3):
            lanes = slice(256 * g, 256 * g + 256)
            p, a = attend_block(r.cq[mine, lanes], r.ck[rows, lanes], r.cv[rows, lanes], ok)
            r.pc[i, g] = p
            r.ca[mine, lanes] = a

    def cross_end():
        r.sum2[...] = keep.u + (mm(r.ca[...], r.wc[3584:4352]) + cross_v(2))
        xh, _ = normed(r.sum2[...])
        r.second[...] = xh * cross_v(3) + cross_v(4)
        r.xg[0, 0, me] = r.second[...].astype(BF)

    sent = []

    def ffn_forward_part(b):
        rows = r.xg[0, b].reshape(256, D)
        r.pre[b] = mm(rows, r.wf[2 * b]) + ffn_b1(b)
        r.act[b] = gelu(r.pre[b]).astype(BF)
        r.part[b] = mm(r.act[b], r.wf[2 * b + 1]).reshape(4, 64, D)

    def ffn_turn(b):
        rows = r.second[...] if b == 0 else rows_of(r.first, 32)
        s3 = rows + (rs_end(0, b) + ffn_v(b, 0))
        xh, _ = normed(s3)
        done = (xh * ffn_v(b, 1) + ffn_v(b, 2)).astype(BF)
        for i in range(2):
            r.mixed[64 * i + 32 * b : 64 * i + 32 * b + 32] = done[32 * i : 32 * i + 32]
        g_out = rows_of(r.cot, 32 * b).astype(F32)
        dsum, dgain, dshift = norm_back(s3, ffn_v(b, 1), g_out)
        r.dsum3[b] = dsum
        low = dsum.astype(BF)
        r.xg[1, b, me] = low
        r.vg[2 * b + 1, 10:11] = rows_sum(low)
        r.vg[2 * b + 1, 11:12] = dgain
        r.vg[2 * b + 1, 12:13] = dshift

    def ffn_backward_part(b):
        up = r.xg[1, b].reshape(256, D)
        r.dpre[b] = (mm_nt(up, r.wf[2 * b + 1]) * gelu_slope(r.pre[b])).astype(BF)
        r.part[b] = mm_nt(r.dpre[b], r.wf[2 * b]).reshape(4, 64, D)
        db1 = rows_sum(r.dpre[b])
        for j in range(4):
            r.vg[2 * b, 10 + j : 11 + j] = jnp.where(j == me, db1, 0.0)

    def ffn_weight_grads(b):
        drain(sent_f[b])
        rows = r.xg[0, b].reshape(256, D)
        up = r.xg[1, b].reshape(256, D)
        r.wf[2 * b] = mm_tn(rows, r.dpre[b]).astype(BF)
        r.wf[2 * b + 1] = mm_tn(r.act[b], up).astype(BF)

    def ffn_sum_start(b):
        for p in (2 * b, 2 * b + 1):
            go(sent, part_f(p, 1 - y, 0, SPLIT), r.yf.at[p], r.yy_s.at[2, p], r.yy_r.at[2, p], yn)
        for p in (2 * b, 2 * b + 1):
            for i, yy in ((4, 1 - y), (3, y)):
                z_out_sum(i, part_f(p, yy, SPLIT, REST), p)

    hop = jnp.where(z < 2, 1, 2)

    def z_out_sum(i, src, p):
        zb, zr = getattr(r, f"zb{i}"), getattr(r, f"zr{i}")
        d = (p - z) % 4
        far = {0: z == 3, 3: z == 0}.get(p)
        later = {0: z == 2, 3: z == 1}.get(p)
        direct = z != p
        if far is not None:
            go(sent, src, zr, r.zq_s.at[i], r.zq_r.at[i], device(x, hop, y, c), far)
            direct = jnp.logical_and(direct, jnp.logical_not(jnp.logical_or(far, later)))
        go(sent, src, zb.at[d - 1], r.zz_s.at[i, p], r.zz_r.at[i, d], device(x, p, y, c), direct)

    def z_add_sum(i, src, p):
        later = {0: z == 2, 3: z == 1}.get(p)
        if later is None:
            return
        zb, zr = getattr(r, f"zb{i}"), getattr(r, f"zr{i}")

        @pl.when(later)
        def _():
            arrived(zr, r.zq_r.at[i])
            zr[...] = add(zr[...], src[...])

        go(sent, zr, zb.at[1], r.zz_s.at[i, p], r.zz_r.at[i, 2], device(x, p, y, c), later)

    def z_total(i, own, out):
        zb = getattr(r, f"zb{i}")
        arrived(zb.at[1], r.zz_r.at[i, 2])
        out[...] = add(own, zb[1])
        for d, without in ((1, 0), (3, 3)):

            @pl.when(z != without)
            def _():
                arrived(zb.at[d - 1], r.zz_r.at[i, d])
                out[...] = add(out[...], zb[d - 1])

    def ffn_sum_y(p):
        arrived(r.yf.at[p], r.yy_r.at[2, p])
        r.yf[p] = add(r.yf[p], part_f(p, y, 0, SPLIT)[...])
        z_out_sum(2, r.yf.at[p], p)

    def ffn_add(p):
        for i, yy in ((4, 1 - y), (3, y)):
            z_add_sum(i, part_f(p, yy, SPLIT, REST), p)

    def ffn_sum_other():
        z_total(4, part_f(z, 1 - y, SPLIT, REST)[...], r.of)
        go(sent, r.of, r.yf2, r.yy_s.at[3, 0], r.yy_r.at[3, 0], yn)

    groups = (
        (shard_s, r.core_s, r.xs, r.ys, r.fin_s, r.nice_s),
        (shard_c, r.core_c, r.xc, r.yc, r.fin_c, r.nice_c),
    )
    order = (3, 1, 2, 0)

    def sum_start(g, far):
        view, cb = groups[g][:2]
        for d in order:
            zz = (z + d) % 4
            go(sent, view(zz, y if far else 1 - y, 1 - c), cb.at[far, zz], r.co_s.at[g, far, d], r.co_r.at[g, far, d], core)

    def sum_core(g, fars=(0, 1)):
        view, cb, xb, yb = groups[g][:4]
        for far in fars:
            for d in order:
                zz = (z + d) % 4
                arrived(cb.at[far, zz], r.co_r.at[g, far, d])
                cb[far, zz] = add(cb[far, zz], view(zz, y if far else 1 - y, c)[...])
                if X_FIRST[g]:
                    go(sent, cb.at[far, zz, :, cols(1 - x)], xb.at[far, zz], r.xx_s.at[g, far, d], r.xx_r.at[g, far, d], xn)
                elif far == 0:
                    go(sent, cb.at[0, zz], yb.at[zz], r.yy_s.at[g, d], r.yy_r.at[g, d], yn)

    def sum_mid(g, fars=(0, 1)):
        view, cb, xb, yb = groups[g][:4]
        for far in fars if X_FIRST[g] else (0,):
            for d in order:
                zz = (z + d) % 4
                if X_FIRST[g]:
                    arrived(xb.at[far, zz], r.xx_r.at[g, far, d])
                    xb[far, zz] = add(xb[far, zz], cb[far, zz, :, cols(x)])
                    if far == 0:
                        go(sent, xb.at[0, zz], yb.at[zz], r.yy_s.at[g, d], r.yy_r.at[g, d], yn)
                else:
                    arrived(yb.at[zz], r.yy_r.at[g, d])
                    yb[zz] = add(yb[zz], cb[1, zz])
                    go(sent, yb.at[zz, :, cols(1 - x)], xb.at[zz], r.xx_s.at[g, 0, d], r.xx_r.at[g, 0, d], xn)

    def to_z(g, mine, d):
        zb, zr = getattr(r, f"zb{g}"), getattr(r, f"zr{g}")
        if d == 2:

            @pl.when(inner)
            def _():
                arrived(zr, r.zq_r.at[g])
                zr[...] = add(zr[...], mine[...])

            go(sent, zr, zb.at[1], r.zz_s.at[g, 2], r.zz_r.at[g, 2], zdev(2), inner)
            go(sent, mine, zb.at[1], r.zz_s.at[g, 2], r.zz_r.at[g, 2], zdev(2), outer)
        elif d:
            far = z == (0 if d == 3 else 3)
            go(sent, mine, zr, r.zq_s.at[g], r.zq_r.at[g], device(x, hop, y, c), far)
            go(sent, mine, zb.at[d - 1], r.zz_s.at[g, d], r.zz_r.at[g, d], zdev(d), jnp.logical_not(far))

    def sum_last(g):
        view, cb, xb, yb = groups[g][:4]
        for d in order:
            zz = (z + d) % 4
            if X_FIRST[g]:
                arrived(yb.at[zz], r.yy_r.at[g, d])
                yb[zz] = add(yb[zz], xb[1, zz])
                to_z(g, yb.at[zz], d)
            else:
                arrived(xb.at[zz], r.xx_r.at[g, 0, d])
                xb[zz] = add(xb[zz], yb[zz, :, cols(x)])
                to_z(g, xb.at[zz], d)

    def sum_z(g):
        view, cb, xb, yb, fin, out = groups[g]
        z_total(g, yb[z] if X_FIRST[g] else xb[z], fin)
        out[:, cols(x)] = fin[...]
        go(sent, fin, out.at[:, cols(x)], r.fi_s.at[g], r.fi_r.at[g], xn)

    def ffn_sum_z():
        z_total(2, r.yf[z], r.fin_f.at[0:SPLIT])
        last = r.fin_f.at[SPLIT:384]
        z_total(3, part_f(z, y, SPLIT, REST)[...], last)
        arrived(r.yf2, r.yy_r.at[3, 0])
        last[...] = add(last[...], r.yf2[...])
        half = lambda j: r.fin_f.at[pl.ds(pl.multiple_of(192 * j, 192), 192)]

        @pl.when(w1)
        def _():
            r.nice_f[me] = half(c)[...]
            remote(half(c), r.nice_f.at[me], r.fi_s.at[2], r.fi_r.at[2], xn).start()
            remote(half(1 - c), r.nice_f.at[me], r.fi_s.at[3], r.fi_r.at[3], core).start()
            remote(half(1 - c), r.nice_f.at[me], r.fi_s.at[4], r.fi_r.at[4], diag).start()

        @pl.when(jnp.logical_not(w1))
        def _():
            for j in range(2):
                r.nice_f[2 * x + j] = half(j)[...]
                remote(half(j), r.nice_f.at[2 * x + j], r.fi_s.at[2 + j], r.fi_r.at[2 + j], xn).start()

    def ffn_end():
        def ends(n):
            for j in range(n):
                remote(r.fin_f.at[0:192], r.nice_f.at[0], r.fi_s.at[2 + j], r.fi_r.at[2 + j], xn).wait()

        pl.when(w1)(lambda: ends(3))
        pl.when(jnp.logical_not(w1))(lambda: ends(2))

    def stack(src, row, n=6):
        return jnp.concatenate(
            [src[pl.ds(pl.multiple_of(row, 16), 16), 128 * j : 128 * j + 128] for j in range(n)], 0
        )

    to_flat = one_hot((96, 96), lambda i: 16 * (i % 6) + i // 6)

    def lay_flat(src, dst, n, base=0):
        def body(i, carry):
            dst[pl.ds(pl.multiple_of(base + 96 * i, 32), 96)] = mm(to_flat, stack(src, 16 * i)).astype(BF)
            return carry

        lax.fori_loop(0, n, body, 0)

    def head_out(g, fl):
        r.heads[g] = fl[0:32]
        go(sent, r.heads.at[g], r.after.at[g], r.head_s.at[g], r.head_r.at[g], preceding)

    def text_end():
        d_text = r.dsum3[1] + rs_end(1, 1)
        for i in range(2):
            r.dfirst[64 * i + 32 : 64 * i + 64] = d_text[32 * i : 32 * i + 32]

    def query_end():
        keep.d_second = r.dsum3[0] + rs_end(1, 0)

    def cross_back():
        du2, dgain, dshift = norm_back(r.sum2[...], cross_v(3), keep.d_second)
        r.vg[3, 8:9] = dgain
        r.vg[3, 9:10] = dshift
        low = keep.low2 = du2.astype(BF)
        r.vg[3, 7:8] = rows_sum(low)
        dca = mm_nt(low, r.wc[3584:4352]).astype(BF)
        dcq = []
        for i in range(2):
            rows = slice(272 * i, 272 * i + 272)
            mine = slice(32 * i, 32 * i + 32)
            blocks = []
            for g in range(3):
                lanes = slice(256 * g, 256 * g + 256)
                dq, dk, dv = attend_block_back(
                    r.cq[mine, lanes], r.ck[rows, lanes], r.cv[rows, lanes], r.pc[i, g], dca[mine, lanes]
                )
                blocks.append(dq)
                r.ck[rows, lanes] = dk
                r.cv[rows, lanes] = dv
            dcq.append(jnp.concatenate(blocks, 1))
        dcq = keep.dcq = jnp.concatenate(dcq, 0)
        r.vg[3, 5:6] = rows_sum(dcq)
        r.vg[3, 6:7] = rows_sum(r.cv[...])
        du = du2 + mm_nt(dcq, r.wc[0:768])
        for i in range(2):
            r.dfirst[64 * i : 64 * i + 32] = du[32 * i : 32 * i + 32]

    def cross_grads():
        drain(sent_w[1])
        r.wc[3584:4352] = mm_tn(r.ca[...], keep.low2).astype(BF)
        r.wc[0:768] = mm_tn(rows_of(r.first, 0).astype(BF), keep.dcq).astype(BF)
        for j in range(11):
            block = [r.feat[i, :, 128 * j : 128 * j + 128] for i in range(2)]
            both = lambda d: mm_tn(block[0], d[0:257]) + mm_tn(block[1], d[272:529])
            r.wc[768 + 128 * j : 896 + 128 * j] = both(r.ck).astype(BF)
            r.wc[2176 + 128 * j : 2304 + 128 * j] = both(r.cv).astype(BF)

    def self_back():
        dsum1, dgain, dshift = norm_back(r.sum1[...], self_v(3), r.dfirst[...])
        r.vg[3, 3:4] = dgain
        r.vg[3, 4:5] = dshift
        keep.dsum1 = dsum1
        low = keep.low1 = dsum1.astype(BF)
        r.vg[3, 2:3] = rows_sum(low)
        da = mm_nt(low, r.ws[3]).astype(BF)
        for i in range(2):
            rows = slice(64 * i, 64 * i + 64)
            for g in range(3):
                lanes = slice(256 * g, 256 * g + 256)
                dq, dk, dv = attend_block_back(
                    r.q[rows, lanes], r.k[rows, lanes], r.v[rows, lanes], r.p[i, g], da[rows, lanes]
                )
                r.q[rows, lanes] = dq
                r.k[rows, lanes] = dk
                r.v[rows, lanes] = dv

    def self_grads():
        drain(sent_w[0])
        r.vg[3, 0:1] = rows_sum(r.q[...])
        r.vg[3, 1:2] = rows_sum(r.v[...])
        total = keep.dsum1 + mm_nt(r.q[...], r.ws[0]) + mm_nt(r.k[...], r.ws[1]) + mm_nt(r.v[...], r.ws[2])
        r.hgrad[...] = total.astype(BF)
        r.ws[0] = mm_tn(r.hid[...], r.q[...]).astype(BF)
        r.ws[1] = mm_tn(r.hid[...], r.k[...]).astype(BF)
        r.ws[2] = mm_tn(r.hid[...], r.v[...]).astype(BF)
        r.ws[3] = mm_tn(r.a[...], keep.low1).astype(BF)

    index = 2 * y + c
    home = device(x, z, 1, 1)

    def vector_sums_out():
        r.v_send[...] = r.vg[...].astype(BF)

        @pl.when(jnp.logical_not(root))
        def _():
            remote(r.v_send, r.v_in.at[index], r.vv_s.at[0], r.vv_r.at[index], home).start()

    def vector_sums_z():
        @pl.when(root)
        def _():
            total = r.vg[...]
            for i in range(3):
                arrived(r.v_in.at[i], r.vv_r.at[i])
                total = total + r.v_in[i].astype(F32)
            r.v_z[...] = total.astype(BF)
            for k in (1, 2, 3):
                zz = (z + k) % 4
                remote(r.v_z.at[zz], r.v_zin.at[k - 1], r.vv_s.at[k], r.vv_r.at[2 + k], device(x, zz, y, c)).start()

    def vector_sums_x():
        @pl.when(root)
        def _():
            total = r.v_z[z].astype(F32)
            for k in (1, 2, 3):
                arrived(r.v_zin.at[k - 1], r.vv_r.at[2 + k])
                total = total + r.v_zin[k - 1].astype(F32)
            r.v_x[...] = total.astype(BF)
            remote(r.v_x, r.v_xin, r.vv_s.at[4], r.vv_r.at[6], xn).start()

    def vector_sums_end():
        @pl.when(root)
        def _():
            arrived(r.v_xin, r.vv_r.at[6])
            r.total_v[...] = add(r.v_x[...], r.v_xin[...])
            for k in (1, 2, 3):
                zz = (z + k) % 4
                remote(r.v_z.at[zz], r.v_zin.at[k - 1], r.vv_s.at[k], r.vv_r.at[2 + k], device(x, zz, y, c)).wait_send()
            remote(r.v_x, r.v_xin, r.vv_s.at[4], r.vv_r.at[6], xn).wait_send()

        @pl.when(jnp.logical_not(root))
        def _():
            r.total_v[...] = jnp.zeros_like(r.total_v)
            remote(r.v_send, r.v_in.at[index], r.vv_s.at[0], r.vv_r.at[index], home).wait_send()

    def flat_sc(g, nice, out, n):
        arrived(nice.at[:, cols(1 - x)], r.fi_r.at[g])
        lay_flat(nice, out, n)
        head_out(g, out)

    def flat_f():
        @pl.when(w1)
        def _():
            def pick(i):
                m, t = i // 24, i % 24
                return 96 * ((t % 12) // 3) + 16 * (3 * (t // 12) + t % 3) + m

            perm = one_hot((384, 384), pick)

            def body(i, carry):
                tiles = jnp.concatenate([stack(r.nice_f.at[q], 16 * i) for q in range(4)], 0)
                r.out_f[pl.ds(pl.multiple_of(384 * i, 128), 384)] = mm(perm, tiles).astype(BF)
                return carry

            lax.fori_loop(0, 12, body, 0)

        @pl.when(jnp.logical_not(w1))
        def _():
            for q in range(4):
                lay_flat(r.nice_f.at[q], r.out_f, 12, 1152 * q)

        head_out(2, r.out_f)

    lay_rows(perm_sc, r.flat_s, mine_s, 12)
    loads.flat_c.wait()
    loads.flat_f.wait()
    r.tails[0:32] = r.flat_s[1122:1154]
    r.tails[32:64] = r.flat_c[1602:1634]
    r.tails[64:96] = r.flat_f[4582:4614]
    pl.semaphore_wait(barrier, len(near))
    tail.start()
    store_rows(r.own_t, 0, mm(tail_v, r.tails[...]).astype(BF))
    lay_rows(perm_sc, r.flat_c, mine_c, 17)
    tail.wait_recv()
    rows_first(0, r.flat_s, mine_s)
    own_z(0)
    own_y(0)
    own_core(0)
    vectors_out()
    pad_rows()
    rows_f()
    gather_y(0, 0)
    own_y(2, 0)
    own_y(3, 1)
    gather_z(0, 0)
    rows_first(1, r.flat_c, mine_c)
    vectors_on()
    own_z(1)
    gather_z(0, 1)
    gather_z(0, 2)
    own_z(2, 0)
    own_core(1)
    own_y(2, 1)
    own_y(1)
    gather_y(0, 1)
    gather_y(0, 3)
    gather_y(0, 2)
    own_z(5, 1)
    gather_z(1, 1)
    gather_z(1, 0)
    gather_x(0)
    gather_z(1, 2)
    own_z(4, 0)
    own_z(2, 1)
    gather_y(1, 2)
    own_y(5, 0)
    gather_y(1, 0)
    ffn_z(2, 1)
    ffn_z(2, 0)
    ffn_z(5, 3)
    gather_y(1, 1)
    gather_core(0, range(15))
    own_y(4, 1)
    own_z(3, 1)
    own_y(3, 0)
    ffn_z(2, 2)
    ffn_z(5, 2)
    gather_y(1, 3)
    own_z(3, 0)
    own_y(4, 0)
    other_z(0)
    vectors_in()
    loads.hid.wait()
    self_attention()
    own_y(5, 1)
    ffn_z(3, 1)
    ffn_z(3, 2)
    own_z(4, 1)
    gather_core(1, range(8))
    loads.feat.wait()
    image_rows(cols(x))
    ffn_z(3, 3)
    ffn_z(2, 3)
    other_z(1)
    ag_start(0, 1)
    ffn_z(4, 2)
    gather_x(1)
    ffn_z(4, 3)
    ffn_z(3, 0)
    gather_core(1, range(8, 15))
    ffn_y(3, 2)
    ffn_z(5, 1, other=True)
    own_z(5, 0)
    image_rows(cols(1 - x))
    ffn_z(4, 1)
    ag_mid(0, 1)
    ffn_y(3, 3)
    cross_start()
    cross_attention(0)
    cross_attention(1)
    cross_end()
    ffn_y(4, 2)
    ffn_z(5, 3, other=True)
    ag_start(0, 0)
    ffn_z(4, 0)
    ffn_y(2, 3)
    ag_end(0, 1)
    ffn_y(3, 1)
    ffn_y(3, 0)
    ffn_y(2, 2)
    ffn_z(5, 2, other=True)
    ffn_y(2, 0)
    ffn_y(4, 3)
    ffn_forward_part(1)
    rs_start(0, 1)
    rs_mid(0, 1)
    ffn_z(5, 0, other=True)
    ffn_y(2, 1)
    ag_mid(0, 0)
    loads.cot.wait()
    ffn_turn(1)
    ag_start(1, 1)
    ffn_y(4, 1)
    ffn_y(4, 0)
    ffn_z(5, 1)
    ag_end(0, 0)
    ffn_z(5, 0)
    ffn_forward_part(0)
    rs_start(0, 0)
    ag_mid(1, 1)
    rs_mid(0, 0)
    ag_end(1, 1)
    ffn_backward_part(1)
    ffn_weight_grads(1)
    ffn_sum_start(1)
    ffn_turn(0)
    ag_start(1, 0)
    rs_start(1, 1)
    rs_mid(1, 1)
    ag_mid(1, 0)
    ag_end(1, 0)
    ffn_backward_part(0)
    rs_start(1, 0)
    text_end()
    rs_mid(1, 0)
    ffn_weight_grads(0)
    ffn_sum_start(0)
    query_end()
    cross_back()
    cross_grads()
    sum_start(1, 0)
    self_back()
    self_grads()
    vector_sums_out()
    sum_core(1, (0,))
    sum_start(0, 0)
    sum_start(0, 1)
    ffn_sum_y(0)
    sum_core(0, (0,))
    ffn_add(3)
    ffn_sum_y(3)
    ffn_sum_y(1)
    sum_core(0, (1,))
    ffn_add(0)
    ffn_sum_y(2)
    sum_start(1, 1)
    z_add_sum(2, r.yf.at[3], 3)
    ffn_sum_other()
    vector_sums_z()
    sum_mid(0, (0,))
    sum_core(1, (1,))
    z_add_sum(2, r.yf.at[0], 0)
    sum_mid(1, (0,))
    sum_last(1)
    ffn_sum_z()
    sum_mid(0, (1,))
    sum_last(0)
    vector_sums_x()
    sum_z(1)
    sum_z(0)
    ffn_end()
    flat_f()
    flat_sc(1, r.nice_c, r.out_c, 17)
    flat_sc(0, r.nice_s, r.out_s, 12)
    vector_sums_end()
    tail.wait_send()

    vectors = stack(r.total_v, 0)
    end = (f == 15, f == 15, f % 4 == 3)
    plain = lambda first: lambda i: 16 * (i % 6) + first + i // 6
    hidden = lambda i: 16 * (3 * (i // 12) + i % 3) + 10 + (i % 12) // 3
    none = -1
    count = jnp.where(w1, 24, 18)

    def from_vectors(g):
        if g < 2:
            return lambda i: jnp.where(jnp.logical_and(end[g], i < 30), plain(5 * g)(i), none)
        pick = lambda i: jnp.where(w1, hidden(i), plain(10)(i))
        return lambda i: jnp.where(jnp.logical_and(end[2], i < count), pick(i), none)

    def from_next(g):
        if g < 2:
            return lambda i: jnp.where(end[g], none, i)
        inside = jnp.logical_or(z == 1, z == 2)
        return lambda i: jnp.where(
            end[2], jnp.where(jnp.logical_and(inside, i >= count), i - count, none), i
        )

    for g, (fl, rows) in enumerate(((r.out_s, 1152), (r.out_c, 1632), (r.out_f, 4608))):
        arrived(r.after.at[g], r.head_r.at[g])
        tail = mm(one_hot((32, 96), from_vectors(g)), vectors) + mm(one_hot((32, 32), from_next(g)), r.after[g])
        fl[rows : rows + 32] = tail.astype(BF)

    drain(sent)


def layer(flat_s, flat_c, flat_f, lens, hid, feat, cot):
    vm = pl.BlockSpec(memory_space=pltpu.VMEM)
    return pl.pallas_call(
        layer_kernel,
        out_shape=(
            jax.ShapeDtypeStruct((128, D), BF),
            jax.ShapeDtypeStruct((128, D), BF),
            *[jax.ShapeDtypeStruct((n, 128), BF) for n in (1184, 1664, 4640)],
        ),
        in_specs=[vm] + [pl.BlockSpec(memory_space=pl.ANY)] * 2 + [pl.BlockSpec(memory_space=pltpu.SMEM)] + [pl.BlockSpec(memory_space=pl.ANY)] * 3,
        out_specs=[vm] * 5,
        scratch_shapes=list(scratch().values()),
        compiler_params=pltpu.CompilerParams(
            collective_id=0, has_side_effects=True, vmem_limit_bytes=VMEM_BYTES
        ),
    )(flat_s, flat_c, flat_f, lens, hid, feat, cot)


def per_device_fast(hidden, lengths, features, cotangent, self_params, cross_params, ffn_params):
    flats = [v.reshape(-1, 128) for v in (self_params, cross_params, ffn_params)]
    mixed, hgrad, *grads = layer(
        *flats, lengths, hidden.reshape(128, D), features, cotangent.reshape(128, D)
    )
    outs = [
        lax.dynamic_slice_in_dim(rows, back, flat.shape[0]).astype(F32).reshape(-1)
        for rows, back, flat in zip(grads, shift_back(), flats)
    ]
    return (mixed.reshape(2, 64, D), hgrad.reshape(2, 64, D), *outs)


def solution(mesh):
    fast = mesh.shape["dp"] == 2 and mesh.shape["fsdp"] == 16
    return jax.shard_map(
        per_device_fast if fast else per_device,
        mesh=mesh,
        in_specs=(
            P(("dp", "fsdp"), None, None),
            P(("dp", "fsdp")),
            P(("dp", "fsdp"), None, None),
            P(("dp", "fsdp"), None, None),
            P("fsdp"),
            P("fsdp"),
            P("fsdp"),
        ),
        out_specs=(
            P(("dp", "fsdp"), None, None),
            P(("dp", "fsdp"), None, None),
            P("fsdp"),
            P("fsdp"),
            P("fsdp"),
        ),
        check_vma=False,
    )
```

```python
from functools import partial
import math
from types import SimpleNamespace

import jax
import jax.numpy as jnp
from jax import lax
from jax.experimental import pallas as pl
from jax.experimental.pallas import tpu as pltpu
from jax.sharding import PartitionSpec as P

D = 768
HEADS = 12
HDIM = 64
F = 3072
E = 1408
NQ = 32


EPS = 1e-06
SCALE = 0.125


def self_layout():
    return [(D, D)] * 4 + [(D,)] * 5


def cross_layout():
    return [(D, D), (E, D), (E, D), (D, D)] + [(D,)] * 5


def ffn_layout():
    return [(D, F), (F,), (F, D), (D,), (D,), (D,)] * 2


def split_flat(flat_vec, layouts):
    pieces = []
    offset = 0
    for layout in layouts:
        amount = math.prod(layout)
        pieces.append(flat_vec[offset : offset + amount].reshape(layout))
        offset = offset + amount
    return pieces


def join_flat(pieces, length):
    flat_vec = jnp.concatenate([piece.reshape(-1) for piece in pieces])
    return jnp.pad(flat_vec, (0, length - flat_vec.shape[0]))


def regroup(flat_vec):
    groups = lax.axis_size("fsdp")
    replicas = lax.axis_size("dp")
    return flat_vec.reshape(groups, replicas, -1).transpose(1, 0, 2).reshape(-1)


def matmul(left, right):
    return jnp.dot(left, right, preferred_element_type=jnp.float32)


def matmul_left(left, right):
    return lax.dot_general(
        left, right, (((0,), (0,)), ((), ())), preferred_element_type=jnp.float32
    )


def matmul_right(left, right):
    return lax.dot_general(
        left, right, (((1,), (1,)), ((), ())), preferred_element_type=jnp.float32
    )


def column_sum(values):
    return jnp.sum(values.astype(jnp.float32), 0)


def layer_norm(values, gain, shift):
    average = jnp.mean(values, -1, keepdims=True)
    centered = values - average
    variance = jnp.mean(centered * centered, -1, keepdims=True)
    return centered * lax.rsqrt(variance + EPS) * gain + shift


def norm_backward(summed, gain, shift, grad_out):
    _, norm_pull = jax.vjp(layer_norm, summed, gain.astype(jnp.float32), shift.astype(jnp.float32))
    return norm_pull(grad_out)


def heads(rows, items):
    return rows.reshape(items, -1, HEADS, HDIM)


def score_block(query, keys, mask):
    scores = jnp.einsum("iqhd,ikhd->ihqk", query, keys, preferred_element_type=jnp.float32) * SCALE
    if mask is not None:
        scores = jnp.where(mask, scores, -1e30)
    return scores


def attend(query, keys, values, mask):
    scores = score_block(query, keys, mask)
    top_sum = jax.nn.logsumexp(scores, axis=-1)
    probs = jnp.exp(scores - top_sum[..., None]).astype(jnp.bfloat16)
    context = jnp.einsum("ihqk,ikhd->iqhd", probs, values, preferred_element_type=jnp.float32)
    return (context, top_sum)


def attend_back(query, keys, values, mask, top_sum, grad_context):
    probs = jnp.exp(score_block(query, keys, mask) - top_sum[..., None])
    grad_probs = jnp.einsum(
        "iqhd,ikhd->ihqk", grad_context, values, preferred_element_type=jnp.float32
    )
    inner = jnp.sum(probs * grad_probs, -1, keepdims=True)
    grad_scores = (probs * (grad_probs - inner)).astype(jnp.bfloat16)
    grad_query = (
        jnp.einsum("ihqk,ikhd->iqhd", grad_scores, keys, preferred_element_type=jnp.float32) * SCALE
    )
    grad_keys = (
        jnp.einsum("ihqk,iqhd->ikhd", grad_scores, query, preferred_element_type=jnp.float32)
        * SCALE
    )
    grad_values = jnp.einsum(
        "ihqk,iqhd->ikhd",
        probs.astype(jnp.bfloat16),
        grad_context,
        preferred_element_type=jnp.float32,
    )
    return (grad_query, grad_keys, grad_values)


def linear_back(inputs, weight, grad_out):
    return (matmul_left(inputs, grad_out), column_sum(grad_out), matmul_right(grad_out, weight))


def ffn_forward(rows, params):
    w_in, b_in, w_out, b_out, gain, shift = params
    rows_low = rows.astype(jnp.bfloat16)
    hidden_pre = matmul(rows_low, w_in) + b_in
    activated = jax.nn.gelu(hidden_pre, approximate=True).astype(jnp.bfloat16)
    summed = rows + (matmul(activated, w_out) + b_out)
    final = layer_norm(summed, gain.astype(jnp.float32), shift.astype(jnp.float32))
    return (final, (rows_low, hidden_pre, activated, summed))


def ffn_backward(grad_out, kept, params):
    w_in, b_in, w_out, b_out, gain, shift = params
    rows_low, hidden_pre, activated, summed = kept
    grad_sum, grad_gain, grad_shift = norm_backward(summed, gain, shift, grad_out)
    grad_branch = grad_sum.astype(jnp.bfloat16)
    grad_w_out, grad_b_out, grad_act = linear_back(activated, w_out, grad_branch)
    _, gelu_pull = jax.vjp(partial(jax.nn.gelu, approximate=True), hidden_pre)
    grad_pre = gelu_pull(grad_act)[0].astype(jnp.bfloat16)
    grad_w_in, grad_b_in, grad_rows = linear_back(rows_low, w_in, grad_pre)
    return (
        grad_sum + grad_rows,
        [grad_w_in, grad_b_in, grad_w_out, grad_b_out, grad_gain, grad_shift],
    )


def per_device(hidden, lengths, features, cotangent, self_params, cross_params, ffn_params):
    items, seq, width = hidden.shape
    self_full = lax.all_gather(self_params, "fsdp", axis=0, tiled=True)
    self_parts = split_flat(self_full, self_layout())
    w_q, w_k, w_v, w_o, b_q, b_v, b_o, gain_one, shift_one = self_parts
    positions = jnp.arange(seq)
    rows_at = positions[:, None]
    cols_at = positions[None, :]
    allowed = (cols_at < NQ)[None] | ((rows_at >= NQ) & (cols_at <= rows_at))[None] & (
        cols_at[None] < NQ + lengths[:, None, None]
    )
    allowed = allowed[:, None]
    inputs = hidden.reshape(-1, width)
    query_low = (matmul(inputs, w_q) + b_q).astype(jnp.bfloat16)
    key_low = matmul(inputs, w_k).astype(jnp.bfloat16)
    value_low = (matmul(inputs, w_v) + b_v).astype(jnp.bfloat16)
    context, self_top = attend(
        heads(query_low, items), heads(key_low, items), heads(value_low, items), allowed
    )
    context_low = context.reshape(-1, width).astype(jnp.bfloat16)
    summed_one = inputs.astype(jnp.float32) + (matmul(context_low, w_o) + b_o)
    first = layer_norm(summed_one, gain_one.astype(jnp.float32), shift_one.astype(jnp.float32))
    first_items = first.reshape(items, seq, width)
    query_rows = first_items[:, :NQ].reshape(-1, width)
    text_rows = first_items[:, NQ:].reshape(-1, width)
    cross_full = lax.all_gather(cross_params, "fsdp", axis=0, tiled=True)
    cross_parts = split_flat(cross_full, cross_layout())
    cross_wq, cross_wk, cross_wv, cross_wo, cross_bq, cross_bv, cross_bo, gain_two, shift_two = (
        cross_parts
    )
    query_in = query_rows.astype(jnp.bfloat16)
    image_rows = features.reshape(-1, features.shape[-1])
    cross_query = (matmul(query_in, cross_wq) + cross_bq).astype(jnp.bfloat16)
    cross_key = matmul(image_rows, cross_wk).astype(jnp.bfloat16)
    cross_value = (matmul(image_rows, cross_wv) + cross_bv).astype(jnp.bfloat16)
    cross_context, cross_top = attend(
        heads(cross_query, items), heads(cross_key, items), heads(cross_value, items), None
    )
    cross_low = cross_context.reshape(-1, width).astype(jnp.bfloat16)
    summed_two = query_rows + (matmul(cross_low, cross_wo) + cross_bo)
    second = layer_norm(summed_two, gain_two.astype(jnp.float32), shift_two.astype(jnp.float32))
    ffn_full = lax.all_gather(ffn_params, "fsdp", axis=0, tiled=True)
    ffn_parts = split_flat(ffn_full, ffn_layout())
    query_final, query_kept = ffn_forward(second, ffn_parts[:6])
    text_final, text_kept = ffn_forward(text_rows, ffn_parts[6:])
    mixed = jnp.concatenate(
        [query_final.reshape(items, NQ, width), text_final.reshape(items, -1, width)], 1
    ).astype(jnp.bfloat16)
    grad_items = cotangent.astype(jnp.float32)
    grad_query_final = grad_items[:, :NQ].reshape(-1, width)
    grad_text_final = grad_items[:, NQ:].reshape(-1, width)
    ffn_back = split_flat(lax.all_gather(ffn_params, "fsdp", axis=0, tiled=True), ffn_layout())
    grad_second, query_grads = ffn_backward(grad_query_final, query_kept, ffn_back[:6])
    grad_text, text_grads = ffn_backward(grad_text_final, text_kept, ffn_back[6:])
    ffn_flat_grad = join_flat(query_grads + text_grads, ffn_full.shape[0])
    ffn_grad = lax.psum_scatter(
        regroup(ffn_flat_grad), ("dp", "fsdp"), scatter_dimension=0, tiled=True
    )
    cross_back = split_flat(
        lax.all_gather(cross_params, "fsdp", axis=0, tiled=True), cross_layout()
    )
    grad_summed_two, grad_gain_two, grad_shift_two = norm_backward(
        summed_two, cross_back[7], cross_back[8], grad_second
    )
    grad_cross_out = grad_summed_two.astype(jnp.bfloat16)
    grad_cross_wo, grad_cross_bo, grad_cross_ctx = linear_back(
        cross_low, cross_back[3], grad_cross_out
    )
    grad_cq, grad_ck, grad_cv = attend_back(
        heads(cross_query, items),
        heads(cross_key, items),
        heads(cross_value, items),
        None,
        cross_top,
        heads(grad_cross_ctx.astype(jnp.bfloat16), items),
    )
    grad_cq = grad_cq.reshape(-1, width).astype(jnp.bfloat16)
    grad_ck = grad_ck.reshape(-1, width).astype(jnp.bfloat16)
    grad_cv = grad_cv.reshape(-1, width).astype(jnp.bfloat16)
    grad_cross_wq, grad_cross_bq, grad_query_in = linear_back(query_in, cross_back[0], grad_cq)
    grad_cross_wk = matmul_left(image_rows, grad_ck)
    grad_cross_wv = matmul_left(image_rows, grad_cv)
    grad_cross_bv = column_sum(grad_cv)
    grad_query_rows = grad_summed_two + grad_query_in
    cross_list = [
        grad_cross_wq,
        grad_cross_wk,
        grad_cross_wv,
        grad_cross_wo,
        grad_cross_bq,
        grad_cross_bv,
        grad_cross_bo,
        grad_gain_two,
        grad_shift_two,
    ]
    cross_flat_grad = join_flat(cross_list, cross_full.shape[0])
    cross_grad = lax.psum_scatter(
        regroup(cross_flat_grad), ("dp", "fsdp"), scatter_dimension=0, tiled=True
    )
    self_back = split_flat(lax.all_gather(self_params, "fsdp", axis=0, tiled=True), self_layout())
    grad_first = jnp.concatenate(
        [grad_query_rows.reshape(items, NQ, width), grad_text.reshape(items, -1, width)], 1
    ).reshape(-1, width)
    grad_summed_one, grad_gain_one, grad_shift_one = norm_backward(
        summed_one, self_back[7], self_back[8], grad_first
    )
    grad_attn = grad_summed_one.astype(jnp.bfloat16)
    grad_w_o, grad_b_o, grad_ctx = linear_back(context_low, self_back[3], grad_attn)
    grad_q, grad_k, grad_v = attend_back(
        heads(query_low, items),
        heads(key_low, items),
        heads(value_low, items),
        allowed,
        self_top,
        heads(grad_ctx.astype(jnp.bfloat16), items),
    )
    grad_q = grad_q.reshape(-1, width).astype(jnp.bfloat16)
    grad_k = grad_k.reshape(-1, width).astype(jnp.bfloat16)
    grad_v = grad_v.reshape(-1, width).astype(jnp.bfloat16)
    grad_w_q, grad_b_q, input_from_q = linear_back(inputs, self_back[0], grad_q)
    grad_w_k = matmul_left(inputs, grad_k)
    input_from_k = matmul_right(grad_k, self_back[1])
    grad_w_v, grad_b_v, input_from_v = linear_back(inputs, self_back[2], grad_v)
    hidden_grad = (
        (grad_summed_one + input_from_q + input_from_k + input_from_v)
        .reshape(items, seq, width)
        .astype(jnp.bfloat16)
    )
    self_list = [
        grad_w_q,
        grad_w_k,
        grad_w_v,
        grad_w_o,
        grad_b_q,
        grad_b_v,
        grad_b_o,
        grad_gain_one,
        grad_shift_one,
    ]
    self_flat_grad = join_flat(self_list, self_full.shape[0])
    self_grad = lax.psum_scatter(
        regroup(self_flat_grad), ("dp", "fsdp"), scatter_dimension=0, tiled=True
    )
    self_grad, cross_grad, ffn_grad = (
        lax.all_gather(self_grad.astype(jnp.bfloat16), "dp", axis=0, tiled=True).astype(
            self_grad.dtype
        ),
        lax.all_gather(cross_grad.astype(jnp.bfloat16), "dp", axis=0, tiled=True).astype(
            cross_grad.dtype
        ),
        lax.all_gather(ffn_grad.astype(jnp.bfloat16), "dp", axis=0, tiled=True).astype(
            ffn_grad.dtype
        ),
    )
    return (mixed, hidden_grad, self_grad, cross_grad, ffn_grad)


MESH = pl.DeviceIdType.MESH
BF = jnp.bfloat16
F32 = jnp.float32
VMEM_BYTES = 62 * 2**20


def place():
    f = lax.axis_index("fsdp")
    return lax.axis_index("dp"), f // 4, (f // 2) % 2, f % 2


def device(x, z, y, c):
    return (x, (z * 2 + y) * 2 + c)


def shift_back():
    f = lax.axis_index("fsdp")
    return 2 * f, 2 * f, 6 * (f % 4) + jnp.where(f >= 8, 6, 0)


def remote(src, dst, send, recv, target):
    return pltpu.make_async_remote_copy(
        src_ref=src,
        dst_ref=dst,
        send_sem=send,
        recv_sem=recv,
        device_id=target,
        device_id_type=MESH,
    )


def mm(a, b):
    return jnp.dot(a, b, preferred_element_type=F32)


def mm_nt(a, b):
    return lax.dot_general(a, b, (((1,), (1,)), ((), ())), preferred_element_type=F32)


def mm_tn(a, b):
    return lax.dot_general(a, b, (((0,), (0,)), ((), ())), preferred_element_type=F32)


def rows_sum(v):
    return jnp.sum(v.astype(F32), 0, keepdims=True)


def add(a, b):
    return (a.astype(F32) + b.astype(F32)).astype(BF)


def normed(v):
    centered = v - jnp.mean(v, -1, keepdims=True)
    r = lax.rsqrt(jnp.mean(centered * centered, -1, keepdims=True) + EPS)
    return centered * r, r


def norm_back(v, gain, g_out):
    xh, r = normed(v)
    gg = g_out * gain
    dv = r * (gg - jnp.mean(gg, -1, keepdims=True) - xh * jnp.mean(gg * xh, -1, keepdims=True))
    return dv, rows_sum(g_out * xh), rows_sum(g_out)


GELU_A = math.sqrt(2.0 / math.pi)
GELU_B = 0.044715


def gelu(v):
    square = v * v
    t = jnp.tanh(GELU_A * (v + GELU_B * (square * v)))
    half = 0.5 + 0.5 * t
    return v * half, half + 0.5 * v * (1.0 - t * t) * (GELU_A * (1.0 + 3.0 * GELU_B * square))


def head_mask(h):
    lane = lax.broadcasted_iota(jnp.int32, (1, 256), 1)
    return jnp.where(lane // HDIM == h, 1.0, 0.0)


def spread(rows):
    wide = rows.astype(F32)
    return jnp.concatenate([(wide * head_mask(h)).astype(BF) for h in range(4)], 0)


def fold(stacked):
    n = stacked.shape[0] // 4
    total = stacked[:n] * head_mask(0)
    for h in range(1, 4):
        total = total + stacked[h * n : (h + 1) * n] * head_mask(h)
    return total


def attend_block(q, k, v, allowed):
    s = mm_nt(spread(q), k) * SCALE
    s = jnp.where(allowed > 0.5, s, -1e30)
    e = jnp.exp(s - jnp.max(s, -1, keepdims=True))
    p = e / jnp.sum(e, -1, keepdims=True)
    return p, fold(mm(p.astype(BF), v)).astype(BF)


def attend_block_back(q, k, v, p, da):
    dax = spread(da)
    dp = mm_nt(dax, v)
    ds = (p * (dp - jnp.sum(p * dp, -1, keepdims=True))).astype(BF)
    dq = (fold(mm(ds, k)) * SCALE).astype(BF)
    dk = (mm_tn(ds, spread(q)) * SCALE).astype(BF)
    dv = mm_tn(p.astype(BF), dax).astype(BF)
    return dq, dk, dv


def rows_of(ref, first):
    return jnp.concatenate([ref[first : first + 32], ref[64 + first : 96 + first]], 0)


SPLIT = 192
REST = 384 - SPLIT
X_FIRST = (True, False)
SIDE = tuple((2, 4) if first else (4,) for first in X_FIRST)
WIDTH = tuple(384 if first else 768 for first in X_FIRST)
STREAMS = ((192, 384), (272, 384), (SPLIT, D), (REST, D), (REST, D))


def scratch():
    dma = lambda *s: pltpu.SemaphoreType.DMA(s)
    b = lambda *s: pltpu.VMEM(s, BF)
    f = lambda *s: pltpu.VMEM(s, F32)
    return dict(
        ws=b(4, D, D), wc=b(4352, D), wf=b(4, D, D), theirs=b(192, D), own_t=b(16, D), tb=b(4, 16, D), before=b(96, 128),
        tv=f(4, 16, D), vg=f(4, 16, D),
        flat_c=b(1634, 128), flat_f=b(4614, 128), hid=b(128, D), feat=b(2, 257, E), cot=b(128, D), in_sem=dma(5),
        tails=b(96, 128),
        q=b(128, D), k=b(128, D), v=b(128, D), a=b(128, D), p=f(2, 3, 256, 64),
        sum1=f(128, D), first=f(128, D), cq=b(64, D), ck=b(544, D), cv=b(544, D), ca=b(64, D),
        pc=f(2, 3, 128, 272), sum2=f(64, D), second=f(64, D),
        xg=b(2, 2, 4, 64, D), pre=f(2, 256, D), act=b(2, 256, D), part=f(2, 4, 64, D),
        send_p=b(2, 2, 2, 64, D), recv_p=b(2, 2, 2, 64, D), send_x=b(2, 2, 64, D), recv_x=b(2, 2, 64, D),
        sum3=f(2, 64, D), dpre=b(2, 256, D), dsum3=f(2, 64, D), dfirst=f(128, D),
        core_s=b(2, 4, 192, D), core_c=b(2, 4, 272, D), xs=b(*SIDE[0], 192, 384), xc=b(*SIDE[1], 272, 384),
        ys=b(4, 192, WIDTH[0]), yc=b(4, 272, WIDTH[1]), yf=b(4, SPLIT, D), yf2=b(REST, D), of=b(REST, D),
        fin_s=b(192, 384), fin_c=b(272, 384), fin_f=b(384, D),
        **{f"{n}{i}": b(*lead, *shape) for i, shape in enumerate(STREAMS) for n, lead in (("zb", (3,)), ("zr", ()))},
        v_send=b(4, 16, D), v_in=b(3, 4, 16, D), v_z=b(4, 16, D), v_zin=b(3, 16, D), v_x=b(16, D), v_xin=b(16, D),
        nice_s=b(192, D), nice_c=b(272, D), nice_f=b(4, 192, D), total_v=b(16, D), heads=b(3, 32, 128), after=b(3, 32, 128),
        loc=dma(1), tail_s=dma(1), tail_r=dma(1), head_s=dma(3), head_r=dma(3), gz_s=dma(7, 4), gz_r=dma(7, 4), gy_s=dma(7, 4), gy_r=dma(7, 4), gx_s=dma(2, 7), gx_r=dma(2, 7),
        gc_s=dma(3, 15), gc_r=dma(3, 15), t_s=dma(6), t_r=dma(4),
        ex_s=dma(2, 2, 3), ex_r=dma(2, 2, 3), rs_s=dma(2, 2, 3), rs_r=dma(2, 2, 3),
        co_s=dma(2, 2, 4), co_r=dma(2, 2, 4), xx_s=dma(2, 2, 4), xx_r=dma(2, 2, 4), yy_s=dma(4, 4), yy_r=dma(4, 4),
        zz_s=dma(5, 4), zz_r=dma(5, 4), zq_s=dma(5), zq_r=dma(5), fi_s=dma(5), fi_r=dma(5), vv_s=dma(5), vv_r=dma(7),
    )


def layer_kernel(*refs):
    names = [
        "flat_s", "in_c", "in_f", "lens", "in_hid", "in_feat", "in_cot",
        "mixed", "hgrad", "out_s", "out_c", "out_f",
    ] + list(scratch())
    r = SimpleNamespace(**dict(zip(names, refs)))
    x, z, y, c = place()
    core, xn, yn = device(x, z, y, 1 - c), device(1 - x, z, y, c), device(x, z, 1 - y, c)
    diag = device(1 - x, z, y, 1 - c)
    zdev = lambda d: device(x, (z + d) % 4, y, c)
    f = lax.axis_index("fsdp")
    following, preceding = (x, (f + 1) % 16), (x, (f + 15) % 16)
    loads = SimpleNamespace(**{
        n: pltpu.make_async_copy(getattr(r, f"in_{n[-1]}" if n[:4] == "flat" else f"in_{n}"), getattr(r, n), r.in_sem.at[i])
        for i, n in enumerate(("flat_c", "flat_f", "hid", "feat", "cot"))
    })
    for load in vars(loads).values():
        load.start()
    near = [core, xn, yn, diag, device(x, z, 1 - y, 1 - c), zdev(1), zdev(2), zdev(3), following, preceding]
    barrier = pltpu.get_barrier_semaphore()
    for d in near:
        pl.semaphore_signal(barrier, inc=1, device_id=d, device_id_type=MESH)
    me = 2 * c + x
    cols = lambda h: pl.ds(pl.multiple_of(384 * h, 384), 384)
    root = jnp.logical_and(y == 1, c == 1)
    w1 = z % 2 == 0

    inner = jnp.logical_and(z > 0, z < 3)
    outer = jnp.logical_not(inner)

    def when(cond, what):
        if cond is None:
            what()
        else:
            pl.when(cond)(what)

    def go(sent, src, dst, send, recv, target, cond=None):
        make = lambda: remote(src, dst, send, recv, target)
        when(cond, lambda: make().start())
        sent.append((make, cond))

    def arrived(view, recv):
        remote(view, view, recv, recv, core).wait_recv()

    def drain(sent):
        for make, cond in sent:
            when(cond, lambda: make().wait_send())

    def shard_s(zz, yy, cc):
        return r.ws.at[zz, pl.ds(pl.multiple_of(192 * (2 * yy + cc), 192), 192)]

    def shard_c(zz, yy, cc):
        return r.wc.at[pl.ds(pl.multiple_of(272 * ((zz * 2 + yy) * 2 + cc), 16), 272)]

    def part_f(zz, yy, lo=0, n=384):
        return r.wf.at[zz, pl.ds(pl.multiple_of(384 * yy + lo, 16), n)]

    shards = (shard_s, shard_c)
    sent_w, sent_f = ([], []), ([], [])
    steps = [jnp.where(z == 0, 3 - i, jnp.where(z == 3, 1 + i, (2, 1, 3)[i])) for i in range(3)]

    def part(g, zz, yy, cc, h):
        if g >= 2:
            return part_f(zz, yy, 96 * (g - 2), 96)
        view = shards[g](zz, yy, cc)
        return view if h is None else view.at[:, cols(h)]

    def own_part(g):
        return part(g, z, y, c, x)

    def both(a, b):
        return a if b is None else b if a is None else jnp.logical_and(a, b)

    branch = (z < 2, z >= 2)

    def sent_of(g, b):
        return sent_w[g] if g < 2 else sent_f[b]

    def z_out(src, dst, g, i, b=None):
        for k in (2, 1, 3):
            cond = both({1: z != 3, 2: None, 3: z != 0}[k], None if b is None else branch[b])
            go(sent_of(g, b), src, dst, r.gz_s.at[i, k], r.gz_r.at[i, k], zdev(k), cond)

    def z_on(view, g, k):
        cond = jnp.logical_and(inner, k == 2)
        go(sent_w[g], view, view, r.gz_s.at[g, 0], r.gz_r.at[g, 2 * z - 1], device(x, 3 * (z - 1), y, c), cond)

    def own_z(g, b=None):
        z_out(own_part(g), part(g, z, y, c, x), g, g, b)

    def own_y(g, b=None):
        cond = None if b is None else branch[b]
        go(sent_of(g, b), own_part(g), part(g, z, y, c, x), r.gy_s.at[g, 0], r.gy_r.at[g, 0], yn, cond)

    def own_core(g):
        own = part(g, z, y, c, None)
        go(sent_w[g], own, own, r.gc_s.at[g, 0], r.gc_r.at[g, 0], core)

    def gather_z(g, i):
        k = steps[i]
        view = part(g, (z - k) % 4, y, c, x)
        arrived(view, r.gz_r.at[g, k])
        z_on(view, g, k)
        go(sent_w[g], view, view, r.gy_s.at[g, k], r.gy_r.at[g, k], yn)
        go(sent_w[g], view, view, r.gx_s.at[g, k - 1], r.gx_r.at[g, k - 1], xn)
        go(sent_w[g], view, view, r.gc_s.at[g, k], r.gc_r.at[g, k], core)

    def gather_y(g, j):
        view = part(g, (z - j) % 4, 1 - y, c, x)
        arrived(view, r.gy_r.at[g, j])
        go(sent_w[g], view, view, r.gx_s.at[g, 3 + j], r.gx_r.at[g, 3 + j], xn)
        go(sent_w[g], view, view, r.gc_s.at[g, 4 + j], r.gc_r.at[g, 4 + j], core)

    def ffn_z(g, p, other=False):
        i = 6 if other else g
        view = part(g, p, 1 - y if other else y, c, x)
        b = p // 2
        k = (z - p) % 4

        @pl.when(z != p)
        def _():
            arrived(view, r.gz_r.at[i, k])

        if p in (0, 3):
            at, to, slot_at = (2, 3, 3) if p == 0 else (1, 0, 1)
            go(sent_f[b], view, view, r.gz_s.at[i, 0], r.gz_r.at[i, slot_at], device(x, to, y, c), z == at)
        if g < 5:
            go(sent_f[b], view, view, r.gy_s.at[g, k], r.gy_r.at[g, k], yn, z != p)

    def ffn_y(g, p):
        arrived(part(g, p, 1 - y, c, x), r.gy_r.at[g, (z - p) % 4])

    def other_z(b):
        view = part(5, z, 1 - y, c, x)

        @pl.when(branch[b])
        def _():
            arrived(view, r.gy_r.at[5, 0])

        z_out(view, view, 5, 6, b)

    def gather_x(g):
        for j in range(7):
            view = part(g, (z - j - 1) % 4, y, c, 1 - x) if j < 3 else part(g, (z - j + 3) % 4, 1 - y, c, 1 - x)
            arrived(view, r.gx_r.at[g, j])
            go(sent_w[g], view, view, r.gc_s.at[g, 8 + j], r.gc_r.at[g, 8 + j], core)

    def gather_core(g, which):
        for j in which:
            if j == 0:
                view = part(g, z, y, 1 - c, None)
            elif j < 4:
                view = part(g, (z - j) % 4, y, 1 - c, x)
            elif j < 8:
                view = part(g, (z - j + 4) % 4, 1 - y, 1 - c, x)
            elif j < 11:
                view = part(g, (z - j + 7) % 4, y, 1 - c, 1 - x)
            else:
                view = part(g, (z - j + 11) % 4, 1 - y, 1 - c, 1 - x)
            arrived(view, r.gc_r.at[g, j])

    tail = remote(r.tails, r.before, r.tail_s.at[0], r.tail_r.at[0], following)
    back = shift_back()

    def one_hot(shape, pick):
        row = lax.broadcasted_iota(jnp.int32, shape, 0)
        col = lax.broadcasted_iota(jnp.int32, shape, 1)
        return jnp.where(col == pick(row), 1.0, 0.0).astype(BF)

    def to_rows(g):
        return one_hot((96, 128), lambda i: 32 - back[g] + 6 * (i % 16) + i // 16)

    def store_rows(dst, row, tiles, n=6):
        for j in range(n):
            dst[pl.ds(pl.multiple_of(row, 16), 16), 128 * j : 128 * j + 128] = tiles[16 * j : 16 * j + 16]

    def first_window(g, flat, n):
        return jnp.concatenate([r.before[32 * g : 32 * g + 32], flat[0:n]], 0)

    def lay_rows(perm, flat, dst, n):
        def body(i, carry):
            window = flat[pl.ds(pl.multiple_of(96 * i - 32, 32), 128)]
            store_rows(dst, 16 * i, mm(perm, window).astype(BF))
            return carry

        lax.fori_loop(1, n, body, 0)

    tail_v = one_hot(
        (96, 96),
        lambda i: jnp.where(
            i % 16 < 5,
            6 * (i % 16) + i // 16,
            jnp.where(
                i % 16 < 10,
                32 + 6 * (i % 16 - 5) + i // 16,
                jnp.where(z < 2, 72, 66)
                + jnp.where(
                    z % 2 == 0,
                    12 * (i // 48) + 3 * (i % 16 - 10) + (i // 16) % 3,
                    6 * (i % 16 - 10) + i // 16,
                ),
            ),
        ),
    )
    mine_s, mine_c = part(0, z, y, c, None), part(1, z, y, c, None)

    perm_sc = to_rows(0)

    def rows_first(g, flat, dst):
        store_rows(dst, 0, mm(perm_sc, first_window(g, flat, 96)).astype(BF))

    def rows_f():
        @pl.when(w1)
        def _():
            def pick(i):
                m, j = i % 16, i // 16
                q = 2 * jnp.where(j < 6, c, 1 - c) + x
                j = j % 6
                return 32 - back[2] + 24 * m + 12 * (j // 3) + 3 * q + j % 3

            perm = one_hot((192, 416), pick)
            mine = part_f(z, y, 192 * c, 192)

            def put(i, window):
                tiles = mm(perm, window).astype(BF)
                store_rows(r.theirs, 16 * i, tiles[96:192])
                store_rows(mine, 16 * i, tiles[0:96])

            def body(i, carry):
                put(i, r.flat_f[pl.ds(pl.multiple_of(384 * i - 32, 32), 416)])
                return carry

            put(0, first_window(2, r.flat_f, 384))
            lax.fori_loop(1, 12, body, 0)
            swap = remote(r.theirs, mine, r.gc_s.at[2, 0], r.gc_r.at[2, 0], core)
            swap.start()
            swap.wait()

        @pl.when(jnp.logical_not(w1))
        def _():
            perm = to_rows(2)
            mine = part_f(z, y)

            def body(i, carry):
                window = r.flat_f[pl.ds(pl.multiple_of(2304 * x + 96 * i - 32, 32), 128)]
                store_rows(mine, 16 * i, mm(perm, window).astype(BF))
                return carry

            lax.fori_loop(1, 24, body, 0)
            lead = jnp.where(x == 0, r.before[64:96], r.flat_f[2304 - 32 : 2304])
            rest = r.flat_f[pl.ds(pl.multiple_of(2304 * x, 32), 96)]
            store_rows(mine, 0, mm(perm, jnp.concatenate([lead, rest], 0)).astype(BF))

    def vectors_out():
        @pl.when(root)
        def _():
            own = pltpu.make_async_copy(r.own_t, r.tb.at[z], r.loc.at[0])
            own.start()
            for k in (1, 2, 3):
                remote(r.own_t, r.tb.at[z], r.t_s.at[k - 1], r.t_r.at[k], zdev(k)).start()
            own.wait()

    def vectors_on():
        @pl.when(root)
        def _():
            for k in (1, 2, 3):
                arrived(r.tb.at[(z - k) % 4], r.t_r.at[k])
            out = []
            for i, (yy, cc) in enumerate(((0, 0), (0, 1), (1, 0))):
                go(out, r.tb, r.tb, r.t_s.at[3 + i], r.t_r.at[0], device(x, z, yy, cc))
            drain(out)
            for k in (1, 2, 3):
                remote(r.own_t, r.tb.at[z], r.t_s.at[k - 1], r.t_r.at[k], zdev(k)).wait_send()

    def vectors_in():
        @pl.when(jnp.logical_not(root))
        def _():
            arrived(r.tb, r.t_r.at[0])

        r.tv[...] = r.tb[...].astype(F32)
        r.vg[...] = jnp.zeros_like(r.vg)

    self_v = lambda j: r.tv[3, j : j + 1]
    cross_v = lambda j: r.tv[3, 5 + j : 6 + j]
    ffn_b1 = lambda b: r.tv[2 * b, pl.ds(10 + me, 1)]
    ffn_v = lambda b, j: r.tv[2 * b + 1, 10 + j : 11 + j]

    def slot(xx, cc):
        return 2 * cc + xx

    def ag_copy(ph, b, i):
        buf = r.xg.at[ph, b]
        pair = [(me, xn), (me, core), (slot(1 - x, c), core)]
        s, t = pair[i]
        return remote(buf.at[s], buf.at[s], r.ex_s.at[ph, b, i], r.ex_r.at[ph, b, i], t)

    def ag_start(ph, b):
        ag_copy(ph, b, 0).start()
        ag_copy(ph, b, 1).start()

    def ag_mid(ph, b):
        ag_copy(ph, b, 0).wait_recv()
        ag_copy(ph, b, 2).start()

    def ag_end(ph, b):
        ag_copy(ph, b, 1).wait_recv()
        ag_copy(ph, b, 2).wait_recv()
        for i in range(3):
            ag_copy(ph, b, i).wait_send()

    def rs_copy(ph, b, i):
        src = r.send_x.at[ph, b] if i == 2 else r.send_p.at[ph, b, i]
        dst = r.recv_x.at[ph, b] if i == 2 else r.recv_p.at[ph, b, i]
        return remote(src, dst, r.rs_s.at[ph, b, i], r.rs_r.at[ph, b, i], xn if i == 2 else core)

    def rs_start(ph, b):
        r.send_p[ph, b, 0] = r.part[b, slot(1 - x, 1 - c)].astype(BF)
        rs_copy(ph, b, 0).start()
        r.send_p[ph, b, 1] = r.part[b, slot(x, 1 - c)].astype(BF)
        rs_copy(ph, b, 1).start()

    def rs_mid(ph, b):
        rs_copy(ph, b, 0).wait_recv()
        r.send_x[ph, b] = (r.part[b, slot(1 - x, c)] + r.recv_p[ph, b, 0].astype(F32)).astype(BF)
        rs_copy(ph, b, 2).start()

    def rs_end(ph, b):
        rs_copy(ph, b, 1).wait_recv()
        rs_copy(ph, b, 2).wait_recv()
        for i in range(3):
            rs_copy(ph, b, i).wait_send()
        return r.part[b, me] + r.recv_p[ph, b, 1].astype(F32) + r.recv_x[ph, b].astype(F32)

    keep = SimpleNamespace()

    def self_attention():
        h = r.hid[...]
        r.q[...] = (mm(h, r.ws[0]) + self_v(0)).astype(BF)
        r.k[...] = mm(h, r.ws[1]).astype(BF)
        r.v[...] = (mm(h, r.ws[2]) + self_v(1)).astype(BF)
        for i in range(2):
            rows = slice(64 * i, 64 * i + 64)
            at = lax.broadcasted_iota(jnp.int32, (256, 64), 0) % 64
            key = lax.broadcasted_iota(jnp.int32, (256, 64), 1)
            caption = jnp.where(at >= NQ, 1.0, 0.0) * jnp.where(key <= at, 1.0, 0.0)
            ok = jnp.where(key < NQ, 1.0, caption * jnp.where(key < NQ + r.lens[i], 1.0, 0.0))
            for g in range(3):
                lanes = slice(256 * g, 256 * g + 256)
                p, a = attend_block(r.q[rows, lanes], r.k[rows, lanes], r.v[rows, lanes], ok)
                r.p[i, g] = p
                r.a[rows, lanes] = a
        r.sum1[...] = h.astype(F32) + (mm(r.a[...], r.ws[3]) + self_v(2))
        xh, _ = normed(r.sum1[...])
        r.first[...] = xh * self_v(3) + self_v(4)
        r.xg[0, 1, me] = rows_of(r.first, 32).astype(BF)

    def image_rows(lanes):
        for i in range(2):
            rows = slice(272 * i, 272 * i + 257)
            r.ck[rows, lanes] = mm(r.feat[i], r.wc[768:2176, lanes]).astype(BF)
            bias = r.tv[3, 6:7, lanes]
            r.cv[rows, lanes] = (mm(r.feat[i], r.wc[2176:3584, lanes]) + bias).astype(BF)

    def pad_rows():
        for i in range(2):
            r.ck[272 * i + 256 : 272 * i + 272] = jnp.zeros((16, D), BF)
            r.cv[272 * i + 256 : 272 * i + 272] = jnp.zeros((16, D), BF)

    def cross_start():
        keep.u = rows_of(r.first, 0)
        r.cq[...] = (mm(keep.u.astype(BF), r.wc[0:768]) + cross_v(0)).astype(BF)

    def cross_attention(i):
        ok = jnp.where(lax.broadcasted_iota(jnp.int32, (128, 272), 1) < 257, 1.0, 0.0)
        rows = slice(272 * i, 272 * i + 272)
        mine = slice(32 * i, 32 * i + 32)
        for g in range(3):
            lanes = slice(256 * g, 256 * g + 256)
            p, a = attend_block(r.cq[mine, lanes], r.ck[rows, lanes], r.cv[rows, lanes], ok)
            r.pc[i, g] = p
            r.ca[mine, lanes] = a

    def cross_end():
        r.sum2[...] = keep.u + (mm(r.ca[...], r.wc[3584:4352]) + cross_v(2))
        xh, _ = normed(r.sum2[...])
        r.second[...] = xh * cross_v(3) + cross_v(4)
        r.xg[0, 0, me] = r.second[...].astype(BF)

    sent = []

    def ffn_forward_part(b):
        rows = r.xg[0, b].reshape(256, D)
        value, slope = gelu(mm(rows, r.wf[2 * b]) + ffn_b1(b))
        r.act[b] = value.astype(BF)
        r.pre[b] = slope
        r.part[b] = mm(r.act[b], r.wf[2 * b + 1]).reshape(4, 64, D)

    def ffn_turn(b):
        rows = r.second[...] if b == 0 else rows_of(r.first, 32)
        s3 = rows + (rs_end(0, b) + ffn_v(b, 0))
        xh, _ = normed(s3)
        done = (xh * ffn_v(b, 1) + ffn_v(b, 2)).astype(BF)
        for i in range(2):
            r.mixed[64 * i + 32 * b : 64 * i + 32 * b + 32] = done[32 * i : 32 * i + 32]
        g_out = rows_of(r.cot, 32 * b).astype(F32)
        dsum, dgain, dshift = norm_back(s3, ffn_v(b, 1), g_out)
        r.dsum3[b] = dsum
        low = dsum.astype(BF)
        r.xg[1, b, me] = low
        r.vg[2 * b + 1, 10:11] = rows_sum(low)
        r.vg[2 * b + 1, 11:12] = dgain
        r.vg[2 * b + 1, 12:13] = dshift

    def ffn_back_hidden(b):
        up = r.xg[1, b].reshape(256, D)
        r.dpre[b] = (mm_nt(up, r.wf[2 * b + 1]) * r.pre[b]).astype(BF)

    def ffn_back_rows(b):
        r.part[b] = mm_nt(r.dpre[b], r.wf[2 * b]).reshape(4, 64, D)

    def ffn_grad_out(b):
        drain(sent_f[b])
        r.wf[2 * b + 1] = mm_tn(r.act[b], r.xg[1, b].reshape(256, D)).astype(BF)

    def ffn_grad_in(b):
        r.wf[2 * b] = mm_tn(r.xg[0, b].reshape(256, D), r.dpre[b]).astype(BF)
        db1 = rows_sum(r.dpre[b])
        for j in range(4):
            r.vg[2 * b, 10 + j : 11 + j] = jnp.where(j == me, db1, 0.0)

    def ffn_sum_start(p):
        go(sent, part_f(p, 1 - y, 0, SPLIT), r.yf.at[p], r.yy_s.at[2, p], r.yy_r.at[2, p], yn)
        for i, yy in ((4, 1 - y), (3, y)):
            z_out_sum(i, part_f(p, yy, SPLIT, REST), p)

    hop = jnp.where(z < 2, 1, 2)

    def z_out_sum(i, src, p):
        zb, zr = getattr(r, f"zb{i}"), getattr(r, f"zr{i}")
        d = (p - z) % 4
        far = {0: z == 3, 3: z == 0}.get(p)
        later = {0: z == 2, 3: z == 1}.get(p)
        direct = z != p
        if far is not None:
            go(sent, src, zr, r.zq_s.at[i], r.zq_r.at[i], device(x, hop, y, c), far)
            direct = jnp.logical_and(direct, jnp.logical_not(jnp.logical_or(far, later)))
        go(sent, src, zb.at[d - 1], r.zz_s.at[i, p], r.zz_r.at[i, d], device(x, p, y, c), direct)

    def z_add_sum(i, src, p):
        later = {0: z == 2, 3: z == 1}.get(p)
        if later is None:
            return
        zb, zr = getattr(r, f"zb{i}"), getattr(r, f"zr{i}")

        @pl.when(later)
        def _():
            arrived(zr, r.zq_r.at[i])
            zr[...] = add(zr[...], src[...])

        go(sent, zr, zb.at[1], r.zz_s.at[i, p], r.zz_r.at[i, 2], device(x, p, y, c), later)

    def z_total(i, own, out):
        zb = getattr(r, f"zb{i}")
        arrived(zb.at[1], r.zz_r.at[i, 2])
        out[...] = add(own, zb[1])
        for d, without in ((1, 0), (3, 3)):

            @pl.when(z != without)
            def _():
                arrived(zb.at[d - 1], r.zz_r.at[i, d])
                out[...] = add(out[...], zb[d - 1])

    def ffn_sum_y(p):
        arrived(r.yf.at[p], r.yy_r.at[2, p])
        r.yf[p] = add(r.yf[p], part_f(p, y, 0, SPLIT)[...])
        z_out_sum(2, r.yf.at[p], p)

    def ffn_add(p):
        for i, yy in ((4, 1 - y), (3, y)):
            z_add_sum(i, part_f(p, yy, SPLIT, REST), p)

    def ffn_sum_other():
        z_total(4, part_f(z, 1 - y, SPLIT, REST)[...], r.of)
        go(sent, r.of, r.yf2, r.yy_s.at[3, 0], r.yy_r.at[3, 0], yn)

    groups = (
        (shard_s, r.core_s, r.xs, r.ys, r.fin_s, r.nice_s),
        (shard_c, r.core_c, r.xc, r.yc, r.fin_c, r.nice_c),
    )
    order = (3, 1, 2, 0)

    def sum_start(g, far):
        view, cb = groups[g][:2]
        for d in order:
            zz = (z + d) % 4
            go(sent, view(zz, y if far else 1 - y, 1 - c), cb.at[far, zz], r.co_s.at[g, far, d], r.co_r.at[g, far, d], core)

    def sum_core(g, fars=(0, 1)):
        view, cb, xb, yb = groups[g][:4]
        for far in fars:
            for d in order:
                zz = (z + d) % 4
                arrived(cb.at[far, zz], r.co_r.at[g, far, d])
                cb[far, zz] = add(cb[far, zz], view(zz, y if far else 1 - y, c)[...])
                if X_FIRST[g]:
                    go(sent, cb.at[far, zz, :, cols(1 - x)], xb.at[far, zz], r.xx_s.at[g, far, d], r.xx_r.at[g, far, d], xn)
                elif far == 0:
                    go(sent, cb.at[0, zz], yb.at[zz], r.yy_s.at[g, d], r.yy_r.at[g, d], yn)

    def sum_mid(g, fars=(0, 1)):
        view, cb, xb, yb = groups[g][:4]
        for far in fars if X_FIRST[g] else (0,):
            for d in order:
                zz = (z + d) % 4
                if X_FIRST[g]:
                    arrived(xb.at[far, zz], r.xx_r.at[g, far, d])
                    xb[far, zz] = add(xb[far, zz], cb[far, zz, :, cols(x)])
                    if far == 0:
                        go(sent, xb.at[0, zz], yb.at[zz], r.yy_s.at[g, d], r.yy_r.at[g, d], yn)
                else:
                    arrived(yb.at[zz], r.yy_r.at[g, d])
                    yb[zz] = add(yb[zz], cb[1, zz])
                    go(sent, yb.at[zz, :, cols(1 - x)], xb.at[zz], r.xx_s.at[g, 0, d], r.xx_r.at[g, 0, d], xn)

    def to_z(g, mine, d):
        zb, zr = getattr(r, f"zb{g}"), getattr(r, f"zr{g}")
        if d == 2:

            @pl.when(inner)
            def _():
                arrived(zr, r.zq_r.at[g])
                zr[...] = add(zr[...], mine[...])

            go(sent, zr, zb.at[1], r.zz_s.at[g, 2], r.zz_r.at[g, 2], zdev(2), inner)
            go(sent, mine, zb.at[1], r.zz_s.at[g, 2], r.zz_r.at[g, 2], zdev(2), outer)
        elif d:
            far = z == (0 if d == 3 else 3)
            go(sent, mine, zr, r.zq_s.at[g], r.zq_r.at[g], device(x, hop, y, c), far)
            go(sent, mine, zb.at[d - 1], r.zz_s.at[g, d], r.zz_r.at[g, d], zdev(d), jnp.logical_not(far))

    def sum_last(g):
        view, cb, xb, yb = groups[g][:4]
        for d in order:
            zz = (z + d) % 4
            if X_FIRST[g]:
                arrived(yb.at[zz], r.yy_r.at[g, d])
                yb[zz] = add(yb[zz], xb[1, zz])
                to_z(g, yb.at[zz], d)
            else:
                arrived(xb.at[zz], r.xx_r.at[g, 0, d])
                xb[zz] = add(xb[zz], yb[zz, :, cols(x)])
                to_z(g, xb.at[zz], d)

    def sum_z(g):
        view, cb, xb, yb, fin, out = groups[g]
        z_total(g, yb[z] if X_FIRST[g] else xb[z], fin)
        out[:, cols(x)] = fin[...]
        go(sent, fin, out.at[:, cols(x)], r.fi_s.at[g], r.fi_r.at[g], xn)

    def ffn_sum_z():
        z_total(2, r.yf[z], r.fin_f.at[0:SPLIT])
        last = r.fin_f.at[SPLIT:384]
        z_total(3, part_f(z, y, SPLIT, REST)[...], last)
        arrived(r.yf2, r.yy_r.at[3, 0])
        last[...] = add(last[...], r.yf2[...])
        half = lambda j: r.fin_f.at[pl.ds(pl.multiple_of(192 * j, 192), 192)]

        @pl.when(w1)
        def _():
            r.nice_f[me] = half(c)[...]
            remote(half(c), r.nice_f.at[me], r.fi_s.at[2], r.fi_r.at[2], xn).start()
            remote(half(1 - c), r.nice_f.at[me], r.fi_s.at[3], r.fi_r.at[3], core).start()
            remote(half(1 - c), r.nice_f.at[me], r.fi_s.at[4], r.fi_r.at[4], diag).start()

        @pl.when(jnp.logical_not(w1))
        def _():
            for j in range(2):
                r.nice_f[2 * x + j] = half(j)[...]
                remote(half(j), r.nice_f.at[2 * x + j], r.fi_s.at[2 + j], r.fi_r.at[2 + j], xn).start()

    def ffn_end():
        def ends(n):
            for j in range(n):
                remote(r.fin_f.at[0:192], r.nice_f.at[0], r.fi_s.at[2 + j], r.fi_r.at[2 + j], xn).wait()

        pl.when(w1)(lambda: ends(3))
        pl.when(jnp.logical_not(w1))(lambda: ends(2))

    def stack(src, row, n=6):
        return jnp.concatenate(
            [src[pl.ds(pl.multiple_of(row, 16), 16), 128 * j : 128 * j + 128] for j in range(n)], 0
        )

    to_flat = one_hot((96, 96), lambda i: 16 * (i % 6) + i // 6)

    def lay_flat(src, dst, n, base=0):
        def body(i, carry):
            dst[pl.ds(pl.multiple_of(base + 96 * i, 32), 96)] = mm(to_flat, stack(src, 16 * i)).astype(BF)
            return carry

        lax.fori_loop(0, n, body, 0)

    def head_out(g, fl):
        r.heads[g] = fl[0:32]
        go(sent, r.heads.at[g], r.after.at[g], r.head_s.at[g], r.head_r.at[g], preceding)

    def text_end():
        d_text = r.dsum3[1] + rs_end(1, 1)
        for i in range(2):
            r.dfirst[64 * i + 32 : 64 * i + 64] = d_text[32 * i : 32 * i + 32]

    def query_end():
        keep.d_second = r.dsum3[0] + rs_end(1, 0)

    def cross_back():
        du2, dgain, dshift = norm_back(r.sum2[...], cross_v(3), keep.d_second)
        r.vg[3, 8:9] = dgain
        r.vg[3, 9:10] = dshift
        low = keep.low2 = du2.astype(BF)
        r.vg[3, 7:8] = rows_sum(low)
        dca = mm_nt(low, r.wc[3584:4352]).astype(BF)
        dcq = []
        for i in range(2):
            rows = slice(272 * i, 272 * i + 272)
            mine = slice(32 * i, 32 * i + 32)
            blocks = []
            for g in range(3):
                lanes = slice(256 * g, 256 * g + 256)
                dq, dk, dv = attend_block_back(
                    r.cq[mine, lanes], r.ck[rows, lanes], r.cv[rows, lanes], r.pc[i, g], dca[mine, lanes]
                )
                blocks.append(dq)
                r.ck[rows, lanes] = dk
                r.cv[rows, lanes] = dv
            dcq.append(jnp.concatenate(blocks, 1))
        dcq = keep.dcq = jnp.concatenate(dcq, 0)
        r.vg[3, 5:6] = rows_sum(dcq)
        r.vg[3, 6:7] = rows_sum(r.cv[...])
        du = du2 + mm_nt(dcq, r.wc[0:768])
        for i in range(2):
            r.dfirst[64 * i : 64 * i + 32] = du[32 * i : 32 * i + 32]

    def cross_grads():
        drain(sent_w[1])
        r.wc[3584:4352] = mm_tn(r.ca[...], keep.low2).astype(BF)
        r.wc[0:768] = mm_tn(rows_of(r.first, 0).astype(BF), keep.dcq).astype(BF)
        last = lambda ref: jnp.concatenate([ref[0].astype(F32), ref[1].astype(F32), jnp.zeros((14, ref[0].shape[1]), F32)], 0).astype(BF)
        rest = {n: last([d[256:257], d[528:529]]) for n, d in (("k", r.ck), ("v", r.cv))}
        for j in range(11):
            lanes = slice(128 * j, 128 * j + 128)
            tail_rows = last([r.feat[i, 256:257, lanes] for i in range(2)])
            both = lambda d, n: (
                mm_tn(r.feat[0, 0:256, lanes], d[0:256]) + mm_tn(r.feat[1, 0:256, lanes], d[272:528]) + mm_tn(tail_rows, rest[n])
            )
            r.wc[768 + 128 * j : 896 + 128 * j] = both(r.ck, "k").astype(BF)
            r.wc[2176 + 128 * j : 2304 + 128 * j] = both(r.cv, "v").astype(BF)

    def self_back():
        dsum1, dgain, dshift = norm_back(r.sum1[...], self_v(3), r.dfirst[...])
        r.vg[3, 3:4] = dgain
        r.vg[3, 4:5] = dshift
        keep.dsum1 = dsum1
        low = keep.low1 = dsum1.astype(BF)
        r.vg[3, 2:3] = rows_sum(low)
        da = mm_nt(low, r.ws[3]).astype(BF)
        for i in range(2):
            rows = slice(64 * i, 64 * i + 64)
            for g in range(3):
                lanes = slice(256 * g, 256 * g + 256)
                dq, dk, dv = attend_block_back(
                    r.q[rows, lanes], r.k[rows, lanes], r.v[rows, lanes], r.p[i, g], da[rows, lanes]
                )
                r.q[rows, lanes] = dq
                r.k[rows, lanes] = dk
                r.v[rows, lanes] = dv

    def self_grads():
        drain(sent_w[0])
        r.vg[3, 0:1] = rows_sum(r.q[...])
        r.vg[3, 1:2] = rows_sum(r.v[...])
        total = keep.dsum1 + mm_nt(r.q[...], r.ws[0]) + mm_nt(r.k[...], r.ws[1]) + mm_nt(r.v[...], r.ws[2])
        r.hgrad[...] = total.astype(BF)
        r.ws[0] = mm_tn(r.hid[...], r.q[...]).astype(BF)
        r.ws[1] = mm_tn(r.hid[...], r.k[...]).astype(BF)
        r.ws[2] = mm_tn(r.hid[...], r.v[...]).astype(BF)
        r.ws[3] = mm_tn(r.a[...], keep.low1).astype(BF)

    index = 2 * y + c
    home = device(x, z, 1, 1)

    def vector_sums_out():
        r.v_send[...] = r.vg[...].astype(BF)

        @pl.when(jnp.logical_not(root))
        def _():
            remote(r.v_send, r.v_in.at[index], r.vv_s.at[0], r.vv_r.at[index], home).start()

    def vector_sums_z():
        @pl.when(root)
        def _():
            total = r.vg[...]
            for i in range(3):
                arrived(r.v_in.at[i], r.vv_r.at[i])
                total = total + r.v_in[i].astype(F32)
            r.v_z[...] = total.astype(BF)
            for k in (1, 2, 3):
                zz = (z + k) % 4
                remote(r.v_z.at[zz], r.v_zin.at[k - 1], r.vv_s.at[k], r.vv_r.at[2 + k], device(x, zz, y, c)).start()

    def vector_sums_x():
        @pl.when(root)
        def _():
            total = r.v_z[z].astype(F32)
            for k in (1, 2, 3):
                arrived(r.v_zin.at[k - 1], r.vv_r.at[2 + k])
                total = total + r.v_zin[k - 1].astype(F32)
            r.v_x[...] = total.astype(BF)
            remote(r.v_x, r.v_xin, r.vv_s.at[4], r.vv_r.at[6], xn).start()

    def vector_sums_end():
        @pl.when(root)
        def _():
            arrived(r.v_xin, r.vv_r.at[6])
            r.total_v[...] = add(r.v_x[...], r.v_xin[...])
            for k in (1, 2, 3):
                zz = (z + k) % 4
                remote(r.v_z.at[zz], r.v_zin.at[k - 1], r.vv_s.at[k], r.vv_r.at[2 + k], device(x, zz, y, c)).wait_send()
            remote(r.v_x, r.v_xin, r.vv_s.at[4], r.vv_r.at[6], xn).wait_send()

        @pl.when(jnp.logical_not(root))
        def _():
            r.total_v[...] = jnp.zeros_like(r.total_v)
            remote(r.v_send, r.v_in.at[index], r.vv_s.at[0], r.vv_r.at[index], home).wait_send()

    def flat_sc(g, nice, out, n):
        arrived(nice.at[:, cols(1 - x)], r.fi_r.at[g])
        lay_flat(nice, out, n)
        head_out(g, out)

    def flat_f():
        @pl.when(w1)
        def _():
            def pick(i):
                m, t = i // 24, i % 24
                return 96 * ((t % 12) // 3) + 16 * (3 * (t // 12) + t % 3) + m

            perm = one_hot((384, 384), pick)

            def body(i, carry):
                tiles = jnp.concatenate([stack(r.nice_f.at[q], 16 * i) for q in range(4)], 0)
                r.out_f[pl.ds(pl.multiple_of(384 * i, 128), 384)] = mm(perm, tiles).astype(BF)
                return carry

            lax.fori_loop(0, 12, body, 0)

        @pl.when(jnp.logical_not(w1))
        def _():
            for q in range(4):
                lay_flat(r.nice_f.at[q], r.out_f, 12, 1152 * q)

        head_out(2, r.out_f)

    lay_rows(perm_sc, r.flat_s, mine_s, 12)
    loads.flat_c.wait()
    loads.flat_f.wait()
    r.tails[0:32] = r.flat_s[1122:1154]
    r.tails[32:64] = r.flat_c[1602:1634]
    r.tails[64:96] = r.flat_f[4582:4614]
    pl.semaphore_wait(barrier, len(near))
    tail.start()
    store_rows(r.own_t, 0, mm(tail_v, r.tails[...]).astype(BF))
    lay_rows(perm_sc, r.flat_c, mine_c, 17)
    tail.wait_recv()
    rows_first(0, r.flat_s, mine_s)
    own_z(0)
    own_y(0)
    own_core(0)
    vectors_out()
    pad_rows()
    rows_f()
    gather_y(0, 0)
    own_y(2, 0)
    own_y(3, 1)
    gather_z(0, 0)
    rows_first(1, r.flat_c, mine_c)
    vectors_on()
    own_z(1)
    gather_z(0, 1)
    gather_z(0, 2)
    own_z(2, 0)
    own_core(1)
    own_y(2, 1)
    own_y(1)
    gather_y(0, 1)
    gather_y(0, 3)
    gather_y(0, 2)
    own_z(5, 1)
    gather_z(1, 1)
    gather_z(1, 0)
    gather_x(0)
    gather_z(1, 2)
    own_z(4, 0)
    own_z(2, 1)
    gather_y(1, 2)
    own_y(5, 0)
    gather_y(1, 0)
    ffn_z(2, 1)
    ffn_z(2, 0)
    ffn_z(5, 3)
    gather_y(1, 1)
    gather_core(0, range(15))
    own_y(4, 1)
    own_z(3, 1)
    own_y(3, 0)
    ffn_z(2, 2)
    ffn_z(5, 2)
    gather_y(1, 3)
    own_z(3, 0)
    own_y(4, 0)
    other_z(0)
    vectors_in()
    loads.hid.wait()
    self_attention()
    own_y(5, 1)
    ffn_z(3, 1)
    ffn_z(3, 2)
    own_z(4, 1)
    gather_core(1, range(8))
    loads.feat.wait()
    image_rows(cols(x))
    ffn_z(3, 3)
    ffn_z(2, 3)
    other_z(1)
    ag_start(0, 1)
    ffn_z(4, 2)
    gather_x(1)
    ffn_z(4, 3)
    ffn_z(3, 0)
    gather_core(1, range(8, 15))
    ffn_y(3, 2)
    ffn_z(5, 1, other=True)
    own_z(5, 0)
    image_rows(cols(1 - x))
    ffn_z(4, 1)
    ag_mid(0, 1)
    ffn_y(3, 3)
    cross_start()
    cross_attention(0)
    cross_attention(1)
    cross_end()
    ffn_y(4, 2)
    ffn_z(5, 3, other=True)
    ag_start(0, 0)
    ffn_z(4, 0)
    ffn_y(2, 3)
    ag_end(0, 1)
    ffn_y(3, 1)
    ffn_y(3, 0)
    ffn_y(2, 2)
    ffn_z(5, 2, other=True)
    ffn_y(2, 0)
    ffn_y(4, 3)
    ffn_forward_part(1)
    rs_start(0, 1)
    rs_mid(0, 1)
    ffn_z(5, 0, other=True)
    ffn_y(2, 1)
    ag_mid(0, 0)
    loads.cot.wait()
    ffn_turn(1)
    ag_start(1, 1)
    ffn_y(4, 1)
    ffn_y(4, 0)
    ffn_z(5, 1)
    ag_end(0, 0)
    ffn_z(5, 0)
    ffn_forward_part(0)
    rs_start(0, 0)
    ag_mid(1, 1)
    rs_mid(0, 0)
    ag_end(1, 1)
    ffn_back_hidden(1)
    ffn_back_rows(1)
    ffn_grad_out(1)
    ffn_grad_in(1)
    ffn_sum_start(3)
    ffn_sum_start(2)
    ffn_turn(0)
    ag_start(1, 0)
    rs_start(1, 1)
    rs_mid(1, 1)
    ag_mid(1, 0)
    ag_end(1, 0)
    ffn_back_hidden(0)
    ffn_back_rows(0)
    rs_start(1, 0)
    text_end()
    rs_mid(1, 0)
    ffn_grad_out(0)
    ffn_grad_in(0)
    ffn_sum_start(1)
    ffn_sum_start(0)
    query_end()
    cross_back()
    cross_grads()
    sum_start(1, 0)
    self_back()
    self_grads()
    vector_sums_out()
    sum_core(1, (0,))
    sum_start(0, 0)
    sum_start(0, 1)
    ffn_sum_y(0)
    sum_core(0, (0,))
    ffn_add(3)
    ffn_sum_y(3)
    ffn_sum_y(1)
    sum_core(0, (1,))
    ffn_add(0)
    ffn_sum_y(2)
    sum_start(1, 1)
    z_add_sum(2, r.yf.at[3], 3)
    ffn_sum_other()
    vector_sums_z()
    sum_mid(0, (0,))
    sum_core(1, (1,))
    z_add_sum(2, r.yf.at[0], 0)
    sum_mid(1, (0,))
    sum_last(1)
    ffn_sum_z()
    sum_mid(0, (1,))
    sum_last(0)
    vector_sums_x()
    sum_z(1)
    sum_z(0)
    ffn_end()
    flat_f()
    flat_sc(1, r.nice_c, r.out_c, 17)
    flat_sc(0, r.nice_s, r.out_s, 12)
    vector_sums_end()
    tail.wait_send()

    vectors = stack(r.total_v, 0)
    end = (f == 15, f == 15, f % 4 == 3)
    plain = lambda first: lambda i: 16 * (i % 6) + first + i // 6
    hidden = lambda i: 16 * (3 * (i // 12) + i % 3) + 10 + (i % 12) // 3
    none = -1
    count = jnp.where(w1, 24, 18)

    def from_vectors(g):
        if g < 2:
            return lambda i: jnp.where(jnp.logical_and(end[g], i < 30), plain(5 * g)(i), none)
        pick = lambda i: jnp.where(w1, hidden(i), plain(10)(i))
        return lambda i: jnp.where(jnp.logical_and(end[2], i < count), pick(i), none)

    def from_next(g):
        if g < 2:
            return lambda i: jnp.where(end[g], none, i)
        inside = jnp.logical_or(z == 1, z == 2)
        return lambda i: jnp.where(
            end[2], jnp.where(jnp.logical_and(inside, i >= count), i - count, none), i
        )

    for g, (fl, rows) in enumerate(((r.out_s, 1152), (r.out_c, 1632), (r.out_f, 4608))):
        arrived(r.after.at[g], r.head_r.at[g])
        tail = mm(one_hot((32, 96), from_vectors(g)), vectors) + mm(one_hot((32, 32), from_next(g)), r.after[g])
        fl[rows : rows + 32] = tail.astype(BF)

    drain(sent)


def layer(flat_s, flat_c, flat_f, lens, hid, feat, cot):
    vm = pl.BlockSpec(memory_space=pltpu.VMEM)
    return pl.pallas_call(
        layer_kernel,
        out_shape=(
            jax.ShapeDtypeStruct((128, D), BF),
            jax.ShapeDtypeStruct((128, D), BF),
            *[jax.ShapeDtypeStruct((n, 128), BF) for n in (1184, 1664, 4640)],
        ),
        in_specs=[vm] + [pl.BlockSpec(memory_space=pl.ANY)] * 2 + [pl.BlockSpec(memory_space=pltpu.SMEM)] + [pl.BlockSpec(memory_space=pl.ANY)] * 3,
        out_specs=[vm] * 5,
        scratch_shapes=list(scratch().values()),
        compiler_params=pltpu.CompilerParams(
            collective_id=0, has_side_effects=True, vmem_limit_bytes=VMEM_BYTES
        ),
    )(flat_s, flat_c, flat_f, lens, hid, feat, cot)


def per_device_fast(hidden, lengths, features, cotangent, self_params, cross_params, ffn_params):
    flats = [v.reshape(-1, 128) for v in (self_params, cross_params, ffn_params)]
    mixed, hgrad, *grads = layer(
        *flats, lengths, hidden.reshape(128, D), features, cotangent.reshape(128, D)
    )
    outs = [
        lax.dynamic_slice_in_dim(rows, back, flat.shape[0]).astype(F32).reshape(-1)
        for rows, back, flat in zip(grads, shift_back(), flats)
    ]
    return (mixed.reshape(2, 64, D), hgrad.reshape(2, 64, D), *outs)


def solution(mesh):
    fast = mesh.shape["dp"] == 2 and mesh.shape["fsdp"] == 16
    return jax.shard_map(
        per_device_fast if fast else per_device,
        mesh=mesh,
        in_specs=(
            P(("dp", "fsdp"), None, None),
            P(("dp", "fsdp")),
            P(("dp", "fsdp"), None, None),
            P(("dp", "fsdp"), None, None),
            P("fsdp"),
            P("fsdp"),
            P("fsdp"),
        ),
        out_specs=(
            P(("dp", "fsdp"), None, None),
            P(("dp", "fsdp"), None, None),
            P("fsdp"),
            P("fsdp"),
            P("fsdp"),
        ),
        check_vma=False,
    )
```

```python
from functools import partial
import math
from types import SimpleNamespace

import jax
import jax.numpy as jnp
from jax import lax
from jax.experimental import pallas as pl
from jax.experimental.pallas import tpu as pltpu
from jax.sharding import PartitionSpec as P

D = 768
HEADS = 12
HDIM = 64
F = 3072
E = 1408
NQ = 32


EPS = 1e-06
SCALE = 0.125


def self_layout():
    return [(D, D)] * 4 + [(D,)] * 5


def cross_layout():
    return [(D, D), (E, D), (E, D), (D, D)] + [(D,)] * 5


def ffn_layout():
    return [(D, F), (F,), (F, D), (D,), (D,), (D,)] * 2


def split_flat(flat_vec, layouts):
    pieces = []
    offset = 0
    for layout in layouts:
        amount = math.prod(layout)
        pieces.append(flat_vec[offset : offset + amount].reshape(layout))
        offset = offset + amount
    return pieces


def join_flat(pieces, length):
    flat_vec = jnp.concatenate([piece.reshape(-1) for piece in pieces])
    return jnp.pad(flat_vec, (0, length - flat_vec.shape[0]))


def regroup(flat_vec):
    groups = lax.axis_size("fsdp")
    replicas = lax.axis_size("dp")
    return flat_vec.reshape(groups, replicas, -1).transpose(1, 0, 2).reshape(-1)


def matmul(left, right):
    return jnp.dot(left, right, preferred_element_type=jnp.float32)


def matmul_left(left, right):
    return lax.dot_general(
        left, right, (((0,), (0,)), ((), ())), preferred_element_type=jnp.float32
    )


def matmul_right(left, right):
    return lax.dot_general(
        left, right, (((1,), (1,)), ((), ())), preferred_element_type=jnp.float32
    )


def column_sum(values):
    return jnp.sum(values.astype(jnp.float32), 0)


def layer_norm(values, gain, shift):
    average = jnp.mean(values, -1, keepdims=True)
    centered = values - average
    variance = jnp.mean(centered * centered, -1, keepdims=True)
    return centered * lax.rsqrt(variance + EPS) * gain + shift


def norm_backward(summed, gain, shift, grad_out):
    _, norm_pull = jax.vjp(layer_norm, summed, gain.astype(jnp.float32), shift.astype(jnp.float32))
    return norm_pull(grad_out)


def heads(rows, items):
    return rows.reshape(items, -1, HEADS, HDIM)


def score_block(query, keys, mask):
    scores = jnp.einsum("iqhd,ikhd->ihqk", query, keys, preferred_element_type=jnp.float32) * SCALE
    if mask is not None:
        scores = jnp.where(mask, scores, -1e30)
    return scores


def attend(query, keys, values, mask):
    scores = score_block(query, keys, mask)
    top_sum = jax.nn.logsumexp(scores, axis=-1)
    probs = jnp.exp(scores - top_sum[..., None]).astype(jnp.bfloat16)
    context = jnp.einsum("ihqk,ikhd->iqhd", probs, values, preferred_element_type=jnp.float32)
    return (context, top_sum)


def attend_back(query, keys, values, mask, top_sum, grad_context):
    probs = jnp.exp(score_block(query, keys, mask) - top_sum[..., None])
    grad_probs = jnp.einsum(
        "iqhd,ikhd->ihqk", grad_context, values, preferred_element_type=jnp.float32
    )
    inner = jnp.sum(probs * grad_probs, -1, keepdims=True)
    grad_scores = (probs * (grad_probs - inner)).astype(jnp.bfloat16)
    grad_query = (
        jnp.einsum("ihqk,ikhd->iqhd", grad_scores, keys, preferred_element_type=jnp.float32) * SCALE
    )
    grad_keys = (
        jnp.einsum("ihqk,iqhd->ikhd", grad_scores, query, preferred_element_type=jnp.float32)
        * SCALE
    )
    grad_values = jnp.einsum(
        "ihqk,iqhd->ikhd",
        probs.astype(jnp.bfloat16),
        grad_context,
        preferred_element_type=jnp.float32,
    )
    return (grad_query, grad_keys, grad_values)


def linear_back(inputs, weight, grad_out):
    return (matmul_left(inputs, grad_out), column_sum(grad_out), matmul_right(grad_out, weight))


def ffn_forward(rows, params):
    w_in, b_in, w_out, b_out, gain, shift = params
    rows_low = rows.astype(jnp.bfloat16)
    hidden_pre = matmul(rows_low, w_in) + b_in
    activated = jax.nn.gelu(hidden_pre, approximate=True).astype(jnp.bfloat16)
    summed = rows + (matmul(activated, w_out) + b_out)
    final = layer_norm(summed, gain.astype(jnp.float32), shift.astype(jnp.float32))
    return (final, (rows_low, hidden_pre, activated, summed))


def ffn_backward(grad_out, kept, params):
    w_in, b_in, w_out, b_out, gain, shift = params
    rows_low, hidden_pre, activated, summed = kept
    grad_sum, grad_gain, grad_shift = norm_backward(summed, gain, shift, grad_out)
    grad_branch = grad_sum.astype(jnp.bfloat16)
    grad_w_out, grad_b_out, grad_act = linear_back(activated, w_out, grad_branch)
    _, gelu_pull = jax.vjp(partial(jax.nn.gelu, approximate=True), hidden_pre)
    grad_pre = gelu_pull(grad_act)[0].astype(jnp.bfloat16)
    grad_w_in, grad_b_in, grad_rows = linear_back(rows_low, w_in, grad_pre)
    return (
        grad_sum + grad_rows,
        [grad_w_in, grad_b_in, grad_w_out, grad_b_out, grad_gain, grad_shift],
    )


def per_device(hidden, lengths, features, cotangent, self_params, cross_params, ffn_params):
    items, seq, width = hidden.shape
    self_full = lax.all_gather(self_params, "fsdp", axis=0, tiled=True)
    self_parts = split_flat(self_full, self_layout())
    w_q, w_k, w_v, w_o, b_q, b_v, b_o, gain_one, shift_one = self_parts
    positions = jnp.arange(seq)
    rows_at = positions[:, None]
    cols_at = positions[None, :]
    allowed = (cols_at < NQ)[None] | ((rows_at >= NQ) & (cols_at <= rows_at))[None] & (
        cols_at[None] < NQ + lengths[:, None, None]
    )
    allowed = allowed[:, None]
    inputs = hidden.reshape(-1, width)
    query_low = (matmul(inputs, w_q) + b_q).astype(jnp.bfloat16)
    key_low = matmul(inputs, w_k).astype(jnp.bfloat16)
    value_low = (matmul(inputs, w_v) + b_v).astype(jnp.bfloat16)
    context, self_top = attend(
        heads(query_low, items), heads(key_low, items), heads(value_low, items), allowed
    )
    context_low = context.reshape(-1, width).astype(jnp.bfloat16)
    summed_one = inputs.astype(jnp.float32) + (matmul(context_low, w_o) + b_o)
    first = layer_norm(summed_one, gain_one.astype(jnp.float32), shift_one.astype(jnp.float32))
    first_items = first.reshape(items, seq, width)
    query_rows = first_items[:, :NQ].reshape(-1, width)
    text_rows = first_items[:, NQ:].reshape(-1, width)
    cross_full = lax.all_gather(cross_params, "fsdp", axis=0, tiled=True)
    cross_parts = split_flat(cross_full, cross_layout())
    cross_wq, cross_wk, cross_wv, cross_wo, cross_bq, cross_bv, cross_bo, gain_two, shift_two = (
        cross_parts
    )
    query_in = query_rows.astype(jnp.bfloat16)
    image_rows = features.reshape(-1, features.shape[-1])
    cross_query = (matmul(query_in, cross_wq) + cross_bq).astype(jnp.bfloat16)
    cross_key = matmul(image_rows, cross_wk).astype(jnp.bfloat16)
    cross_value = (matmul(image_rows, cross_wv) + cross_bv).astype(jnp.bfloat16)
    cross_context, cross_top = attend(
        heads(cross_query, items), heads(cross_key, items), heads(cross_value, items), None
    )
    cross_low = cross_context.reshape(-1, width).astype(jnp.bfloat16)
    summed_two = query_rows + (matmul(cross_low, cross_wo) + cross_bo)
    second = layer_norm(summed_two, gain_two.astype(jnp.float32), shift_two.astype(jnp.float32))
    ffn_full = lax.all_gather(ffn_params, "fsdp", axis=0, tiled=True)
    ffn_parts = split_flat(ffn_full, ffn_layout())
    query_final, query_kept = ffn_forward(second, ffn_parts[:6])
    text_final, text_kept = ffn_forward(text_rows, ffn_parts[6:])
    mixed = jnp.concatenate(
        [query_final.reshape(items, NQ, width), text_final.reshape(items, -1, width)], 1
    ).astype(jnp.bfloat16)
    grad_items = cotangent.astype(jnp.float32)
    grad_query_final = grad_items[:, :NQ].reshape(-1, width)
    grad_text_final = grad_items[:, NQ:].reshape(-1, width)
    ffn_back = split_flat(lax.all_gather(ffn_params, "fsdp", axis=0, tiled=True), ffn_layout())
    grad_second, query_grads = ffn_backward(grad_query_final, query_kept, ffn_back[:6])
    grad_text, text_grads = ffn_backward(grad_text_final, text_kept, ffn_back[6:])
    ffn_flat_grad = join_flat(query_grads + text_grads, ffn_full.shape[0])
    ffn_grad = lax.psum_scatter(
        regroup(ffn_flat_grad), ("dp", "fsdp"), scatter_dimension=0, tiled=True
    )
    cross_back = split_flat(
        lax.all_gather(cross_params, "fsdp", axis=0, tiled=True), cross_layout()
    )
    grad_summed_two, grad_gain_two, grad_shift_two = norm_backward(
        summed_two, cross_back[7], cross_back[8], grad_second
    )
    grad_cross_out = grad_summed_two.astype(jnp.bfloat16)
    grad_cross_wo, grad_cross_bo, grad_cross_ctx = linear_back(
        cross_low, cross_back[3], grad_cross_out
    )
    grad_cq, grad_ck, grad_cv = attend_back(
        heads(cross_query, items),
        heads(cross_key, items),
        heads(cross_value, items),
        None,
        cross_top,
        heads(grad_cross_ctx.astype(jnp.bfloat16), items),
    )
    grad_cq = grad_cq.reshape(-1, width).astype(jnp.bfloat16)
    grad_ck = grad_ck.reshape(-1, width).astype(jnp.bfloat16)
    grad_cv = grad_cv.reshape(-1, width).astype(jnp.bfloat16)
    grad_cross_wq, grad_cross_bq, grad_query_in = linear_back(query_in, cross_back[0], grad_cq)
    grad_cross_wk = matmul_left(image_rows, grad_ck)
    grad_cross_wv = matmul_left(image_rows, grad_cv)
    grad_cross_bv = column_sum(grad_cv)
    grad_query_rows = grad_summed_two + grad_query_in
    cross_list = [
        grad_cross_wq,
        grad_cross_wk,
        grad_cross_wv,
        grad_cross_wo,
        grad_cross_bq,
        grad_cross_bv,
        grad_cross_bo,
        grad_gain_two,
        grad_shift_two,
    ]
    cross_flat_grad = join_flat(cross_list, cross_full.shape[0])
    cross_grad = lax.psum_scatter(
        regroup(cross_flat_grad), ("dp", "fsdp"), scatter_dimension=0, tiled=True
    )
    self_back = split_flat(lax.all_gather(self_params, "fsdp", axis=0, tiled=True), self_layout())
    grad_first = jnp.concatenate(
        [grad_query_rows.reshape(items, NQ, width), grad_text.reshape(items, -1, width)], 1
    ).reshape(-1, width)
    grad_summed_one, grad_gain_one, grad_shift_one = norm_backward(
        summed_one, self_back[7], self_back[8], grad_first
    )
    grad_attn = grad_summed_one.astype(jnp.bfloat16)
    grad_w_o, grad_b_o, grad_ctx = linear_back(context_low, self_back[3], grad_attn)
    grad_q, grad_k, grad_v = attend_back(
        heads(query_low, items),
        heads(key_low, items),
        heads(value_low, items),
        allowed,
        self_top,
        heads(grad_ctx.astype(jnp.bfloat16), items),
    )
    grad_q = grad_q.reshape(-1, width).astype(jnp.bfloat16)
    grad_k = grad_k.reshape(-1, width).astype(jnp.bfloat16)
    grad_v = grad_v.reshape(-1, width).astype(jnp.bfloat16)
    grad_w_q, grad_b_q, input_from_q = linear_back(inputs, self_back[0], grad_q)
    grad_w_k = matmul_left(inputs, grad_k)
    input_from_k = matmul_right(grad_k, self_back[1])
    grad_w_v, grad_b_v, input_from_v = linear_back(inputs, self_back[2], grad_v)
    hidden_grad = (
        (grad_summed_one + input_from_q + input_from_k + input_from_v)
        .reshape(items, seq, width)
        .astype(jnp.bfloat16)
    )
    self_list = [
        grad_w_q,
        grad_w_k,
        grad_w_v,
        grad_w_o,
        grad_b_q,
        grad_b_v,
        grad_b_o,
        grad_gain_one,
        grad_shift_one,
    ]
    self_flat_grad = join_flat(self_list, self_full.shape[0])
    self_grad = lax.psum_scatter(
        regroup(self_flat_grad), ("dp", "fsdp"), scatter_dimension=0, tiled=True
    )
    self_grad, cross_grad, ffn_grad = (
        lax.all_gather(self_grad.astype(jnp.bfloat16), "dp", axis=0, tiled=True).astype(
            self_grad.dtype
        ),
        lax.all_gather(cross_grad.astype(jnp.bfloat16), "dp", axis=0, tiled=True).astype(
            cross_grad.dtype
        ),
        lax.all_gather(ffn_grad.astype(jnp.bfloat16), "dp", axis=0, tiled=True).astype(
            ffn_grad.dtype
        ),
    )
    return (mixed, hidden_grad, self_grad, cross_grad, ffn_grad)


MESH = pl.DeviceIdType.MESH
BF = jnp.bfloat16
F32 = jnp.float32
VMEM_BYTES = 62 * 2**20


def place():
    f = lax.axis_index("fsdp")
    return lax.axis_index("dp"), f // 4, (f // 2) % 2, f % 2


def device(x, z, y, c):
    return (x, (z * 2 + y) * 2 + c)


def shift_back():
    f = lax.axis_index("fsdp")
    return 2 * f, 2 * f, 6 * (f % 4) + jnp.where(f >= 8, 6, 0)


def remote(src, dst, send, recv, target):
    return pltpu.make_async_remote_copy(
        src_ref=src,
        dst_ref=dst,
        send_sem=send,
        recv_sem=recv,
        device_id=target,
        device_id_type=MESH,
    )


def mm(a, b):
    return jnp.dot(a, b, preferred_element_type=F32)


def mm_nt(a, b):
    return lax.dot_general(a, b, (((1,), (1,)), ((), ())), preferred_element_type=F32)


def mm_tn(a, b):
    return lax.dot_general(a, b, (((0,), (0,)), ((), ())), preferred_element_type=F32)


def rows_sum(v):
    return jnp.sum(v.astype(F32), 0, keepdims=True)


def add(a, b):
    return (a.astype(F32) + b.astype(F32)).astype(BF)


def normed(v):
    centered = v - jnp.mean(v, -1, keepdims=True)
    r = lax.rsqrt(jnp.mean(centered * centered, -1, keepdims=True) + EPS)
    return centered * r, r


def norm_back(v, gain, g_out):
    xh, r = normed(v)
    gg = g_out * gain
    dv = r * (gg - jnp.mean(gg, -1, keepdims=True) - xh * jnp.mean(gg * xh, -1, keepdims=True))
    return dv, rows_sum(g_out * xh), rows_sum(g_out)


GELU_A = math.sqrt(2.0 / math.pi)
GELU_B = 0.044715


def gelu(v):
    square = v * v
    t = jnp.tanh(GELU_A * (v + GELU_B * (square * v)))
    half = 0.5 + 0.5 * t
    return v * half, half + 0.5 * v * (1.0 - t * t) * (GELU_A * (1.0 + 3.0 * GELU_B * square))


def head_mask(h):
    lane = lax.broadcasted_iota(jnp.int32, (1, 256), 1)
    return jnp.where(lane // HDIM == h, 1.0, 0.0)


def spread(rows):
    wide = rows.astype(F32)
    return jnp.concatenate([(wide * head_mask(h)).astype(BF) for h in range(4)], 0)


def fold(stacked):
    n = stacked.shape[0] // 4
    total = stacked[:n] * head_mask(0)
    for h in range(1, 4):
        total = total + stacked[h * n : (h + 1) * n] * head_mask(h)
    return total


def attend_block(q, k, v, allowed):
    s = mm_nt(spread(q), k) * SCALE
    s = jnp.where(allowed > 0.5, s, -1e30)
    e = jnp.exp(s - jnp.max(s, -1, keepdims=True))
    p = e / jnp.sum(e, -1, keepdims=True)
    return p, fold(mm(p.astype(BF), v)).astype(BF)


def attend_block_back(q, k, v, p, da):
    dax = spread(da)
    dp = mm_nt(dax, v)
    ds = (p * (dp - jnp.sum(p * dp, -1, keepdims=True))).astype(BF)
    dq = (fold(mm(ds, k)) * SCALE).astype(BF)
    dk = (mm_tn(ds, spread(q)) * SCALE).astype(BF)
    dv = mm_tn(p.astype(BF), dax).astype(BF)
    return dq, dk, dv


def rows_of(ref, first):
    return jnp.concatenate([ref[first : first + 32], ref[64 + first : 96 + first]], 0)


SPLIT = 192
REST = 384 - SPLIT
X_FIRST = (True, False)
SIDE = tuple((2, 4) if first else (4,) for first in X_FIRST)
WIDTH = tuple(384 if first else 768 for first in X_FIRST)
STREAMS = ((192, 384), (272, 384), (SPLIT, D), (REST, D), (REST, D))


def scratch():
    dma = lambda *s: pltpu.SemaphoreType.DMA(s)
    b = lambda *s: pltpu.VMEM(s, BF)
    f = lambda *s: pltpu.VMEM(s, F32)
    return dict(
        ws=b(4, D, D), wc=b(4352, D), wf=b(4, D, D), theirs=b(192, D), own_t=b(16, D), tb=b(4, 16, D), before=b(96, 128),
        tv=f(4, 16, D), vg=f(4, 16, D),
        flat_c=b(1634, 128), flat_f=b(4614, 128), hid=b(128, D), feat=b(2, 257, E), cot=b(128, D), in_sem=dma(5),
        tails=b(96, 128),
        q=b(128, D), k=b(128, D), v=b(128, D), a=b(128, D), p=f(2, 3, 256, 64),
        sum1=f(128, D), first=f(128, D), cq=b(64, D), ck=b(544, D), cv=b(544, D), ca=b(64, D),
        pc=f(2, 3, 128, 272), sum2=f(64, D), second=f(64, D),
        xg=b(2, 2, 4, 64, D), pre=f(2, 256, D), act=b(2, 256, D), part=f(2, 4, 64, D),
        send_p=b(2, 2, 2, 64, D), recv_p=b(2, 2, 2, 64, D), send_x=b(2, 2, 64, D), recv_x=b(2, 2, 64, D),
        sum3=f(2, 64, D), dpre=b(2, 256, D), dsum3=f(2, 64, D), dfirst=f(128, D),
        core_s=b(2, 4, 192, D), core_c=b(2, 4, 272, D), xs=b(*SIDE[0], 192, 384), xc=b(*SIDE[1], 272, 384),
        ys=b(4, 192, WIDTH[0]), yc=b(4, 272, WIDTH[1]), yf=b(4, SPLIT, D), yf2=b(REST, D), of=b(REST, D),
        fin_s=b(192, 384), fin_c=b(272, 384), fin_f=b(384, D),
        **{f"{n}{i}": b(*lead, *shape) for i, shape in enumerate(STREAMS) for n, lead in (("zb", (3,)), ("zr", ()))},
        v_send=b(4, 16, D), v_in=b(3, 4, 16, D), v_z=b(4, 16, D), v_zin=b(3, 16, D), v_x=b(16, D), v_xin=b(16, D),
        nice_s=b(192, D), nice_c=b(272, D), nice_f=b(4, 192, D), total_v=b(16, D), heads=b(3, 32, 128), after=b(3, 32, 128),
        loc=dma(1), tail_s=dma(1), tail_r=dma(1), head_s=dma(3), head_r=dma(3), gz_s=dma(7, 4), gz_r=dma(7, 4), gy_s=dma(7, 4), gy_r=dma(7, 4), gx_s=dma(2, 7), gx_r=dma(2, 7),
        gc_s=dma(3, 15), gc_r=dma(3, 15), t_s=dma(6), t_r=dma(4),
        ex_s=dma(2, 2, 3), ex_r=dma(2, 2, 3), rs_s=dma(2, 2, 3), rs_r=dma(2, 2, 3),
        co_s=dma(2, 2, 4), co_r=dma(2, 2, 4), xx_s=dma(2, 2, 4), xx_r=dma(2, 2, 4), yy_s=dma(4, 4), yy_r=dma(4, 4),
        zz_s=dma(5, 4), zz_r=dma(5, 4), zq_s=dma(5), zq_r=dma(5), fi_s=dma(5), fi_r=dma(5), vv_s=dma(5), vv_r=dma(7),
    )


def layer_kernel(*refs):
    names = [
        "flat_s", "in_c", "in_f", "lens", "in_hid", "in_feat", "in_cot",
        "mixed", "hgrad", "out_s", "out_c", "out_f",
    ] + list(scratch())
    r = SimpleNamespace(**dict(zip(names, refs)))
    x, z, y, c = place()
    core, xn, yn = device(x, z, y, 1 - c), device(1 - x, z, y, c), device(x, z, 1 - y, c)
    diag = device(1 - x, z, y, 1 - c)
    zdev = lambda d: device(x, (z + d) % 4, y, c)
    f = lax.axis_index("fsdp")
    following, preceding = (x, (f + 1) % 16), (x, (f + 15) % 16)
    loads = SimpleNamespace(**{
        n: pltpu.make_async_copy(getattr(r, f"in_{n[-1]}" if n[:4] == "flat" else f"in_{n}"), getattr(r, n), r.in_sem.at[i])
        for i, n in enumerate(("flat_c", "flat_f", "hid", "feat", "cot"))
    })
    for load in vars(loads).values():
        load.start()
    near = [core, xn, yn, diag, device(x, z, 1 - y, 1 - c), zdev(1), zdev(2), zdev(3), following, preceding]
    barrier = pltpu.get_barrier_semaphore()
    for d in near:
        pl.semaphore_signal(barrier, inc=1, device_id=d, device_id_type=MESH)
    me = 2 * c + x
    cols = lambda h: pl.ds(pl.multiple_of(384 * h, 384), 384)
    root = jnp.logical_and(y == 1, c == 1)
    w1 = z % 2 == 0

    inner = jnp.logical_and(z > 0, z < 3)
    outer = jnp.logical_not(inner)

    def when(cond, what):
        if cond is None:
            what()
        else:
            pl.when(cond)(what)

    def go(sent, src, dst, send, recv, target, cond=None):
        make = lambda: remote(src, dst, send, recv, target)
        when(cond, lambda: make().start())
        sent.append((make, cond))

    def arrived(view, recv):
        remote(view, view, recv, recv, core).wait_recv()

    def drain(sent):
        for make, cond in sent:
            when(cond, lambda: make().wait_send())

    def shard_s(zz, yy, cc):
        return r.ws.at[zz, pl.ds(pl.multiple_of(192 * (2 * yy + cc), 192), 192)]

    def shard_c(zz, yy, cc):
        return r.wc.at[pl.ds(pl.multiple_of(272 * ((zz * 2 + yy) * 2 + cc), 16), 272)]

    def part_f(zz, yy, lo=0, n=384):
        return r.wf.at[zz, pl.ds(pl.multiple_of(384 * yy + lo, 16), n)]

    shards = (shard_s, shard_c)
    sent_w, sent_f = ([], []), ([], [])
    steps = [jnp.where(z == 0, 3 - i, jnp.where(z == 3, 1 + i, (2, 1, 3)[i])) for i in range(3)]

    def part(g, zz, yy, cc, h):
        if g >= 2:
            return part_f(zz, yy, 96 * (g - 2), 96)
        view = shards[g](zz, yy, cc)
        return view if h is None else view.at[:, cols(h)]

    def own_part(g):
        return part(g, z, y, c, x)

    def both(a, b):
        return a if b is None else b if a is None else jnp.logical_and(a, b)

    branch = (z < 2, z >= 2)

    def sent_of(g, b):
        return sent_w[g] if g < 2 else sent_f[b]

    def z_out(src, dst, g, i, b=None):
        for k in (1, 3, 2):
            cond = both({1: z != 3, 2: None, 3: z != 0}[k], None if b is None else branch[b])
            go(sent_of(g, b), src, dst, r.gz_s.at[i, k], r.gz_r.at[i, k], zdev(k), cond)

    def z_on(view, g, k):
        cond = jnp.logical_and(inner, k == 2)
        go(sent_w[g], view, view, r.gz_s.at[g, 0], r.gz_r.at[g, 2 * z - 1], device(x, 3 * (z - 1), y, c), cond)

    def own_z(g, b=None):
        z_out(own_part(g), part(g, z, y, c, x), g, g, b)

    def own_y(g, b=None):
        cond = None if b is None else branch[b]
        go(sent_of(g, b), own_part(g), part(g, z, y, c, x), r.gy_s.at[g, 0], r.gy_r.at[g, 0], yn, cond)

    def own_core(g):
        own = part(g, z, y, c, None)
        go(sent_w[g], own, own, r.gc_s.at[g, 0], r.gc_r.at[g, 0], core)

    def gather_z(g, i):
        k = steps[i]
        view = part(g, (z - k) % 4, y, c, x)
        arrived(view, r.gz_r.at[g, k])
        z_on(view, g, k)
        go(sent_w[g], view, view, r.gy_s.at[g, k], r.gy_r.at[g, k], yn)
        go(sent_w[g], view, view, r.gx_s.at[g, k - 1], r.gx_r.at[g, k - 1], xn)
        go(sent_w[g], view, view, r.gc_s.at[g, k], r.gc_r.at[g, k], core)

    def gather_y(g, j):
        view = part(g, (z - j) % 4, 1 - y, c, x)
        arrived(view, r.gy_r.at[g, j])
        go(sent_w[g], view, view, r.gx_s.at[g, 3 + j], r.gx_r.at[g, 3 + j], xn)
        go(sent_w[g], view, view, r.gc_s.at[g, 4 + j], r.gc_r.at[g, 4 + j], core)

    def ffn_z(g, p, other=False):
        i = 6 if other else g
        view = part(g, p, 1 - y if other else y, c, x)
        b = p // 2
        k = (z - p) % 4

        @pl.when(z != p)
        def _():
            arrived(view, r.gz_r.at[i, k])

        if p in (0, 3):
            at, to, slot_at = (2, 3, 3) if p == 0 else (1, 0, 1)
            go(sent_f[b], view, view, r.gz_s.at[i, 0], r.gz_r.at[i, slot_at], device(x, to, y, c), z == at)
        if g < 5:
            go(sent_f[b], view, view, r.gy_s.at[g, k], r.gy_r.at[g, k], yn, z != p)

    def ffn_y(g, p):
        arrived(part(g, p, 1 - y, c, x), r.gy_r.at[g, (z - p) % 4])

    def other_z(b):
        view = part(5, z, 1 - y, c, x)

        @pl.when(branch[b])
        def _():
            arrived(view, r.gy_r.at[5, 0])

        z_out(view, view, 5, 6, b)

    def gather_x(g):
        for j in range(7):
            view = part(g, (z - j - 1) % 4, y, c, 1 - x) if j < 3 else part(g, (z - j + 3) % 4, 1 - y, c, 1 - x)
            arrived(view, r.gx_r.at[g, j])
            go(sent_w[g], view, view, r.gc_s.at[g, 8 + j], r.gc_r.at[g, 8 + j], core)

    def gather_core(g, which):
        for j in which:
            if j == 0:
                view = part(g, z, y, 1 - c, None)
            elif j < 4:
                view = part(g, (z - j) % 4, y, 1 - c, x)
            elif j < 8:
                view = part(g, (z - j + 4) % 4, 1 - y, 1 - c, x)
            elif j < 11:
                view = part(g, (z - j + 7) % 4, y, 1 - c, 1 - x)
            else:
                view = part(g, (z - j + 11) % 4, 1 - y, 1 - c, 1 - x)
            arrived(view, r.gc_r.at[g, j])

    tail = remote(r.tails, r.before, r.tail_s.at[0], r.tail_r.at[0], following)
    back = shift_back()

    def one_hot(shape, pick):
        row = lax.broadcasted_iota(jnp.int32, shape, 0)
        col = lax.broadcasted_iota(jnp.int32, shape, 1)
        return jnp.where(col == pick(row), 1.0, 0.0).astype(BF)

    def to_rows(g):
        return one_hot((96, 128), lambda i: 32 - back[g] + 6 * (i % 16) + i // 16)

    def store_rows(dst, row, tiles, n=6):
        for j in range(n):
            dst[pl.ds(pl.multiple_of(row, 16), 16), 128 * j : 128 * j + 128] = tiles[16 * j : 16 * j + 16]

    def first_window(g, flat, n):
        return jnp.concatenate([r.before[32 * g : 32 * g + 32], flat[0:n]], 0)

    def lay_rows(perm, flat, dst, n):
        def body(i, carry):
            window = flat[pl.ds(pl.multiple_of(96 * i - 32, 32), 128)]
            store_rows(dst, 16 * i, mm(perm, window).astype(BF))
            return carry

        lax.fori_loop(1, n, body, 0)

    tail_v = one_hot(
        (96, 96),
        lambda i: jnp.where(
            i % 16 < 5,
            6 * (i % 16) + i // 16,
            jnp.where(
                i % 16 < 10,
                32 + 6 * (i % 16 - 5) + i // 16,
                jnp.where(z < 2, 72, 66)
                + jnp.where(
                    z % 2 == 0,
                    12 * (i // 48) + 3 * (i % 16 - 10) + (i // 16) % 3,
                    6 * (i % 16 - 10) + i // 16,
                ),
            ),
        ),
    )
    mine_s, mine_c = part(0, z, y, c, None), part(1, z, y, c, None)

    perm_sc = to_rows(0)

    def rows_first(g, flat, dst):
        store_rows(dst, 0, mm(perm_sc, first_window(g, flat, 96)).astype(BF))

    def rows_f():
        @pl.when(w1)
        def _():
            def pick(i):
                m, j = i % 16, i // 16
                q = 2 * jnp.where(j < 6, c, 1 - c) + x
                j = j % 6
                return 32 - back[2] + 24 * m + 12 * (j // 3) + 3 * q + j % 3

            perm = one_hot((192, 416), pick)
            mine = part_f(z, y, 192 * c, 192)

            def put(i, window):
                tiles = mm(perm, window).astype(BF)
                store_rows(r.theirs, 16 * i, tiles[96:192])
                store_rows(mine, 16 * i, tiles[0:96])

            def body(i, carry):
                put(i, r.flat_f[pl.ds(pl.multiple_of(384 * i - 32, 32), 416)])
                return carry

            put(0, first_window(2, r.flat_f, 384))
            lax.fori_loop(1, 12, body, 0)
            swap = remote(r.theirs, mine, r.gc_s.at[2, 0], r.gc_r.at[2, 0], core)
            swap.start()
            swap.wait()

        @pl.when(jnp.logical_not(w1))
        def _():
            perm = to_rows(2)
            mine = part_f(z, y)

            def body(i, carry):
                window = r.flat_f[pl.ds(pl.multiple_of(2304 * x + 96 * i - 32, 32), 128)]
                store_rows(mine, 16 * i, mm(perm, window).astype(BF))
                return carry

            lax.fori_loop(1, 24, body, 0)
            lead = jnp.where(x == 0, r.before[64:96], r.flat_f[2304 - 32 : 2304])
            rest = r.flat_f[pl.ds(pl.multiple_of(2304 * x, 32), 96)]
            store_rows(mine, 0, mm(perm, jnp.concatenate([lead, rest], 0)).astype(BF))

    def vectors_out():
        @pl.when(root)
        def _():
            own = pltpu.make_async_copy(r.own_t, r.tb.at[z], r.loc.at[0])
            own.start()
            for k in (1, 2, 3):
                remote(r.own_t, r.tb.at[z], r.t_s.at[k - 1], r.t_r.at[k], zdev(k)).start()
            own.wait()

    def vectors_on():
        @pl.when(root)
        def _():
            for k in (1, 2, 3):
                arrived(r.tb.at[(z - k) % 4], r.t_r.at[k])
            out = []
            for i, (yy, cc) in enumerate(((0, 0), (0, 1), (1, 0))):
                go(out, r.tb, r.tb, r.t_s.at[3 + i], r.t_r.at[0], device(x, z, yy, cc))
            drain(out)
            for k in (1, 2, 3):
                remote(r.own_t, r.tb.at[z], r.t_s.at[k - 1], r.t_r.at[k], zdev(k)).wait_send()

    def vectors_in():
        @pl.when(jnp.logical_not(root))
        def _():
            arrived(r.tb, r.t_r.at[0])

        r.tv[...] = r.tb[...].astype(F32)
        r.vg[...] = jnp.zeros_like(r.vg)

    self_v = lambda j: r.tv[3, j : j + 1]
    cross_v = lambda j: r.tv[3, 5 + j : 6 + j]
    ffn_b1 = lambda b: r.tv[2 * b, pl.ds(10 + me, 1)]
    ffn_v = lambda b, j: r.tv[2 * b + 1, 10 + j : 11 + j]

    def slot(xx, cc):
        return 2 * cc + xx

    def ag_copy(ph, b, i):
        buf = r.xg.at[ph, b]
        pair = [(me, xn), (me, core), (slot(1 - x, c), core)]
        s, t = pair[i]
        return remote(buf.at[s], buf.at[s], r.ex_s.at[ph, b, i], r.ex_r.at[ph, b, i], t)

    def ag_start(ph, b):
        ag_copy(ph, b, 0).start()
        ag_copy(ph, b, 1).start()

    def ag_mid(ph, b):
        ag_copy(ph, b, 0).wait_recv()
        ag_copy(ph, b, 2).start()

    def ag_end(ph, b):
        ag_copy(ph, b, 1).wait_recv()
        ag_copy(ph, b, 2).wait_recv()
        for i in range(3):
            ag_copy(ph, b, i).wait_send()

    def rs_copy(ph, b, i):
        src = r.send_x.at[ph, b] if i == 2 else r.send_p.at[ph, b, i]
        dst = r.recv_x.at[ph, b] if i == 2 else r.recv_p.at[ph, b, i]
        return remote(src, dst, r.rs_s.at[ph, b, i], r.rs_r.at[ph, b, i], xn if i == 2 else core)

    def rs_start(ph, b):
        r.send_p[ph, b, 0] = r.part[b, slot(1 - x, 1 - c)].astype(BF)
        rs_copy(ph, b, 0).start()
        r.send_p[ph, b, 1] = r.part[b, slot(x, 1 - c)].astype(BF)
        rs_copy(ph, b, 1).start()

    def rs_mid(ph, b):
        rs_copy(ph, b, 0).wait_recv()
        r.send_x[ph, b] = (r.part[b, slot(1 - x, c)] + r.recv_p[ph, b, 0].astype(F32)).astype(BF)
        rs_copy(ph, b, 2).start()

    def rs_end(ph, b):
        rs_copy(ph, b, 1).wait_recv()
        rs_copy(ph, b, 2).wait_recv()
        for i in range(3):
            rs_copy(ph, b, i).wait_send()
        return r.part[b, me] + r.recv_p[ph, b, 1].astype(F32) + r.recv_x[ph, b].astype(F32)

    keep = SimpleNamespace()

    def self_attention():
        h = r.hid[...]
        r.q[...] = (mm(h, r.ws[0]) + self_v(0)).astype(BF)
        r.k[...] = mm(h, r.ws[1]).astype(BF)
        r.v[...] = (mm(h, r.ws[2]) + self_v(1)).astype(BF)
        for i in range(2):
            rows = slice(64 * i, 64 * i + 64)
            at = lax.broadcasted_iota(jnp.int32, (256, 64), 0) % 64
            key = lax.broadcasted_iota(jnp.int32, (256, 64), 1)
            caption = jnp.where(at >= NQ, 1.0, 0.0) * jnp.where(key <= at, 1.0, 0.0)
            ok = jnp.where(key < NQ, 1.0, caption * jnp.where(key < NQ + r.lens[i], 1.0, 0.0))
            for g in range(3):
                lanes = slice(256 * g, 256 * g + 256)
                p, a = attend_block(r.q[rows, lanes], r.k[rows, lanes], r.v[rows, lanes], ok)
                r.p[i, g] = p
                r.a[rows, lanes] = a
        r.sum1[...] = h.astype(F32) + (mm(r.a[...], r.ws[3]) + self_v(2))
        xh, _ = normed(r.sum1[...])
        r.first[...] = xh * self_v(3) + self_v(4)
        r.xg[0, 1, me] = rows_of(r.first, 32).astype(BF)

    def image_rows(lanes):
        for i in range(2):
            rows = slice(272 * i, 272 * i + 257)
            r.ck[rows, lanes] = mm(r.feat[i], r.wc[768:2176, lanes]).astype(BF)
            bias = r.tv[3, 6:7, lanes]
            r.cv[rows, lanes] = (mm(r.feat[i], r.wc[2176:3584, lanes]) + bias).astype(BF)

    def pad_rows():
        for i in range(2):
            r.ck[272 * i + 256 : 272 * i + 272] = jnp.zeros((16, D), BF)
            r.cv[272 * i + 256 : 272 * i + 272] = jnp.zeros((16, D), BF)

    def cross_start():
        keep.u = rows_of(r.first, 0)
        r.cq[...] = (mm(keep.u.astype(BF), r.wc[0:768]) + cross_v(0)).astype(BF)

    def cross_attention(i):
        ok = jnp.where(lax.broadcasted_iota(jnp.int32, (128, 272), 1) < 257, 1.0, 0.0)
        rows = slice(272 * i, 272 * i + 272)
        mine = slice(32 * i, 32 * i + 32)
        for g in range(3):
            lanes = slice(256 * g, 256 * g + 256)
            p, a = attend_block(r.cq[mine, lanes], r.ck[rows, lanes], r.cv[rows, lanes], ok)
            r.pc[i, g] = p
            r.ca[mine, lanes] = a

    def cross_end():
        r.sum2[...] = keep.u + (mm(r.ca[...], r.wc[3584:4352]) + cross_v(2))
        xh, _ = normed(r.sum2[...])
        r.second[...] = xh * cross_v(3) + cross_v(4)
        r.xg[0, 0, me] = r.second[...].astype(BF)

    sent = []

    def ffn_forward_part(b):
        rows = r.xg[0, b].reshape(256, D)
        value, slope = gelu(mm(rows, r.wf[2 * b]) + ffn_b1(b))
        r.act[b] = value.astype(BF)
        r.pre[b] = slope
        r.part[b] = mm(r.act[b], r.wf[2 * b + 1]).reshape(4, 64, D)

    def ffn_turn(b):
        rows = r.second[...] if b == 0 else rows_of(r.first, 32)
        s3 = rows + (rs_end(0, b) + ffn_v(b, 0))
        xh, _ = normed(s3)
        done = (xh * ffn_v(b, 1) + ffn_v(b, 2)).astype(BF)
        for i in range(2):
            r.mixed[64 * i + 32 * b : 64 * i + 32 * b + 32] = done[32 * i : 32 * i + 32]
        g_out = rows_of(r.cot, 32 * b).astype(F32)
        dsum, dgain, dshift = norm_back(s3, ffn_v(b, 1), g_out)
        r.dsum3[b] = dsum
        low = dsum.astype(BF)
        r.xg[1, b, me] = low
        r.vg[2 * b + 1, 10:11] = rows_sum(low)
        r.vg[2 * b + 1, 11:12] = dgain
        r.vg[2 * b + 1, 12:13] = dshift

    def ffn_back_hidden(b):
        up = r.xg[1, b].reshape(256, D)
        r.dpre[b] = (mm_nt(up, r.wf[2 * b + 1]) * r.pre[b]).astype(BF)

    def ffn_back_rows(b):
        r.part[b] = mm_nt(r.dpre[b], r.wf[2 * b]).reshape(4, 64, D)

    def ffn_grad_out(b):
        drain(sent_f[b])
        r.wf[2 * b + 1] = mm_tn(r.act[b], r.xg[1, b].reshape(256, D)).astype(BF)

    def ffn_grad_in(b):
        r.wf[2 * b] = mm_tn(r.xg[0, b].reshape(256, D), r.dpre[b]).astype(BF)
        db1 = rows_sum(r.dpre[b])
        for j in range(4):
            r.vg[2 * b, 10 + j : 11 + j] = jnp.where(j == me, db1, 0.0)

    def ffn_sum_start(p):
        go(sent, part_f(p, 1 - y, 0, SPLIT), r.yf.at[p], r.yy_s.at[2, p], r.yy_r.at[2, p], yn)
        for i, yy in ((4, 1 - y), (3, y)):
            z_out_sum(i, part_f(p, yy, SPLIT, REST), p)

    hop = jnp.where(z < 2, 1, 2)

    def z_out_sum(i, src, p):
        zb, zr = getattr(r, f"zb{i}"), getattr(r, f"zr{i}")
        d = (p - z) % 4
        far = {0: z == 3, 3: z == 0}.get(p)
        later = {0: z == 2, 3: z == 1}.get(p)
        direct = z != p
        if far is not None:
            go(sent, src, zr, r.zq_s.at[i], r.zq_r.at[i], device(x, hop, y, c), far)
            direct = jnp.logical_and(direct, jnp.logical_not(jnp.logical_or(far, later)))
        go(sent, src, zb.at[d - 1], r.zz_s.at[i, p], r.zz_r.at[i, d], device(x, p, y, c), direct)

    def z_add_sum(i, src, p):
        later = {0: z == 2, 3: z == 1}.get(p)
        if later is None:
            return
        zb, zr = getattr(r, f"zb{i}"), getattr(r, f"zr{i}")

        @pl.when(later)
        def _():
            arrived(zr, r.zq_r.at[i])
            zr[...] = add(zr[...], src[...])

        go(sent, zr, zb.at[1], r.zz_s.at[i, p], r.zz_r.at[i, 2], device(x, p, y, c), later)

    def z_total(i, own, out):
        zb = getattr(r, f"zb{i}")
        arrived(zb.at[1], r.zz_r.at[i, 2])
        out[...] = add(own, zb[1])
        for d, without in ((1, 0), (3, 3)):

            @pl.when(z != without)
            def _():
                arrived(zb.at[d - 1], r.zz_r.at[i, d])
                out[...] = add(out[...], zb[d - 1])

    def ffn_sum_y(p):
        arrived(r.yf.at[p], r.yy_r.at[2, p])
        r.yf[p] = add(r.yf[p], part_f(p, y, 0, SPLIT)[...])
        z_out_sum(2, r.yf.at[p], p)

    def ffn_add(p):
        for i, yy in ((4, 1 - y), (3, y)):
            z_add_sum(i, part_f(p, yy, SPLIT, REST), p)

    def ffn_sum_other():
        z_total(4, part_f(z, 1 - y, SPLIT, REST)[...], r.of)
        go(sent, r.of, r.yf2, r.yy_s.at[3, 0], r.yy_r.at[3, 0], yn)

    groups = (
        (shard_s, r.core_s, r.xs, r.ys, r.fin_s, r.nice_s),
        (shard_c, r.core_c, r.xc, r.yc, r.fin_c, r.nice_c),
    )
    order = (3, 1, 2, 0)

    def sum_start(g, far):
        view, cb = groups[g][:2]
        for d in order:
            zz = (z + d) % 4
            go(sent, view(zz, y if far else 1 - y, 1 - c), cb.at[far, zz], r.co_s.at[g, far, d], r.co_r.at[g, far, d], core)

    def sum_core(g, fars=(0, 1)):
        view, cb, xb, yb = groups[g][:4]
        for far in fars:
            for d in order:
                zz = (z + d) % 4
                arrived(cb.at[far, zz], r.co_r.at[g, far, d])
                cb[far, zz] = add(cb[far, zz], view(zz, y if far else 1 - y, c)[...])
                if X_FIRST[g]:
                    go(sent, cb.at[far, zz, :, cols(1 - x)], xb.at[far, zz], r.xx_s.at[g, far, d], r.xx_r.at[g, far, d], xn)
                elif far == 0:
                    go(sent, cb.at[0, zz], yb.at[zz], r.yy_s.at[g, d], r.yy_r.at[g, d], yn)

    def sum_mid(g, fars=(0, 1)):
        view, cb, xb, yb = groups[g][:4]
        for far in fars if X_FIRST[g] else (0,):
            for d in order:
                zz = (z + d) % 4
                if X_FIRST[g]:
                    arrived(xb.at[far, zz], r.xx_r.at[g, far, d])
                    xb[far, zz] = add(xb[far, zz], cb[far, zz, :, cols(x)])
                    if far == 0:
                        go(sent, xb.at[0, zz], yb.at[zz], r.yy_s.at[g, d], r.yy_r.at[g, d], yn)
                else:
                    arrived(yb.at[zz], r.yy_r.at[g, d])
                    yb[zz] = add(yb[zz], cb[1, zz])
                    go(sent, yb.at[zz, :, cols(1 - x)], xb.at[zz], r.xx_s.at[g, 0, d], r.xx_r.at[g, 0, d], xn)

    def to_z(g, mine, d):
        zb, zr = getattr(r, f"zb{g}"), getattr(r, f"zr{g}")
        if d == 2:

            @pl.when(inner)
            def _():
                arrived(zr, r.zq_r.at[g])
                zr[...] = add(zr[...], mine[...])

            go(sent, zr, zb.at[1], r.zz_s.at[g, 2], r.zz_r.at[g, 2], zdev(2), inner)
            go(sent, mine, zb.at[1], r.zz_s.at[g, 2], r.zz_r.at[g, 2], zdev(2), outer)
        elif d:
            far = z == (0 if d == 3 else 3)
            go(sent, mine, zr, r.zq_s.at[g], r.zq_r.at[g], device(x, hop, y, c), far)
            go(sent, mine, zb.at[d - 1], r.zz_s.at[g, d], r.zz_r.at[g, d], zdev(d), jnp.logical_not(far))

    def sum_last(g):
        view, cb, xb, yb = groups[g][:4]
        for d in order:
            zz = (z + d) % 4
            if X_FIRST[g]:
                arrived(yb.at[zz], r.yy_r.at[g, d])
                yb[zz] = add(yb[zz], xb[1, zz])
                to_z(g, yb.at[zz], d)
            else:
                arrived(xb.at[zz], r.xx_r.at[g, 0, d])
                xb[zz] = add(xb[zz], yb[zz, :, cols(x)])
                to_z(g, xb.at[zz], d)

    def sum_z(g):
        view, cb, xb, yb, fin, out = groups[g]
        z_total(g, yb[z] if X_FIRST[g] else xb[z], fin)
        out[:, cols(x)] = fin[...]
        go(sent, fin, out.at[:, cols(x)], r.fi_s.at[g], r.fi_r.at[g], xn)

    def ffn_sum_z():
        z_total(2, r.yf[z], r.fin_f.at[0:SPLIT])
        last = r.fin_f.at[SPLIT:384]
        z_total(3, part_f(z, y, SPLIT, REST)[...], last)
        arrived(r.yf2, r.yy_r.at[3, 0])
        last[...] = add(last[...], r.yf2[...])
        half = lambda j: r.fin_f.at[pl.ds(pl.multiple_of(192 * j, 192), 192)]

        @pl.when(w1)
        def _():
            r.nice_f[me] = half(c)[...]
            remote(half(c), r.nice_f.at[me], r.fi_s.at[2], r.fi_r.at[2], xn).start()
            remote(half(1 - c), r.nice_f.at[me], r.fi_s.at[3], r.fi_r.at[3], core).start()
            remote(half(1 - c), r.nice_f.at[me], r.fi_s.at[4], r.fi_r.at[4], diag).start()

        @pl.when(jnp.logical_not(w1))
        def _():
            for j in range(2):
                r.nice_f[2 * x + j] = half(j)[...]
                remote(half(j), r.nice_f.at[2 * x + j], r.fi_s.at[2 + j], r.fi_r.at[2 + j], xn).start()

    def ffn_end():
        def ends(n):
            for j in range(n):
                remote(r.fin_f.at[0:192], r.nice_f.at[0], r.fi_s.at[2 + j], r.fi_r.at[2 + j], xn).wait()

        pl.when(w1)(lambda: ends(3))
        pl.when(jnp.logical_not(w1))(lambda: ends(2))

    def stack(src, row, n=6):
        return jnp.concatenate(
            [src[pl.ds(pl.multiple_of(row, 16), 16), 128 * j : 128 * j + 128] for j in range(n)], 0
        )

    to_flat = one_hot((96, 96), lambda i: 16 * (i % 6) + i // 6)

    def lay_flat(src, dst, n, base=0):
        def body(i, carry):
            dst[pl.ds(pl.multiple_of(base + 96 * i, 32), 96)] = mm(to_flat, stack(src, 16 * i)).astype(BF)
            return carry

        lax.fori_loop(0, n, body, 0)

    def head_out(g, fl):
        r.heads[g] = fl[0:32]
        go(sent, r.heads.at[g], r.after.at[g], r.head_s.at[g], r.head_r.at[g], preceding)

    def text_end():
        d_text = r.dsum3[1] + rs_end(1, 1)
        for i in range(2):
            r.dfirst[64 * i + 32 : 64 * i + 64] = d_text[32 * i : 32 * i + 32]

    def query_end():
        keep.d_second = r.dsum3[0] + rs_end(1, 0)

    def cross_back():
        du2, dgain, dshift = norm_back(r.sum2[...], cross_v(3), keep.d_second)
        r.vg[3, 8:9] = dgain
        r.vg[3, 9:10] = dshift
        low = keep.low2 = du2.astype(BF)
        r.vg[3, 7:8] = rows_sum(low)
        dca = mm_nt(low, r.wc[3584:4352]).astype(BF)
        dcq = []
        for i in range(2):
            rows = slice(272 * i, 272 * i + 272)
            mine = slice(32 * i, 32 * i + 32)
            blocks = []
            for g in range(3):
                lanes = slice(256 * g, 256 * g + 256)
                dq, dk, dv = attend_block_back(
                    r.cq[mine, lanes], r.ck[rows, lanes], r.cv[rows, lanes], r.pc[i, g], dca[mine, lanes]
                )
                blocks.append(dq)
                r.ck[rows, lanes] = dk
                r.cv[rows, lanes] = dv
            dcq.append(jnp.concatenate(blocks, 1))
        dcq = keep.dcq = jnp.concatenate(dcq, 0)
        r.vg[3, 5:6] = rows_sum(dcq)
        r.vg[3, 6:7] = rows_sum(r.cv[...])
        du = du2 + mm_nt(dcq, r.wc[0:768])
        for i in range(2):
            r.dfirst[64 * i : 64 * i + 32] = du[32 * i : 32 * i + 32]

    def cross_grads():
        drain(sent_w[1])
        r.wc[3584:4352] = mm_tn(r.ca[...], keep.low2).astype(BF)
        r.wc[0:768] = mm_tn(rows_of(r.first, 0).astype(BF), keep.dcq).astype(BF)
        last = lambda ref: jnp.concatenate([ref[0].astype(F32), ref[1].astype(F32), jnp.zeros((14, ref[0].shape[1]), F32)], 0).astype(BF)
        rest = {n: last([d[256:257], d[528:529]]) for n, d in (("k", r.ck), ("v", r.cv))}
        for j in range(11):
            lanes = slice(128 * j, 128 * j + 128)
            tail_rows = last([r.feat[i, 256:257, lanes] for i in range(2)])
            both = lambda d, n: (
                mm_tn(r.feat[0, 0:256, lanes], d[0:256]) + mm_tn(r.feat[1, 0:256, lanes], d[272:528]) + mm_tn(tail_rows, rest[n])
            )
            r.wc[768 + 128 * j : 896 + 128 * j] = both(r.ck, "k").astype(BF)
            r.wc[2176 + 128 * j : 2304 + 128 * j] = both(r.cv, "v").astype(BF)

    def self_back():
        dsum1, dgain, dshift = norm_back(r.sum1[...], self_v(3), r.dfirst[...])
        r.vg[3, 3:4] = dgain
        r.vg[3, 4:5] = dshift
        keep.dsum1 = dsum1
        low = keep.low1 = dsum1.astype(BF)
        r.vg[3, 2:3] = rows_sum(low)
        da = mm_nt(low, r.ws[3]).astype(BF)
        for i in range(2):
            rows = slice(64 * i, 64 * i + 64)
            for g in range(3):
                lanes = slice(256 * g, 256 * g + 256)
                dq, dk, dv = attend_block_back(
                    r.q[rows, lanes], r.k[rows, lanes], r.v[rows, lanes], r.p[i, g], da[rows, lanes]
                )
                r.q[rows, lanes] = dq
                r.k[rows, lanes] = dk
                r.v[rows, lanes] = dv

    def self_grads():
        drain(sent_w[0])
        r.vg[3, 0:1] = rows_sum(r.q[...])
        r.vg[3, 1:2] = rows_sum(r.v[...])
        total = keep.dsum1 + mm_nt(r.q[...], r.ws[0]) + mm_nt(r.k[...], r.ws[1]) + mm_nt(r.v[...], r.ws[2])
        r.hgrad[...] = total.astype(BF)
        r.ws[0] = mm_tn(r.hid[...], r.q[...]).astype(BF)
        r.ws[1] = mm_tn(r.hid[...], r.k[...]).astype(BF)
        r.ws[2] = mm_tn(r.hid[...], r.v[...]).astype(BF)
        r.ws[3] = mm_tn(r.a[...], keep.low1).astype(BF)

    index = 2 * y + c
    home = device(x, z, 1, 1)

    def vector_sums_out():
        r.v_send[...] = r.vg[...].astype(BF)

        @pl.when(jnp.logical_not(root))
        def _():
            remote(r.v_send, r.v_in.at[index], r.vv_s.at[0], r.vv_r.at[index], home).start()

    def vector_sums_z():
        @pl.when(root)
        def _():
            total = r.vg[...]
            for i in range(3):
                arrived(r.v_in.at[i], r.vv_r.at[i])
                total = total + r.v_in[i].astype(F32)
            r.v_z[...] = total.astype(BF)
            for k in (1, 2, 3):
                zz = (z + k) % 4
                remote(r.v_z.at[zz], r.v_zin.at[k - 1], r.vv_s.at[k], r.vv_r.at[2 + k], device(x, zz, y, c)).start()

    def vector_sums_x():
        @pl.when(root)
        def _():
            total = r.v_z[z].astype(F32)
            for k in (1, 2, 3):
                arrived(r.v_zin.at[k - 1], r.vv_r.at[2 + k])
                total = total + r.v_zin[k - 1].astype(F32)
            r.v_x[...] = total.astype(BF)
            remote(r.v_x, r.v_xin, r.vv_s.at[4], r.vv_r.at[6], xn).start()

    def vector_sums_end():
        @pl.when(root)
        def _():
            arrived(r.v_xin, r.vv_r.at[6])
            r.total_v[...] = add(r.v_x[...], r.v_xin[...])
            for k in (1, 2, 3):
                zz = (z + k) % 4
                remote(r.v_z.at[zz], r.v_zin.at[k - 1], r.vv_s.at[k], r.vv_r.at[2 + k], device(x, zz, y, c)).wait_send()
            remote(r.v_x, r.v_xin, r.vv_s.at[4], r.vv_r.at[6], xn).wait_send()

        @pl.when(jnp.logical_not(root))
        def _():
            r.total_v[...] = jnp.zeros_like(r.total_v)
            remote(r.v_send, r.v_in.at[index], r.vv_s.at[0], r.vv_r.at[index], home).wait_send()

    def flat_sc(g, nice, out, n):
        arrived(nice.at[:, cols(1 - x)], r.fi_r.at[g])
        lay_flat(nice, out, n)
        head_out(g, out)

    def flat_f():
        @pl.when(w1)
        def _():
            def pick(i):
                m, t = i // 24, i % 24
                return 96 * ((t % 12) // 3) + 16 * (3 * (t // 12) + t % 3) + m

            perm = one_hot((384, 384), pick)

            def body(i, carry):
                tiles = jnp.concatenate([stack(r.nice_f.at[q], 16 * i) for q in range(4)], 0)
                r.out_f[pl.ds(pl.multiple_of(384 * i, 128), 384)] = mm(perm, tiles).astype(BF)
                return carry

            lax.fori_loop(0, 12, body, 0)

        @pl.when(jnp.logical_not(w1))
        def _():
            for q in range(4):
                lay_flat(r.nice_f.at[q], r.out_f, 12, 1152 * q)

        head_out(2, r.out_f)

    lay_rows(perm_sc, r.flat_s, mine_s, 12)
    loads.flat_c.wait()
    loads.flat_f.wait()
    r.tails[0:32] = r.flat_s[1122:1154]
    r.tails[32:64] = r.flat_c[1602:1634]
    r.tails[64:96] = r.flat_f[4582:4614]
    pl.semaphore_wait(barrier, len(near))
    tail.start()
    store_rows(r.own_t, 0, mm(tail_v, r.tails[...]).astype(BF))
    lay_rows(perm_sc, r.flat_c, mine_c, 17)
    tail.wait_recv()
    rows_first(0, r.flat_s, mine_s)
    own_z(0)
    own_y(0)
    own_core(0)
    vectors_out()
    pad_rows()
    rows_f()
    gather_y(0, 0)
    own_y(2, 0)
    own_y(3, 1)
    gather_z(0, 0)
    rows_first(1, r.flat_c, mine_c)
    vectors_on()
    own_z(1)
    gather_z(0, 1)
    gather_z(0, 2)
    own_z(2, 0)
    own_core(1)
    own_y(2, 1)
    own_y(1)
    gather_y(0, 1)
    gather_y(0, 3)
    gather_y(0, 2)
    own_z(5, 1)
    gather_z(1, 1)
    gather_z(1, 0)
    gather_x(0)
    gather_z(1, 2)
    own_z(4, 0)
    own_z(2, 1)
    gather_y(1, 2)
    own_y(5, 0)
    gather_y(1, 0)
    ffn_z(2, 1)
    ffn_z(2, 0)
    ffn_z(5, 3)
    gather_y(1, 1)
    gather_core(0, range(15))
    own_y(4, 1)
    own_z(3, 1)
    own_y(3, 0)
    ffn_z(2, 2)
    ffn_z(5, 2)
    gather_y(1, 3)
    own_z(3, 0)
    own_y(4, 0)
    other_z(0)
    vectors_in()
    loads.hid.wait()
    self_attention()
    own_y(5, 1)
    ffn_z(3, 1)
    ffn_z(3, 2)
    own_z(4, 1)
    gather_core(1, range(8))
    loads.feat.wait()
    image_rows(cols(x))
    ffn_z(3, 3)
    ffn_z(2, 3)
    other_z(1)
    ag_start(0, 1)
    ffn_z(4, 2)
    gather_x(1)
    ffn_z(4, 3)
    ffn_z(3, 0)
    gather_core(1, range(8, 15))
    ffn_y(3, 2)
    ffn_z(5, 1, other=True)
    own_z(5, 0)
    image_rows(cols(1 - x))
    ffn_z(4, 1)
    ag_mid(0, 1)
    ffn_y(3, 3)
    cross_start()
    cross_attention(0)
    cross_attention(1)
    cross_end()
    ffn_y(4, 2)
    ffn_z(5, 3, other=True)
    ag_start(0, 0)
    ffn_z(4, 0)
    ffn_y(2, 3)
    ag_end(0, 1)
    ffn_y(3, 1)
    ffn_y(3, 0)
    ffn_y(2, 2)
    ffn_z(5, 2, other=True)
    ffn_y(2, 0)
    ffn_y(4, 3)
    ffn_forward_part(1)
    rs_start(0, 1)
    rs_mid(0, 1)
    ffn_z(5, 0, other=True)
    ffn_y(2, 1)
    ag_mid(0, 0)
    loads.cot.wait()
    ffn_turn(1)
    ag_start(1, 1)
    ffn_y(4, 1)
    ffn_y(4, 0)
    ffn_z(5, 1)
    ag_end(0, 0)
    ffn_z(5, 0)
    ffn_forward_part(0)
    rs_start(0, 0)
    ag_mid(1, 1)
    rs_mid(0, 0)
    ag_end(1, 1)
    ffn_back_hidden(1)
    ffn_back_rows(1)
    ffn_grad_out(1)
    ffn_sum_start(3)
    ffn_grad_in(1)
    ffn_sum_start(2)
    ffn_turn(0)
    ag_start(1, 0)
    rs_start(1, 1)
    rs_mid(1, 1)
    ag_mid(1, 0)
    ag_end(1, 0)
    ffn_back_hidden(0)
    ffn_back_rows(0)
    rs_start(1, 0)
    text_end()
    rs_mid(1, 0)
    ffn_grad_out(0)
    ffn_sum_start(1)
    ffn_grad_in(0)
    ffn_sum_start(0)
    query_end()
    cross_back()
    cross_grads()
    sum_start(1, 0)
    self_back()
    self_grads()
    vector_sums_out()
    sum_core(1, (0,))
    sum_start(0, 0)
    sum_start(0, 1)
    ffn_sum_y(0)
    sum_core(0, (0,))
    ffn_add(3)
    ffn_sum_y(3)
    ffn_sum_y(1)
    sum_core(0, (1,))
    ffn_add(0)
    ffn_sum_y(2)
    sum_start(1, 1)
    z_add_sum(2, r.yf.at[3], 3)
    ffn_sum_other()
    vector_sums_z()
    sum_mid(0, (0,))
    sum_core(1, (1,))
    z_add_sum(2, r.yf.at[0], 0)
    sum_mid(1, (0,))
    sum_last(1)
    ffn_sum_z()
    sum_mid(0, (1,))
    sum_last(0)
    vector_sums_x()
    sum_z(1)
    sum_z(0)
    ffn_end()
    flat_f()
    flat_sc(1, r.nice_c, r.out_c, 17)
    flat_sc(0, r.nice_s, r.out_s, 12)
    vector_sums_end()
    tail.wait_send()

    vectors = stack(r.total_v, 0)
    end = (f == 15, f == 15, f % 4 == 3)
    plain = lambda first: lambda i: 16 * (i % 6) + first + i // 6
    hidden = lambda i: 16 * (3 * (i // 12) + i % 3) + 10 + (i % 12) // 3
    none = -1
    count = jnp.where(w1, 24, 18)

    def from_vectors(g):
        if g < 2:
            return lambda i: jnp.where(jnp.logical_and(end[g], i < 30), plain(5 * g)(i), none)
        pick = lambda i: jnp.where(w1, hidden(i), plain(10)(i))
        return lambda i: jnp.where(jnp.logical_and(end[2], i < count), pick(i), none)

    def from_next(g):
        if g < 2:
            return lambda i: jnp.where(end[g], none, i)
        inside = jnp.logical_or(z == 1, z == 2)
        return lambda i: jnp.where(
            end[2], jnp.where(jnp.logical_and(inside, i >= count), i - count, none), i
        )

    for g, (fl, rows) in enumerate(((r.out_s, 1152), (r.out_c, 1632), (r.out_f, 4608))):
        arrived(r.after.at[g], r.head_r.at[g])
        tail = mm(one_hot((32, 96), from_vectors(g)), vectors) + mm(one_hot((32, 32), from_next(g)), r.after[g])
        fl[rows : rows + 32] = tail.astype(BF)

    drain(sent)


def layer(flat_s, flat_c, flat_f, lens, hid, feat, cot):
    vm = pl.BlockSpec(memory_space=pltpu.VMEM)
    return pl.pallas_call(
        layer_kernel,
        out_shape=(
            jax.ShapeDtypeStruct((128, D), BF),
            jax.ShapeDtypeStruct((128, D), BF),
            *[jax.ShapeDtypeStruct((n, 128), BF) for n in (1184, 1664, 4640)],
        ),
        in_specs=[vm] + [pl.BlockSpec(memory_space=pl.ANY)] * 2 + [pl.BlockSpec(memory_space=pltpu.SMEM)] + [pl.BlockSpec(memory_space=pl.ANY)] * 3,
        out_specs=[vm] * 5,
        scratch_shapes=list(scratch().values()),
        compiler_params=pltpu.CompilerParams(
            collective_id=0, has_side_effects=True, vmem_limit_bytes=VMEM_BYTES
        ),
    )(flat_s, flat_c, flat_f, lens, hid, feat, cot)


def per_device_fast(hidden, lengths, features, cotangent, self_params, cross_params, ffn_params):
    flats = [v.reshape(-1, 128) for v in (self_params, cross_params, ffn_params)]
    mixed, hgrad, *grads = layer(
        *flats, lengths, hidden.reshape(128, D), features, cotangent.reshape(128, D)
    )
    outs = [
        lax.dynamic_slice_in_dim(rows, back, flat.shape[0]).astype(F32).reshape(-1)
        for rows, back, flat in zip(grads, shift_back(), flats)
    ]
    return (mixed.reshape(2, 64, D), hgrad.reshape(2, 64, D), *outs)


def solution(mesh):
    fast = mesh.shape["dp"] == 2 and mesh.shape["fsdp"] == 16
    return jax.shard_map(
        per_device_fast if fast else per_device,
        mesh=mesh,
        in_specs=(
            P(("dp", "fsdp"), None, None),
            P(("dp", "fsdp")),
            P(("dp", "fsdp"), None, None),
            P(("dp", "fsdp"), None, None),
            P("fsdp"),
            P("fsdp"),
            P("fsdp"),
        ),
        out_specs=(
            P(("dp", "fsdp"), None, None),
            P(("dp", "fsdp"), None, None),
            P("fsdp"),
            P("fsdp"),
            P("fsdp"),
        ),
        check_vma=False,
    )
```
